32 devices in a mesh: groups: 2 (over y), tm: 8 (over z, x), height: 2 (over core).
Axes of the slice: x: 2, y: 2, z: 4, core: 2. Of those that a mesh axis runs over, the one named last changes fastest.
Arguments:
- video: bfloat16 [32, 8, 64, 256], P(('groups', 'tm'), 'height'), parts along dimension 0, may hold values from -6 to 6
- block_ids: int32 [32], P('groups'), parts along dimension 0, may hold values from 0 to 4, never falling along the last dimension, each value on 1 to 4 neighbouring positions
- conv_weight: bfloat16 [3, 3, 3, 256, 256], replicated, may hold values from -0.078125 to 0.078125
- w_query: bfloat16 [256, 256], replicated, may hold values from -4 to 4
- w_key: bfloat16 [256, 256], replicated, may hold values from -4 to 4
- w_value: bfloat16 [256, 256], replicated, may hold values from -0.375 to 0.375
- w_output: bfloat16 [256, 256], replicated, may hold values from -0.375 to 0.375
Outputs:
- encoded: bfloat16 [32, 8, 64, 256], P(('groups', 'tm'), 'height'), parts along dimension 0
The draws below stay inside these ranges and needn't reach their ends.
There are 2 independent parts, one for each index of `groups`. The reference program is written for one: setup_inputs(seed, part) draws one part's arguments, and reference() takes and returns one part's arrays. A program takes and returns all parts, laid end to end along the dimension named above; an argument that names none is the same for every part. Nothing has to cross between parts.
Inputs may be any that keep to these rules, and one draw needn't show every extreme that they name: `block_ids`: block ids never fall along the frames and start at 0; each block has 1 to 4 frames, and some block has exactly 4.
All inputs are finite; a program needn't handle non-finite values.
Results may differ from the reference program's by a relative error of at most 0.012.
Values may be sent and summed in bfloat16 or wider, within the bound.
No kernel may reach another device: no remote copies, remote signals or barrier semaphores. Data moves between devices by JAX's collectives and lax.ppermute only.
A program may use at most 64 MiB of HBM per device.

```python
import math
import jax
import jax.numpy as jnp
import numpy as np
from jax import lax

C = 256
HD = 64
BLOCK = 4
WIDTH = 64
FRAMES = 16
ROWS = 8
BLOCKS = 5


def pair_weights(key):
    base_key, noise_key = jax.random.split(jax.random.fold_in(key, 11), 2)
    keys_part = jax.random.truncated_normal(base_key, -2.0, 2.0, (C, C), jnp.float32) * C ** (-0.5)
    other = jax.random.truncated_normal(noise_key, -2.0, 2.0, (C, C), jnp.float32) * C ** (-0.5)
    return (keys_part, other)


def draw_w_key(key, part):
    keys_part, other = pair_weights(key)
    return keys_part.astype(jnp.bfloat16)


def draw_w_query(key, part):
    keys_part, other = pair_weights(key)
    return other.astype(jnp.bfloat16)


def shard_levels(own_key, extent, pieces, low, high):
    def one(axis_at, shards_of):
        steps = jax.random.uniform(jax.random.fold_in(jax.random.fold_in(own_key, 6), axis_at), (shards_of,), jnp.float32, low / len(pieces), high / len(pieces))
        return jnp.repeat(jnp.exp(steps), extent[axis_at] // shards_of).reshape((-1,) + (1,) * (len(extent) - axis_at - 1))

    level = one(*pieces[0])
    for cut in pieces[1:]:
        level = level * one(*cut)
    return level


def length_profile(amount, total, bound, slope):
    loads = [(1 << 20) // math.isqrt(grade ** slope) + 1 for grade in range(2, amount + 1)]
    rest, counts = total - bound - (amount - 1), [1] * (amount - 1)
    while rest > 0:
        free = [i for i in range(amount - 1) if counts[i] < bound]
        pool, budget = sum([loads[i] for i in free]), rest
        for i in free:
            addition = min(bound - counts[i], max(1, budget * loads[i] // pool), rest)
            counts[i] = counts[i] + addition
            rest = rest - addition
    return np.array([bound] + counts)


def ragged(stream_key, count, total, bound, lean):
    if count == 2:
        one = jax.random.randint(stream_key, (), max(1, total - bound), min(bound, total - 1) + 1)
        return jnp.stack([one, total - one])
    sizes = jnp.asarray(length_profile(count, total, bound, lean), jnp.int32)
    couples = (count - 1) // 2
    giver, receiver = sizes[1:1 + 2 * couples:2], sizes[2:2 + 2 * couples:2]
    slack = jnp.minimum(giver - 1, bound - receiver)
    moved = jax.random.randint(jax.random.fold_in(stream_key, 1), (couples,), 0, 1 << 20) % (slack + 1)
    sizes = sizes.at[1:1 + 2 * couples:2].set(giver - moved).at[2:2 + 2 * couples:2].set(receiver + moved)
    return sizes[jax.random.permutation(jax.random.fold_in(stream_key, 2), count)]


def gaussian(own_key, dims, spread, most, cuts=(), held_as=jnp.bfloat16):
    loudness = shard_levels(own_key, dims, cuts, -0.22, 0.18) if cuts else 1.0
    entries = jax.random.normal(own_key, dims, jnp.float32) * spread * loudness
    return jnp.minimum(jnp.maximum(entries, -most), most).astype(held_as)


def setup_inputs(seed: int = 0, part: int = 0) -> dict:
    splits = jax.random.split(jax.random.key(seed), 8)
    own_keys = jax.random.split(jax.random.fold_in(splits[7], part), 8)
    video = gaussian(own_keys[0], (FRAMES, ROWS, WIDTH, C), 1.0, 6.0, ((0, 8), (1, 2)))
    block_ids = jnp.searchsorted(jnp.cumsum(ragged(own_keys[1], BLOCKS, FRAMES, BLOCK, 1)), jnp.arange(FRAMES), side="right").astype(jnp.int32)
    conv_weight = gaussian(splits[2], (3, 3, 3, C, C), (27 * C) ** -0.5, 0.078125)
    w_query = draw_w_query(jax.random.fold_in(splits[7], 71), part)
    w_key = draw_w_key(jax.random.fold_in(splits[7], 71), part)
    w_value = gaussian(splits[5], (C, C), C ** -0.5, 0.375)
    w_output = gaussian(splits[6], (C, C), C ** -0.5, 0.375)
    return dict(video=video, block_ids=block_ids, conv_weight=conv_weight, w_query=w_query, w_key=w_key, w_value=w_value, w_output=w_output)


def normalize(values):
    wide = values.astype(jnp.float32)
    return wide * lax.rsqrt(lax.optimization_barrier(jnp.mean(wide * wide, axis=-1, keepdims=True)) + 1e-06)

def project(flat, weight):
    return jnp.dot(flat, weight, preferred_element_type=jnp.float32).astype(jnp.bfloat16)

def reference(video, block_ids, conv_weight, w_query, w_key, w_value, w_output):
    frames, rows, cols, chans = video.shape
    heads = chans // HD
    activated = jax.nn.silu(normalize(video)).astype(jnp.bfloat16)
    padded = jnp.pad(activated, ((2, 0), (1, 1), (1, 1), (0, 0)))
    total = jnp.zeros((frames * rows * cols, chans), jnp.float32)
    for tap_t in range(3):
        for tap_r in range(3):
            for tap_w in range(3):
                window = padded[tap_t:tap_t + frames, tap_r:tap_r + rows, tap_w:tap_w + cols].reshape(-1, chans)
                total = total + jnp.dot(window, conv_weight[tap_t, tap_r, tap_w], preferred_element_type=jnp.float32)
    hidden = (video.astype(jnp.float32) + total.reshape(video.shape)).astype(jnp.bfloat16)
    normed = normalize(hidden).astype(jnp.bfloat16).reshape(-1, chans)
    query = project(normed, w_query).reshape(frames, rows, cols, heads, HD)
    keys = project(normed, w_key).reshape(frames, rows, cols, heads, HD)
    values = project(normed, w_value).reshape(frames, rows, cols, heads, HD)
    order = jnp.arange(frames, dtype=jnp.int32)
    allowed = (order[None, :] <= order[:, None]) & (block_ids[None, :] >= block_ids[:, None] - 1)

    def one_row(packed):
        q_row, k_row, v_row = packed
        scores = jnp.einsum('fwhd,kwhd->whfk', q_row.astype(jnp.float32), k_row.astype(jnp.float32)) * HD ** (-0.5)
        scores = jnp.where(allowed[None, None], scores, -1e+30)
        top = lax.optimization_barrier(jnp.max(scores, axis=-1, keepdims=True))
        expo = jnp.exp(scores - top)
        weights = (expo / lax.optimization_barrier(jnp.sum(expo, axis=-1, keepdims=True))).astype(jnp.bfloat16)
        out = jnp.einsum('whfk,kwhd->fwhd', weights.astype(jnp.float32), v_row.astype(jnp.float32))
        return out.astype(jnp.bfloat16)
    attended = lax.map(one_row, (jnp.moveaxis(query, 1, 0), jnp.moveaxis(keys, 1, 0), jnp.moveaxis(values, 1, 0)))
    attended = jnp.moveaxis(attended, 0, 1).reshape(-1, chans)
    mixed = hidden.astype(jnp.float32).reshape(-1, chans) + jnp.dot(attended, w_output, preferred_element_type=jnp.float32)
    return mixed.astype(jnp.bfloat16).reshape(video.shape)
```

```python
import functools

import jax
import jax.numpy as jnp
import numpy as np
from jax import lax
from jax.experimental import pallas as pl
from jax.experimental.pallas import tpu as pltpu
from jax.sharding import Mesh, PartitionSpec as P

HD = 64
BLOCK = 4
TAPS = 3
REACH = 2 * BLOCK - 1 + TAPS - 1
LANES = 128
VMEM = 40 * 2**20

bf16, f32 = jnp.bfloat16, jnp.float32


def get(ref, start, size, stride):
    return jnp.concatenate([ref[i, pl.ds(start, size, stride=stride), :] for i in range(ref.shape[0])], axis=1)


def put(ref, start, size, stride, value):
    for i in range(ref.shape[0]):
        ref[i, pl.ds(start, size, stride=stride), :] = value[:, i * LANES : (i + 1) * LANES]


def fill(ref, value):
    for i in range(ref.shape[0]):
        ref[i] = value[:, i * LANES : (i + 1) * LANES]


def scratch(rows, chans):
    return pltpu.VMEM((chans // LANES, rows, LANES), f32)


def pack_kernel(video, out, wide):
    count, rows, cols, chans = video.shape
    lines = count * rows
    fill(wide, video[...].reshape(lines * cols, chans).astype(f32))
    chunks = out.shape[0]
    span = out.shape[1] // lines
    own = span - 2
    pieces = 16 // lines

    def column(w):
        if 0 <= w < cols:
            return get(wide, w, lines, cols)
        return jnp.zeros((lines, chans), f32)

    for d in range(chunks):
        for k in range(0, span, pieces):
            tile = jnp.concatenate([column(d * own - 1 + k + i) for i in range(pieces)], axis=0)
            out[d, pl.ds(k * lines, 16), :] = tile.astype(bf16)


def unpack_kernel(packed, out, wide):
    count, rows, cols, chans = out.shape
    lines = count * rows
    fill(wide, packed[...].reshape(lines * cols, chans).astype(f32))
    for t in range(count):
        for r in range(rows):
            out[t, r] = get(wide, t * rows + r, cols, lines).astype(bf16)


def rms(wide):
    return wide * lax.rsqrt(jnp.mean(wide * wide, axis=-1, keepdims=True) + 1e-06)


def main_kernel(
    count, rows, ids, video, conv_weight, w_query, w_key, w_value, w_output, out,
    vid, act, grid, res,
):
    sources, halves, _, chans = video.shape
    owners = out.shape[0]
    lines = count * rows
    span = video.shape[2] // lines
    own = span - 2
    high = halves * rows
    frames = sources * count
    heads = chans // HD
    step = halves * span * lines
    back = halves * own * lines

    xs = video[...].reshape(-1, chans).astype(f32)
    fill(vid, xs)
    normal = rms(xs)
    fill(act, normal / (1.0 + jnp.exp(-normal)))

    def pixel(ref, w, r):
        half, line = divmod(r, rows)
        return [
            get(ref, (half * span + w) * lines + t * rows + line, sources, step)
            for t in range(count)
        ]

    first = lax.broadcasted_iota(jnp.int32, (sources, chans), 0) == 0

    def earlier(x):
        return jnp.where(first, 0.0, pltpu.roll(x, 1, 0))

    zero = jnp.zeros((frames, TAPS * chans), bf16)
    for w in range(span):
        grid[w, 0] = zero
        grid[w, high + 1] = zero
        for r in range(high):
            now = pixel(act, w, r)
            past = [earlier(x) for x in now]
            ordered = past + now
            for a in range(TAPS):
                shift = TAPS - 1 - a
                picked = [ordered[count + t - shift] for t in range(count)]
                grid[w, r + 1, :, a * chans : (a + 1) * chans] = jnp.concatenate(picked, 0).astype(bf16)

    area = high * frames
    row_at = lax.broadcasted_iota(jnp.int32, (area, area), 0)
    col_at = lax.broadcasted_iota(jnp.int32, (area, area), 1)

    def frame_of(at):
        place = at % frames
        return (place % sources) * count + place // sources

    row_t, col_t = frame_of(row_at), frame_of(col_at)

    def block_of(t):
        found = jnp.zeros(t.shape, jnp.int32)
        for s in range(frames):
            found = jnp.where(t == s, ids[s], found)
        return found

    row_b, col_b = block_of(row_t), block_of(col_t)
    permit = (row_at // frames == col_at // frames) & (col_t <= row_t) & (col_b >= row_b - 1)
    head_of = lax.broadcasted_iota(jnp.int32, (area, chans), 1) // HD

    for w in range(own):
        total = jnp.zeros((area, chans), f32)
        for e in range(TAPS):
            for b in range(TAPS):
                window = grid[w + e, b : b + high].reshape(area, TAPS * chans)
                weight = jnp.concatenate([conv_weight[a, b, e] for a in range(TAPS)], axis=0)
                total = total + jnp.dot(window, weight, preferred_element_type=f32)
        shown = jnp.concatenate([x for r in range(high) for x in pixel(vid, w + 1, r)], axis=0)
        hidden = (shown + total).astype(bf16).astype(f32)
        normed = rms(hidden).astype(bf16)
        query = jnp.dot(normed, w_query[...], preferred_element_type=f32).astype(bf16)
        keys = jnp.dot(normed, w_key[...], preferred_element_type=f32).astype(bf16)
        values = jnp.dot(normed, w_value[...], preferred_element_type=f32).astype(bf16)
        attended = jnp.zeros((area, chans), f32)
        for h in range(heads):
            single = jnp.where(head_of == h, query, jnp.zeros((), bf16))
            scores = lax.dot_general(single, keys, (((1,), (1,)), ((), ())), preferred_element_type=f32)
            scores = jnp.where(permit, scores * HD ** (-0.5), -1e30)
            expo = jnp.exp(scores - jnp.max(scores, axis=-1, keepdims=True))
            weights = (expo / jnp.sum(expo, axis=-1, keepdims=True)).astype(bf16)
            mixed = jnp.dot(weights, values, preferred_element_type=f32)
            attended = jnp.where(head_of == h, mixed, attended)
        encoded = hidden + jnp.dot(attended.astype(bf16), w_output[...], preferred_element_type=f32)
        for r in range(high):
            half, line = divmod(r, rows)
            for t in range(count):
                start = (r * count + t + 1) * sources - owners
                place = (half * own + w) * lines + t * rows + line
                put(res, place, owners, back, encoded[start : start + owners])
    done = jnp.concatenate([res[i] for i in range(res.shape[0])], axis=1)
    out[...] = done.astype(bf16).reshape(out.shape)


def per_device(outer, video, block_ids, conv_weight, w_query, w_key, w_value, w_output):
    count, rows, cols, chans = video.shape
    group, halves = lax.axis_size("tm"), lax.axis_size("height")
    chunks = group * halves
    own = cols // chunks
    span = own + 2
    lines = count * rows
    whole = pl.BlockSpec(memory_space=pltpu.VMEM)
    params = pltpu.CompilerParams(vmem_limit_bytes=VMEM)

    packed = pl.pallas_call(
        pack_kernel,
        out_shape=jax.ShapeDtypeStruct((chunks, span * lines, chans), bf16),
        in_specs=[whole],
        out_specs=whole,
        scratch_shapes=[scratch(lines * cols, chans)],
        compiler_params=params,
    )(video)
    piece = lax.all_to_all(packed, ("tm", "height"), split_axis=0, concat_axis=0, tiled=True)
    piece = piece.reshape(group, halves, span * lines, chans)
    ids = block_ids
    if outer > 1:
        before = lax.ppermute(piece, "outer", [(i, i + 1) for i in range(outer - 1)])
        piece = jnp.concatenate([before, piece], axis=0)
        ids = jnp.concatenate([jnp.full((group * count,), -2, jnp.int32), ids])
        ids = lax.dynamic_slice(ids, (lax.axis_index("outer") * group * count,), (2 * group * count,))
    sources = piece.shape[0]
    frames = sources * count
    done = pl.pallas_call(
        functools.partial(main_kernel, count, rows),
        out_shape=jax.ShapeDtypeStruct((group, halves, own * lines, chans), bf16),
        in_specs=[pl.BlockSpec(memory_space=pltpu.SMEM)] + [whole] * 6,
        out_specs=whole,
        scratch_shapes=[
            scratch(sources * halves * span * lines, chans),
            scratch(sources * halves * span * lines, chans),
            pltpu.VMEM((span, halves * rows + 2, frames, TAPS * chans), bf16),
            scratch(chunks * own * lines, chans),
        ],
        compiler_params=params,
    )(ids, piece, conv_weight, w_query, w_key, w_value, w_output)
    done = done.reshape(chunks, own * lines, chans)
    returned = lax.all_to_all(done, ("tm", "height"), split_axis=0, concat_axis=0, tiled=True)
    return pl.pallas_call(
        unpack_kernel,
        out_shape=jax.ShapeDtypeStruct(video.shape, bf16),
        in_specs=[whole],
        out_specs=whole,
        scratch_shapes=[scratch(lines * cols, chans)],
        compiler_params=params,
    )(returned)


def solution(mesh):
    parts, along, halves = (mesh.shape[a] for a in ("groups", "tm", "height"))

    def run(video, *rest):
        count = video.shape[0] // (parts * along)
        group = min(g for g in range(1, along + 1) if along % g == 0 and (g * count >= REACH or g == along))
        outer = along // group
        split = Mesh(
            np.asarray(mesh.devices).reshape(parts, outer, group, halves),
            ("groups", "outer", "tm", "height"),
        )
        spec = P(("groups", "outer", "tm"), "height", None, None)
        placed = (spec, P("groups"), P(), P(), P(), P(), P())
        return jax.shard_map(
            functools.partial(per_device, outer),
            mesh=split,
            in_specs=placed,
            out_specs=spec,
            check_vma=False,
        )(video, *rest)

    return run
```

```python
import functools

import jax
import jax.numpy as jnp
import numpy as np
from jax import lax
from jax.experimental import pallas as pl
from jax.experimental.pallas import tpu as pltpu
from jax.sharding import Mesh, PartitionSpec as P

HD = 64
BLOCK = 4
TAPS = 3
REACH = 2 * BLOCK - 1 + TAPS - 1
LANES = 128
VMEM = 40 * 2**20

bf16, f32 = jnp.bfloat16, jnp.float32


def get(ref, start, size, stride):
    return jnp.concatenate([ref[i, pl.ds(start, size, stride=stride), :] for i in range(ref.shape[0])], axis=1)


def put(ref, start, size, stride, value):
    for i in range(ref.shape[0]):
        ref[i, pl.ds(start, size, stride=stride), :] = value[:, i * LANES : (i + 1) * LANES]


def fill(ref, value):
    for i in range(ref.shape[0]):
        ref[i] = value[:, i * LANES : (i + 1) * LANES]


def scratch(rows, chans):
    return pltpu.VMEM((chans // LANES, rows, LANES), f32)


def pack_kernel(video, out, local, wide, sems):
    count, rows, cols, chans = video.shape
    lines = count * rows
    copies = []
    for t in range(count):
        for r in range(rows):
            copy = pltpu.make_async_copy(video.at[t, r], local.at[t, r], sems.at[t * rows + r])
            copy.start()
            copies.append(copy)
    for at, copy in enumerate(copies):
        copy.wait()
        for i in range(wide.shape[0]):
            wide[i, pl.ds(at * cols, cols), :] = local[at // rows, at % rows, :, i * LANES : (i + 1) * LANES].astype(f32)
    chunks = out.shape[0]
    span = out.shape[1] // lines
    own = span - 2
    pieces = 16 // lines

    def column(w):
        if 0 <= w < cols:
            return get(wide, w, lines, cols)
        return jnp.zeros((lines, chans), f32)

    for d in range(chunks):
        for k in range(0, span, pieces):
            tile = jnp.concatenate([column(d * own - 1 + k + i) for i in range(pieces)], axis=0)
            out[d, pl.ds(k * lines, 16), :] = tile.astype(bf16)


def unpack_kernel(packed, out, local, wide, sems):
    count, rows, cols, chans = out.shape
    lines = count * rows
    fill(wide, packed[...].reshape(lines * cols, chans).astype(f32))
    copies = []
    for t in range(count):
        for r in range(rows):
            local[t, r] = get(wide, t * rows + r, cols, lines).astype(bf16)
            copy = pltpu.make_async_copy(local.at[t, r], out.at[t, r], sems.at[t * rows + r])
            copy.start()
            copies.append(copy)
    for copy in copies:
        copy.wait()


def rms(wide):
    return wide * lax.rsqrt(jnp.mean(wide * wide, axis=-1, keepdims=True) + 1e-06)


def divided(at, by):
    if by & (by - 1) == 0:
        bits = by.bit_length() - 1
        return at >> bits, at & (by - 1)
    return lax.div(at, jnp.int32(by)), lax.rem(at, jnp.int32(by))


def main_kernel(
    count, rows, ids_far, video, conv_far, query_far, key_far, value_far, output_far, out,
    ids, conv_weight, w_query, w_key, w_value, w_output, vid, act, grid, total, shown, res, conv_sems, sems,
):
    taps = [pltpu.make_async_copy(conv_far.at[:, b], conv_weight.at[:, b], conv_sems.at[b]) for b in range(TAPS)]
    near = (ids, w_query, w_key, w_value, w_output)
    far = (ids_far, query_far, key_far, value_far, output_far)
    others = [pltpu.make_async_copy(src, dst, sems.at[i]) for i, (src, dst) in enumerate(zip(far, near))]
    for copy in taps + others:
        copy.start()

    sources, halves, _, chans = video.shape
    owners = out.shape[0]
    lines = count * rows
    span = video.shape[2] // lines
    own = span - 2
    high = halves * rows
    frames = sources * count
    heads = chans // HD
    step = halves * span * lines
    back = halves * own * lines
    area = high * frames

    xs = video[...].reshape(-1, chans).astype(f32)
    fill(vid, xs)
    normal = rms(xs)
    fill(act, normal / (1.0 + jnp.exp(-normal)))

    def pixel(ref, w, r):
        half, line = divmod(r, rows)
        return [
            get(ref, (half * span + w) * lines + t * rows + line, sources, step) for t in range(count)
        ]

    first = lax.broadcasted_iota(jnp.int32, (sources, chans), 0) == 0

    def earlier(x):
        return jnp.where(first, 0.0, pltpu.roll(x, 1, 0))

    zero = jnp.zeros((frames, TAPS * chans), bf16)
    for w in range(span):
        grid[w, 0] = zero
        grid[w, high + 1] = zero
        for r in range(high):
            now = pixel(act, w, r)
            past = [earlier(x) for x in now]
            ordered = past + now
            for a in range(TAPS):
                shift = TAPS - 1 - a
                picked = [ordered[count + t - shift] for t in range(count)]
                grid[w, r + 1, :, a * chans : (a + 1) * chans] = jnp.concatenate(picked, 0).astype(bf16)
            if 1 <= w <= own:
                place = ((w - 1) * high + r) * frames
                shown[pl.ds(place, frames), :] = jnp.concatenate(pixel(vid, w, r), 0)

    others[0].wait()

    def frame_and_block(shape, dim):
        inner, source = divided(lax.broadcasted_iota(jnp.int32, shape, dim), sources)
        frame = source * count + inner
        block = jnp.zeros(shape, jnp.int32)
        for s in range(frames):
            block = jnp.where(frame == s, ids[s], block)
        return frame, block

    row_t, row_b = (jnp.concatenate([x] * high, 0) for x in frame_and_block((frames, area), 0))
    wrap = divided(lax.broadcasted_iota(jnp.int32, (1, area), 1), frames)[1]
    col_inner, col_source = divided(wrap, sources)
    col_t = col_source * count + col_inner
    col_b = jnp.zeros((1, area), jnp.int32)
    for s in range(frames):
        col_b = jnp.where(col_t == s, ids[s], col_b)
    row_p = divided(lax.broadcasted_iota(jnp.int32, (area, area), 0), frames)[0]
    col_p = divided(lax.broadcasted_iota(jnp.int32, (area, area), 1), frames)[0]
    permit = (row_p == col_p) & (col_t <= row_t) & (col_b >= row_b - 1)
    bias = jnp.where(permit, 0.0, -1e30)
    head_of = lax.broadcasted_iota(jnp.int32, (area, chans), 1) // HD

    for b in range(TAPS):
        taps[b].wait()
        for e in range(TAPS):
            window = grid[e : e + own, b : b + high].reshape(own * area, TAPS * chans)
            weight = jnp.concatenate([conv_weight[a, b, e] for a in range(TAPS)], axis=0)
            part = jnp.dot(window, weight, preferred_element_type=f32)
            total[...] = part if b == e == 0 else total[...] + part

    hidden = (shown[...] + total[...]).astype(bf16).astype(f32)
    shown[...] = hidden
    normed = rms(hidden).astype(bf16)
    for copy in others[1:]:
        copy.wait()
    query, keys, values = (
        jnp.dot(normed, weight[...], preferred_element_type=f32).astype(bf16) for weight in (w_query, w_key, w_value)
    )
    gone = []
    for w in range(own):
        part = slice(w * area, (w + 1) * area)
        single = jnp.concatenate(
            [jnp.where(head_of == h, query[part], jnp.zeros((), bf16)) for h in range(heads)], axis=0
        )
        scores = lax.dot_general(single, keys[part], (((1,), (1,)), ((), ())), preferred_element_type=f32)
        scores = scores * HD ** (-0.5) + jnp.concatenate([bias] * heads, axis=0)
        expo = jnp.exp(scores - jnp.max(scores, axis=-1, keepdims=True))
        weights = (expo * (1.0 / jnp.sum(expo, axis=-1, keepdims=True))).astype(bf16)
        mixed = jnp.dot(weights, values[part], preferred_element_type=f32)
        attended = mixed[:area]
        for h in range(1, heads):
            attended = jnp.where(head_of == h, mixed[h * area : (h + 1) * area], attended)
        gone.append(attended.astype(bf16))
    attended = jnp.concatenate(gone, axis=0)
    encoded = shown[...] + jnp.dot(attended, w_output[...], preferred_element_type=f32)
    for w in range(own):
        for r in range(high):
            half, line = divmod(r, rows)
            for t in range(count):
                start = ((w * high + r) * count + t + 1) * sources - owners
                place = (half * own + w) * lines + t * rows + line
                put(res, place, owners, back, encoded[start : start + owners])
    done = jnp.concatenate([res[i] for i in range(res.shape[0])], axis=1)
    out[...] = done.astype(bf16).reshape(out.shape)


def per_device(outer, video, block_ids, conv_weight, w_query, w_key, w_value, w_output):
    count, rows, cols, chans = video.shape
    group, halves = lax.axis_size("tm"), lax.axis_size("height")
    chunks = group * halves
    own = cols // chunks
    span = own + 2
    lines = count * rows
    whole = pl.BlockSpec(memory_space=pltpu.VMEM)
    far = pl.BlockSpec(memory_space=pl.ANY)
    params = pltpu.CompilerParams(vmem_limit_bytes=VMEM)

    packed = pl.pallas_call(
        pack_kernel,
        out_shape=jax.ShapeDtypeStruct((chunks, span * lines, chans), bf16),
        in_specs=[far],
        out_specs=whole,
        scratch_shapes=[
            pltpu.VMEM(video.shape, bf16),
            scratch(lines * cols, chans),
            pltpu.SemaphoreType.DMA((lines,)),
        ],
        compiler_params=params,
    )(video)
    piece = lax.all_to_all(packed, ("tm", "height"), split_axis=0, concat_axis=0, tiled=True)
    piece = piece.reshape(group, halves, span * lines, chans)
    ids = block_ids
    if outer > 1:
        before = lax.ppermute(piece, "outer", [(i, i + 1) for i in range(outer - 1)])
        piece = jnp.concatenate([before, piece], axis=0)
        ids = jnp.concatenate([jnp.full((group * count,), -2, jnp.int32), ids])
        ids = lax.dynamic_slice(ids, (lax.axis_index("outer") * group * count,), (2 * group * count,))
    sources = piece.shape[0]
    frames = sources * count
    done = pl.pallas_call(
        functools.partial(main_kernel, count, rows),
        out_shape=jax.ShapeDtypeStruct((group, halves, own * lines, chans), bf16),
        in_specs=[far, whole] + [far] * 5,
        out_specs=whole,
        scratch_shapes=[
            pltpu.SMEM((frames,), jnp.int32),
            pltpu.VMEM(conv_weight.shape, bf16),
        ]
        + [pltpu.VMEM((chans, chans), bf16)] * 4
        + [scratch(sources * halves * span * lines, chans)] * 2
        + [
            pltpu.VMEM((span, halves * rows + 2, frames, TAPS * chans), bf16),
            pltpu.VMEM((own * halves * rows * frames, chans), f32),
            pltpu.VMEM((own * halves * rows * frames, chans), f32),
            scratch(chunks * own * lines, chans),
            pltpu.SemaphoreType.DMA((TAPS,)),
            pltpu.SemaphoreType.DMA((5,)),
        ],
        compiler_params=params,
    )(ids, piece, conv_weight, w_query, w_key, w_value, w_output)
    done = done.reshape(chunks, own * lines, chans)
    returned = lax.all_to_all(done, ("tm", "height"), split_axis=0, concat_axis=0, tiled=True)
    return pl.pallas_call(
        unpack_kernel,
        out_shape=jax.ShapeDtypeStruct(video.shape, bf16),
        in_specs=[whole],
        out_specs=far,
        scratch_shapes=[
            pltpu.VMEM(video.shape, bf16),
            scratch(lines * cols, chans),
            pltpu.SemaphoreType.DMA((lines,)),
        ],
        compiler_params=params,
    )(returned)


def solution(mesh):
    parts, along, halves = (mesh.shape[a] for a in ("groups", "tm", "height"))

    def run(video, *rest):
        count = video.shape[0] // (parts * along)
        group = min(g for g in range(1, along + 1) if along % g == 0 and (g * count >= REACH or g == along))
        outer = along // group
        split = Mesh(
            np.asarray(mesh.devices).reshape(parts, outer, group, halves),
            ("groups", "outer", "tm", "height"),
        )
        spec = P(("groups", "outer", "tm"), "height", None, None)
        placed = (spec, P("groups"), P(), P(), P(), P(), P())
        return jax.shard_map(
            functools.partial(per_device, outer),
            mesh=split,
            in_specs=placed,
            out_specs=spec,
            check_vma=False,
        )(video, *rest)

    return run
```

```python
import functools

import jax
import jax.numpy as jnp
import numpy as np
from jax import lax
from jax.experimental import pallas as pl
from jax.experimental.pallas import tpu as pltpu
from jax.sharding import Mesh, PartitionSpec as P

HD = 64
BLOCK = 4
TAPS = 3
REACH = 2 * BLOCK - 1 + TAPS - 1
LANES = 128
VMEM = 40 * 2**20

bf16, f32 = jnp.bfloat16, jnp.float32


def get(ref, start, size, stride):
    return jnp.concatenate([ref[i, pl.ds(start, size, stride=stride), :] for i in range(ref.shape[0])], axis=1)


def put(ref, start, size, stride, value):
    for i in range(ref.shape[0]):
        ref[i, pl.ds(start, size, stride=stride), :] = value[:, i * LANES : (i + 1) * LANES]


def fill(ref, value):
    for i in range(ref.shape[0]):
        ref[i] = value[:, i * LANES : (i + 1) * LANES]


def scratch(rows, chans):
    return pltpu.VMEM((chans // LANES, rows, LANES), f32)


def pack_kernel(video, out, local, wide, sems):
    count, rows, cols, chans = video.shape
    lines = count * rows
    copies = []
    for t in range(count):
        for r in range(rows):
            copy = pltpu.make_async_copy(video.at[t, r], local.at[t, r], sems.at[t * rows + r])
            copy.start()
            copies.append(copy)
    for at, copy in enumerate(copies):
        copy.wait()
        for i in range(wide.shape[0]):
            wide[i, pl.ds(at * cols, cols), :] = local[at // rows, at % rows, :, i * LANES : (i + 1) * LANES].astype(f32)
    chunks = out.shape[0]
    span = out.shape[1] // lines
    own = span - 2
    pieces = 16 // lines

    def column(w):
        if 0 <= w < cols:
            return get(wide, w, lines, cols)
        return jnp.zeros((lines, chans), f32)

    for d in range(chunks):
        for k in range(0, span, pieces):
            tile = jnp.concatenate([column(d * own - 1 + k + i) for i in range(pieces)], axis=0)
            out[d, pl.ds(k * lines, 16), :] = tile.astype(bf16)


def unpack_kernel(packed, out, local, wide, sems):
    count, rows, cols, chans = out.shape
    lines = count * rows
    fill(wide, packed[...].reshape(lines * cols, chans).astype(f32))
    copies = []
    for t in range(count):
        for r in range(rows):
            local[t, r] = get(wide, t * rows + r, cols, lines).astype(bf16)
            copy = pltpu.make_async_copy(local.at[t, r], out.at[t, r], sems.at[t * rows + r])
            copy.start()
            copies.append(copy)
    for copy in copies:
        copy.wait()


def rms(wide):
    return wide * lax.rsqrt(jnp.mean(wide * wide, axis=-1, keepdims=True) + 1e-06)


def divided(at, by):
    if by & (by - 1) == 0:
        bits = by.bit_length() - 1
        return at >> bits, at & (by - 1)
    return lax.div(at, jnp.int32(by)), lax.rem(at, jnp.int32(by))


def main_kernel(
    count, rows, ids_far, video, conv_far, query_far, key_far, value_far, output_far, out,
    ids, conv_weight, w_query, w_key, w_value, w_output, vid, act, grid, total, shown, res, conv_sems, sems,
):
    taps = [pltpu.make_async_copy(conv_far.at[:, b], conv_weight.at[:, b], conv_sems.at[b]) for b in range(TAPS)]
    near = (ids, w_query, w_key, w_value, w_output)
    far = (ids_far, query_far, key_far, value_far, output_far)
    others = [pltpu.make_async_copy(src, dst, sems.at[i]) for i, (src, dst) in enumerate(zip(far, near))]
    for copy in taps + others:
        copy.start()

    sources, halves, _, chans = video.shape
    owners = out.shape[0]
    lines = count * rows
    span = video.shape[2] // lines
    own = span - 2
    high = halves * rows
    frames = sources * count
    heads = chans // HD
    step = halves * span * lines
    back = halves * own * lines
    area = high * frames

    xs = video[...].reshape(-1, chans).astype(f32)
    fill(vid, xs)
    normal = rms(xs)
    fill(act, normal / (1.0 + jnp.exp(-normal)))

    def pixel(ref, w, r):
        half, line = divmod(r, rows)
        return [
            get(ref, (half * span + w) * lines + t * rows + line, sources, step) for t in range(count)
        ]

    first = lax.broadcasted_iota(jnp.int32, (sources, chans), 0) == 0

    def earlier(x):
        return jnp.where(first, 0.0, pltpu.roll(x, 1, 0))

    zero = jnp.zeros((frames, TAPS * chans), bf16)
    for w in range(span):
        grid[w, 0] = zero
        grid[w, high + 1] = zero
        for r in range(high):
            now = pixel(act, w, r)
            past = [earlier(x) for x in now]
            ordered = past + now
            for a in range(TAPS):
                shift = TAPS - 1 - a
                picked = [ordered[count + t - shift] for t in range(count)]
                grid[w, r + 1, :, a * chans : (a + 1) * chans] = jnp.concatenate(picked, 0).astype(bf16)
            if 1 <= w <= own:
                place = ((w - 1) * high + r) * frames
                shown[pl.ds(place, frames), :] = jnp.concatenate(pixel(vid, w, r), 0)

    others[0].wait()

    def frame_and_block(shape, dim):
        inner, source = divided(lax.broadcasted_iota(jnp.int32, shape, dim), sources)
        frame = source * count + inner
        block = jnp.zeros(shape, jnp.int32)
        for s in range(frames):
            block = jnp.where(frame == s, ids[s], block)
        return frame, block

    row_t, row_b = (jnp.concatenate([x] * high, 0) for x in frame_and_block((frames, area), 0))
    wrap = divided(lax.broadcasted_iota(jnp.int32, (1, area), 1), frames)[1]
    col_inner, col_source = divided(wrap, sources)
    col_t = col_source * count + col_inner
    col_b = jnp.zeros((1, area), jnp.int32)
    for s in range(frames):
        col_b = jnp.where(col_t == s, ids[s], col_b)
    row_p = divided(lax.broadcasted_iota(jnp.int32, (area, area), 0), frames)[0]
    col_p = divided(lax.broadcasted_iota(jnp.int32, (area, area), 1), frames)[0]
    permit = (row_p == col_p) & (col_t <= row_t) & (col_b >= row_b - 1)
    bias = jnp.where(permit, 0.0, -1e30)
    head_of = lax.broadcasted_iota(jnp.int32, (area, chans), 1) // HD

    for b in range(TAPS):
        taps[b].wait()
        for e in range(TAPS):
            window = grid[e : e + own, b : b + high].reshape(own * area, TAPS * chans)
            weight = jnp.concatenate([conv_weight[a, b, e] for a in range(TAPS)], axis=0)
            part = jnp.dot(window, weight, preferred_element_type=f32)
            total[...] = part if b == e == 0 else total[...] + part

    hidden = (shown[...] + total[...]).astype(bf16).astype(f32)
    shown[...] = hidden
    normed = rms(hidden).astype(bf16)
    for copy in others[1:]:
        copy.wait()
    query, keys, values = (
        jnp.dot(normed, weight[...], preferred_element_type=f32).astype(bf16) for weight in (w_query, w_key, w_value)
    )
    gone = []
    for w in range(own):
        part = slice(w * area, (w + 1) * area)
        single = jnp.concatenate(
            [jnp.where(head_of == h, query[part], jnp.zeros((), bf16)) for h in range(heads)], axis=0
        )
        scores = lax.dot_general(single, keys[part], (((1,), (1,)), ((), ())), preferred_element_type=f32)
        scores = scores * HD ** (-0.5) + jnp.concatenate([bias] * heads, axis=0)
        expo = jnp.exp(scores - jnp.max(scores, axis=-1, keepdims=True))
        weights = (expo * (1.0 / jnp.sum(expo, axis=-1, keepdims=True))).astype(bf16)
        mixed = jnp.dot(weights, values[part], preferred_element_type=f32)
        attended = mixed[:area]
        for h in range(1, heads):
            attended = jnp.where(head_of == h, mixed[h * area : (h + 1) * area], attended)
        gone.append(attended.astype(bf16))
    attended = jnp.concatenate(gone, axis=0)
    encoded = shown[...] + jnp.dot(attended, w_output[...], preferred_element_type=f32)
    for w in range(own):
        for r in range(high):
            half, line = divmod(r, rows)
            for t in range(count):
                start = ((w * high + r) * count + t + 1) * sources - owners
                place = (half * own + w) * lines + t * rows + line
                put(res, place, owners, back, encoded[start : start + owners])
    done = jnp.concatenate([res[i] for i in range(res.shape[0])], axis=1)
    out[...] = done.astype(bf16).reshape(out.shape)


def per_device(outer, video, block_ids, conv_weight, w_query, w_key, w_value, w_output):
    count, rows, cols, chans = video.shape
    group, halves = lax.axis_size("tm"), lax.axis_size("height")
    chunks = group * halves
    own = cols // chunks
    span = own + 2
    lines = count * rows
    whole = pl.BlockSpec(memory_space=pltpu.VMEM)
    far = pl.BlockSpec(memory_space=pltpu.HBM)
    params = pltpu.CompilerParams(vmem_limit_bytes=VMEM)
    video, conv_weight, w_query, w_key, w_value, w_output = (
        pltpu.with_memory_space_constraint(x, pltpu.HBM)
        for x in (video, conv_weight, w_query, w_key, w_value, w_output)
    )

    packed = pl.pallas_call(
        pack_kernel,
        out_shape=jax.ShapeDtypeStruct((chunks, span * lines, chans), bf16),
        in_specs=[far],
        out_specs=whole,
        scratch_shapes=[
            pltpu.VMEM(video.shape, bf16),
            scratch(lines * cols, chans),
            pltpu.SemaphoreType.DMA((lines,)),
        ],
        compiler_params=params,
    )(video)
    piece = lax.all_to_all(packed, ("tm", "height"), split_axis=0, concat_axis=0, tiled=True)
    piece = piece.reshape(group, halves, span * lines, chans)
    ids = block_ids
    if outer > 1:
        before = lax.ppermute(piece, "outer", [(i, i + 1) for i in range(outer - 1)])
        piece = jnp.concatenate([before, piece], axis=0)
        ids = jnp.concatenate([jnp.full((group * count,), -2, jnp.int32), ids])
        ids = lax.dynamic_slice(ids, (lax.axis_index("outer") * group * count,), (2 * group * count,))
    ids = pltpu.with_memory_space_constraint(ids, pltpu.HBM)
    sources = piece.shape[0]
    frames = sources * count
    done = pl.pallas_call(
        functools.partial(main_kernel, count, rows),
        out_shape=jax.ShapeDtypeStruct((group, halves, own * lines, chans), bf16),
        in_specs=[far, whole] + [far] * 5,
        out_specs=whole,
        scratch_shapes=[
            pltpu.SMEM((frames,), jnp.int32),
            pltpu.VMEM(conv_weight.shape, bf16),
        ]
        + [pltpu.VMEM((chans, chans), bf16)] * 4
        + [scratch(sources * halves * span * lines, chans)] * 2
        + [
            pltpu.VMEM((span, halves * rows + 2, frames, TAPS * chans), bf16),
            pltpu.VMEM((own * halves * rows * frames, chans), f32),
            pltpu.VMEM((own * halves * rows * frames, chans), f32),
            scratch(chunks * own * lines, chans),
            pltpu.SemaphoreType.DMA((TAPS,)),
            pltpu.SemaphoreType.DMA((5,)),
        ],
        compiler_params=params,
    )(ids, piece, conv_weight, w_query, w_key, w_value, w_output)
    done = done.reshape(chunks, own * lines, chans)
    returned = lax.all_to_all(done, ("tm", "height"), split_axis=0, concat_axis=0, tiled=True)
    return pl.pallas_call(
        unpack_kernel,
        out_shape=jax.ShapeDtypeStruct(video.shape, bf16),
        in_specs=[whole],
        out_specs=far,
        scratch_shapes=[
            pltpu.VMEM(video.shape, bf16),
            scratch(lines * cols, chans),
            pltpu.SemaphoreType.DMA((lines,)),
        ],
        compiler_params=params,
    )(returned)


def solution(mesh):
    parts, along, halves = (mesh.shape[a] for a in ("groups", "tm", "height"))

    def run(video, *rest):
        count = video.shape[0] // (parts * along)
        group = min(g for g in range(1, along + 1) if along % g == 0 and (g * count >= REACH or g == along))
        outer = along // group
        split = Mesh(
            np.asarray(mesh.devices).reshape(parts, outer, group, halves),
            ("groups", "outer", "tm", "height"),
        )
        spec = P(("groups", "outer", "tm"), "height", None, None)
        placed = (spec, P("groups"), P(), P(), P(), P(), P())
        return jax.shard_map(
            functools.partial(per_device, outer),
            mesh=split,
            in_specs=placed,
            out_specs=spec,
            check_vma=False,
        )(video, *rest)

    return run
```

```python
import functools

import jax
import jax.numpy as jnp
import numpy as np
from jax import lax
from jax.experimental import pallas as pl
from jax.experimental.pallas import tpu as pltpu
from jax.sharding import Mesh, PartitionSpec as P

HD = 64
BLOCK = 4
TAPS = 3
REACH = 2 * BLOCK - 1 + TAPS - 1
LANES = 128
EDGE = 8
VMEM = 28 * 2**20

bf16, f32 = jnp.bfloat16, jnp.float32


def get(ref, start, size, stride):
    return jnp.concatenate([ref[i, pl.ds(start, size, stride=stride), :] for i in range(ref.shape[0])], axis=1)


def put(ref, start, size, stride, value):
    for i in range(ref.shape[0]):
        ref[i, pl.ds(start, size, stride=stride), :] = value[:, i * LANES : (i + 1) * LANES]


def fill(ref, start, value):
    for i in range(ref.shape[0]):
        ref[i, pl.ds(start, value.shape[0]), :] = value[:, i * LANES : (i + 1) * LANES]


def scratch(rows, chans):
    return pltpu.VMEM((chans // LANES, rows, LANES), f32)


def partner(me, k, group):
    return me ^ k if group & (group - 1) == 0 else (k - me) % group


def rms(wide):
    return wide * lax.rsqrt(jnp.mean(wide * wide, axis=-1, keepdims=True) + 1e-06)


def divided(at, by):
    if by & (by - 1) == 0:
        bits = by.bit_length() - 1
        return at >> bits, at & (by - 1)
    return lax.div(at, jnp.int32(by)), lax.rem(at, jnp.int32(by))


def pack_kernel(group, video, *refs):
    blocks, (local, wide, sems) = refs[:group], refs[group:]
    count, rows, cols, chans = video.shape
    lines = count * rows
    stride = cols + 2 * EDGE
    own = cols // group
    span = own + 2
    copies = []
    for at in range(lines):
        place = (at // rows, at % rows)
        copy = pltpu.make_async_copy(video.at[place], local.at[place], sems.at[at])
        copy.start()
        copies.append(copy)
    nothing = jnp.zeros((EDGE, chans), f32)
    for at in range(lines):
        fill(wide, at * stride, nothing)
        fill(wide, at * stride + EDGE + cols, nothing)
    for at, copy in enumerate(copies):
        copy.wait()
        fill(wide, at * stride + EDGE, local[at // rows, at % rows].astype(f32))
    me = lax.axis_index("tm")
    together = 16 // lines
    for k in range(group):
        start = partner(me, k, group) * own + EDGE - 1
        for w in range(0, span, together):
            tile = jnp.concatenate([get(wide, start + w + i, lines, stride) for i in range(together)], axis=0)
            blocks[k][pl.ds(w * lines, 16), :] = tile.astype(bf16)


def shift_kernel(count, rows, group, before, *refs):
    blocks, refs = refs[:group], refs[group:]
    past, refs = (refs[0], refs[1:]) if before else (None, refs)
    far, refs = refs[:5], refs[5:]
    grid, edge, shown, refs = refs[0], refs[1], refs[2], refs[3:]
    near, (vid, act, sems) = refs[:5], refs[5:]
    copies = [pltpu.make_async_copy(src, dst, sems.at[i]) for i, (src, dst) in enumerate(zip(far, near))]
    for copy in copies:
        copy.start()
    step, chans = blocks[0].shape
    lines = count * rows
    span = step // lines
    own = span - 2
    frames = grid.shape[2]
    sources = frames // count
    me = lax.axis_index("tm")

    def take(block, source):
        start = pl.multiple_of(source * step, 16)
        wide = block.astype(f32)
        fill(vid, start, wide)
        normal = rms(wide)
        fill(act, start, normal / (1.0 + jnp.exp(-normal)))

    for k in range(group):
        source = partner(me, k, group)
        take(blocks[k][...], source + sources - group)
        if before:
            take(past[k], source)

    def pixel(ref, w, r):
        return [get(ref, w * lines + t * rows + r, sources, step) for t in range(count)]

    first = lax.broadcasted_iota(jnp.int32, (sources, chans), 0) == 0

    def earlier(x):
        return jnp.where(first, 0.0, pltpu.roll(x, 1, 0))

    for w in range(span):
        for r in range(rows):
            now = pixel(act, w, r)
            ordered = [earlier(x) for x in now] + now
            for a in range(TAPS):
                shift = TAPS - 1 - a
                picked = [ordered[count + t - shift] for t in range(count)]
                grid[w, r, :, a * chans : (a + 1) * chans] = jnp.concatenate(picked, 0).astype(bf16)
            if 1 <= w <= own:
                shown[pl.ds(((w - 1) * rows + r) * frames, frames), :] = jnp.concatenate(pixel(vid, w, r), 0)
    lower = lax.axis_index("height")
    edge[...] = grid[:, (rows - 1) * (1 - lower)]
    for copy in copies:
        copy.wait()


def main_kernel(
    count, rows, group, ids_far, grid, edge, given, conv_weight, w_query, w_key, w_value, w_output, *refs
):
    blocks, (ids, border, total, shown, res, sem) = refs[:group], refs[group:]
    ids_copy = pltpu.make_async_copy(ids_far, ids, sem)
    ids_copy.start()
    span, _, frames, _ = grid.shape
    chans = w_query.shape[0]
    own = span - 2
    sources = frames // count
    lines = count * rows
    heads = chans // HD
    back = own * lines
    several = own // 2 if own % 2 == 0 else own
    area = several * rows * frames
    lower = lax.axis_index("height")
    border[1 - lower] = edge[...]
    border[lower] = jnp.zeros(edge.shape, bf16)

    for b in range(TAPS):
        for e in range(TAPS):
            ahead = [border[0, e : e + own][:, None]] if b == 0 else []
            after = [border[1, e : e + own][:, None]] if b == TAPS - 1 else []
            inner = grid[e : e + own, max(b - 1, 0) : min(b - 1 + rows, rows)]
            window = jnp.concatenate(ahead + [inner] + after, axis=1) if ahead or after else inner
            window = window.reshape(own * rows * frames, TAPS * chans)
            weight = jnp.concatenate([conv_weight[a, b, e] for a in range(TAPS)], axis=0)
            part = jnp.dot(window, weight, preferred_element_type=f32)
            total[...] = part if b == e == 0 else total[...] + part

    hidden = (given[...] + total[...]).astype(bf16).astype(f32)
    shown[...] = hidden
    normed = rms(hidden).astype(bf16)
    query, keys, values = (
        jnp.dot(normed, weight[...], preferred_element_type=f32).astype(bf16) for weight in (w_query, w_key, w_value)
    )

    ids_copy.wait()

    def place_of(shape, dim):
        inner, source = divided(lax.broadcasted_iota(jnp.int32, shape, dim) % frames, sources)
        frame = source * count + inner
        block = jnp.zeros(shape, jnp.int32)
        for s in range(frames):
            block = jnp.where(frame == s, ids[s], block)
        return frame, block

    pixels = several * rows
    row_t, row_b = (jnp.concatenate([x] * pixels, 0) for x in place_of((frames, area), 0))
    col_t, col_b = place_of((1, area), 1)
    row_p = divided(lax.broadcasted_iota(jnp.int32, (area, area), 0), frames)[0]
    col_p = divided(lax.broadcasted_iota(jnp.int32, (area, area), 1), frames)[0]
    permit = (row_p == col_p) & (col_t <= row_t) & (col_b >= row_b - 1)
    bias = jnp.where(permit, 0.0, -1e30)
    head_of = lax.broadcasted_iota(jnp.int32, (area, chans), 1) // HD

    gone = []
    for w in range(0, own, several):
        part = slice(w * rows * frames, w * rows * frames + area)
        single = jnp.concatenate(
            [jnp.where(head_of == h, query[part], jnp.zeros((), bf16)) for h in range(heads)], axis=0
        )
        scores = lax.dot_general(single, keys[part], (((1,), (1,)), ((), ())), preferred_element_type=f32)
        scores = scores * HD ** (-0.5) + jnp.concatenate([bias] * heads, axis=0)
        expo = jnp.exp(scores - jnp.max(scores, axis=-1, keepdims=True))
        weights = (expo * (1.0 / jnp.sum(expo, axis=-1, keepdims=True))).astype(bf16)
        mixed = jnp.dot(weights, values[part], preferred_element_type=f32)
        attended = mixed[:area]
        for h in range(1, heads):
            attended = jnp.where(head_of == h, mixed[h * area : (h + 1) * area], attended)
        gone.append(attended.astype(bf16))
    attended = jnp.concatenate(gone, axis=0)
    encoded = shown[...] + jnp.dot(attended, w_output[...], preferred_element_type=f32)
    for w in range(own):
        for r in range(rows):
            for t in range(count):
                start = ((w * rows + r) * count + t + 1) * sources - group
                put(res, w * lines + t * rows + r, group, back, encoded[start : start + group])
    me = lax.axis_index("tm")
    for k in range(group):
        start = pl.multiple_of(partner(me, k, group) * back, 16)
        block = jnp.concatenate([res[i, pl.ds(start, back), :] for i in range(res.shape[0])], axis=1)
        blocks[k][...] = block.astype(bf16)


def unpack_kernel(group, *refs):
    blocks, (out, local, wide, sems) = refs[:group], refs[group:]
    count, rows, cols, chans = out.shape
    lines = count * rows
    me = lax.axis_index("tm")
    for k in range(group):
        start = pl.multiple_of(partner(me, k, group) * blocks[k].shape[0], 16)
        fill(wide, start, blocks[k][...].astype(f32))
    copies = []
    for at in range(lines):
        place = (at // rows, at % rows)
        local[place] = get(wide, at, cols, lines).astype(bf16)
        copy = pltpu.make_async_copy(local.at[place], out.at[place], sems.at[at])
        copy.start()
        copies.append(copy)
    for copy in copies:
        copy.wait()


def exchanged(blocks, group):
    back = [blocks[0]]
    for k in range(1, group):
        back.append(lax.ppermute(blocks[k], "tm", [(i, partner(i, k, group)) for i in range(group)]))
    return back


def per_device(outer, video, block_ids, conv_weight, w_query, w_key, w_value, w_output):
    count, rows, cols, chans = video.shape
    group = lax.axis_size("tm")
    own = cols // group
    span = own + 2
    lines = count * rows
    near = pl.BlockSpec(memory_space=pltpu.VMEM)
    far = pl.BlockSpec(memory_space=pltpu.HBM)
    params = pltpu.CompilerParams(vmem_limit_bytes=VMEM)
    in_far = functools.partial(pltpu.with_memory_space_constraint, memory_space=pltpu.HBM)
    weights = [in_far(x) for x in (conv_weight, w_query, w_key, w_value, w_output)]

    blocks = pl.pallas_call(
        functools.partial(pack_kernel, group),
        out_shape=[jax.ShapeDtypeStruct((span * lines, chans), bf16)] * group,
        in_specs=[far],
        out_specs=[near] * group,
        scratch_shapes=[
            pltpu.VMEM(video.shape, bf16),
            scratch(lines * (cols + 2 * EDGE), chans),
            pltpu.SemaphoreType.DMA((lines,)),
        ],
        compiler_params=params,
    )(in_far(video))
    pieces = exchanged(blocks, group)
    ids = block_ids
    if outer > 1:
        before = lax.ppermute(jnp.stack(pieces), "outer", [(i, i + 1) for i in range(outer - 1)])
        pieces = pieces + [before]
        ids = jnp.concatenate([jnp.full((group * count,), -2, jnp.int32), ids])
        ids = lax.dynamic_slice(ids, (lax.axis_index("outer") * group * count,), (2 * group * count,))
    sources = group * (2 if outer > 1 else 1)
    frames = sources * count
    total = own * rows * frames
    grid, edge, shown, *weights = pl.pallas_call(
        functools.partial(shift_kernel, count, rows, group, outer > 1),
        out_shape=[
            jax.ShapeDtypeStruct((span, rows, frames, TAPS * chans), bf16),
            jax.ShapeDtypeStruct((span, frames, TAPS * chans), bf16),
            jax.ShapeDtypeStruct((total, chans), f32),
        ]
        + [jax.ShapeDtypeStruct(x.shape, bf16) for x in weights],
        in_specs=[near] * len(pieces) + [far] * 5,
        out_specs=[near] * 8,
        scratch_shapes=[scratch(sources * span * lines, chans)] * 2 + [pltpu.SemaphoreType.DMA((5,))],
        compiler_params=params,
    )(*pieces, *weights)
    edge = lax.ppermute(edge, "height", [(0, 1), (1, 0)])
    blocks = pl.pallas_call(
        functools.partial(main_kernel, count, rows, group),
        out_shape=[jax.ShapeDtypeStruct((own * lines, chans), bf16)] * group,
        in_specs=[far] + [near] * 8,
        out_specs=[near] * group,
        scratch_shapes=[
            pltpu.SMEM((frames,), jnp.int32),
            pltpu.VMEM((2,) + edge.shape, bf16),
            pltpu.VMEM((total, chans), f32),
            pltpu.VMEM((total, chans), f32),
            scratch(group * own * lines, chans),
            pltpu.SemaphoreType.DMA(()),
        ],
        compiler_params=params,
    )(in_far(ids), grid, edge, shown, *weights)
    return pl.pallas_call(
        functools.partial(unpack_kernel, group),
        out_shape=jax.ShapeDtypeStruct(video.shape, bf16),
        in_specs=[near] * group,
        out_specs=far,
        scratch_shapes=[
            pltpu.VMEM(video.shape, bf16),
            scratch(lines * cols, chans),
            pltpu.SemaphoreType.DMA((lines,)),
        ],
        compiler_params=params,
    )(*exchanged(blocks, group))


def solution(mesh):
    parts, along, halves = (mesh.shape[a] for a in ("groups", "tm", "height"))

    def run(video, *rest):
        count = video.shape[0] // (parts * along)
        group = min(g for g in range(1, along + 1) if along % g == 0 and (g * count >= REACH or g == along))
        outer = along // group
        split = Mesh(
            np.asarray(mesh.devices).reshape(parts, outer, group, halves),
            ("groups", "outer", "tm", "height"),
        )
        spec = P(("groups", "outer", "tm"), "height", None, None)
        placed = (spec, P("groups"), P(), P(), P(), P(), P())
        return jax.shard_map(
            functools.partial(per_device, outer),
            mesh=split,
            in_specs=placed,
            out_specs=spec,
            check_vma=False,
        )(video, *rest)

    return run
```

```python
import functools

import jax
import jax.numpy as jnp
import numpy as np
from jax import lax
from jax.experimental import pallas as pl
from jax.experimental.pallas import tpu as pltpu
from jax.sharding import Mesh, PartitionSpec as P

HD = 64
BLOCK = 4
TAPS = 3
REACH = 2 * BLOCK - 1 + TAPS - 1
LANES = 128
EDGE = 8
VMEM = 28 * 2**20

bf16, f32 = jnp.bfloat16, jnp.float32


def get(ref, start, size, stride):
    return jnp.concatenate([ref[i, pl.ds(start, size, stride=stride), :] for i in range(ref.shape[0])], axis=1)


def put(ref, start, size, stride, value):
    for i in range(ref.shape[0]):
        ref[i, pl.ds(start, size, stride=stride), :] = value[:, i * LANES : (i + 1) * LANES]


def fill(ref, start, value):
    for i in range(ref.shape[0]):
        ref[i, pl.ds(start, value.shape[0]), :] = value[:, i * LANES : (i + 1) * LANES]


def scratch(rows, chans):
    return pltpu.VMEM((chans // LANES, rows, LANES), f32)


def rms(wide):
    return wide * lax.rsqrt(jnp.mean(wide * wide, axis=-1, keepdims=True) + 1e-06)


def divided(at, by):
    if by & (by - 1) == 0:
        bits = by.bit_length() - 1
        return at >> bits, at & (by - 1)
    return lax.div(at, jnp.int32(by)), lax.rem(at, jnp.int32(by))


def pack_kernel(group, video, *refs):
    out, local, wide, sems = refs
    count, rows, cols, chans = video.shape
    lines = count * rows
    stride = cols + 2 * EDGE
    own = cols // group
    span = own + 2
    copies = []
    for at in range(lines):
        place = (at // rows, at % rows)
        copy = pltpu.make_async_copy(video.at[place], local.at[place], sems.at[at])
        copy.start()
        copies.append(copy)
    nothing = jnp.zeros((EDGE, chans), f32)
    for at in range(lines):
        fill(wide, at * stride, nothing)
        fill(wide, at * stride + EDGE + cols, nothing)
    for at, copy in enumerate(copies):
        copy.wait()
        fill(wide, at * stride + EDGE, local[at // rows, at % rows].astype(f32))
    together = 16 // lines
    for k in range(group):
        start = k * own + EDGE - 1
        for w in range(0, span, together):
            tile = jnp.concatenate([get(wide, start + w + i, lines, stride) for i in range(together)], axis=0)
            out[k, pl.ds(w * lines, 16), :] = tile.astype(bf16)


def shift_kernel(count, rows, *refs):
    video, far, refs = refs[0], refs[1:6], refs[6:]
    grid, edge, shown, refs = refs[0], refs[1], refs[2], refs[3:]
    near, (vid, act, sems) = refs[:5], refs[5:]
    copies = [pltpu.make_async_copy(src, dst, sems.at[i]) for i, (src, dst) in enumerate(zip(far, near))]
    for copy in copies:
        copy.start()
    sources, step, chans = video.shape
    lines = count * rows
    span = step // lines
    own = span - 2
    frames = sources * count
    xs = video[...].reshape(sources * step, chans).astype(f32)
    fill(vid, 0, xs)
    normal = rms(xs)
    fill(act, 0, normal / (1.0 + jnp.exp(-normal)))

    def pixel(ref, w, r):
        return [get(ref, w * lines + t * rows + r, sources, step) for t in range(count)]

    first = lax.broadcasted_iota(jnp.int32, (sources, chans), 0) == 0

    def earlier(x):
        return jnp.where(first, 0.0, pltpu.roll(x, 1, 0))

    for w in range(span):
        for r in range(rows):
            now = pixel(act, w, r)
            ordered = [earlier(x) for x in now] + now
            for a in range(TAPS):
                shift = TAPS - 1 - a
                picked = [ordered[count + t - shift] for t in range(count)]
                grid[w, r, :, a * chans : (a + 1) * chans] = jnp.concatenate(picked, 0).astype(bf16)
            if 1 <= w <= own:
                shown[pl.ds(((w - 1) * rows + r) * frames, frames), :] = jnp.concatenate(pixel(vid, w, r), 0)
    lower = lax.axis_index("height")
    edge[...] = grid[:, (rows - 1) * (1 - lower)]
    for copy in copies:
        copy.wait()


def main_kernel(
    count, rows, group, ids_far, grid, edge, given, conv_weight, w_query, w_key, w_value, w_output, *refs
):
    out, ids, border, total, shown, res, sem = refs
    ids_copy = pltpu.make_async_copy(ids_far, ids, sem)
    ids_copy.start()
    span, _, frames, _ = grid.shape
    chans = w_query.shape[0]
    own = span - 2
    sources = frames // count
    lines = count * rows
    heads = chans // HD
    back = own * lines
    several = own // 2 if own % 2 == 0 else own
    area = several * rows * frames
    lower = lax.axis_index("height")
    border[1 - lower] = edge[...]
    border[lower] = jnp.zeros(edge.shape, bf16)

    for b in range(TAPS):
        for e in range(TAPS):
            ahead = [border[0, e : e + own][:, None]] if b == 0 else []
            after = [border[1, e : e + own][:, None]] if b == TAPS - 1 else []
            inner = grid[e : e + own, max(b - 1, 0) : min(b - 1 + rows, rows)]
            window = jnp.concatenate(ahead + [inner] + after, axis=1) if ahead or after else inner
            window = window.reshape(own * rows * frames, TAPS * chans)
            weight = jnp.concatenate([conv_weight[a, b, e] for a in range(TAPS)], axis=0)
            part = jnp.dot(window, weight, preferred_element_type=f32)
            total[...] = part if b == e == 0 else total[...] + part

    hidden = (given[...] + total[...]).astype(bf16).astype(f32)
    shown[...] = hidden
    normed = rms(hidden).astype(bf16)
    query, keys, values = (
        jnp.dot(normed, weight[...], preferred_element_type=f32).astype(bf16) for weight in (w_query, w_key, w_value)
    )

    ids_copy.wait()

    def place_of(shape, dim):
        inner, source = divided(lax.broadcasted_iota(jnp.int32, shape, dim) % frames, sources)
        frame = source * count + inner
        block = jnp.zeros(shape, jnp.int32)
        for s in range(frames):
            block = jnp.where(frame == s, ids[s], block)
        return frame, block

    pixels = several * rows
    row_t, row_b = (jnp.concatenate([x] * pixels, 0) for x in place_of((frames, area), 0))
    col_t, col_b = place_of((1, area), 1)
    row_p = divided(lax.broadcasted_iota(jnp.int32, (area, area), 0), frames)[0]
    col_p = divided(lax.broadcasted_iota(jnp.int32, (area, area), 1), frames)[0]
    permit = (row_p == col_p) & (col_t <= row_t) & (col_b >= row_b - 1)
    bias = jnp.where(permit, 0.0, -1e30)
    head_of = lax.broadcasted_iota(jnp.int32, (area, chans), 1) // HD

    gone = []
    for w in range(0, own, several):
        part = slice(w * rows * frames, w * rows * frames + area)
        single = jnp.concatenate(
            [jnp.where(head_of == h, query[part], jnp.zeros((), bf16)) for h in range(heads)], axis=0
        )
        scores = lax.dot_general(single, keys[part], (((1,), (1,)), ((), ())), preferred_element_type=f32)
        scores = scores * HD ** (-0.5) + jnp.concatenate([bias] * heads, axis=0)
        expo = jnp.exp(scores - jnp.max(scores, axis=-1, keepdims=True))
        weights = (expo * (1.0 / jnp.sum(expo, axis=-1, keepdims=True))).astype(bf16)
        mixed = jnp.dot(weights, values[part], preferred_element_type=f32)
        attended = mixed[:area]
        for h in range(1, heads):
            attended = jnp.where(head_of == h, mixed[h * area : (h + 1) * area], attended)
        gone.append(attended.astype(bf16))
    attended = jnp.concatenate(gone, axis=0)
    encoded = shown[...] + jnp.dot(attended, w_output[...], preferred_element_type=f32)
    for w in range(own):
        for r in range(rows):
            for t in range(count):
                start = ((w * rows + r) * count + t + 1) * sources - group
                put(res, w * lines + t * rows + r, group, back, encoded[start : start + group])
    done = jnp.concatenate([res[i] for i in range(res.shape[0])], axis=1)
    out[...] = done.astype(bf16).reshape(out.shape)


def unpack_kernel(packed, out, local, wide, sems):
    count, rows, cols, chans = out.shape
    lines = count * rows
    fill(wide, 0, packed[...].reshape(lines * cols, chans).astype(f32))
    copies = []
    for at in range(lines):
        place = (at // rows, at % rows)
        local[place] = get(wide, at, cols, lines).astype(bf16)
        copy = pltpu.make_async_copy(local.at[place], out.at[place], sems.at[at])
        copy.start()
        copies.append(copy)
    for copy in copies:
        copy.wait()


def exchanged(blocks):
    return lax.all_to_all(blocks, "tm", split_axis=0, concat_axis=0, tiled=True)


def per_device(outer, video, block_ids, conv_weight, w_query, w_key, w_value, w_output):
    count, rows, cols, chans = video.shape
    group = lax.axis_size("tm")
    own = cols // group
    span = own + 2
    lines = count * rows
    near = pl.BlockSpec(memory_space=pltpu.VMEM)
    far = pl.BlockSpec(memory_space=pltpu.HBM)
    params = pltpu.CompilerParams(vmem_limit_bytes=VMEM)
    in_far = functools.partial(pltpu.with_memory_space_constraint, memory_space=pltpu.HBM)
    weights = [in_far(x) for x in (conv_weight, w_query, w_key, w_value, w_output)]

    blocks = pl.pallas_call(
        functools.partial(pack_kernel, group),
        out_shape=jax.ShapeDtypeStruct((group, span * lines, chans), bf16),
        in_specs=[far],
        out_specs=near,
        scratch_shapes=[
            pltpu.VMEM(video.shape, bf16),
            scratch(lines * (cols + 2 * EDGE), chans),
            pltpu.SemaphoreType.DMA((lines,)),
        ],
        compiler_params=params,
    )(in_far(video))
    piece = exchanged(blocks)
    ids = block_ids
    if outer > 1:
        before = lax.ppermute(piece, "outer", [(i, i + 1) for i in range(outer - 1)])
        piece = jnp.concatenate([before, piece], axis=0)
        ids = jnp.concatenate([jnp.full((group * count,), -2, jnp.int32), ids])
        ids = lax.dynamic_slice(ids, (lax.axis_index("outer") * group * count,), (2 * group * count,))
    sources = piece.shape[0]
    frames = sources * count
    total = own * rows * frames
    grid, edge, shown, *weights = pl.pallas_call(
        functools.partial(shift_kernel, count, rows),
        out_shape=[
            jax.ShapeDtypeStruct((span, rows, frames, TAPS * chans), bf16),
            jax.ShapeDtypeStruct((span, frames, TAPS * chans), bf16),
            jax.ShapeDtypeStruct((total, chans), f32),
        ]
        + [jax.ShapeDtypeStruct(x.shape, bf16) for x in weights],
        in_specs=[near] + [far] * 5,
        out_specs=[near] * 8,
        scratch_shapes=[scratch(sources * span * lines, chans)] * 2 + [pltpu.SemaphoreType.DMA((5,))],
        compiler_params=params,
    )(piece, *weights)
    edge = lax.ppermute(edge, "height", [(0, 1), (1, 0)])
    blocks = pl.pallas_call(
        functools.partial(main_kernel, count, rows, group),
        out_shape=jax.ShapeDtypeStruct((group, own * lines, chans), bf16),
        in_specs=[far] + [near] * 8,
        out_specs=near,
        scratch_shapes=[
            pltpu.SMEM((frames,), jnp.int32),
            pltpu.VMEM((2,) + edge.shape, bf16),
            pltpu.VMEM((total, chans), f32),
            pltpu.VMEM((total, chans), f32),
            scratch(group * own * lines, chans),
            pltpu.SemaphoreType.DMA(()),
        ],
        compiler_params=params,
    )(in_far(ids), grid, edge, shown, *weights)
    return pl.pallas_call(
        unpack_kernel,
        out_shape=jax.ShapeDtypeStruct(video.shape, bf16),
        in_specs=[near],
        out_specs=far,
        scratch_shapes=[
            pltpu.VMEM(video.shape, bf16),
            scratch(lines * cols, chans),
            pltpu.SemaphoreType.DMA((lines,)),
        ],
        compiler_params=params,
    )(exchanged(blocks))


def solution(mesh):
    parts, along, halves = (mesh.shape[a] for a in ("groups", "tm", "height"))

    def run(video, *rest):
        count = video.shape[0] // (parts * along)
        group = min(g for g in range(1, along + 1) if along % g == 0 and (g * count >= REACH or g == along))
        outer = along // group
        split = Mesh(
            np.asarray(mesh.devices).reshape(parts, outer, group, halves),
            ("groups", "outer", "tm", "height"),
        )
        spec = P(("groups", "outer", "tm"), "height", None, None)
        placed = (spec, P("groups"), P(), P(), P(), P(), P())
        return jax.shard_map(
            functools.partial(per_device, outer),
            mesh=split,
            in_specs=placed,
            out_specs=spec,
            check_vma=False,
        )(video, *rest)

    return run
```

```python
import functools

import jax
import jax.numpy as jnp
import numpy as np
from jax import lax
from jax.experimental import pallas as pl
from jax.experimental.pallas import tpu as pltpu
from jax.sharding import Mesh, PartitionSpec as P

HD = 64
BLOCK = 4
TAPS = 3
REACH = 2 * BLOCK - 1 + TAPS - 1
LANES = 128
EDGE = 8
VMEM = 28 * 2**20

bf16, f32 = jnp.bfloat16, jnp.float32


def get(ref, start, size, stride):
    return jnp.concatenate([ref[i, pl.ds(start, size, stride=stride), :] for i in range(ref.shape[0])], axis=1)


def put(ref, start, size, stride, value):
    for i in range(ref.shape[0]):
        ref[i, pl.ds(start, size, stride=stride), :] = value[:, i * LANES : (i + 1) * LANES]


def fill(ref, start, value):
    for i in range(ref.shape[0]):
        ref[i, pl.ds(start, value.shape[0]), :] = value[:, i * LANES : (i + 1) * LANES]


def scratch(rows, chans):
    return pltpu.VMEM((chans // LANES, rows, LANES), f32)


def rms(wide):
    return wide * lax.rsqrt(jnp.mean(wide * wide, axis=-1, keepdims=True) + 1e-06)


def divided(at, by):
    if by & (by - 1) == 0:
        bits = by.bit_length() - 1
        return at >> bits, at & (by - 1)
    return lax.div(at, jnp.int32(by)), lax.rem(at, jnp.int32(by))


def pack_kernel(group, video, *refs):
    out, local, wide, sems = refs
    count, rows, cols, chans = video.shape
    lines = count * rows
    stride = cols + 2 * EDGE
    own = cols // group
    span = own + 2
    copies = []
    for at in range(lines):
        place = (at // rows, at % rows)
        copy = pltpu.make_async_copy(video.at[place], local.at[place], sems.at[at])
        copy.start()
        copies.append(copy)
    nothing = jnp.zeros((EDGE, chans), f32)
    for at in range(lines):
        fill(wide, at * stride, nothing)
        fill(wide, at * stride + EDGE + cols, nothing)
    for at, copy in enumerate(copies):
        copy.wait()
        fill(wide, at * stride + EDGE, local[at // rows, at % rows].astype(f32))
    together = 16 // lines
    for k in range(group):
        start = k * own + EDGE - 1
        for w in range(0, span, together):
            tile = jnp.concatenate([get(wide, start + w + i, lines, stride) for i in range(together)], axis=0)
            out[k, pl.ds(w * lines, 16), :] = tile.astype(bf16)


def frames_of(ref, w, r, count, rows, sources, step):
    return [get(ref, w * count * rows + t * rows + r, sources, step) for t in range(count)]


def shifted(now):
    count = len(now)
    sources, chans = now[0].shape
    first = lax.broadcasted_iota(jnp.int32, (sources, chans), 0) == 0
    past = [jnp.where(first, 0.0, pltpu.roll(x, 1, 0)) for x in now]
    ordered = past + now
    taps = []
    for a in range(TAPS):
        start = count - (TAPS - 1 - a)
        taps.append(jnp.concatenate(ordered[start : start + count], 0).astype(bf16))
    return jnp.concatenate(taps, axis=1)


def activated(wide):
    normal = rms(wide)
    return normal / (1.0 + jnp.exp(-normal))


def depth(parts):
    return parts[0] if len(parts) == 1 else jnp.concatenate(parts, axis=-1)


def edge_kernel(count, rows, video, edge, vid):
    sources, step, chans = video.shape
    span = step // (count * rows)
    fill(vid, 0, video[...].reshape(sources * step, chans).astype(f32))
    row = (rows - 1) * (1 - lax.axis_index("height"))
    for w in range(span):
        edge[w] = shifted([activated(x) for x in frames_of(vid, w, row, count, rows, sources, step)])


def shift_kernel(count, rows, video, *refs):
    far, (total, *near), (vid, act, grid, conv_sems, sems) = refs[:5], refs[5:11], refs[11:]
    conv_far, conv_weight = far[0], near[0]
    order = [1, 0, 2]
    taps = {b: pltpu.make_async_copy(conv_far.at[:, b], conv_weight.at[:, b], conv_sems.at[b]) for b in order}
    others = [pltpu.make_async_copy(far[i], near[i], sems.at[i - 1]) for i in range(1, 5)]
    for copy in list(taps.values()) + others:
        copy.start()
    sources, step, chans = video.shape
    span = step // (count * rows)
    own = span - 2
    frames = sources * count
    xs = video[...].reshape(sources * step, chans).astype(f32)
    fill(vid, 0, xs)
    fill(act, 0, activated(xs))
    for w in range(span):
        for r in range(rows):
            grid[w, r] = shifted(frames_of(act, w, r, count, rows, sources, step))
            if 1 <= w <= own:
                total[w - 1, r] = jnp.concatenate(frames_of(vid, w, r, count, rows, sources, step), 0)

    for b in order:
        taps[b].wait()
        low, high = max(0, 1 - b), min(rows, rows + 1 - b)
        window = depth([grid[e : e + own, low + b - 1 : high + b - 1] for e in range(TAPS)])
        window = window.reshape(own * (high - low) * frames, TAPS * TAPS * chans)
        weight = jnp.concatenate([conv_weight[a, b, e] for e in range(TAPS) for a in range(TAPS)], axis=0)
        part = jnp.dot(window, weight, preferred_element_type=f32)
        total[:, low:high] = total[:, low:high] + part.reshape(own, high - low, frames, chans)
    for copy in others:
        copy.wait()


def main_kernel(
    count, rows, group, ids_far, edge, given, conv_weight, w_query, w_key, w_value, w_output, *refs
):
    out, ids, shown, res, sem = refs
    ids_copy = pltpu.make_async_copy(ids_far, ids, sem)
    ids_copy.start()
    own, _, frames, chans = given.shape
    sources = frames // count
    lines = count * rows
    heads = chans // HD
    back = own * lines
    several = max(n for n in range(1, own + 1) if own % n == 0 and (n == 1 or n * rows * frames <= LANES))
    area = several * rows * frames

    lower = lax.axis_index("height")
    window = depth([edge[e : e + own] for e in range(TAPS)]).reshape(own * frames, TAPS * TAPS * chans)
    b = (TAPS - 1) * (1 - lower)
    weight = jnp.concatenate([conv_weight[a, b, e] for e in range(TAPS) for a in range(TAPS)], axis=0)
    part = jnp.dot(window, weight, preferred_element_type=f32).reshape(own, frames, chans)
    for r in range(rows):
        shown[:, r] = given[:, r] + jnp.where(r == (rows - 1) * (1 - lower), part, 0.0)

    hidden = shown[...].reshape(own * rows * frames, chans).astype(bf16).astype(f32)
    normed = rms(hidden).astype(bf16)
    query, keys, values = (
        jnp.dot(normed, weight[...], preferred_element_type=f32).astype(bf16) for weight in (w_query, w_key, w_value)
    )

    ids_copy.wait()

    def place_of(shape, dim):
        inner, source = divided(lax.broadcasted_iota(jnp.int32, shape, dim) % frames, sources)
        frame = source * count + inner
        block = jnp.zeros(shape, jnp.int32)
        for s in range(frames):
            block = jnp.where(frame == s, ids[s], block)
        return frame, block

    pixels = several * rows
    row_t, row_b = (jnp.concatenate([x] * pixels, 0) for x in place_of((frames, area), 0))
    col_t, col_b = place_of((1, area), 1)
    row_p = divided(lax.broadcasted_iota(jnp.int32, (area, area), 0), frames)[0]
    col_p = divided(lax.broadcasted_iota(jnp.int32, (area, area), 1), frames)[0]
    permit = (row_p == col_p) & (col_t <= row_t) & (col_b >= row_b - 1)
    bias = jnp.where(permit, 0.0, -1e30)
    head_of = lax.broadcasted_iota(jnp.int32, (area, chans), 1) // HD

    gone = []
    for w in range(0, own, several):
        part = slice(w * rows * frames, w * rows * frames + area)
        single = jnp.concatenate(
            [jnp.where(head_of == h, query[part], jnp.zeros((), bf16)) for h in range(heads)], axis=0
        )
        scores = lax.dot_general(single, keys[part], (((1,), (1,)), ((), ())), preferred_element_type=f32)
        scores = scores * HD ** (-0.5) + jnp.concatenate([bias] * heads, axis=0)
        expo = jnp.exp(scores - jnp.max(scores, axis=-1, keepdims=True))
        weights = (expo * (1.0 / jnp.sum(expo, axis=-1, keepdims=True))).astype(bf16)
        mixed = jnp.dot(weights, values[part], preferred_element_type=f32)
        attended = mixed[:area]
        for h in range(1, heads):
            attended = jnp.where(head_of == h, mixed[h * area : (h + 1) * area], attended)
        gone.append(attended.astype(bf16))
    attended = jnp.concatenate(gone, axis=0)
    encoded = hidden + jnp.dot(attended, w_output[...], preferred_element_type=f32)
    for w in range(own):
        for r in range(rows):
            for t in range(count):
                start = ((w * rows + r) * count + t + 1) * sources - group
                put(res, w * lines + t * rows + r, group, back, encoded[start : start + group])
    done = jnp.concatenate([res[i] for i in range(res.shape[0])], axis=1)
    out[...] = done.astype(bf16).reshape(out.shape)


def unpack_kernel(packed, out, local, wide, sems):
    count, rows, cols, chans = out.shape
    lines = count * rows
    fill(wide, 0, packed[...].reshape(lines * cols, chans).astype(f32))
    copies = []
    for at in range(lines):
        place = (at // rows, at % rows)
        local[place] = get(wide, at, cols, lines).astype(bf16)
        copy = pltpu.make_async_copy(local.at[place], out.at[place], sems.at[at])
        copy.start()
        copies.append(copy)
    for copy in copies:
        copy.wait()


def exchanged(blocks):
    return lax.all_to_all(blocks, "tm", split_axis=0, concat_axis=0, tiled=True)


def per_device(outer, video, block_ids, conv_weight, w_query, w_key, w_value, w_output):
    count, rows, cols, chans = video.shape
    group = lax.axis_size("tm")
    own = cols // group
    span = own + 2
    lines = count * rows
    near = pl.BlockSpec(memory_space=pltpu.VMEM)
    far = pl.BlockSpec(memory_space=pltpu.HBM)
    params = pltpu.CompilerParams(vmem_limit_bytes=VMEM)
    in_far = functools.partial(pltpu.with_memory_space_constraint, memory_space=pltpu.HBM)
    weights = [in_far(x) for x in (conv_weight, w_query, w_key, w_value, w_output)]

    blocks = pl.pallas_call(
        functools.partial(pack_kernel, group),
        out_shape=jax.ShapeDtypeStruct((group, span * lines, chans), bf16),
        in_specs=[far],
        out_specs=near,
        scratch_shapes=[
            pltpu.VMEM(video.shape, bf16),
            scratch(lines * (cols + 2 * EDGE), chans),
            pltpu.SemaphoreType.DMA((lines,)),
        ],
        compiler_params=params,
    )(in_far(video))
    piece = exchanged(blocks)
    ids = block_ids
    if outer > 1:
        before = lax.ppermute(piece, "outer", [(i, i + 1) for i in range(outer - 1)])
        piece = jnp.concatenate([before, piece], axis=0)
        ids = jnp.concatenate([jnp.full((group * count,), -2, jnp.int32), ids])
        ids = lax.dynamic_slice(ids, (lax.axis_index("outer") * group * count,), (2 * group * count,))
    sources = piece.shape[0]
    frames = sources * count
    stored = scratch(sources * span * lines, chans)
    edge = pl.pallas_call(
        functools.partial(edge_kernel, count, rows),
        out_shape=jax.ShapeDtypeStruct((span, frames, TAPS * chans), bf16),
        in_specs=[near],
        out_specs=near,
        scratch_shapes=[stored],
        compiler_params=params,
    )(piece)
    edge = lax.ppermute(edge, "height", [(0, 1), (1, 0)])
    total, *weights = pl.pallas_call(
        functools.partial(shift_kernel, count, rows),
        out_shape=[jax.ShapeDtypeStruct((own, rows, frames, chans), f32)]
        + [jax.ShapeDtypeStruct(x.shape, bf16) for x in weights],
        in_specs=[near] + [far] * 5,
        out_specs=[near] * 6,
        scratch_shapes=[
            stored,
            stored,
            pltpu.VMEM((span, rows, frames, TAPS * chans), bf16),
            pltpu.SemaphoreType.DMA((TAPS,)),
            pltpu.SemaphoreType.DMA((4,)),
        ],
        compiler_params=params,
    )(piece, *weights)
    blocks = pl.pallas_call(
        functools.partial(main_kernel, count, rows, group),
        out_shape=jax.ShapeDtypeStruct((group, own * lines, chans), bf16),
        in_specs=[far] + [near] * 7,
        out_specs=near,
        scratch_shapes=[
            pltpu.SMEM((frames,), jnp.int32),
            pltpu.VMEM((own, rows, frames, chans), f32),
            scratch(group * own * lines, chans),
            pltpu.SemaphoreType.DMA(()),
        ],
        compiler_params=params,
    )(in_far(ids), edge, total, *weights)
    return pl.pallas_call(
        unpack_kernel,
        out_shape=jax.ShapeDtypeStruct(video.shape, bf16),
        in_specs=[near],
        out_specs=far,
        scratch_shapes=[
            pltpu.VMEM(video.shape, bf16),
            scratch(lines * cols, chans),
            pltpu.SemaphoreType.DMA((lines,)),
        ],
        compiler_params=params,
    )(exchanged(blocks))


def solution(mesh):
    parts, along, halves = (mesh.shape[a] for a in ("groups", "tm", "height"))

    def run(video, *rest):
        count = video.shape[0] // (parts * along)
        group = min(g for g in range(1, along + 1) if along % g == 0 and (g * count >= REACH or g == along))
        outer = along // group
        split = Mesh(
            np.asarray(mesh.devices).reshape(parts, outer, group, halves),
            ("groups", "outer", "tm", "height"),
        )
        spec = P(("groups", "outer", "tm"), "height", None, None)
        placed = (spec, P("groups"), P(), P(), P(), P(), P())
        return jax.shard_map(
            functools.partial(per_device, outer),
            mesh=split,
            in_specs=placed,
            out_specs=spec,
            check_vma=False,
        )(video, *rest)

    return run
```

```python
import functools

import jax
import jax.numpy as jnp
import numpy as np
from jax import lax
from jax.experimental import pallas as pl
from jax.experimental.pallas import tpu as pltpu
from jax.sharding import Mesh, PartitionSpec as P

HD = 64
BLOCK = 4
TAPS = 3
REACH = 2 * BLOCK - 1 + TAPS - 1
LANES = 128
EDGE = 8
VMEM = 28 * 2**20

bf16, f32 = jnp.bfloat16, jnp.float32


def get(ref, start, size, stride):
    return jnp.concatenate([ref[i, pl.ds(start, size, stride=stride), :] for i in range(ref.shape[0])], axis=1)


def put(ref, start, size, stride, value):
    for i in range(ref.shape[0]):
        ref[i, pl.ds(start, size, stride=stride), :] = value[:, i * LANES : (i + 1) * LANES]


def fill(ref, start, value):
    for i in range(ref.shape[0]):
        ref[i, pl.ds(start, value.shape[0]), :] = value[:, i * LANES : (i + 1) * LANES]


def scratch(rows, chans):
    return pltpu.VMEM((chans // LANES, rows, LANES), f32)


def rms(wide):
    return wide * lax.rsqrt(jnp.mean(wide * wide, axis=-1, keepdims=True) + 1e-06)


def divided(at, by):
    if by & (by - 1) == 0:
        bits = by.bit_length() - 1
        return at >> bits, at & (by - 1)
    return lax.div(at, jnp.int32(by)), lax.rem(at, jnp.int32(by))


def pack_kernel(group, video, *refs):
    out, local, wide, sems = refs
    count, rows, cols, chans = video.shape
    lines = count * rows
    stride = cols + 2 * EDGE
    own = cols // group
    span = own + 2
    copies = []
    for at in range(lines):
        place = (at // rows, at % rows)
        copy = pltpu.make_async_copy(video.at[place], local.at[place], sems.at[at])
        copy.start()
        copies.append(copy)
    nothing = jnp.zeros((EDGE, chans), f32)
    for at in range(lines):
        fill(wide, at * stride, nothing)
        fill(wide, at * stride + EDGE + cols, nothing)
    for at, copy in enumerate(copies):
        copy.wait()
        fill(wide, at * stride + EDGE, local[at // rows, at % rows].astype(f32))
    together = 16 // lines
    for k in range(group):
        start = k * own + EDGE - 1
        for w in range(0, span, together):
            tile = jnp.concatenate([get(wide, start + w + i, lines, stride) for i in range(together)], axis=0)
            out[k, pl.ds(w * lines, 16), :] = tile.astype(bf16)


def frames_of(ref, w, r, count, rows, sources, step):
    return [get(ref, w * count * rows + t * rows + r, sources, step) for t in range(count)]


def shifted(now):
    count = len(now)
    sources, chans = now[0].shape
    first = lax.broadcasted_iota(jnp.int32, (sources, chans), 0) == 0
    past = [jnp.where(first, 0.0, pltpu.roll(x, 1, 0)) for x in now]
    ordered = past + now
    taps = []
    for a in range(TAPS):
        start = count - (TAPS - 1 - a)
        taps.append(jnp.concatenate(ordered[start : start + count], 0).astype(bf16))
    return jnp.concatenate(taps, axis=1)


def activated(wide):
    normal = rms(wide)
    return normal / (1.0 + jnp.exp(-normal))


def depth(parts):
    return parts[0] if len(parts) == 1 else jnp.concatenate(parts, axis=-1)


def edge_kernel(count, rows, video, edge, vid):
    sources, step, chans = video.shape
    span = step // (count * rows)
    fill(vid, 0, video[...].reshape(sources * step, chans).astype(f32))
    row = (rows - 1) * (1 - lax.axis_index("height"))
    for w in range(span):
        edge[w] = shifted([activated(x) for x in frames_of(vid, w, row, count, rows, sources, step)])


def shift_kernel(count, rows, video, *refs):
    far, (total, *near), (vid, grid, conv_sems, sems) = refs[:5], refs[5:11], refs[11:]
    conv_far, conv_weight = far[0], near[0]
    order = [1, 0, 2]
    taps = {b: pltpu.make_async_copy(conv_far.at[:, b], conv_weight.at[:, b], conv_sems.at[b]) for b in order}
    others = [pltpu.make_async_copy(far[i], near[i], sems.at[i - 1]) for i in range(1, 5)]
    for copy in list(taps.values()) + others:
        copy.start()
    sources, step, chans = video.shape
    span = step // (count * rows)
    own = span - 2
    frames = sources * count
    fill(vid, 0, video[...].reshape(sources * step, chans).astype(f32))
    for w in range(span):
        for r in range(rows):
            now = frames_of(vid, w, r, count, rows, sources, step)
            grid[w, r] = shifted([activated(x) for x in now])
            if 1 <= w <= own:
                total[w - 1, r] = jnp.concatenate(now, 0)

    for b in order:
        taps[b].wait()
        low, high = max(0, 1 - b), min(rows, rows + 1 - b)
        window = depth([grid[e : e + own, low + b - 1 : high + b - 1] for e in range(TAPS)])
        window = window.reshape(own * (high - low) * frames, TAPS * TAPS * chans)
        weight = jnp.concatenate([conv_weight[a, b, e] for e in range(TAPS) for a in range(TAPS)], axis=0)
        part = jnp.dot(window, weight, preferred_element_type=f32)
        total[:, low:high] = total[:, low:high] + part.reshape(own, high - low, frames, chans)
    for copy in others:
        copy.wait()


def main_kernel(
    count, rows, group, ids_far, edge, given, conv_weight, w_query, w_key, w_value, w_output, *refs
):
    out, ids, shown, res, sem = refs
    ids_copy = pltpu.make_async_copy(ids_far, ids, sem)
    ids_copy.start()
    own, _, frames, chans = given.shape
    sources = frames // count
    lines = count * rows
    heads = chans // HD
    back = own * lines
    several = max(n for n in range(1, own + 1) if own % n == 0 and (n == 1 or n * rows * frames <= LANES))
    area = several * rows * frames

    lower = lax.axis_index("height")
    window = depth([edge[e : e + own] for e in range(TAPS)]).reshape(own * frames, TAPS * TAPS * chans)
    b = (TAPS - 1) * (1 - lower)
    weight = jnp.concatenate([conv_weight[a, b, e] for e in range(TAPS) for a in range(TAPS)], axis=0)
    part = jnp.dot(window, weight, preferred_element_type=f32).reshape(own, frames, chans)
    for r in range(rows):
        shown[:, r] = given[:, r] + jnp.where(r == (rows - 1) * (1 - lower), part, 0.0)

    hidden = shown[...].reshape(own * rows * frames, chans).astype(bf16).astype(f32)
    normed = rms(hidden).astype(bf16)
    query, keys, values = (
        jnp.dot(normed, weight[...], preferred_element_type=f32).astype(bf16) for weight in (w_query, w_key, w_value)
    )

    ids_copy.wait()

    def place_of(shape, dim):
        inner, source = divided(lax.broadcasted_iota(jnp.int32, shape, dim) % frames, sources)
        frame = source * count + inner
        block = jnp.zeros(shape, jnp.int32)
        for s in range(frames):
            block = jnp.where(frame == s, ids[s], block)
        return frame, block

    pixels = several * rows
    row_t, row_b = (jnp.concatenate([x] * pixels, 0) for x in place_of((frames, area), 0))
    col_t, col_b = place_of((1, area), 1)
    row_p = divided(lax.broadcasted_iota(jnp.int32, (area, area), 0), frames)[0]
    col_p = divided(lax.broadcasted_iota(jnp.int32, (area, area), 1), frames)[0]
    permit = (row_p == col_p) & (col_t <= row_t) & (col_b >= row_b - 1)
    bias = jnp.where(permit, 0.0, -1e30)
    head_of = divided(lax.broadcasted_iota(jnp.int32, (area, chans), 1), HD)[0]
    scaled = [jnp.where(head_of == h, HD ** (-0.5), 0.0).astype(bf16) for h in range(heads)]
    ones = jnp.ones((area, LANES), bf16)

    gone = []
    for w in range(0, own, several):
        part = slice(w * rows * frames, w * rows * frames + area)
        single = jnp.concatenate([query[part] * scaled[h] for h in range(heads)], axis=0)
        scores = lax.dot_general(single, keys[part], (((1,), (1,)), ((), ())), preferred_element_type=f32)
        scores = scores + jnp.concatenate([bias] * heads, axis=0)
        expo = jnp.exp(scores - jnp.max(scores, axis=-1, keepdims=True)).astype(bf16)
        mixed = jnp.dot(expo, values[part], preferred_element_type=f32)
        sums = jnp.dot(expo, ones, preferred_element_type=f32)
        sums = jnp.concatenate([sums] * (chans // LANES), axis=1)
        attended, under = mixed[:area], sums[:area]
        for h in range(1, heads):
            rows_of = slice(h * area, (h + 1) * area)
            attended = jnp.where(head_of == h, mixed[rows_of], attended)
            under = jnp.where(head_of == h, sums[rows_of], under)
        gone.append((attended / under).astype(bf16))
    attended = jnp.concatenate(gone, axis=0)
    encoded = hidden + jnp.dot(attended, w_output[...], preferred_element_type=f32)
    for w in range(own):
        for r in range(rows):
            for t in range(count):
                start = ((w * rows + r) * count + t + 1) * sources - group
                put(res, w * lines + t * rows + r, group, back, encoded[start : start + group])
    done = jnp.concatenate([res[i] for i in range(res.shape[0])], axis=1)
    out[...] = done.astype(bf16).reshape(out.shape)


def unpack_kernel(packed, out, local, wide, sems):
    count, rows, cols, chans = out.shape
    lines = count * rows
    fill(wide, 0, packed[...].reshape(lines * cols, chans).astype(f32))
    copies = []
    for at in range(lines):
        place = (at // rows, at % rows)
        local[place] = get(wide, at, cols, lines).astype(bf16)
        copy = pltpu.make_async_copy(local.at[place], out.at[place], sems.at[at])
        copy.start()
        copies.append(copy)
    for copy in copies:
        copy.wait()


def exchanged(blocks):
    return lax.all_to_all(blocks, "tm", split_axis=0, concat_axis=0, tiled=True)


def per_device(outer, video, block_ids, conv_weight, w_query, w_key, w_value, w_output):
    count, rows, cols, chans = video.shape
    group = lax.axis_size("tm")
    own = cols // group
    span = own + 2
    lines = count * rows
    near = pl.BlockSpec(memory_space=pltpu.VMEM)
    far = pl.BlockSpec(memory_space=pltpu.HBM)
    params = pltpu.CompilerParams(vmem_limit_bytes=VMEM)
    in_far = functools.partial(pltpu.with_memory_space_constraint, memory_space=pltpu.HBM)
    weights = [in_far(x) for x in (conv_weight, w_query, w_key, w_value, w_output)]

    blocks = pl.pallas_call(
        functools.partial(pack_kernel, group),
        out_shape=jax.ShapeDtypeStruct((group, span * lines, chans), bf16),
        in_specs=[far],
        out_specs=near,
        scratch_shapes=[
            pltpu.VMEM(video.shape, bf16),
            scratch(lines * (cols + 2 * EDGE), chans),
            pltpu.SemaphoreType.DMA((lines,)),
        ],
        compiler_params=params,
    )(in_far(video))
    piece = exchanged(blocks)
    ids = block_ids
    if outer > 1:
        before = lax.ppermute(piece, "outer", [(i, i + 1) for i in range(outer - 1)])
        piece = jnp.concatenate([before, piece], axis=0)
        ids = jnp.concatenate([jnp.full((group * count,), -2, jnp.int32), ids])
        ids = lax.dynamic_slice(ids, (lax.axis_index("outer") * group * count,), (2 * group * count,))
    sources = piece.shape[0]
    frames = sources * count
    stored = scratch(sources * span * lines, chans)
    edge = pl.pallas_call(
        functools.partial(edge_kernel, count, rows),
        out_shape=jax.ShapeDtypeStruct((span, frames, TAPS * chans), bf16),
        in_specs=[near],
        out_specs=near,
        scratch_shapes=[stored],
        compiler_params=params,
    )(piece)
    edge = lax.ppermute(edge, "height", [(0, 1), (1, 0)])
    total, *weights = pl.pallas_call(
        functools.partial(shift_kernel, count, rows),
        out_shape=[jax.ShapeDtypeStruct((own, rows, frames, chans), f32)]
        + [jax.ShapeDtypeStruct(x.shape, bf16) for x in weights],
        in_specs=[near] + [far] * 5,
        out_specs=[near] * 6,
        scratch_shapes=[
            stored,
            pltpu.VMEM((span, rows, frames, TAPS * chans), bf16),
            pltpu.SemaphoreType.DMA((TAPS,)),
            pltpu.SemaphoreType.DMA((4,)),
        ],
        compiler_params=params,
    )(piece, *weights)
    blocks = pl.pallas_call(
        functools.partial(main_kernel, count, rows, group),
        out_shape=jax.ShapeDtypeStruct((group, own * lines, chans), bf16),
        in_specs=[far] + [near] * 7,
        out_specs=near,
        scratch_shapes=[
            pltpu.SMEM((frames,), jnp.int32),
            pltpu.VMEM((own, rows, frames, chans), f32),
            scratch(group * own * lines, chans),
            pltpu.SemaphoreType.DMA(()),
        ],
        compiler_params=params,
    )(in_far(ids), edge, total, *weights)
    return pl.pallas_call(
        unpack_kernel,
        out_shape=jax.ShapeDtypeStruct(video.shape, bf16),
        in_specs=[near],
        out_specs=far,
        scratch_shapes=[
            pltpu.VMEM(video.shape, bf16),
            scratch(lines * cols, chans),
            pltpu.SemaphoreType.DMA((lines,)),
        ],
        compiler_params=params,
    )(exchanged(blocks))


def solution(mesh):
    parts, along, halves = (mesh.shape[a] for a in ("groups", "tm", "height"))

    def run(video, *rest):
        count = video.shape[0] // (parts * along)
        group = min(g for g in range(1, along + 1) if along % g == 0 and (g * count >= REACH or g == along))
        outer = along // group
        split = Mesh(
            np.asarray(mesh.devices).reshape(parts, outer, group, halves),
            ("groups", "outer", "tm", "height"),
        )
        spec = P(("groups", "outer", "tm"), "height", None, None)
        placed = (spec, P("groups"), P(), P(), P(), P(), P())
        return jax.shard_map(
            functools.partial(per_device, outer),
            mesh=split,
            in_specs=placed,
            out_specs=spec,
            check_vma=False,
        )(video, *rest)

    return run
```

```python
import functools

import jax
import jax.numpy as jnp
import numpy as np
from jax import lax
from jax.experimental import pallas as pl
from jax.experimental.pallas import tpu as pltpu
from jax.sharding import Mesh, PartitionSpec as P

HD = 64
BLOCK = 4
TAPS = 3
REACH = 2 * BLOCK - 1 + TAPS - 1
LANES = 128
EDGE = 8
VMEM = 28 * 2**20

bf16, f32 = jnp.bfloat16, jnp.float32


def get(ref, start, size, stride):
    return jnp.concatenate([ref[i, pl.ds(start, size, stride=stride), :] for i in range(ref.shape[0])], axis=1)


def put(ref, start, size, stride, value):
    for i in range(ref.shape[0]):
        ref[i, pl.ds(start, size, stride=stride), :] = value[:, i * LANES : (i + 1) * LANES]


def fill(ref, start, value):
    for i in range(ref.shape[0]):
        ref[i, pl.ds(start, value.shape[0]), :] = value[:, i * LANES : (i + 1) * LANES]


def scratch(rows, chans):
    return pltpu.VMEM((chans // LANES, rows, LANES), f32)


def rms(wide):
    return wide * lax.rsqrt(jnp.mean(wide * wide, axis=-1, keepdims=True) + 1e-06)


def divided(at, by):
    if by & (by - 1) == 0:
        bits = by.bit_length() - 1
        return at >> bits, at & (by - 1)
    return lax.div(at, jnp.int32(by)), lax.rem(at, jnp.int32(by))


def pack_kernel(group, video, *refs):
    out, local, wide, sems = refs
    count, rows, cols, chans = video.shape
    lines = count * rows
    stride = cols + 2 * EDGE
    own = cols // group
    span = own + 2
    copies = []
    for at in range(lines):
        place = (at // rows, at % rows)
        copy = pltpu.make_async_copy(video.at[place], local.at[place], sems.at[at])
        copy.start()
        copies.append(copy)
    nothing = jnp.zeros((EDGE, chans), f32)
    for at in range(lines):
        fill(wide, at * stride, nothing)
        fill(wide, at * stride + EDGE + cols, nothing)
    for at, copy in enumerate(copies):
        copy.wait()
        fill(wide, at * stride + EDGE, local[at // rows, at % rows].astype(f32))
    together = 16 // lines
    for k in range(group):
        start = k * own + EDGE - 1
        for w in range(0, span, together):
            tile = jnp.concatenate([get(wide, start + w + i, lines, stride) for i in range(together)], axis=0)
            out[k, pl.ds(w * lines, 16), :] = tile.astype(bf16)


def frames_of(ref, w, r, count, rows, sources, step):
    return [get(ref, w * count * rows + t * rows + r, sources, step) for t in range(count)]


def shifted(now):
    count = len(now)
    sources, chans = now[0].shape
    first = lax.broadcasted_iota(jnp.int32, (sources, chans), 0) == 0
    past = [jnp.where(first, 0.0, pltpu.roll(x, 1, 0)) for x in now]
    ordered = past + now
    taps = []
    for a in range(TAPS):
        start = count - (TAPS - 1 - a)
        taps.append(jnp.concatenate(ordered[start : start + count], 0).astype(bf16))
    return jnp.concatenate(taps, axis=1)


def activated(wide):
    normal = rms(wide)
    return normal / (1.0 + jnp.exp(-normal))


def depth(parts):
    return parts[0] if len(parts) == 1 else jnp.concatenate(parts, axis=-1)


def edge_kernel(count, rows, video, edge, vid):
    sources, step, chans = video.shape
    span = step // (count * rows)
    fill(vid, 0, video[...].reshape(sources * step, chans).astype(f32))
    row = (rows - 1) * (1 - lax.axis_index("height"))
    for w in range(span):
        edge[w] = shifted([activated(x) for x in frames_of(vid, w, row, count, rows, sources, step)])


def shift_kernel(count, rows, video, *refs):
    far, (total, *near), (vid, grid, conv_sems, sems) = refs[:5], refs[5:11], refs[11:]
    conv_far, conv_weight = far[0], near[0]
    order = [1, 0, 2]
    taps = {b: pltpu.make_async_copy(conv_far.at[:, b], conv_weight.at[:, b], conv_sems.at[b]) for b in order}
    others = [pltpu.make_async_copy(far[i], near[i], sems.at[i - 1]) for i in range(1, 5)]
    for copy in list(taps.values()) + others:
        copy.start()
    sources, step, chans = video.shape
    span = step // (count * rows)
    own = span - 2
    frames = sources * count
    half = own // 2 if own % 2 == 0 else own
    fill(vid, 0, video[...].reshape(sources * step, chans).astype(f32))
    for w in range(span):
        for r in range(rows):
            now = frames_of(vid, w, r, count, rows, sources, step)
            grid[w, r] = shifted([activated(x) for x in now])
            if 1 <= w <= own:
                total[w - 1, r] = jnp.concatenate(now, 0)

    for b in order:
        taps[b].wait()
        low, high = max(0, 1 - b), min(rows, rows + 1 - b)
        weight = jnp.concatenate([conv_weight[a, b, e] for e in range(TAPS) for a in range(TAPS)], axis=0)
        for w in range(0, own, half):
            window = depth([grid[w + e : w + e + half, low + b - 1 : high + b - 1] for e in range(TAPS)])
            window = window.reshape(half * (high - low) * frames, TAPS * TAPS * chans)
            part = jnp.dot(window, weight, preferred_element_type=f32)
            some = total.at[w : w + half, low:high]
            some[...] = some[...] + part.reshape(half, high - low, frames, chans)
    for copy in others:
        copy.wait()


def main_kernel(
    count, rows, group, ids_far, edge, given, conv_weight, w_query, w_key, w_value, w_output, *refs
):
    out, ids, shown, res, sem = refs
    ids_copy = pltpu.make_async_copy(ids_far, ids, sem)
    ids_copy.start()
    own, _, frames, chans = given.shape
    sources = frames // count
    lines = count * rows
    heads = chans // HD
    back = own * lines
    several = max(n for n in range(1, own + 1) if own % n == 0 and (n == 1 or n * rows * frames <= LANES))
    area = several * rows * frames

    lower = lax.axis_index("height")
    window = depth([edge[e : e + own] for e in range(TAPS)]).reshape(own * frames, TAPS * TAPS * chans)
    b = (TAPS - 1) * (1 - lower)
    weight = jnp.concatenate([conv_weight[a, b, e] for e in range(TAPS) for a in range(TAPS)], axis=0)
    part = jnp.dot(window, weight, preferred_element_type=f32).reshape(own, frames, chans)
    for r in range(rows):
        shown[:, r] = given[:, r] + jnp.where(r == (rows - 1) * (1 - lower), part, 0.0)

    hidden = shown[...].reshape(own * rows * frames, chans).astype(bf16).astype(f32)
    normed = rms(hidden).astype(bf16)
    query, keys, values = (
        jnp.dot(normed, weight[...], preferred_element_type=f32).astype(bf16) for weight in (w_query, w_key, w_value)
    )

    ids_copy.wait()

    def place_of(shape, dim):
        inner, source = divided(lax.broadcasted_iota(jnp.int32, shape, dim) % frames, sources)
        frame = source * count + inner
        block = jnp.zeros(shape, jnp.int32)
        for s in range(frames):
            block = jnp.where(frame == s, ids[s], block)
        return frame, block

    pixels = several * rows
    row_t, row_b = (jnp.concatenate([x] * pixels, 0) for x in place_of((frames, area), 0))
    col_t, col_b = place_of((1, area), 1)
    row_p = divided(lax.broadcasted_iota(jnp.int32, (area, area), 0), frames)[0]
    col_p = divided(lax.broadcasted_iota(jnp.int32, (area, area), 1), frames)[0]
    permit = (row_p == col_p) & (col_t <= row_t) & (col_b >= row_b - 1)
    bias = jnp.where(permit, 0.0, -1e30)
    head_of = divided(lax.broadcasted_iota(jnp.int32, (area, chans), 1), HD)[0]
    single = [jnp.where(head_of == h, 1.0, 0.0).astype(bf16) for h in range(heads)]

    gone = []
    for w in range(0, own, several):
        part = slice(w * rows * frames, w * rows * frames + area)
        heads_keys = jnp.concatenate([keys[part] * mask for mask in single], axis=0)
        heads_values = jnp.concatenate([values[part] * mask for mask in single], axis=0)
        scores = lax.dot_general(query[part], heads_keys, (((1,), (1,)), ((), ())), preferred_element_type=f32)
        weights = []
        for h in range(heads):
            score = scores[:, h * area : (h + 1) * area] * HD ** (-0.5) + bias
            expo = jnp.exp(score - jnp.max(score, axis=-1, keepdims=True))
            weights.append((expo * (1.0 / jnp.sum(expo, axis=-1, keepdims=True))).astype(bf16))
        attended = jnp.dot(jnp.concatenate(weights, axis=1), heads_values, preferred_element_type=f32)
        gone.append(attended.astype(bf16))
    attended = jnp.concatenate(gone, axis=0)
    encoded = hidden + jnp.dot(attended, w_output[...], preferred_element_type=f32)
    for w in range(own):
        for r in range(rows):
            for t in range(count):
                start = ((w * rows + r) * count + t + 1) * sources - group
                put(res, w * lines + t * rows + r, group, back, encoded[start : start + group])
    done = jnp.concatenate([res[i] for i in range(res.shape[0])], axis=1)
    out[...] = done.astype(bf16).reshape(out.shape)


def unpack_kernel(packed, out, local, wide, sems):
    count, rows, cols, chans = out.shape
    lines = count * rows
    fill(wide, 0, packed[...].reshape(lines * cols, chans).astype(f32))
    copies = []
    for at in range(lines):
        place = (at // rows, at % rows)
        local[place] = get(wide, at, cols, lines).astype(bf16)
        copy = pltpu.make_async_copy(local.at[place], out.at[place], sems.at[at])
        copy.start()
        copies.append(copy)
    for copy in copies:
        copy.wait()


def exchanged(blocks):
    return lax.all_to_all(blocks, "tm", split_axis=0, concat_axis=0, tiled=True)


def per_device(outer, video, block_ids, conv_weight, w_query, w_key, w_value, w_output):
    count, rows, cols, chans = video.shape
    group = lax.axis_size("tm")
    own = cols // group
    span = own + 2
    lines = count * rows
    near = pl.BlockSpec(memory_space=pltpu.VMEM)
    far = pl.BlockSpec(memory_space=pltpu.HBM)
    params = pltpu.CompilerParams(vmem_limit_bytes=VMEM)
    in_far = functools.partial(pltpu.with_memory_space_constraint, memory_space=pltpu.HBM)
    weights = [in_far(x) for x in (conv_weight, w_query, w_key, w_value, w_output)]

    blocks = pl.pallas_call(
        functools.partial(pack_kernel, group),
        out_shape=jax.ShapeDtypeStruct((group, span * lines, chans), bf16),
        in_specs=[far],
        out_specs=near,
        scratch_shapes=[
            pltpu.VMEM(video.shape, bf16),
            scratch(lines * (cols + 2 * EDGE), chans),
            pltpu.SemaphoreType.DMA((lines,)),
        ],
        compiler_params=params,
    )(in_far(video))
    piece = exchanged(blocks)
    ids = block_ids
    if outer > 1:
        before = lax.ppermute(piece, "outer", [(i, i + 1) for i in range(outer - 1)])
        piece = jnp.concatenate([before, piece], axis=0)
        ids = jnp.concatenate([jnp.full((group * count,), -2, jnp.int32), ids])
        ids = lax.dynamic_slice(ids, (lax.axis_index("outer") * group * count,), (2 * group * count,))
    sources = piece.shape[0]
    frames = sources * count
    stored = scratch(sources * span * lines, chans)
    edge = pl.pallas_call(
        functools.partial(edge_kernel, count, rows),
        out_shape=jax.ShapeDtypeStruct((span, frames, TAPS * chans), bf16),
        in_specs=[near],
        out_specs=near,
        scratch_shapes=[stored],
        compiler_params=params,
    )(piece)
    edge = lax.ppermute(edge, "height", [(0, 1), (1, 0)])
    total, *weights = pl.pallas_call(
        functools.partial(shift_kernel, count, rows),
        out_shape=[jax.ShapeDtypeStruct((own, rows, frames, chans), f32)]
        + [jax.ShapeDtypeStruct(x.shape, bf16) for x in weights],
        in_specs=[near] + [far] * 5,
        out_specs=[near] * 6,
        scratch_shapes=[
            stored,
            pltpu.VMEM((span, rows, frames, TAPS * chans), bf16),
            pltpu.SemaphoreType.DMA((TAPS,)),
            pltpu.SemaphoreType.DMA((4,)),
        ],
        compiler_params=params,
    )(piece, *weights)
    blocks = pl.pallas_call(
        functools.partial(main_kernel, count, rows, group),
        out_shape=jax.ShapeDtypeStruct((group, own * lines, chans), bf16),
        in_specs=[far] + [near] * 7,
        out_specs=near,
        scratch_shapes=[
            pltpu.SMEM((frames,), jnp.int32),
            pltpu.VMEM((own, rows, frames, chans), f32),
            scratch(group * own * lines, chans),
            pltpu.SemaphoreType.DMA(()),
        ],
        compiler_params=params,
    )(in_far(ids), edge, total, *weights)
    return pl.pallas_call(
        unpack_kernel,
        out_shape=jax.ShapeDtypeStruct(video.shape, bf16),
        in_specs=[near],
        out_specs=far,
        scratch_shapes=[
            pltpu.VMEM(video.shape, bf16),
            scratch(lines * cols, chans),
            pltpu.SemaphoreType.DMA((lines,)),
        ],
        compiler_params=params,
    )(exchanged(blocks))


def solution(mesh):
    parts, along, halves = (mesh.shape[a] for a in ("groups", "tm", "height"))

    def run(video, *rest):
        count = video.shape[0] // (parts * along)
        group = min(g for g in range(1, along + 1) if along % g == 0 and (g * count >= REACH or g == along))
        outer = along // group
        split = Mesh(
            np.asarray(mesh.devices).reshape(parts, outer, group, halves),
            ("groups", "outer", "tm", "height"),
        )
        spec = P(("groups", "outer", "tm"), "height", None, None)
        placed = (spec, P("groups"), P(), P(), P(), P(), P())
        return jax.shard_map(
            functools.partial(per_device, outer),
            mesh=split,
            in_specs=placed,
            out_specs=spec,
            check_vma=False,
        )(video, *rest)

    return run
```

```python
import functools

import jax
import jax.numpy as jnp
import numpy as np
from jax import lax
from jax.experimental import pallas as pl
from jax.experimental.pallas import tpu as pltpu
from jax.sharding import Mesh, PartitionSpec as P

HD = 64
BLOCK = 4
TAPS = 3
REACH = 2 * BLOCK - 1 + TAPS - 1
LANES = 128
EDGE = 8
VMEM = 28 * 2**20

bf16, f32 = jnp.bfloat16, jnp.float32


def get(ref, start, size, stride):
    return jnp.concatenate([ref[i, pl.ds(start, size, stride=stride), :] for i in range(ref.shape[0])], axis=1)


def put(ref, start, size, stride, value):
    for i in range(ref.shape[0]):
        ref[i, pl.ds(start, size, stride=stride), :] = value[:, i * LANES : (i + 1) * LANES]


def fill(ref, start, value):
    for i in range(ref.shape[0]):
        ref[i, pl.ds(start, value.shape[0]), :] = value[:, i * LANES : (i + 1) * LANES]


def scratch(rows, chans):
    return pltpu.VMEM((chans // LANES, rows, LANES), f32)


def rms(wide):
    return wide * lax.rsqrt(jnp.mean(wide * wide, axis=-1, keepdims=True) + 1e-06)


def divided(at, by):
    if by & (by - 1) == 0:
        bits = by.bit_length() - 1
        return at >> bits, at & (by - 1)
    return lax.div(at, jnp.int32(by)), lax.rem(at, jnp.int32(by))


def pack_kernel(group, video, *refs):
    out, local, wide, sems = refs
    count, rows, cols, chans = video.shape
    lines = count * rows
    stride = cols + 2 * EDGE
    own = cols // group
    span = own + 2
    copies = []
    for at in range(lines):
        place = (at // rows, at % rows)
        copy = pltpu.make_async_copy(video.at[place], local.at[place], sems.at[at])
        copy.start()
        copies.append(copy)
    nothing = jnp.zeros((EDGE, chans), f32)
    for at in range(lines):
        fill(wide, at * stride, nothing)
        fill(wide, at * stride + EDGE + cols, nothing)
    for at, copy in enumerate(copies):
        copy.wait()
        fill(wide, at * stride + EDGE, local[at // rows, at % rows].astype(f32))
    together = 16 // lines
    for k in range(group):
        start = k * own + EDGE - 1
        for w in range(0, span, together):
            tile = jnp.concatenate([get(wide, start + w + i, lines, stride) for i in range(together)], axis=0)
            out[k, pl.ds(w * lines, 16), :] = tile.astype(bf16)


def frames_of(ref, w, r, count, rows, sources, step):
    return [get(ref, w * count * rows + t * rows + r, sources, step) for t in range(count)]


def shifted(now):
    count = len(now)
    sources, chans = now[0].shape
    first = lax.broadcasted_iota(jnp.int32, (sources, chans), 0) == 0
    past = [jnp.where(first, 0.0, pltpu.roll(x, 1, 0)) for x in now]
    ordered = past + now
    taps = []
    for a in range(TAPS):
        start = count - (TAPS - 1 - a)
        taps.append(jnp.concatenate(ordered[start : start + count], 0).astype(bf16))
    return jnp.concatenate(taps, axis=1)


def activated(wide):
    normal = rms(wide)
    return normal / (1.0 + jnp.exp(-normal))


def depth(parts):
    return parts[0] if len(parts) == 1 else jnp.concatenate(parts, axis=-1)


def edge_kernel(count, rows, video, edge, vid):
    sources, step, chans = video.shape
    span = step // (count * rows)
    fill(vid, 0, video[...].reshape(sources * step, chans).astype(f32))
    row = (rows - 1) * (1 - lax.axis_index("height"))
    for w in range(span):
        edge[w] = shifted([activated(x) for x in frames_of(vid, w, row, count, rows, sources, step)])


def fill_bias(bias, ids, frames, count):
    area = bias.shape[0]
    sources = frames // count

    def place_of(at):
        pixel, place = divided(at, frames)
        inner, source = divided(place, sources)
        frame = source * count + inner
        block = jnp.zeros(at.shape, jnp.int32)
        for s in range(frames):
            block = jnp.where(frame == s, ids[s], block)
        return pixel, frame, block

    row_p, row_t, row_b = place_of(lax.broadcasted_iota(jnp.int32, (area, area), 0))
    col_p, col_t, col_b = place_of(lax.broadcasted_iota(jnp.int32, (1, area), 1))
    permit = (row_p == col_p) & (col_t <= row_t) & (col_b >= row_b - 1)
    bias[...] = jnp.where(permit, 0.0, -1e30)


def shift_kernel(count, rows, video, ids_far, *refs):
    far, (total, bias, *near), (vid, grid, ids, conv_sems, sems, ids_sem) = refs[:5], refs[5:12], refs[12:]
    ids_copy = pltpu.make_async_copy(ids_far, ids, ids_sem)
    ids_copy.start()
    conv_far, conv_weight = far[0], near[0]
    order = [1, 0, 2]
    taps = {b: pltpu.make_async_copy(conv_far.at[:, b], conv_weight.at[:, b], conv_sems.at[b]) for b in order}
    others = [pltpu.make_async_copy(far[i], near[i], sems.at[i - 1]) for i in range(1, 5)]
    for copy in list(taps.values()) + others:
        copy.start()
    sources, step, chans = video.shape
    span = step // (count * rows)
    own = span - 2
    frames = sources * count
    half = own // 4 if own % 4 == 0 else own
    fill(vid, 0, video[...].reshape(sources * step, chans).astype(f32))
    for w in range(span):
        for r in range(rows):
            now = frames_of(vid, w, r, count, rows, sources, step)
            grid[w, r] = shifted([activated(x) for x in now])
            if 1 <= w <= own:
                total[w - 1, r] = jnp.concatenate(now, 0)

    ids_copy.wait()
    fill_bias(bias, ids, frames, count)
    for b in order:
        taps[b].wait()
        low, high = max(0, 1 - b), min(rows, rows + 1 - b)
        weight = jnp.concatenate([conv_weight[a, b, e] for e in range(TAPS) for a in range(TAPS)], axis=0)
        for w in range(0, own, half):
            window = depth([grid[w + e : w + e + half, low + b - 1 : high + b - 1] for e in range(TAPS)])
            window = window.reshape(half * (high - low) * frames, TAPS * TAPS * chans)
            part = jnp.dot(window, weight, preferred_element_type=f32)
            some = total.at[w : w + half, low:high]
            some[...] = some[...] + part.reshape(half, high - low, frames, chans)
    for copy in others:
        copy.wait()


def main_kernel(
    count, rows, group, edge, given, bias, conv_weight, w_query, w_key, w_value, w_output, *refs
):
    out, res = refs
    own, _, frames, chans = given.shape
    sources = frames // count
    lines = count * rows
    heads = chans // HD
    back = own * lines
    area = bias.shape[0]
    several = area // (rows * frames)

    lower = lax.axis_index("height")
    b = (TAPS - 1) * (1 - lower)
    part = jnp.zeros((own * frames, chans), f32)
    for e in range(TAPS):
        window = edge[e : e + own].reshape(own * frames, TAPS * chans)
        weight = jnp.concatenate([conv_weight[a, b, e] for a in range(TAPS)], axis=0)
        part = part + jnp.dot(window, weight, preferred_element_type=f32)
    part = part.reshape(own, frames, chans)

    head_of = divided(lax.broadcasted_iota(jnp.int32, (area, chans), 1), HD)[0]
    single = [jnp.where(head_of == h, 1.0, 0.0).astype(bf16) for h in range(heads)]
    scaled = [mask * jnp.asarray(HD ** (-0.5), bf16) for mask in single]

    half = own // 2 if own % (2 * several) == 0 else own
    for start in range(0, own, half):
        lines_of = []
        for r in range(rows):
            row = given[start : start + half, r]
            row = row + jnp.where(r == (rows - 1) * (1 - lower), part[start : start + half], 0.0)
            lines_of.append(row[:, None])
        hidden = jnp.concatenate(lines_of, axis=1).reshape(half * rows * frames, chans).astype(bf16).astype(f32)
        normed = rms(hidden).astype(bf16)
        query, keys, values = (
            jnp.dot(normed, weight[...], preferred_element_type=f32).astype(bf16)
            for weight in (w_query, w_key, w_value)
        )
        gone = []
        for at in range(0, half * rows * frames, area):
            group_of = slice(at, at + area)
            queries = jnp.concatenate([query[group_of] * mask for mask in scaled], axis=0)
            scores = lax.dot_general(
                queries, keys[group_of], (((1,), (1,)), ((), ())), preferred_element_type=f32
            )
            weights = []
            for h in range(heads):
                score = scores[h * area : (h + 1) * area] + bias[...]
                expo = jnp.exp(score - jnp.max(score, axis=-1, keepdims=True))
                weights.append((expo * (1.0 / jnp.sum(expo, axis=-1, keepdims=True))).astype(bf16))
            heads_values = jnp.concatenate([values[group_of] * mask for mask in single], axis=0)
            attended = jnp.dot(jnp.concatenate(weights, axis=1), heads_values, preferred_element_type=f32)
            gone.append(attended.astype(bf16))
        attended = jnp.concatenate(gone, axis=0)
        encoded = hidden + jnp.dot(attended, w_output[...], preferred_element_type=f32)
        for w in range(half):
            for r in range(rows):
                for t in range(count):
                    first = ((w * rows + r) * count + t + 1) * sources - group
                    place = (start + w) * lines + t * rows + r
                    put(res, place, group, back, encoded[first : first + group])
    done = jnp.concatenate([res[i] for i in range(res.shape[0])], axis=1)
    out[...] = done.astype(bf16).reshape(out.shape)


def unpack_kernel(packed, out, local, wide, sems):
    count, rows, cols, chans = out.shape
    lines = count * rows
    fill(wide, 0, packed[...].reshape(lines * cols, chans).astype(f32))
    copies = []
    for at in range(lines):
        place = (at // rows, at % rows)
        local[place] = get(wide, at, cols, lines).astype(bf16)
        copy = pltpu.make_async_copy(local.at[place], out.at[place], sems.at[at])
        copy.start()
        copies.append(copy)
    for copy in copies:
        copy.wait()


def exchanged(blocks):
    return lax.all_to_all(blocks, "tm", split_axis=0, concat_axis=0, tiled=True)


def per_device(outer, video, block_ids, conv_weight, w_query, w_key, w_value, w_output):
    count, rows, cols, chans = video.shape
    group = lax.axis_size("tm")
    own = cols // group
    span = own + 2
    lines = count * rows
    near = pl.BlockSpec(memory_space=pltpu.VMEM)
    far = pl.BlockSpec(memory_space=pltpu.HBM)
    params = pltpu.CompilerParams(vmem_limit_bytes=VMEM)
    in_far = functools.partial(pltpu.with_memory_space_constraint, memory_space=pltpu.HBM)
    weights = [in_far(x) for x in (conv_weight, w_query, w_key, w_value, w_output)]

    blocks = pl.pallas_call(
        functools.partial(pack_kernel, group),
        out_shape=jax.ShapeDtypeStruct((group, span * lines, chans), bf16),
        in_specs=[far],
        out_specs=near,
        scratch_shapes=[
            pltpu.VMEM(video.shape, bf16),
            scratch(lines * (cols + 2 * EDGE), chans),
            pltpu.SemaphoreType.DMA((lines,)),
        ],
        compiler_params=params,
    )(in_far(video))
    piece = exchanged(blocks)
    ids = block_ids
    if outer > 1:
        before = lax.ppermute(piece, "outer", [(i, i + 1) for i in range(outer - 1)])
        piece = jnp.concatenate([before, piece], axis=0)
        ids = jnp.concatenate([jnp.full((group * count,), -2, jnp.int32), ids])
        ids = lax.dynamic_slice(ids, (lax.axis_index("outer") * group * count,), (2 * group * count,))
    sources = piece.shape[0]
    frames = sources * count
    stored = scratch(sources * span * lines, chans)
    edge = pl.pallas_call(
        functools.partial(edge_kernel, count, rows),
        out_shape=jax.ShapeDtypeStruct((span, frames, TAPS * chans), bf16),
        in_specs=[near],
        out_specs=near,
        scratch_shapes=[stored],
        compiler_params=params,
    )(piece)
    edge = lax.ppermute(edge, "height", [(0, 1), (1, 0)])
    several = max(n for n in range(1, own + 1) if own % n == 0 and (n == 1 or n * rows * frames <= LANES))
    area = several * rows * frames
    total, bias, *weights = pl.pallas_call(
        functools.partial(shift_kernel, count, rows),
        out_shape=[
            jax.ShapeDtypeStruct((own, rows, frames, chans), f32),
            jax.ShapeDtypeStruct((area, area), f32),
        ]
        + [jax.ShapeDtypeStruct(x.shape, bf16) for x in weights],
        in_specs=[near] + [far] * 6,
        out_specs=[near] * 7,
        scratch_shapes=[
            stored,
            pltpu.VMEM((span, rows, frames, TAPS * chans), bf16),
            pltpu.SMEM((frames,), jnp.int32),
            pltpu.SemaphoreType.DMA((TAPS,)),
            pltpu.SemaphoreType.DMA((4,)),
            pltpu.SemaphoreType.DMA(()),
        ],
        compiler_params=params,
    )(piece, in_far(ids), *weights)
    blocks = pl.pallas_call(
        functools.partial(main_kernel, count, rows, group),
        out_shape=jax.ShapeDtypeStruct((group, own * lines, chans), bf16),
        in_specs=[near] * 8,
        out_specs=near,
        scratch_shapes=[scratch(group * own * lines, chans)],
        compiler_params=params,
    )(edge, total, bias, *weights)
    return pl.pallas_call(
        unpack_kernel,
        out_shape=jax.ShapeDtypeStruct(video.shape, bf16),
        in_specs=[near],
        out_specs=far,
        scratch_shapes=[
            pltpu.VMEM(video.shape, bf16),
            scratch(lines * cols, chans),
            pltpu.SemaphoreType.DMA((lines,)),
        ],
        compiler_params=params,
    )(exchanged(blocks))


def solution(mesh):
    parts, along, halves = (mesh.shape[a] for a in ("groups", "tm", "height"))

    def run(video, *rest):
        count = video.shape[0] // (parts * along)
        group = min(g for g in range(1, along + 1) if along % g == 0 and (g * count >= REACH or g == along))
        outer = along // group
        split = Mesh(
            np.asarray(mesh.devices).reshape(parts, outer, group, halves),
            ("groups", "outer", "tm", "height"),
        )
        spec = P(("groups", "outer", "tm"), "height", None, None)
        placed = (spec, P("groups"), P(), P(), P(), P(), P())
        return jax.shard_map(
            functools.partial(per_device, outer),
            mesh=split,
            in_specs=placed,
            out_specs=spec,
            check_vma=False,
        )(video, *rest)

    return run
```

```python
import functools

import jax
import jax.numpy as jnp
import numpy as np
from jax import lax
from jax.experimental import pallas as pl
from jax.experimental.pallas import tpu as pltpu
from jax.sharding import Mesh, PartitionSpec as P

HD = 64
BLOCK = 4
TAPS = 3
REACH = 2 * BLOCK - 1 + TAPS - 1
LANES = 128
EDGE = 8
VMEM = 28 * 2**20

bf16, f32 = jnp.bfloat16, jnp.float32


def get(ref, start, size, stride):
    return jnp.concatenate([ref[i, pl.ds(start, size, stride=stride), :] for i in range(ref.shape[0])], axis=1)


def put(ref, start, size, stride, value):
    for i in range(ref.shape[0]):
        ref[i, pl.ds(start, size, stride=stride), :] = value[:, i * LANES : (i + 1) * LANES]


def fill(ref, start, value):
    for i in range(ref.shape[0]):
        ref[i, pl.ds(start, value.shape[0]), :] = value[:, i * LANES : (i + 1) * LANES]


def scratch(rows, chans):
    return pltpu.VMEM((chans // LANES, rows, LANES), f32)


def rms(wide):
    return wide * lax.rsqrt(jnp.mean(wide * wide, axis=-1, keepdims=True) + 1e-06)


def divided(at, by):
    if by & (by - 1) == 0:
        bits = by.bit_length() - 1
        return at >> bits, at & (by - 1)
    return lax.div(at, jnp.int32(by)), lax.rem(at, jnp.int32(by))


def pack_kernel(group, video, *refs):
    out, local, wide, sems = refs
    count, rows, cols, chans = video.shape
    lines = count * rows
    stride = cols + 2 * EDGE
    own = cols // group
    span = own + 2
    copies = []
    for at in range(lines):
        place = (at // rows, at % rows)
        copy = pltpu.make_async_copy(video.at[place], local.at[place], sems.at[at])
        copy.start()
        copies.append(copy)
    nothing = jnp.zeros((EDGE, chans), f32)
    for at in range(lines):
        fill(wide, at * stride, nothing)
        fill(wide, at * stride + EDGE + cols, nothing)
    for at, copy in enumerate(copies):
        copy.wait()
        fill(wide, at * stride + EDGE, local[at // rows, at % rows].astype(f32))
    together = 16 // lines
    for k in range(group):
        start = k * own + EDGE - 1
        for w in range(0, span, together):
            tile = jnp.concatenate([get(wide, start + w + i, lines, stride) for i in range(together)], axis=0)
            out[k, pl.ds(w * lines, 16), :] = tile.astype(bf16)


def frames_of(ref, w, r, count, rows, sources, step):
    return [get(ref, w * count * rows + t * rows + r, sources, step) for t in range(count)]


def shifted(now):
    count = len(now)
    sources, chans = now[0].shape
    first = lax.broadcasted_iota(jnp.int32, (sources, chans), 0) == 0
    past = [jnp.where(first, 0.0, pltpu.roll(x, 1, 0)) for x in now]
    ordered = past + now
    taps = []
    for a in range(TAPS):
        start = count - (TAPS - 1 - a)
        taps.append(jnp.concatenate(ordered[start : start + count], 0).astype(bf16))
    return jnp.concatenate(taps, axis=1)


def activated(wide):
    normal = rms(wide)
    return normal / (1.0 + jnp.exp(-normal))


def depth(parts):
    return parts[0] if len(parts) == 1 else jnp.concatenate(parts, axis=-1)


def edge_kernel(count, rows, video, edge, vid):
    sources, step, chans = video.shape
    span = step // (count * rows)
    fill(vid, 0, video[...].reshape(sources * step, chans).astype(f32))
    row = (rows - 1) * (1 - lax.axis_index("height"))
    for w in range(span):
        edge[w] = shifted([activated(x) for x in frames_of(vid, w, row, count, rows, sources, step)])


def fill_bias(bias, ids, frames, count):
    area = bias.shape[0]
    sources = frames // count

    def place_of(at):
        pixel, place = divided(at, frames)
        inner, source = divided(place, sources)
        frame = source * count + inner
        block = jnp.zeros(at.shape, jnp.int32)
        for s in range(frames):
            block = jnp.where(frame == s, ids[s], block)
        return pixel, frame, block

    row_p, row_t, row_b = place_of(lax.broadcasted_iota(jnp.int32, (area, area), 0))
    col_p, col_t, col_b = place_of(lax.broadcasted_iota(jnp.int32, (1, area), 1))
    permit = (row_p == col_p) & (col_t <= row_t) & (col_b >= row_b - 1)
    bias[...] = jnp.where(permit, 0.0, -1e30)


def shift_kernel(count, rows, video, ids_far, *refs):
    far, (total, bias, *near), (vid, grid, ids, conv_sems, sems, ids_sem) = refs[:5], refs[5:12], refs[12:]
    ids_copy = pltpu.make_async_copy(ids_far, ids, ids_sem)
    ids_copy.start()
    conv_far, conv_weight = far[0], near[0]
    order = [1, 0, 2]
    taps = {b: pltpu.make_async_copy(conv_far.at[:, b], conv_weight.at[:, b], conv_sems.at[b]) for b in order}
    others = [pltpu.make_async_copy(far[i], near[i], sems.at[i - 1]) for i in range(1, 5)]
    taps[order[0]].start()
    sources, step, chans = video.shape
    span = step // (count * rows)
    own = span - 2
    frames = sources * count
    half = own // 2 if own % 2 == 0 else own
    fill(vid, 0, video[...].reshape(sources * step, chans).astype(f32))
    for w in range(span):
        for r in range(rows):
            now = frames_of(vid, w, r, count, rows, sources, step)
            grid[w, r] = shifted([activated(x) for x in now])
            if 1 <= w <= own:
                total[w - 1, r] = jnp.concatenate(now, 0)
        if w == span // 2:
            taps[order[1]].start()
    taps[order[2]].start()
    for copy in others:
        copy.start()

    ids_copy.wait()
    fill_bias(bias, ids, frames, count)
    for b in order:
        taps[b].wait()
        low, high = max(0, 1 - b), min(rows, rows + 1 - b)
        weight = jnp.concatenate([conv_weight[a, b, e] for e in range(TAPS) for a in range(TAPS)], axis=0)
        for w in range(0, own, half):
            window = depth([grid[w + e : w + e + half, low + b - 1 : high + b - 1] for e in range(TAPS)])
            window = window.reshape(half * (high - low) * frames, TAPS * TAPS * chans)
            part = jnp.dot(window, weight, preferred_element_type=f32)
            some = total.at[w : w + half, low:high]
            some[...] = some[...] + part.reshape(half, high - low, frames, chans)
    for copy in others:
        copy.wait()


def main_kernel(
    count, rows, group, edge, given, bias, conv_weight, w_query, w_key, w_value, w_output, *refs
):
    out, res = refs
    own, _, frames, chans = given.shape
    sources = frames // count
    lines = count * rows
    heads = chans // HD
    back = own * lines
    area = bias.shape[0]
    several = area // (rows * frames)

    lower = lax.axis_index("height")
    b = (TAPS - 1) * (1 - lower)
    part = jnp.zeros((own * frames, chans), f32)
    for e in range(TAPS):
        window = edge[e : e + own].reshape(own * frames, TAPS * chans)
        weight = jnp.concatenate([conv_weight[a, b, e] for a in range(TAPS)], axis=0)
        part = part + jnp.dot(window, weight, preferred_element_type=f32)
    part = part.reshape(own, frames, chans)

    head_of = divided(lax.broadcasted_iota(jnp.int32, (area, chans), 1), HD)[0]
    single = [jnp.where(head_of == h, 1.0, 0.0).astype(bf16) for h in range(heads)]
    scaled = [mask * jnp.asarray(HD ** (-0.5), bf16) for mask in single]

    half = own // 2 if own % (2 * several) == 0 else own
    for start in range(0, own, half):
        lines_of = []
        for r in range(rows):
            row = given[start : start + half, r]
            row = row + jnp.where(r == (rows - 1) * (1 - lower), part[start : start + half], 0.0)
            lines_of.append(row[:, None])
        hidden = jnp.concatenate(lines_of, axis=1).reshape(half * rows * frames, chans).astype(bf16).astype(f32)
        normed = rms(hidden).astype(bf16)
        query, keys, values = (
            jnp.dot(normed, weight[...], preferred_element_type=f32).astype(bf16)
            for weight in (w_query, w_key, w_value)
        )
        gone = []
        for at in range(0, half * rows * frames, area):
            group_of = slice(at, at + area)
            queries = jnp.concatenate([query[group_of] * mask for mask in scaled], axis=0)
            scores = lax.dot_general(
                queries, keys[group_of], (((1,), (1,)), ((), ())), preferred_element_type=f32
            )
            weights = []
            for h in range(heads):
                score = scores[h * area : (h + 1) * area] + bias[...]
                expo = jnp.exp(score - jnp.max(score, axis=-1, keepdims=True))
                weights.append((expo * (1.0 / jnp.sum(expo, axis=-1, keepdims=True))).astype(bf16))
            heads_values = jnp.concatenate([values[group_of] * mask for mask in single], axis=0)
            attended = jnp.dot(jnp.concatenate(weights, axis=1), heads_values, preferred_element_type=f32)
            gone.append(attended.astype(bf16))
        attended = jnp.concatenate(gone, axis=0)
        encoded = hidden + jnp.dot(attended, w_output[...], preferred_element_type=f32)
        for w in range(half):
            for r in range(rows):
                for t in range(count):
                    first = ((w * rows + r) * count + t + 1) * sources - group
                    place = (t * rows + r) * own + start + w
                    put(res, place, group, back, encoded[first : first + group])
    done = jnp.concatenate([res[i] for i in range(res.shape[0])], axis=1)
    out[...] = done.astype(bf16).reshape(out.shape)


def unpack_kernel(packed, out, local, sems):
    count, rows, cols, chans = out.shape
    lines = count * rows
    regions = packed.shape[0]
    own = cols // regions
    wide = packed[...].astype(f32).reshape(regions, lines, own, chans)
    copies = []
    for at in range(lines):
        place = (at // rows, at % rows)
        local[place] = wide[:, at].reshape(cols, chans).astype(bf16)
        copy = pltpu.make_async_copy(local.at[place], out.at[place], sems.at[at])
        copy.start()
        copies.append(copy)
    for copy in copies:
        copy.wait()


def exchanged(blocks):
    return lax.all_to_all(blocks, "tm", split_axis=0, concat_axis=0, tiled=True)


def per_device(outer, video, block_ids, conv_weight, w_query, w_key, w_value, w_output):
    count, rows, cols, chans = video.shape
    group = lax.axis_size("tm")
    own = cols // group
    span = own + 2
    lines = count * rows
    near = pl.BlockSpec(memory_space=pltpu.VMEM)
    far = pl.BlockSpec(memory_space=pltpu.HBM)
    params = pltpu.CompilerParams(vmem_limit_bytes=VMEM)
    in_far = functools.partial(pltpu.with_memory_space_constraint, memory_space=pltpu.HBM)
    weights = [in_far(x) for x in (conv_weight, w_query, w_key, w_value, w_output)]

    blocks = pl.pallas_call(
        functools.partial(pack_kernel, group),
        out_shape=jax.ShapeDtypeStruct((group, span * lines, chans), bf16),
        in_specs=[far],
        out_specs=near,
        scratch_shapes=[
            pltpu.VMEM(video.shape, bf16),
            scratch(lines * (cols + 2 * EDGE), chans),
            pltpu.SemaphoreType.DMA((lines,)),
        ],
        compiler_params=params,
    )(in_far(video))
    piece = exchanged(blocks)
    ids = block_ids
    if outer > 1:
        before = lax.ppermute(piece, "outer", [(i, i + 1) for i in range(outer - 1)])
        piece = jnp.concatenate([before, piece], axis=0)
        ids = jnp.concatenate([jnp.full((group * count,), -2, jnp.int32), ids])
        ids = lax.dynamic_slice(ids, (lax.axis_index("outer") * group * count,), (2 * group * count,))
    sources = piece.shape[0]
    frames = sources * count
    stored = scratch(sources * span * lines, chans)
    edge = pl.pallas_call(
        functools.partial(edge_kernel, count, rows),
        out_shape=jax.ShapeDtypeStruct((span, frames, TAPS * chans), bf16),
        in_specs=[near],
        out_specs=near,
        scratch_shapes=[stored],
        compiler_params=params,
    )(piece)
    edge = lax.ppermute(edge, "height", [(0, 1), (1, 0)])
    several = max(n for n in range(1, own + 1) if own % n == 0 and (n == 1 or n * rows * frames <= LANES))
    area = several * rows * frames
    total, bias, *weights = pl.pallas_call(
        functools.partial(shift_kernel, count, rows),
        out_shape=[
            jax.ShapeDtypeStruct((own, rows, frames, chans), f32),
            jax.ShapeDtypeStruct((area, area), f32),
        ]
        + [jax.ShapeDtypeStruct(x.shape, bf16) for x in weights],
        in_specs=[near] + [far] * 6,
        out_specs=[near] * 7,
        scratch_shapes=[
            stored,
            pltpu.VMEM((span, rows, frames, TAPS * chans), bf16),
            pltpu.SMEM((frames,), jnp.int32),
            pltpu.SemaphoreType.DMA((TAPS,)),
            pltpu.SemaphoreType.DMA((4,)),
            pltpu.SemaphoreType.DMA(()),
        ],
        compiler_params=params,
    )(piece, in_far(ids), *weights)
    blocks = pl.pallas_call(
        functools.partial(main_kernel, count, rows, group),
        out_shape=jax.ShapeDtypeStruct((group, own * lines, chans), bf16),
        in_specs=[near] * 8,
        out_specs=near,
        scratch_shapes=[scratch(group * own * lines, chans)],
        compiler_params=params,
    )(edge, total, bias, *weights)
    return pl.pallas_call(
        unpack_kernel,
        out_shape=jax.ShapeDtypeStruct(video.shape, bf16),
        in_specs=[near],
        out_specs=far,
        scratch_shapes=[
            pltpu.VMEM(video.shape, bf16),
            pltpu.SemaphoreType.DMA((lines,)),
        ],
        compiler_params=params,
    )(exchanged(blocks))


def solution(mesh):
    parts, along, halves = (mesh.shape[a] for a in ("groups", "tm", "height"))

    def run(video, *rest):
        count = video.shape[0] // (parts * along)
        group = min(g for g in range(1, along + 1) if along % g == 0 and (g * count >= REACH or g == along))
        outer = along // group
        split = Mesh(
            np.asarray(mesh.devices).reshape(parts, outer, group, halves),
            ("groups", "outer", "tm", "height"),
        )
        spec = P(("groups", "outer", "tm"), "height", None, None)
        placed = (spec, P("groups"), P(), P(), P(), P(), P())
        return jax.shard_map(
            functools.partial(per_device, outer),
            mesh=split,
            in_specs=placed,
            out_specs=spec,
            check_vma=False,
        )(video, *rest)

    return run
```

```python
import functools

import jax
import jax.numpy as jnp
import numpy as np
from jax import lax
from jax.experimental import pallas as pl
from jax.experimental.pallas import tpu as pltpu
from jax.sharding import Mesh, PartitionSpec as P

HD = 64
BLOCK = 4
TAPS = 3
REACH = 2 * BLOCK - 1 + TAPS - 1
LANES = 128
EDGE = 8
VMEM = 28 * 2**20

bf16, f32 = jnp.bfloat16, jnp.float32


def get(ref, start, size, stride):
    return jnp.concatenate([ref[i, pl.ds(start, size, stride=stride), :] for i in range(ref.shape[0])], axis=1)


def put(ref, start, size, stride, value):
    for i in range(ref.shape[0]):
        ref[i, pl.ds(start, size, stride=stride), :] = value[:, i * LANES : (i + 1) * LANES]


def fill(ref, start, value):
    for i in range(ref.shape[0]):
        ref[i, pl.ds(start, value.shape[0]), :] = value[:, i * LANES : (i + 1) * LANES]


def scratch(rows, chans):
    return pltpu.VMEM((chans // LANES, rows, LANES), f32)


def rms(wide):
    return wide * lax.rsqrt(jnp.mean(wide * wide, axis=-1, keepdims=True) + 1e-06)


def divided(at, by):
    if by & (by - 1) == 0:
        bits = by.bit_length() - 1
        return at >> bits, at & (by - 1)
    return lax.div(at, jnp.int32(by)), lax.rem(at, jnp.int32(by))


def pack_kernel(group, video, *refs):
    out, local, wide, sems = refs
    count, rows, cols, chans = video.shape
    lines = count * rows
    stride = cols + 2 * EDGE
    own = cols // group
    span = own + 2
    copies = []
    for at in range(lines):
        place = (at // rows, at % rows)
        copy = pltpu.make_async_copy(video.at[place], local.at[place], sems.at[at])
        copy.start()
        copies.append(copy)
    nothing = jnp.zeros((EDGE, chans), f32)
    for at in range(lines):
        fill(wide, at * stride, nothing)
        fill(wide, at * stride + EDGE + cols, nothing)
    for at, copy in enumerate(copies):
        copy.wait()
        fill(wide, at * stride + EDGE, local[at // rows, at % rows].astype(f32))
    together = 16 // lines
    for k in range(group):
        start = k * own + EDGE - 1
        for w in range(0, span, together):
            tile = jnp.concatenate([get(wide, start + w + i, lines, stride) for i in range(together)], axis=0)
            out[k, pl.ds(w * lines, 16), :] = tile.astype(bf16)


def frames_of(ref, w, r, count, rows, sources, step):
    return [get(ref, w * count * rows + t * rows + r, sources, step) for t in range(count)]


def shifted(now):
    count = len(now)
    sources, chans = now[0].shape
    first = lax.broadcasted_iota(jnp.int32, (sources, chans), 0) == 0
    past = [jnp.where(first, 0.0, pltpu.roll(x, 1, 0)) for x in now]
    ordered = past + now
    taps = []
    for a in range(TAPS):
        start = count - (TAPS - 1 - a)
        taps.append(jnp.concatenate(ordered[start : start + count], 0).astype(bf16))
    return jnp.concatenate(taps, axis=1)


def activated(wide):
    part = 0.5 * rms(wide)
    return part + part * jnp.tanh(part)


def depth(parts):
    return parts[0] if len(parts) == 1 else jnp.concatenate(parts, axis=-1)


def edge_kernel(count, rows, video, edge, vid):
    sources, step, chans = video.shape
    span = step // (count * rows)
    fill(vid, 0, video[...].reshape(sources * step, chans).astype(f32))
    row = (rows - 1) * (1 - lax.axis_index("height"))
    for w in range(span):
        edge[w] = shifted([activated(x) for x in frames_of(vid, w, row, count, rows, sources, step)])


def fill_bias(bias, ids, frames, count):
    area = bias.shape[0]
    sources = frames // count

    def place_of(at):
        pixel, place = divided(at, frames)
        inner, source = divided(place, sources)
        frame = source * count + inner
        block = jnp.zeros(at.shape, jnp.int32)
        for s in range(frames):
            block = jnp.where(frame == s, ids[s], block)
        return pixel, frame, block

    row_p, row_t, row_b = place_of(lax.broadcasted_iota(jnp.int32, (area, area), 0))
    col_p, col_t, col_b = place_of(lax.broadcasted_iota(jnp.int32, (1, area), 1))
    permit = (row_p == col_p) & (col_t <= row_t) & (col_b >= row_b - 1)
    bias[...] = jnp.where(permit, 0.0, -1e30)


def shift_kernel(count, rows, video, ids_far, *refs):
    far, (total, bias, *near), (vid, grid, ids, conv_sems, sems, ids_sem) = refs[:5], refs[5:12], refs[12:]
    ids_copy = pltpu.make_async_copy(ids_far, ids, ids_sem)
    ids_copy.start()
    conv_far, conv_weight = far[0], near[0]
    order = [1, 0, 2]
    taps = {b: pltpu.make_async_copy(conv_far.at[:, b], conv_weight.at[:, b], conv_sems.at[b]) for b in order}
    others = [pltpu.make_async_copy(far[i], near[i], sems.at[i - 1]) for i in range(1, 5)]
    taps[order[0]].start()
    sources, step, chans = video.shape
    span = step // (count * rows)
    own = span - 2
    frames = sources * count
    of_taps = [(e, a) for e in range(TAPS) for a in range(TAPS)]
    fill(vid, 0, video[...].reshape(sources * step, chans).astype(f32))
    for w in range(span):
        for r in range(rows):
            now = frames_of(vid, w, r, count, rows, sources, step)
            grid[w, r] = shifted([activated(x) for x in now])
            if 1 <= w <= own:
                total[w - 1, r] = jnp.concatenate(now, 0)
        if w == span // 2:
            taps[order[1]].start()
    taps[order[2]].start()
    for copy in others:
        copy.start()

    ids_copy.wait()
    fill_bias(bias, ids, frames, count)
    for b in order:
        taps[b].wait()
        low, high = max(0, 1 - b), min(rows, rows + 1 - b)
        size = own * (high - low) * frames
        some = total.at[:, low:high]
        result = some[...]
        for chain in (of_taps[: len(of_taps) // 2], of_taps[len(of_taps) // 2 :]):
            window = [
                grid[e : e + own, low + b - 1 : high + b - 1, :, a * chans : (a + 1) * chans] for e, a in chain
            ]
            weight = jnp.concatenate([conv_weight[a, b, e] for e, a in chain], axis=0)
            part = jnp.dot(depth(window).reshape(size, len(chain) * chans), weight, preferred_element_type=f32)
            result = result + part.reshape(some.shape)
        some[...] = result
    for copy in others:
        copy.wait()


def main_kernel(
    count, rows, group, edge, given, bias, conv_weight, w_query, w_key, w_value, w_output, *refs
):
    out, res = refs
    own, _, frames, chans = given.shape
    sources = frames // count
    lines = count * rows
    heads = chans // HD
    back = own * lines
    area = bias.shape[0]
    several = area // (rows * frames)

    lower = lax.axis_index("height")
    b = (TAPS - 1) * (1 - lower)
    part = jnp.zeros((own * frames, chans), f32)
    for e in range(TAPS):
        window = edge[e : e + own].reshape(own * frames, TAPS * chans)
        weight = jnp.concatenate([conv_weight[a, b, e] for a in range(TAPS)], axis=0)
        part = part + jnp.dot(window, weight, preferred_element_type=f32)
    part = part.reshape(own, frames, chans)

    head_of = divided(lax.broadcasted_iota(jnp.int32, (area, chans), 1), HD)[0]
    single = [jnp.where(head_of == h, 1.0, 0.0).astype(bf16) for h in range(heads)]
    scaled = [mask * jnp.asarray(HD ** (-0.5), bf16) for mask in single]

    lines_of = []
    for r in range(rows):
        row = given[:, r] + jnp.where(r == (rows - 1) * (1 - lower), part, 0.0)
        lines_of.append(row[:, None])
    hidden = jnp.concatenate(lines_of, axis=1).reshape(own * rows * frames, chans).astype(bf16).astype(f32)
    normed = rms(hidden).astype(bf16)
    query, keys, values = (
        jnp.dot(normed, weight[...], preferred_element_type=f32).astype(bf16) for weight in (w_query, w_key, w_value)
    )
    half = own // 2 if own % (2 * several) == 0 else own
    for start in range(0, own, half):
        gone = []
        for at in range(start * rows * frames, (start + half) * rows * frames, area):
            group_of = slice(at, at + area)
            queries = jnp.concatenate([query[group_of] * mask for mask in scaled], axis=0)
            scores = lax.dot_general(
                queries, keys[group_of], (((1,), (1,)), ((), ())), preferred_element_type=f32
            )
            weights, under = [], jnp.zeros((area, chans), f32)
            for h in range(heads):
                score = scores[h * area : (h + 1) * area] + bias[...]
                expo = jnp.exp(score - jnp.max(score, axis=-1, keepdims=True))
                under = jnp.where(head_of == h, jnp.sum(expo, axis=-1, keepdims=True), under)
                weights.append(expo.astype(bf16))
            heads_values = jnp.concatenate([values[group_of] * mask for mask in single], axis=0)
            attended = jnp.dot(jnp.concatenate(weights, axis=1), heads_values, preferred_element_type=f32)
            gone.append((attended / under).astype(bf16))
        attended = jnp.concatenate(gone, axis=0)
        encoded = hidden[start * rows * frames : (start + half) * rows * frames] + jnp.dot(
            attended, w_output[...], preferred_element_type=f32
        )
        for w in range(half):
            for r in range(rows):
                for t in range(count):
                    first = ((w * rows + r) * count + t + 1) * sources - group
                    place = (t * rows + r) * own + start + w
                    put(res, place, group, back, encoded[first : first + group])
    done = jnp.concatenate([res[i] for i in range(res.shape[0])], axis=1)
    out[...] = done.astype(bf16).reshape(out.shape)


def unpack_kernel(packed, out, local, sems):
    count, rows, cols, chans = out.shape
    lines = count * rows
    regions = packed.shape[0]
    own = cols // regions
    wide = packed[...].astype(f32).reshape(regions, lines, own, chans)
    copies = []
    for at in range(lines):
        place = (at // rows, at % rows)
        local[place] = wide[:, at].reshape(cols, chans).astype(bf16)
        copy = pltpu.make_async_copy(local.at[place], out.at[place], sems.at[at])
        copy.start()
        copies.append(copy)
    for copy in copies:
        copy.wait()


def exchanged(blocks):
    return lax.all_to_all(blocks, "tm", split_axis=0, concat_axis=0, tiled=True)


def per_device(outer, video, block_ids, conv_weight, w_query, w_key, w_value, w_output):
    count, rows, cols, chans = video.shape
    group = lax.axis_size("tm")
    own = cols // group
    span = own + 2
    lines = count * rows
    near = pl.BlockSpec(memory_space=pltpu.VMEM)
    far = pl.BlockSpec(memory_space=pltpu.HBM)
    params = pltpu.CompilerParams(vmem_limit_bytes=VMEM)
    in_far = functools.partial(pltpu.with_memory_space_constraint, memory_space=pltpu.HBM)
    weights = [in_far(x) for x in (conv_weight, w_query, w_key, w_value, w_output)]

    blocks = pl.pallas_call(
        functools.partial(pack_kernel, group),
        out_shape=jax.ShapeDtypeStruct((group, span * lines, chans), bf16),
        in_specs=[far],
        out_specs=near,
        scratch_shapes=[
            pltpu.VMEM(video.shape, bf16),
            scratch(lines * (cols + 2 * EDGE), chans),
            pltpu.SemaphoreType.DMA((lines,)),
        ],
        compiler_params=params,
    )(in_far(video))
    piece = exchanged(blocks)
    ids = block_ids
    if outer > 1:
        before = lax.ppermute(piece, "outer", [(i, i + 1) for i in range(outer - 1)])
        piece = jnp.concatenate([before, piece], axis=0)
        ids = jnp.concatenate([jnp.full((group * count,), -2, jnp.int32), ids])
        ids = lax.dynamic_slice(ids, (lax.axis_index("outer") * group * count,), (2 * group * count,))
    sources = piece.shape[0]
    frames = sources * count
    stored = scratch(sources * span * lines, chans)
    edge = pl.pallas_call(
        functools.partial(edge_kernel, count, rows),
        out_shape=jax.ShapeDtypeStruct((span, frames, TAPS * chans), bf16),
        in_specs=[near],
        out_specs=near,
        scratch_shapes=[stored],
        compiler_params=params,
    )(piece)
    edge = lax.ppermute(edge, "height", [(0, 1), (1, 0)])
    several = max(n for n in range(1, own + 1) if own % n == 0 and (n == 1 or n * rows * frames <= LANES))
    area = several * rows * frames
    total, bias, *weights = pl.pallas_call(
        functools.partial(shift_kernel, count, rows),
        out_shape=[
            jax.ShapeDtypeStruct((own, rows, frames, chans), f32),
            jax.ShapeDtypeStruct((area, area), f32),
        ]
        + [jax.ShapeDtypeStruct(x.shape, bf16) for x in weights],
        in_specs=[near] + [far] * 6,
        out_specs=[near] * 7,
        scratch_shapes=[
            stored,
            pltpu.VMEM((span, rows, frames, TAPS * chans), bf16),
            pltpu.SMEM((frames,), jnp.int32),
            pltpu.SemaphoreType.DMA((TAPS,)),
            pltpu.SemaphoreType.DMA((4,)),
            pltpu.SemaphoreType.DMA(()),
        ],
        compiler_params=params,
    )(piece, in_far(ids), *weights)
    blocks = pl.pallas_call(
        functools.partial(main_kernel, count, rows, group),
        out_shape=jax.ShapeDtypeStruct((group, own * lines, chans), bf16),
        in_specs=[near] * 8,
        out_specs=near,
        scratch_shapes=[scratch(group * own * lines, chans)],
        compiler_params=params,
    )(edge, total, bias, *weights)
    return pl.pallas_call(
        unpack_kernel,
        out_shape=jax.ShapeDtypeStruct(video.shape, bf16),
        in_specs=[near],
        out_specs=far,
        scratch_shapes=[
            pltpu.VMEM(video.shape, bf16),
            pltpu.SemaphoreType.DMA((lines,)),
        ],
        compiler_params=params,
    )(exchanged(blocks))


def solution(mesh):
    parts, along, halves = (mesh.shape[a] for a in ("groups", "tm", "height"))

    def run(video, *rest):
        count = video.shape[0] // (parts * along)
        group = min(g for g in range(1, along + 1) if along % g == 0 and (g * count >= REACH or g == along))
        outer = along // group
        split = Mesh(
            np.asarray(mesh.devices).reshape(parts, outer, group, halves),
            ("groups", "outer", "tm", "height"),
        )
        spec = P(("groups", "outer", "tm"), "height", None, None)
        placed = (spec, P("groups"), P(), P(), P(), P(), P())
        return jax.shard_map(
            functools.partial(per_device, outer),
            mesh=split,
            in_specs=placed,
            out_specs=spec,
            check_vma=False,
        )(video, *rest)

    return run
```

```python
import functools

import jax
import jax.numpy as jnp
import numpy as np
from jax import lax
from jax.experimental import pallas as pl
from jax.experimental.pallas import tpu as pltpu
from jax.sharding import Mesh, PartitionSpec as P

HD = 64
BLOCK = 4
TAPS = 3
REACH = 2 * BLOCK - 1 + TAPS - 1
LANES = 128
EDGE = 8
VMEM = 28 * 2**20

bf16, f32 = jnp.bfloat16, jnp.float32


def get(ref, start, size, stride):
    return jnp.concatenate([ref[i, pl.ds(start, size, stride=stride), :] for i in range(ref.shape[0])], axis=1)


def put(ref, start, size, stride, value):
    for i in range(ref.shape[0]):
        ref[i, pl.ds(start, size, stride=stride), :] = value[:, i * LANES : (i + 1) * LANES]


def fill(ref, start, value):
    for i in range(ref.shape[0]):
        ref[i, pl.ds(start, value.shape[0]), :] = value[:, i * LANES : (i + 1) * LANES]


def scratch(rows, chans):
    return pltpu.VMEM((chans // LANES, rows, LANES), f32)


def rms(wide):
    return wide * lax.rsqrt(jnp.mean(wide * wide, axis=-1, keepdims=True) + 1e-06)


def divided(at, by):
    if by & (by - 1) == 0:
        bits = by.bit_length() - 1
        return at >> bits, at & (by - 1)
    return lax.div(at, jnp.int32(by)), lax.rem(at, jnp.int32(by))


def pack_kernel(group, video, *refs):
    out, local, wide, sems = refs
    count, rows, cols, chans = video.shape
    lines = count * rows
    stride = cols + 2 * EDGE
    own = cols // group
    span = own + 2
    copies = []
    for at in range(lines):
        place = (at // rows, at % rows)
        copy = pltpu.make_async_copy(video.at[place], local.at[place], sems.at[at])
        copy.start()
        copies.append(copy)
    nothing = jnp.zeros((EDGE, chans), f32)
    for at in range(lines):
        fill(wide, at * stride, nothing)
        fill(wide, at * stride + EDGE + cols, nothing)
    for at, copy in enumerate(copies):
        copy.wait()
        fill(wide, at * stride + EDGE, local[at // rows, at % rows].astype(f32))
    together = 16 // lines
    for k in range(group):
        start = k * own + EDGE - 1
        for w in range(0, span, together):
            tile = jnp.concatenate([get(wide, start + w + i, lines, stride) for i in range(together)], axis=0)
            out[k, pl.ds(w * lines, 16), :] = tile.astype(bf16)


def frames_of(ref, w, r, count, rows, sources, step):
    return [get(ref, w * count * rows + t * rows + r, sources, step) for t in range(count)]


def shifted(now):
    count = len(now)
    sources, chans = now[0].shape
    first = lax.broadcasted_iota(jnp.int32, (sources, chans), 0) == 0
    past = [jnp.where(first, 0.0, pltpu.roll(x, 1, 0)) for x in now]
    ordered = past + now
    taps = []
    for a in range(TAPS):
        start = count - (TAPS - 1 - a)
        taps.append(jnp.concatenate(ordered[start : start + count], 0).astype(bf16))
    return jnp.concatenate(taps, axis=1)


def activated(wide):
    part = 0.5 * rms(wide)
    return part + part * jnp.tanh(part)


def depth(parts):
    return parts[0] if len(parts) == 1 else jnp.concatenate(parts, axis=-1)


def edge_kernel(count, rows, video, edge, vid):
    sources, step, chans = video.shape
    span = step // (count * rows)
    fill(vid, 0, video[...].reshape(sources * step, chans).astype(f32))
    row = (rows - 1) * (1 - lax.axis_index("height"))
    for w in range(span):
        edge[w] = shifted([activated(x) for x in frames_of(vid, w, row, count, rows, sources, step)])


def fill_bias(bias, ids, frames, count):
    area = bias.shape[0]
    sources = frames // count

    def place_of(at):
        pixel, place = divided(at, frames)
        inner, source = divided(place, sources)
        frame = source * count + inner
        block = jnp.zeros(at.shape, jnp.int32)
        for s in range(frames):
            block = jnp.where(frame == s, ids[s], block)
        return pixel, frame, block

    row_p, row_t, row_b = place_of(lax.broadcasted_iota(jnp.int32, (area, area), 0))
    col_p, col_t, col_b = place_of(lax.broadcasted_iota(jnp.int32, (1, area), 1))
    permit = (row_p == col_p) & (col_t <= row_t) & (col_b >= row_b - 1)
    bias[...] = jnp.where(permit, 0.0, -1e30)


def shift_kernel(count, rows, video, ids_far, *refs):
    far, (total, bias, *near), (vid, grid, ids, conv_sems, sems, ids_sem) = refs[:5], refs[5:12], refs[12:]
    ids_copy = pltpu.make_async_copy(ids_far, ids, ids_sem)
    ids_copy.start()
    conv_far, conv_weight = far[0], near[0]
    order = [1, 0, 2]
    taps = {b: pltpu.make_async_copy(conv_far.at[:, b], conv_weight.at[:, b], conv_sems.at[b]) for b in order}
    others = [pltpu.make_async_copy(far[i], near[i], sems.at[i - 1]) for i in range(1, 5)]
    taps[order[0]].start()
    sources, step, chans = video.shape
    span = step // (count * rows)
    own = span - 2
    frames = sources * count
    half = own // 2 if own % 2 == 0 else own
    fill(vid, 0, video[...].reshape(sources * step, chans).astype(f32))
    for w in range(span):
        for r in range(rows):
            now = frames_of(vid, w, r, count, rows, sources, step)
            grid[w, r] = shifted([activated(x) for x in now])
            if 1 <= w <= own:
                total[w - 1, r] = jnp.concatenate(now, 0)
        if w == span // 2:
            taps[order[1]].start()
    taps[order[2]].start()
    for copy in others:
        copy.start()

    ids_copy.wait()
    fill_bias(bias, ids, frames, count)
    for b in order:
        taps[b].wait()
        low, high = max(0, 1 - b), min(rows, rows + 1 - b)
        weight = jnp.concatenate([conv_weight[a, b, e] for e in range(TAPS) for a in range(TAPS)], axis=0)
        for w in range(0, own, half):
            window = depth([grid[w + e : w + e + half, low + b - 1 : high + b - 1] for e in range(TAPS)])
            window = window.reshape(half * (high - low) * frames, TAPS * TAPS * chans)
            part = jnp.dot(window, weight, preferred_element_type=f32)
            some = total.at[w : w + half, low:high]
            some[...] = some[...] + part.reshape(half, high - low, frames, chans)
    for copy in others:
        copy.wait()


def main_kernel(
    count, rows, group, edge, given, bias, conv_weight, w_query, w_key, w_value, w_output, *refs
):
    out, res = refs
    own, _, frames, chans = given.shape
    sources = frames // count
    lines = count * rows
    heads = chans // HD
    back = own * lines
    area = bias.shape[0]
    several = area // (rows * frames)

    lower = lax.axis_index("height")
    b = (TAPS - 1) * (1 - lower)
    part = jnp.zeros((own * frames, chans), f32)
    for e in range(TAPS):
        window = edge[e : e + own].reshape(own * frames, TAPS * chans)
        weight = jnp.concatenate([conv_weight[a, b, e] for a in range(TAPS)], axis=0)
        part = part + jnp.dot(window, weight, preferred_element_type=f32)
    part = part.reshape(own, frames, chans)

    head_of = divided(lax.broadcasted_iota(jnp.int32, (area, chans), 1), HD)[0]
    single = [jnp.where(head_of == h, 1.0, 0.0).astype(bf16) for h in range(heads)]
    scaled = [mask * jnp.asarray(HD ** (-0.5), bf16) for mask in single]

    lines_of = []
    for r in range(rows):
        row = given[:, r] + jnp.where(r == (rows - 1) * (1 - lower), part, 0.0)
        lines_of.append(row[:, None])
    hidden = jnp.concatenate(lines_of, axis=1).reshape(own * rows * frames, chans).astype(bf16).astype(f32)
    normed = rms(hidden).astype(bf16)
    query, keys, values = (
        jnp.dot(normed, weight[...], preferred_element_type=f32).astype(bf16) for weight in (w_query, w_key, w_value)
    )
    half = own // 2 if own % (2 * several) == 0 else own
    for start in range(0, own, half):
        gone = []
        for at in range(start * rows * frames, (start + half) * rows * frames, area):
            group_of = slice(at, at + area)
            queries = jnp.concatenate([query[group_of] * mask for mask in scaled], axis=0)
            scores = lax.dot_general(
                queries, keys[group_of], (((1,), (1,)), ((), ())), preferred_element_type=f32
            )
            weights, under = [], jnp.zeros((area, chans), f32)
            for h in range(heads):
                score = scores[h * area : (h + 1) * area] + bias[...]
                expo = jnp.exp(score - jnp.max(score, axis=-1, keepdims=True))
                under = jnp.where(head_of == h, jnp.sum(expo, axis=-1, keepdims=True), under)
                weights.append(expo.astype(bf16))
            heads_values = jnp.concatenate([values[group_of] * mask for mask in single], axis=0)
            attended = jnp.dot(jnp.concatenate(weights, axis=1), heads_values, preferred_element_type=f32)
            gone.append((attended / under).astype(bf16))
        attended = jnp.concatenate(gone, axis=0)
        encoded = hidden[start * rows * frames : (start + half) * rows * frames] + jnp.dot(
            attended, w_output[...], preferred_element_type=f32
        )
        for w in range(half):
            for r in range(rows):
                for t in range(count):
                    first = ((w * rows + r) * count + t + 1) * sources - group
                    place = (t * rows + r) * own + start + w
                    put(res, place, group, back, encoded[first : first + group])
    done = jnp.concatenate([res[i] for i in range(res.shape[0])], axis=1)
    out[...] = done.astype(bf16).reshape(out.shape)


def unpack_kernel(packed, out, local, sems):
    count, rows, cols, chans = out.shape
    lines = count * rows
    regions = packed.shape[0]
    own = cols // regions
    wide = packed[...].astype(f32).reshape(regions, lines, own, chans)
    copies = []
    for at in range(lines):
        place = (at // rows, at % rows)
        local[place] = wide[:, at].reshape(cols, chans).astype(bf16)
        copy = pltpu.make_async_copy(local.at[place], out.at[place], sems.at[at])
        copy.start()
        copies.append(copy)
    for copy in copies:
        copy.wait()


def exchanged(blocks):
    return lax.all_to_all(blocks, "tm", split_axis=0, concat_axis=0, tiled=True)


def per_device(outer, video, block_ids, conv_weight, w_query, w_key, w_value, w_output):
    count, rows, cols, chans = video.shape
    group = lax.axis_size("tm")
    own = cols // group
    span = own + 2
    lines = count * rows
    near = pl.BlockSpec(memory_space=pltpu.VMEM)
    far = pl.BlockSpec(memory_space=pltpu.HBM)
    params = pltpu.CompilerParams(vmem_limit_bytes=VMEM)
    in_far = functools.partial(pltpu.with_memory_space_constraint, memory_space=pltpu.HBM)
    weights = [in_far(x) for x in (conv_weight, w_query, w_key, w_value, w_output)]

    blocks = pl.pallas_call(
        functools.partial(pack_kernel, group),
        out_shape=jax.ShapeDtypeStruct((group, span * lines, chans), bf16),
        in_specs=[far],
        out_specs=near,
        scratch_shapes=[
            pltpu.VMEM(video.shape, bf16),
            scratch(lines * (cols + 2 * EDGE), chans),
            pltpu.SemaphoreType.DMA((lines,)),
        ],
        compiler_params=params,
    )(in_far(video))
    piece = exchanged(blocks)
    ids = block_ids
    if outer > 1:
        before = lax.ppermute(piece, "outer", [(i, i + 1) for i in range(outer - 1)])
        piece = jnp.concatenate([before, piece], axis=0)
        ids = jnp.concatenate([jnp.full((group * count,), -2, jnp.int32), ids])
        ids = lax.dynamic_slice(ids, (lax.axis_index("outer") * group * count,), (2 * group * count,))
    sources = piece.shape[0]
    frames = sources * count
    stored = scratch(sources * span * lines, chans)
    edge = pl.pallas_call(
        functools.partial(edge_kernel, count, rows),
        out_shape=jax.ShapeDtypeStruct((span, frames, TAPS * chans), bf16),
        in_specs=[near],
        out_specs=near,
        scratch_shapes=[stored],
        compiler_params=params,
    )(piece)
    edge = lax.ppermute(edge, "height", [(0, 1), (1, 0)])
    several = max(n for n in range(1, own + 1) if own % n == 0 and (n == 1 or n * rows * frames <= LANES))
    area = several * rows * frames
    total, bias, *weights = pl.pallas_call(
        functools.partial(shift_kernel, count, rows),
        out_shape=[
            jax.ShapeDtypeStruct((own, rows, frames, chans), f32),
            jax.ShapeDtypeStruct((area, area), f32),
        ]
        + [jax.ShapeDtypeStruct(x.shape, bf16) for x in weights],
        in_specs=[near] + [far] * 6,
        out_specs=[near] * 7,
        scratch_shapes=[
            stored,
            pltpu.VMEM((span, rows, frames, TAPS * chans), bf16),
            pltpu.SMEM((frames,), jnp.int32),
            pltpu.SemaphoreType.DMA((TAPS,)),
            pltpu.SemaphoreType.DMA((4,)),
            pltpu.SemaphoreType.DMA(()),
        ],
        compiler_params=params,
    )(piece, in_far(ids), *weights)
    blocks = pl.pallas_call(
        functools.partial(main_kernel, count, rows, group),
        out_shape=jax.ShapeDtypeStruct((group, own * lines, chans), bf16),
        in_specs=[near] * 8,
        out_specs=near,
        scratch_shapes=[scratch(group * own * lines, chans)],
        compiler_params=params,
    )(edge, total, bias, *weights)
    return pl.pallas_call(
        unpack_kernel,
        out_shape=jax.ShapeDtypeStruct(video.shape, bf16),
        in_specs=[near],
        out_specs=far,
        scratch_shapes=[
            pltpu.VMEM(video.shape, bf16),
            pltpu.SemaphoreType.DMA((lines,)),
        ],
        compiler_params=params,
    )(exchanged(blocks))


def solution(mesh):
    parts, along, halves = (mesh.shape[a] for a in ("groups", "tm", "height"))

    def run(video, *rest):
        count = video.shape[0] // (parts * along)
        group = min(g for g in range(1, along + 1) if along % g == 0 and (g * count >= REACH or g == along))
        outer = along // group
        split = Mesh(
            np.asarray(mesh.devices).reshape(parts, outer, group, halves),
            ("groups", "outer", "tm", "height"),
        )
        spec = P(("groups", "outer", "tm"), "height", None, None)
        placed = (spec, P("groups"), P(), P(), P(), P(), P())
        return jax.shard_map(
            functools.partial(per_device, outer),
            mesh=split,
            in_specs=placed,
            out_specs=spec,
            check_vma=False,
        )(video, *rest)

    return run
```

```python
import functools

import jax
import jax.numpy as jnp
import numpy as np
from jax import lax
from jax.experimental import pallas as pl
from jax.experimental.pallas import tpu as pltpu
from jax.sharding import Mesh, PartitionSpec as P

HD = 64
BLOCK = 4
TAPS = 3
REACH = 2 * BLOCK - 1 + TAPS - 1
LANES = 128
EDGE = 8
VMEM = 28 * 2**20

bf16, f32 = jnp.bfloat16, jnp.float32


def get(ref, start, size, stride):
    return jnp.concatenate([ref[i, pl.ds(start, size, stride=stride), :] for i in range(ref.shape[0])], axis=1)


def put(ref, start, size, stride, value):
    for i in range(ref.shape[0]):
        ref[i, pl.ds(start, size, stride=stride), :] = value[:, i * LANES : (i + 1) * LANES]


def fill(ref, start, value):
    for i in range(ref.shape[0]):
        ref[i, pl.ds(start, value.shape[0]), :] = value[:, i * LANES : (i + 1) * LANES]


def scratch(rows, chans):
    return pltpu.VMEM((chans // LANES, rows, LANES), f32)


def rms(wide):
    return wide * lax.rsqrt(jnp.mean(wide * wide, axis=-1, keepdims=True) + 1e-06)


def divided(at, by):
    if by & (by - 1) == 0:
        bits = by.bit_length() - 1
        return at >> bits, at & (by - 1)
    return lax.div(at, jnp.int32(by)), lax.rem(at, jnp.int32(by))


def pack_kernel(group, video, *refs):
    out, local, wide, sems = refs
    count, rows, cols, chans = video.shape
    lines = count * rows
    stride = cols + 2 * EDGE
    own = cols // group
    span = own + 2
    copies = []
    for at in range(lines):
        place = (at // rows, at % rows)
        copy = pltpu.make_async_copy(video.at[place], local.at[place], sems.at[at])
        copy.start()
        copies.append(copy)
    nothing = jnp.zeros((EDGE, chans), f32)
    for at in range(lines):
        fill(wide, at * stride, nothing)
        fill(wide, at * stride + EDGE + cols, nothing)
    for at, copy in enumerate(copies):
        copy.wait()
        fill(wide, at * stride + EDGE, local[at // rows, at % rows].astype(f32))
    together = 16 // lines
    for k in range(group):
        start = k * own + EDGE - 1
        for w in range(0, span, together):
            tile = jnp.concatenate([get(wide, start + w + i, lines, stride) for i in range(together)], axis=0)
            out[k, pl.ds(w * lines, 16), :] = tile.astype(bf16)


def frames_of(ref, w, r, count, rows, sources, step):
    return [get(ref, w * count * rows + t * rows + r, sources, step) for t in range(count)]


def shifted(now):
    count = len(now)
    sources, chans = now[0].shape
    first = lax.broadcasted_iota(jnp.int32, (sources, chans), 0) == 0
    past = [jnp.where(first, 0.0, pltpu.roll(x, 1, 0)) for x in now]
    ordered = past + now
    taps = []
    for a in range(TAPS):
        start = count - (TAPS - 1 - a)
        taps.append(jnp.concatenate(ordered[start : start + count], 0).astype(bf16))
    return jnp.concatenate(taps, axis=1)


def activated(wide):
    part = 0.5 * rms(wide)
    return part + part * jnp.tanh(part)


def depth(parts):
    return parts[0] if len(parts) == 1 else jnp.concatenate(parts, axis=-1)


def edge_kernel(count, rows, video, edge, vid):
    sources, step, chans = video.shape
    span = step // (count * rows)
    fill(vid, 0, video[...].reshape(sources * step, chans).astype(f32))
    row = (rows - 1) * (1 - lax.axis_index("height"))
    for w in range(span):
        edge[w] = shifted([activated(x) for x in frames_of(vid, w, row, count, rows, sources, step)])


def fill_bias(bias, ids, frames, count):
    area = bias.shape[0]
    sources = frames // count

    def place_of(at):
        pixel, place = divided(at, frames)
        inner, source = divided(place, sources)
        frame = source * count + inner
        block = jnp.zeros(at.shape, jnp.int32)
        for s in range(frames):
            block = jnp.where(frame == s, ids[s], block)
        return pixel, frame, block

    row_p, row_t, row_b = place_of(lax.broadcasted_iota(jnp.int32, (area, area), 0))
    col_p, col_t, col_b = place_of(lax.broadcasted_iota(jnp.int32, (1, area), 1))
    permit = (row_p == col_p) & (col_t <= row_t) & (col_b >= row_b - 1)
    bias[...] = jnp.where(permit, 0.0, -1e30)


def shift_kernel(count, rows, video, ids_far, *refs):
    conv_weight, far, (total, bias, *near) = refs[0], refs[1:5], refs[5:11]
    vid, grid, ids, sems, ids_sem = refs[11:]
    ids_copy = pltpu.make_async_copy(ids_far, ids, ids_sem)
    ids_copy.start()
    others = [pltpu.make_async_copy(src, dst, sems.at[i]) for i, (src, dst) in enumerate(zip(far, near))]
    for copy in others:
        copy.start()
    sources, step, chans = video.shape
    span = step // (count * rows)
    own = span - 2
    frames = sources * count
    half = own // 2 if own % 2 == 0 else own
    fill(vid, 0, video[...].reshape(sources * step, chans).astype(f32))
    for w in range(span):
        for r in range(rows):
            now = frames_of(vid, w, r, count, rows, sources, step)
            grid[w, r] = shifted([activated(x) for x in now])
            if 1 <= w <= own:
                total[w - 1, r] = jnp.concatenate(now, 0)

    for b in range(TAPS):
        low, high = max(0, 1 - b), min(rows, rows + 1 - b)
        weight = jnp.concatenate([conv_weight[a, b, e] for e in range(TAPS) for a in range(TAPS)], axis=0)
        for w in range(0, own, half):
            window = depth([grid[w + e : w + e + half, low + b - 1 : high + b - 1] for e in range(TAPS)])
            window = window.reshape(half * (high - low) * frames, TAPS * TAPS * chans)
            part = jnp.dot(window, weight, preferred_element_type=f32)
            some = total.at[w : w + half, low:high]
            some[...] = some[...] + part.reshape(half, high - low, frames, chans)
    ids_copy.wait()
    fill_bias(bias, ids, frames, count)
    for copy in others:
        copy.wait()


def main_kernel(
    count, rows, group, edge, given, bias, conv_weight, w_query, w_key, w_value, w_output, *refs
):
    out, res = refs
    own, _, frames, chans = given.shape
    sources = frames // count
    lines = count * rows
    heads = chans // HD
    back = own * lines
    area = bias.shape[0]
    several = area // (rows * frames)

    lower = lax.axis_index("height")
    b = (TAPS - 1) * (1 - lower)
    part = jnp.zeros((own * frames, chans), f32)
    for e in range(TAPS):
        window = edge[e : e + own].reshape(own * frames, TAPS * chans)
        weight = jnp.concatenate([conv_weight[a, b, e] for a in range(TAPS)], axis=0)
        part = part + jnp.dot(window, weight, preferred_element_type=f32)
    part = part.reshape(own, frames, chans)

    head_of = divided(lax.broadcasted_iota(jnp.int32, (area, chans), 1), HD)[0]
    single = [jnp.where(head_of == h, 1.0, 0.0).astype(bf16) for h in range(heads)]
    scaled = [mask * jnp.asarray(HD ** (-0.5), bf16) for mask in single]

    lines_of = []
    for r in range(rows):
        row = given[:, r] + jnp.where(r == (rows - 1) * (1 - lower), part, 0.0)
        lines_of.append(row[:, None])
    hidden = jnp.concatenate(lines_of, axis=1).reshape(own * rows * frames, chans).astype(bf16).astype(f32)
    normed = rms(hidden).astype(bf16)
    query, keys, values = (
        jnp.dot(normed, weight[...], preferred_element_type=f32).astype(bf16) for weight in (w_query, w_key, w_value)
    )
    half = own // 2 if own % (2 * several) == 0 else own
    for start in range(0, own, half):
        gone = []
        for at in range(start * rows * frames, (start + half) * rows * frames, area):
            group_of = slice(at, at + area)
            queries = jnp.concatenate([query[group_of] * mask for mask in scaled], axis=0)
            scores = lax.dot_general(
                queries, keys[group_of], (((1,), (1,)), ((), ())), preferred_element_type=f32
            )
            weights, under = [], jnp.zeros((area, chans), f32)
            for h in range(heads):
                score = scores[h * area : (h + 1) * area] + bias[...]
                expo = jnp.exp(score - jnp.max(score, axis=-1, keepdims=True))
                under = jnp.where(head_of == h, jnp.sum(expo, axis=-1, keepdims=True), under)
                weights.append(expo.astype(bf16))
            heads_values = jnp.concatenate([values[group_of] * mask for mask in single], axis=0)
            attended = jnp.dot(jnp.concatenate(weights, axis=1), heads_values, preferred_element_type=f32)
            gone.append((attended / under).astype(bf16))
        attended = jnp.concatenate(gone, axis=0)
        encoded = hidden[start * rows * frames : (start + half) * rows * frames] + jnp.dot(
            attended, w_output[...], preferred_element_type=f32
        )
        for w in range(half):
            for r in range(rows):
                for t in range(count):
                    first = ((w * rows + r) * count + t + 1) * sources - group
                    place = (t * rows + r) * own + start + w
                    put(res, place, group, back, encoded[first : first + group])
    done = jnp.concatenate([res[i] for i in range(res.shape[0])], axis=1)
    out[...] = done.astype(bf16).reshape(out.shape)


def unpack_kernel(packed, out, local, sems):
    count, rows, cols, chans = out.shape
    lines = count * rows
    regions = packed.shape[0]
    own = cols // regions
    wide = packed[...].astype(f32).reshape(regions, lines, own, chans)
    copies = []
    for at in range(lines):
        place = (at // rows, at % rows)
        local[place] = wide[:, at].reshape(cols, chans).astype(bf16)
        copy = pltpu.make_async_copy(local.at[place], out.at[place], sems.at[at])
        copy.start()
        copies.append(copy)
    for copy in copies:
        copy.wait()


def exchanged(blocks):
    return lax.all_to_all(blocks, "tm", split_axis=0, concat_axis=0, tiled=True)


def per_device(outer, video, block_ids, conv_weight, w_query, w_key, w_value, w_output):
    count, rows, cols, chans = video.shape
    group = lax.axis_size("tm")
    own = cols // group
    span = own + 2
    lines = count * rows
    near = pl.BlockSpec(memory_space=pltpu.VMEM)
    far = pl.BlockSpec(memory_space=pltpu.HBM)
    params = pltpu.CompilerParams(vmem_limit_bytes=VMEM)
    in_far = functools.partial(pltpu.with_memory_space_constraint, memory_space=pltpu.HBM)
    weights = [in_far(x) for x in (w_query, w_key, w_value, w_output)]
    conv_weight = lax.ppermute(conv_weight, "height", [(0, 1), (1, 0)])

    blocks = pl.pallas_call(
        functools.partial(pack_kernel, group),
        out_shape=jax.ShapeDtypeStruct((group, span * lines, chans), bf16),
        in_specs=[far],
        out_specs=near,
        scratch_shapes=[
            pltpu.VMEM(video.shape, bf16),
            scratch(lines * (cols + 2 * EDGE), chans),
            pltpu.SemaphoreType.DMA((lines,)),
        ],
        compiler_params=params,
    )(in_far(video))
    piece = exchanged(blocks)
    ids = block_ids
    if outer > 1:
        before = lax.ppermute(piece, "outer", [(i, i + 1) for i in range(outer - 1)])
        piece = jnp.concatenate([before, piece], axis=0)
        ids = jnp.concatenate([jnp.full((group * count,), -2, jnp.int32), ids])
        ids = lax.dynamic_slice(ids, (lax.axis_index("outer") * group * count,), (2 * group * count,))
    sources = piece.shape[0]
    frames = sources * count
    stored = scratch(sources * span * lines, chans)
    edge = pl.pallas_call(
        functools.partial(edge_kernel, count, rows),
        out_shape=jax.ShapeDtypeStruct((span, frames, TAPS * chans), bf16),
        in_specs=[near],
        out_specs=near,
        scratch_shapes=[stored],
        compiler_params=params,
    )(piece)
    edge = lax.ppermute(edge, "height", [(0, 1), (1, 0)])
    several = max(n for n in range(1, own + 1) if own % n == 0 and (n == 1 or n * rows * frames <= LANES))
    area = several * rows * frames
    total, bias, *weights = pl.pallas_call(
        functools.partial(shift_kernel, count, rows),
        out_shape=[
            jax.ShapeDtypeStruct((own, rows, frames, chans), f32),
            jax.ShapeDtypeStruct((area, area), f32),
        ]
        + [jax.ShapeDtypeStruct(x.shape, bf16) for x in weights],
        in_specs=[near, far, near] + [far] * 4,
        out_specs=[near] * 6,
        scratch_shapes=[
            stored,
            pltpu.VMEM((span, rows, frames, TAPS * chans), bf16),
            pltpu.SMEM((frames,), jnp.int32),
            pltpu.SemaphoreType.DMA((4,)),
            pltpu.SemaphoreType.DMA(()),
        ],
        compiler_params=params,
    )(piece, in_far(ids), conv_weight, *weights)
    blocks = pl.pallas_call(
        functools.partial(main_kernel, count, rows, group),
        out_shape=jax.ShapeDtypeStruct((group, own * lines, chans), bf16),
        in_specs=[near] * 8,
        out_specs=near,
        scratch_shapes=[scratch(group * own * lines, chans)],
        compiler_params=params,
    )(edge, total, bias, conv_weight, *weights)
    return pl.pallas_call(
        unpack_kernel,
        out_shape=jax.ShapeDtypeStruct(video.shape, bf16),
        in_specs=[near],
        out_specs=far,
        scratch_shapes=[
            pltpu.VMEM(video.shape, bf16),
            pltpu.SemaphoreType.DMA((lines,)),
        ],
        compiler_params=params,
    )(exchanged(blocks))


def solution(mesh):
    parts, along, halves = (mesh.shape[a] for a in ("groups", "tm", "height"))

    def run(video, *rest):
        count = video.shape[0] // (parts * along)
        group = min(g for g in range(1, along + 1) if along % g == 0 and (g * count >= REACH or g == along))
        outer = along // group
        split = Mesh(
            np.asarray(mesh.devices).reshape(parts, outer, group, halves),
            ("groups", "outer", "tm", "height"),
        )
        spec = P(("groups", "outer", "tm"), "height", None, None)
        placed = (spec, P("groups"), P(), P(), P(), P(), P())
        return jax.shard_map(
            functools.partial(per_device, outer),
            mesh=split,
            in_specs=placed,
            out_specs=spec,
            check_vma=False,
        )(video, *rest)

    return run
```

```python
import functools

import jax
import jax.numpy as jnp
import numpy as np
from jax import lax
from jax.experimental import pallas as pl
from jax.experimental.pallas import tpu as pltpu
from jax.sharding import Mesh, PartitionSpec as P

HD = 64
BLOCK = 4
TAPS = 3
REACH = 2 * BLOCK - 1 + TAPS - 1
LANES = 128
EDGE = 8
VMEM = 28 * 2**20

bf16, f32 = jnp.bfloat16, jnp.float32


def get(ref, start, size, stride):
    return jnp.concatenate([ref[i, pl.ds(start, size, stride=stride), :] for i in range(ref.shape[0])], axis=1)


def put(ref, start, size, stride, value):
    for i in range(ref.shape[0]):
        ref[i, pl.ds(start, size, stride=stride), :] = value[:, i * LANES : (i + 1) * LANES]


def fill(ref, start, value):
    for i in range(ref.shape[0]):
        ref[i, pl.ds(start, value.shape[0]), :] = value[:, i * LANES : (i + 1) * LANES]


def scratch(rows, chans):
    return pltpu.VMEM((chans // LANES, rows, LANES), f32)


def rms(wide):
    return wide * lax.rsqrt(jnp.mean(wide * wide, axis=-1, keepdims=True) + 1e-06)


def divided(at, by):
    if by & (by - 1) == 0:
        bits = by.bit_length() - 1
        return at >> bits, at & (by - 1)
    return lax.div(at, jnp.int32(by)), lax.rem(at, jnp.int32(by))


def pack_kernel(group, video, *refs):
    out, local, wide, sems = refs
    count, rows, cols, chans = video.shape
    lines = count * rows
    stride = cols + 2 * EDGE
    own = cols // group
    span = own + 2
    copies = []
    for at in range(lines):
        place = (at // rows, at % rows)
        copy = pltpu.make_async_copy(video.at[place], local.at[place], sems.at[at])
        copy.start()
        copies.append(copy)
    nothing = jnp.zeros((EDGE, chans), f32)
    for at in range(lines):
        fill(wide, at * stride, nothing)
        fill(wide, at * stride + EDGE + cols, nothing)
    for at, copy in enumerate(copies):
        copy.wait()
        fill(wide, at * stride + EDGE, local[at // rows, at % rows].astype(f32))
    together = 16 // lines
    for k in range(group):
        start = k * own + EDGE - 1
        for w in range(0, span, together):
            tile = jnp.concatenate([get(wide, start + w + i, lines, stride) for i in range(together)], axis=0)
            out[k, pl.ds(w * lines, 16), :] = tile.astype(bf16)


def frames_of(ref, w, r, count, rows, sources, step):
    return [get(ref, w * count * rows + t * rows + r, sources, step) for t in range(count)]


def shifted(now):
    count = len(now)
    sources, chans = now[0].shape
    first = lax.broadcasted_iota(jnp.int32, (sources, chans), 0) == 0
    past = [jnp.where(first, 0.0, pltpu.roll(x, 1, 0)) for x in now]
    ordered = past + now
    taps = []
    for a in range(TAPS):
        start = count - (TAPS - 1 - a)
        taps.append(jnp.concatenate(ordered[start : start + count], 0).astype(bf16))
    return jnp.concatenate(taps, axis=1)


def activated(wide):
    part = 0.5 * rms(wide)
    return part + part * jnp.tanh(part)


def depth(parts):
    return parts[0] if len(parts) == 1 else jnp.concatenate(parts, axis=-1)


def edge_kernel(count, rows, video, edge, vid):
    sources, step, chans = video.shape
    span = step // (count * rows)
    fill(vid, 0, video[...].reshape(sources * step, chans).astype(f32))
    row = (rows - 1) * (1 - lax.axis_index("height"))
    for w in range(span):
        edge[w] = shifted([activated(x) for x in frames_of(vid, w, row, count, rows, sources, step)])


def fill_bias(bias, ids, frames, count):
    area = bias.shape[0]
    sources = frames // count

    def place_of(at):
        pixel, place = divided(at, frames)
        inner, source = divided(place, sources)
        frame = source * count + inner
        block = jnp.zeros(at.shape, jnp.int32)
        for s in range(frames):
            block = jnp.where(frame == s, ids[s], block)
        return pixel, frame, block

    row_p, row_t, row_b = place_of(lax.broadcasted_iota(jnp.int32, (area, area), 0))
    col_p, col_t, col_b = place_of(lax.broadcasted_iota(jnp.int32, (1, area), 1))
    permit = (row_p == col_p) & (col_t <= row_t) & (col_b >= row_b - 1)
    bias[...] = jnp.where(permit, 0.0, -1e30)


def shift_kernel(count, rows, video, ids_far, *refs):
    conv_weight, far, (total, bias, *near) = refs[0], refs[1:5], refs[5:11]
    vid, grid, ids, sems, ids_sem = refs[11:]
    ids_copy = pltpu.make_async_copy(ids_far, ids, ids_sem)
    ids_copy.start()
    others = [pltpu.make_async_copy(src, dst, sems.at[i]) for i, (src, dst) in enumerate(zip(far, near))]
    for copy in others:
        copy.start()
    sources, step, chans = video.shape
    span = step // (count * rows)
    own = span - 2
    frames = sources * count
    half = own // 2 if own % 2 == 0 else own
    fill(vid, 0, video[...].reshape(sources * step, chans).astype(f32))
    for w in range(span):
        for r in range(rows):
            now = frames_of(vid, w, r, count, rows, sources, step)
            grid[w, r] = shifted([activated(x) for x in now])
            if 1 <= w <= own:
                total[w - 1, r] = jnp.concatenate(now, 0)

    for b in range(TAPS):
        low, high = max(0, 1 - b), min(rows, rows + 1 - b)
        weight = jnp.concatenate([conv_weight[a, b, e] for e in range(TAPS) for a in range(TAPS)], axis=0)
        for w in range(0, own, half):
            window = depth([grid[w + e : w + e + half, low + b - 1 : high + b - 1] for e in range(TAPS)])
            window = window.reshape(half * (high - low) * frames, TAPS * TAPS * chans)
            part = jnp.dot(window, weight, preferred_element_type=f32)
            some = total.at[w : w + half, low:high]
            some[...] = some[...] + part.reshape(half, high - low, frames, chans)
    ids_copy.wait()
    fill_bias(bias, ids, frames, count)
    for copy in others:
        copy.wait()


def main_kernel(
    count, rows, group, edge, given, bias, conv_weight, w_query, w_key, w_value, w_output, *refs
):
    out, res = refs
    own, _, frames, chans = given.shape
    sources = frames // count
    lines = count * rows
    heads = chans // HD
    back = own * lines
    area = bias.shape[0]
    several = area // (rows * frames)

    lower = lax.axis_index("height")
    b = (TAPS - 1) * (1 - lower)
    part = jnp.zeros((own * frames, chans), f32)
    for e in range(TAPS):
        window = edge[e : e + own].reshape(own * frames, TAPS * chans)
        weight = jnp.concatenate([conv_weight[a, b, e] for a in range(TAPS)], axis=0)
        part = part + jnp.dot(window, weight, preferred_element_type=f32)
    part = part.reshape(own, frames, chans)

    head_of = divided(lax.broadcasted_iota(jnp.int32, (area, chans), 1), HD)[0]
    single = [jnp.where(head_of == h, 1.0, 0.0).astype(bf16) for h in range(heads)]
    scaled = [mask * jnp.asarray(HD ** (-0.5), bf16) for mask in single]

    lines_of = []
    for r in range(rows):
        row = given[:, r] + jnp.where(r == (rows - 1) * (1 - lower), part, 0.0)
        lines_of.append(row[:, None])
    hidden = jnp.concatenate(lines_of, axis=1).reshape(own * rows * frames, chans).astype(bf16).astype(f32)
    normed = rms(hidden).astype(bf16)
    query, keys, values = (
        jnp.dot(normed, weight[...], preferred_element_type=f32).astype(bf16) for weight in (w_query, w_key, w_value)
    )
    half = own // 2 if own % (2 * several) == 0 else own
    for start in range(0, own, half):
        gone = []
        for at in range(start * rows * frames, (start + half) * rows * frames, area):
            group_of = slice(at, at + area)
            queries = jnp.concatenate([query[group_of] * mask for mask in scaled], axis=0)
            scores = lax.dot_general(
                queries, keys[group_of], (((1,), (1,)), ((), ())), preferred_element_type=f32
            )
            weights, under = [], jnp.zeros((area, chans), f32)
            for h in range(heads):
                score = scores[h * area : (h + 1) * area] + bias[...]
                expo = jnp.exp(score - jnp.max(score, axis=-1, keepdims=True))
                under = jnp.where(head_of == h, jnp.sum(expo, axis=-1, keepdims=True), under)
                weights.append(expo.astype(bf16))
            heads_values = jnp.concatenate([values[group_of] * mask for mask in single], axis=0)
            attended = jnp.dot(jnp.concatenate(weights, axis=1), heads_values, preferred_element_type=f32)
            gone.append((attended / under).astype(bf16))
        attended = jnp.concatenate(gone, axis=0)
        encoded = hidden[start * rows * frames : (start + half) * rows * frames] + jnp.dot(
            attended, w_output[...], preferred_element_type=f32
        )
        for w in range(half):
            for r in range(rows):
                for t in range(count):
                    first = ((w * rows + r) * count + t + 1) * sources - group
                    place = (t * rows + r) * own + start + w
                    put(res, place, group, back, encoded[first : first + group])
    done = jnp.concatenate([res[i] for i in range(res.shape[0])], axis=1)
    out[...] = done.astype(bf16).reshape(out.shape)


def unpack_kernel(packed, out, local, sems):
    count, rows, cols, chans = out.shape
    lines = count * rows
    regions = packed.shape[0]
    own = cols // regions
    wide = packed[...].astype(f32).reshape(regions, lines, own, chans)
    copies = []
    for at in range(lines):
        place = (at // rows, at % rows)
        local[place] = wide[:, at].reshape(cols, chans).astype(bf16)
        copy = pltpu.make_async_copy(local.at[place], out.at[place], sems.at[at])
        copy.start()
        copies.append(copy)
    for copy in copies:
        copy.wait()


def exchanged(blocks):
    return lax.all_to_all(blocks, "tm", split_axis=0, concat_axis=0, tiled=True)


def per_device(outer, video, block_ids, conv_weight, w_query, w_key, w_value, w_output):
    count, rows, cols, chans = video.shape
    group = lax.axis_size("tm")
    own = cols // group
    span = own + 2
    lines = count * rows
    near = pl.BlockSpec(memory_space=pltpu.VMEM)
    far = pl.BlockSpec(memory_space=pltpu.HBM)
    params = pltpu.CompilerParams(vmem_limit_bytes=VMEM)
    in_far = functools.partial(pltpu.with_memory_space_constraint, memory_space=pltpu.HBM)
    weights = [in_far(x) for x in (w_query, w_key, w_value, w_output)]
    conv_weight = lax.ppermute(conv_weight, "height", [(i, i) for i in range(lax.axis_size("height"))])

    blocks = pl.pallas_call(
        functools.partial(pack_kernel, group),
        out_shape=jax.ShapeDtypeStruct((group, span * lines, chans), bf16),
        in_specs=[far],
        out_specs=near,
        scratch_shapes=[
            pltpu.VMEM(video.shape, bf16),
            scratch(lines * (cols + 2 * EDGE), chans),
            pltpu.SemaphoreType.DMA((lines,)),
        ],
        compiler_params=params,
    )(in_far(video))
    piece = exchanged(blocks)
    ids = block_ids
    if outer > 1:
        before = lax.ppermute(piece, "outer", [(i, i + 1) for i in range(outer - 1)])
        piece = jnp.concatenate([before, piece], axis=0)
        ids = jnp.concatenate([jnp.full((group * count,), -2, jnp.int32), ids])
        ids = lax.dynamic_slice(ids, (lax.axis_index("outer") * group * count,), (2 * group * count,))
    sources = piece.shape[0]
    frames = sources * count
    stored = scratch(sources * span * lines, chans)
    edge = pl.pallas_call(
        functools.partial(edge_kernel, count, rows),
        out_shape=jax.ShapeDtypeStruct((span, frames, TAPS * chans), bf16),
        in_specs=[near],
        out_specs=near,
        scratch_shapes=[stored],
        compiler_params=params,
    )(piece)
    edge = lax.ppermute(edge, "height", [(0, 1), (1, 0)])
    several = max(n for n in range(1, own + 1) if own % n == 0 and (n == 1 or n * rows * frames <= LANES))
    area = several * rows * frames
    total, bias, *weights = pl.pallas_call(
        functools.partial(shift_kernel, count, rows),
        out_shape=[
            jax.ShapeDtypeStruct((own, rows, frames, chans), f32),
            jax.ShapeDtypeStruct((area, area), f32),
        ]
        + [jax.ShapeDtypeStruct(x.shape, bf16) for x in weights],
        in_specs=[near, far, near] + [far] * 4,
        out_specs=[near] * 6,
        scratch_shapes=[
            stored,
            pltpu.VMEM((span, rows, frames, TAPS * chans), bf16),
            pltpu.SMEM((frames,), jnp.int32),
            pltpu.SemaphoreType.DMA((4,)),
            pltpu.SemaphoreType.DMA(()),
        ],
        compiler_params=params,
    )(piece, in_far(ids), conv_weight, *weights)
    blocks = pl.pallas_call(
        functools.partial(main_kernel, count, rows, group),
        out_shape=jax.ShapeDtypeStruct((group, own * lines, chans), bf16),
        in_specs=[near] * 8,
        out_specs=near,
        scratch_shapes=[scratch(group * own * lines, chans)],
        compiler_params=params,
    )(edge, total, bias, conv_weight, *weights)
    return pl.pallas_call(
        unpack_kernel,
        out_shape=jax.ShapeDtypeStruct(video.shape, bf16),
        in_specs=[near],
        out_specs=far,
        scratch_shapes=[
            pltpu.VMEM(video.shape, bf16),
            pltpu.SemaphoreType.DMA((lines,)),
        ],
        compiler_params=params,
    )(exchanged(blocks))


def solution(mesh):
    parts, along, halves = (mesh.shape[a] for a in ("groups", "tm", "height"))

    def run(video, *rest):
        count = video.shape[0] // (parts * along)
        group = min(g for g in range(1, along + 1) if along % g == 0 and (g * count >= REACH or g == along))
        outer = along // group
        split = Mesh(
            np.asarray(mesh.devices).reshape(parts, outer, group, halves),
            ("groups", "outer", "tm", "height"),
        )
        spec = P(("groups", "outer", "tm"), "height", None, None)
        placed = (spec, P("groups"), P(), P(), P(), P(), P())
        return jax.shard_map(
            functools.partial(per_device, outer),
            mesh=split,
            in_specs=placed,
            out_specs=spec,
            check_vma=False,
        )(video, *rest)

    return run
```

```python
import functools

import jax
import jax.numpy as jnp
import numpy as np
from jax import lax
from jax.experimental import pallas as pl
from jax.experimental.pallas import tpu as pltpu
from jax.sharding import Mesh, PartitionSpec as P

HD = 64
BLOCK = 4
TAPS = 3
REACH = 2 * BLOCK - 1 + TAPS - 1
LANES = 128
EDGE = 8
VMEM = 28 * 2**20

bf16, f32 = jnp.bfloat16, jnp.float32


def get(ref, start, size, stride):
    return jnp.concatenate([ref[i, pl.ds(start, size, stride=stride), :] for i in range(ref.shape[0])], axis=1)


def put(ref, start, size, stride, value):
    for i in range(ref.shape[0]):
        ref[i, pl.ds(start, size, stride=stride), :] = value[:, i * LANES : (i + 1) * LANES]


def fill(ref, start, value):
    for i in range(ref.shape[0]):
        ref[i, pl.ds(start, value.shape[0]), :] = value[:, i * LANES : (i + 1) * LANES]


def scratch(rows, chans):
    return pltpu.VMEM((chans // LANES, rows, LANES), f32)


def rms(wide):
    return wide * lax.rsqrt(jnp.mean(wide * wide, axis=-1, keepdims=True) + 1e-06)


def divided(at, by):
    if by & (by - 1) == 0:
        bits = by.bit_length() - 1
        return at >> bits, at & (by - 1)
    return lax.div(at, jnp.int32(by)), lax.rem(at, jnp.int32(by))


def pack_kernel(group, video, conv_far, *refs):
    out, conv_own, local, wide, sems, conv_sem = refs
    count, rows, cols, chans = video.shape
    lines = count * rows
    stride = cols + 2 * EDGE
    own = cols // group
    span = own + 2
    copies = []
    for at in range(lines):
        place = (at // rows, at % rows)
        copy = pltpu.make_async_copy(video.at[place], local.at[place], sems.at[at])
        copy.start()
        copies.append(copy)
    taps = pltpu.make_async_copy(conv_far.at[:, 1], conv_own, conv_sem)
    taps.start()
    nothing = jnp.zeros((EDGE, chans), f32)
    for at in range(lines):
        fill(wide, at * stride, nothing)
        fill(wide, at * stride + EDGE + cols, nothing)
    for at, copy in enumerate(copies):
        copy.wait()
        fill(wide, at * stride + EDGE, local[at // rows, at % rows].astype(f32))
    together = 16 // lines
    for k in range(group):
        start = k * own + EDGE - 1
        for w in range(0, span, together):
            tile = jnp.concatenate([get(wide, start + w + i, lines, stride) for i in range(together)], axis=0)
            out[k, pl.ds(w * lines, 16), :] = tile.astype(bf16)
    taps.wait()


def frames_of(ref, w, r, count, rows, sources, step):
    return [get(ref, w * count * rows + t * rows + r, sources, step) for t in range(count)]


def shifted(now):
    count = len(now)
    sources, chans = now[0].shape
    first = lax.broadcasted_iota(jnp.int32, (sources, chans), 0) == 0
    past = [jnp.where(first, 0.0, pltpu.roll(x, 1, 0)) for x in now]
    ordered = past + now
    taps = []
    for a in range(TAPS):
        start = count - (TAPS - 1 - a)
        taps.append(jnp.concatenate(ordered[start : start + count], 0).astype(bf16))
    return jnp.concatenate(taps, axis=1)


def activated(wide):
    part = 0.5 * rms(wide)
    return part + part * jnp.tanh(part)


def depth(parts):
    return parts[0] if len(parts) == 1 else jnp.concatenate(parts, axis=-1)


def edge_kernel(count, rows, video, edge, vid):
    sources, step, chans = video.shape
    span = step // (count * rows)
    fill(vid, 0, video[...].reshape(sources * step, chans).astype(f32))
    row = (rows - 1) * (1 - lax.axis_index("height"))
    for w in range(span):
        edge[w] = shifted([activated(x) for x in frames_of(vid, w, row, count, rows, sources, step)])


def fill_bias(bias, ids, frames, count):
    area = bias.shape[0]
    sources = frames // count

    def place_of(at):
        pixel, place = divided(at, frames)
        inner, source = divided(place, sources)
        frame = source * count + inner
        block = jnp.zeros(at.shape, jnp.int32)
        for s in range(frames):
            block = jnp.where(frame == s, ids[s], block)
        return pixel, frame, block

    row_p, row_t, row_b = place_of(lax.broadcasted_iota(jnp.int32, (area, area), 0))
    col_p, col_t, col_b = place_of(lax.broadcasted_iota(jnp.int32, (1, area), 1))
    permit = (row_p == col_p) & (col_t <= row_t) & (col_b >= row_b - 1)
    bias[...] = jnp.where(permit, 0.0, -1e30)


def shift_kernel(count, rows, video, ids_far, *refs):
    conv_own, conv_far, far, (total, bias, *near) = refs[0], refs[1], refs[2:6], refs[6:14]
    vid, grid, ids, sems, ids_sem = refs[14:]
    taps = {1: conv_own, 0: near[0], 2: near[1]}
    far = (conv_far.at[:, 0], conv_far.at[:, 2]) + tuple(far)
    ids_copy = pltpu.make_async_copy(ids_far, ids, ids_sem)
    ids_copy.start()
    others = [pltpu.make_async_copy(src, dst, sems.at[i]) for i, (src, dst) in enumerate(zip(far, near))]
    for copy in others:
        copy.start()
    sources, step, chans = video.shape
    span = step // (count * rows)
    own = span - 2
    frames = sources * count
    half = own // 2 if own % 2 == 0 else own
    fill(vid, 0, video[...].reshape(sources * step, chans).astype(f32))
    for w in range(span):
        for r in range(rows):
            now = frames_of(vid, w, r, count, rows, sources, step)
            grid[w, r] = shifted([activated(x) for x in now])
            if 1 <= w <= own:
                total[w - 1, r] = jnp.concatenate(now, 0)

    for b in taps:
        if b != 1:
            others[b // 2].wait()
        low, high = max(0, 1 - b), min(rows, rows + 1 - b)
        weight = jnp.concatenate([taps[b][a, e] for e in range(TAPS) for a in range(TAPS)], axis=0)
        for w in range(0, own, half):
            window = depth([grid[w + e : w + e + half, low + b - 1 : high + b - 1] for e in range(TAPS)])
            window = window.reshape(half * (high - low) * frames, TAPS * TAPS * chans)
            part = jnp.dot(window, weight, preferred_element_type=f32)
            some = total.at[w : w + half, low:high]
            some[...] = some[...] + part.reshape(half, high - low, frames, chans)
    ids_copy.wait()
    fill_bias(bias, ids, frames, count)
    for copy in others[2:]:
        copy.wait()


def main_kernel(
    count, rows, group, edge, given, bias, conv_above, conv_below, w_query, w_key, w_value, w_output, *refs
):
    out, res = refs
    own, _, frames, chans = given.shape
    sources = frames // count
    lines = count * rows
    heads = chans // HD
    back = own * lines
    area = bias.shape[0]
    several = area // (rows * frames)

    lower = lax.axis_index("height")
    part = jnp.zeros((own * frames, chans), f32)
    for e in range(TAPS):
        window = edge[e : e + own].reshape(own * frames, TAPS * chans)
        above, below = (
            jnp.concatenate([taps[a, e] for a in range(TAPS)], axis=0) for taps in (conv_above, conv_below)
        )
        part = part + jnp.dot(window, jnp.where(lower == 1, above, below), preferred_element_type=f32)
    part = part.reshape(own, frames, chans)

    head_of = divided(lax.broadcasted_iota(jnp.int32, (area, chans), 1), HD)[0]
    single = [jnp.where(head_of == h, 1.0, 0.0).astype(bf16) for h in range(heads)]
    scaled = [mask * jnp.asarray(HD ** (-0.5), bf16) for mask in single]

    lines_of = []
    for r in range(rows):
        row = given[:, r] + jnp.where(r == (rows - 1) * (1 - lower), part, 0.0)
        lines_of.append(row[:, None])
    hidden = jnp.concatenate(lines_of, axis=1).reshape(own * rows * frames, chans).astype(bf16).astype(f32)
    normed = rms(hidden).astype(bf16)
    query, keys, values = (
        jnp.dot(normed, weight[...], preferred_element_type=f32).astype(bf16) for weight in (w_query, w_key, w_value)
    )
    half = own // 2 if own % (2 * several) == 0 else own
    for start in range(0, own, half):
        gone = []
        for at in range(start * rows * frames, (start + half) * rows * frames, area):
            group_of = slice(at, at + area)
            queries = jnp.concatenate([query[group_of] * mask for mask in scaled], axis=0)
            scores = lax.dot_general(
                queries, keys[group_of], (((1,), (1,)), ((), ())), preferred_element_type=f32
            )
            weights, under = [], jnp.zeros((area, chans), f32)
            for h in range(heads):
                score = scores[h * area : (h + 1) * area] + bias[...]
                expo = jnp.exp(score - jnp.max(score, axis=-1, keepdims=True))
                under = jnp.where(head_of == h, jnp.sum(expo, axis=-1, keepdims=True), under)
                weights.append(expo.astype(bf16))
            heads_values = jnp.concatenate([values[group_of] * mask for mask in single], axis=0)
            attended = jnp.dot(jnp.concatenate(weights, axis=1), heads_values, preferred_element_type=f32)
            gone.append((attended / under).astype(bf16))
        attended = jnp.concatenate(gone, axis=0)
        encoded = hidden[start * rows * frames : (start + half) * rows * frames] + jnp.dot(
            attended, w_output[...], preferred_element_type=f32
        )
        for w in range(half):
            for r in range(rows):
                for t in range(count):
                    first = ((w * rows + r) * count + t + 1) * sources - group
                    place = (t * rows + r) * own + start + w
                    put(res, place, group, back, encoded[first : first + group])
    done = jnp.concatenate([res[i] for i in range(res.shape[0])], axis=1)
    out[...] = done.astype(bf16).reshape(out.shape)


def unpack_kernel(packed, out, local, sems):
    count, rows, cols, chans = out.shape
    lines = count * rows
    regions = packed.shape[0]
    own = cols // regions
    wide = packed[...].astype(f32).reshape(regions, lines, own, chans)
    copies = []
    for at in range(lines):
        place = (at // rows, at % rows)
        local[place] = wide[:, at].reshape(cols, chans).astype(bf16)
        copy = pltpu.make_async_copy(local.at[place], out.at[place], sems.at[at])
        copy.start()
        copies.append(copy)
    for copy in copies:
        copy.wait()


def exchanged(blocks):
    return lax.all_to_all(blocks, "tm", split_axis=0, concat_axis=0, tiled=True)


def per_device(outer, video, block_ids, conv_weight, w_query, w_key, w_value, w_output):
    count, rows, cols, chans = video.shape
    group = lax.axis_size("tm")
    own = cols // group
    span = own + 2
    lines = count * rows
    near = pl.BlockSpec(memory_space=pltpu.VMEM)
    far = pl.BlockSpec(memory_space=pltpu.HBM)
    params = pltpu.CompilerParams(vmem_limit_bytes=VMEM)
    in_far = functools.partial(pltpu.with_memory_space_constraint, memory_space=pltpu.HBM)
    conv_weight, *weights = (in_far(x) for x in (conv_weight, w_query, w_key, w_value, w_output))

    slab = (TAPS, TAPS, chans, chans)
    blocks, conv_own = pl.pallas_call(
        functools.partial(pack_kernel, group),
        out_shape=[
            jax.ShapeDtypeStruct((group, span * lines, chans), bf16),
            jax.ShapeDtypeStruct(slab, bf16),
        ],
        in_specs=[far, far],
        out_specs=[near, near],
        scratch_shapes=[
            pltpu.VMEM(video.shape, bf16),
            scratch(lines * (cols + 2 * EDGE), chans),
            pltpu.SemaphoreType.DMA((lines,)),
            pltpu.SemaphoreType.DMA(()),
        ],
        compiler_params=params,
    )(in_far(video), conv_weight)
    piece = exchanged(blocks)
    ids = block_ids
    if outer > 1:
        before = lax.ppermute(piece, "outer", [(i, i + 1) for i in range(outer - 1)])
        piece = jnp.concatenate([before, piece], axis=0)
        ids = jnp.concatenate([jnp.full((group * count,), -2, jnp.int32), ids])
        ids = lax.dynamic_slice(ids, (lax.axis_index("outer") * group * count,), (2 * group * count,))
    sources = piece.shape[0]
    frames = sources * count
    stored = scratch(sources * span * lines, chans)
    edge = pl.pallas_call(
        functools.partial(edge_kernel, count, rows),
        out_shape=jax.ShapeDtypeStruct((span, frames, TAPS * chans), bf16),
        in_specs=[near],
        out_specs=near,
        scratch_shapes=[stored],
        compiler_params=params,
    )(piece)
    edge = lax.ppermute(edge, "height", [(0, 1), (1, 0)])
    several = max(n for n in range(1, own + 1) if own % n == 0 and (n == 1 or n * rows * frames <= LANES))
    area = several * rows * frames
    total, bias, *weights = pl.pallas_call(
        functools.partial(shift_kernel, count, rows),
        out_shape=[
            jax.ShapeDtypeStruct((own, rows, frames, chans), f32),
            jax.ShapeDtypeStruct((area, area), f32),
        ]
        + [jax.ShapeDtypeStruct(slab, bf16)] * 2
        + [jax.ShapeDtypeStruct(x.shape, bf16) for x in weights],
        in_specs=[near, far, near] + [far] * 5,
        out_specs=[near] * 8,
        scratch_shapes=[
            stored,
            pltpu.VMEM((span, rows, frames, TAPS * chans), bf16),
            pltpu.SMEM((frames,), jnp.int32),
            pltpu.SemaphoreType.DMA((6,)),
            pltpu.SemaphoreType.DMA(()),
        ],
        compiler_params=params,
    )(piece, in_far(ids), conv_own, conv_weight, *weights)
    blocks = pl.pallas_call(
        functools.partial(main_kernel, count, rows, group),
        out_shape=jax.ShapeDtypeStruct((group, own * lines, chans), bf16),
        in_specs=[near] * 9,
        out_specs=near,
        scratch_shapes=[scratch(group * own * lines, chans)],
        compiler_params=params,
    )(edge, total, bias, *weights)
    return pl.pallas_call(
        unpack_kernel,
        out_shape=jax.ShapeDtypeStruct(video.shape, bf16),
        in_specs=[near],
        out_specs=far,
        scratch_shapes=[
            pltpu.VMEM(video.shape, bf16),
            pltpu.SemaphoreType.DMA((lines,)),
        ],
        compiler_params=params,
    )(exchanged(blocks))


def solution(mesh):
    parts, along, halves = (mesh.shape[a] for a in ("groups", "tm", "height"))

    def run(video, *rest):
        count = video.shape[0] // (parts * along)
        group = min(g for g in range(1, along + 1) if along % g == 0 and (g * count >= REACH or g == along))
        outer = along // group
        split = Mesh(
            np.asarray(mesh.devices).reshape(parts, outer, group, halves),
            ("groups", "outer", "tm", "height"),
        )
        spec = P(("groups", "outer", "tm"), "height", None, None)
        placed = (spec, P("groups"), P(), P(), P(), P(), P())
        return jax.shard_map(
            functools.partial(per_device, outer),
            mesh=split,
            in_specs=placed,
            out_specs=spec,
            check_vma=False,
        )(video, *rest)

    return run
```

```python
import functools

import jax
import jax.numpy as jnp
import numpy as np
from jax import lax
from jax.experimental import pallas as pl
from jax.experimental.pallas import tpu as pltpu
from jax.sharding import Mesh, PartitionSpec as P

HD = 64
BLOCK = 4
TAPS = 3
REACH = 2 * BLOCK - 1 + TAPS - 1
LANES = 128
EDGE = 8
VMEM = 28 * 2**20

bf16, f32 = jnp.bfloat16, jnp.float32


def get(ref, start, size, stride):
    return jnp.concatenate([ref[i, pl.ds(start, size, stride=stride), :] for i in range(ref.shape[0])], axis=1)


def put(ref, start, size, stride, value):
    for i in range(ref.shape[0]):
        ref[i, pl.ds(start, size, stride=stride), :] = value[:, i * LANES : (i + 1) * LANES]


def fill(ref, start, value):
    for i in range(ref.shape[0]):
        ref[i, pl.ds(start, value.shape[0]), :] = value[:, i * LANES : (i + 1) * LANES]


def scratch(rows, chans):
    return pltpu.VMEM((chans // LANES, rows, LANES), f32)


def rms(wide):
    return wide * lax.rsqrt(jnp.mean(wide * wide, axis=-1, keepdims=True) + 1e-06)


def divided(at, by):
    if by & (by - 1) == 0:
        bits = by.bit_length() - 1
        return at >> bits, at & (by - 1)
    return lax.div(at, jnp.int32(by)), lax.rem(at, jnp.int32(by))


def pack_kernel(group, video, *refs):
    out, local, wide, sems = refs
    count, rows, cols, chans = video.shape
    lines = count * rows
    stride = cols + 2 * EDGE
    own = cols // group
    span = own + 2
    copies = []
    for at in range(lines):
        place = (at // rows, at % rows)
        copy = pltpu.make_async_copy(video.at[place], local.at[place], sems.at[at])
        copy.start()
        copies.append(copy)
    nothing = jnp.zeros((EDGE, chans), f32)
    for at in range(lines):
        fill(wide, at * stride, nothing)
        fill(wide, at * stride + EDGE + cols, nothing)
    for at, copy in enumerate(copies):
        copy.wait()
        fill(wide, at * stride + EDGE, local[at // rows, at % rows].astype(f32))
    together = 16 // lines
    for k in range(group):
        start = k * own + EDGE - 1
        for w in range(0, span, together):
            tile = jnp.concatenate([get(wide, start + w + i, lines, stride) for i in range(together)], axis=0)
            out[k, pl.ds(w * lines, 16), :] = tile.astype(bf16)


def frames_of(ref, w, r, count, rows, sources, step):
    return [get(ref, w * count * rows + t * rows + r, sources, step) for t in range(count)]


def shifted(now):
    count = len(now)
    sources, chans = now[0].shape
    first = lax.broadcasted_iota(jnp.int32, (sources, chans), 0) == 0
    past = [jnp.where(first, 0.0, pltpu.roll(x, 1, 0)) for x in now]
    ordered = past + now
    taps = []
    for a in range(TAPS):
        start = count - (TAPS - 1 - a)
        taps.append(jnp.concatenate(ordered[start : start + count], 0).astype(bf16))
    return jnp.concatenate(taps, axis=1)


def activated(wide):
    part = 0.5 * rms(wide)
    return part + part * jnp.tanh(part)


def depth(parts):
    return parts[0] if len(parts) == 1 else jnp.concatenate(parts, axis=-1)


def edge_kernel(count, rows, video, edge, vid):
    sources, step, chans = video.shape
    span = step // (count * rows)
    fill(vid, 0, video[...].reshape(sources * step, chans).astype(f32))
    row = (rows - 1) * (1 - lax.axis_index("height"))
    for w in range(span):
        frames = frames_of(vid, w, row, count, rows, sources, step)
        edge[w] = jnp.concatenate([activated(x) for x in frames], axis=0).astype(bf16)


def fill_bias(bias, ids, frames, count):
    area = bias.shape[0]
    sources = frames // count

    def place_of(at):
        pixel, place = divided(at, frames)
        inner, source = divided(place, sources)
        frame = source * count + inner
        block = jnp.zeros(at.shape, jnp.int32)
        for s in range(frames):
            block = jnp.where(frame == s, ids[s], block)
        return pixel, frame, block

    row_p, row_t, row_b = place_of(lax.broadcasted_iota(jnp.int32, (area, area), 0))
    col_p, col_t, col_b = place_of(lax.broadcasted_iota(jnp.int32, (1, area), 1))
    permit = (row_p == col_p) & (col_t <= row_t) & (col_b >= row_b - 1)
    bias[...] = jnp.where(permit, 0.0, -1e30)


def convolve(total, grid, conv_weight, start):
    own, rows, frames, chans = total.shape
    for b in range(TAPS):
        low, high = max(0, 1 - b), min(rows, rows + 1 - b)
        weight = jnp.concatenate([conv_weight[a, b, e] for e in range(TAPS) for a in range(TAPS)], axis=0)
        window = depth(
            [grid[start + e : start + e + own, low + b - 1 : high + b - 1] for e in range(TAPS)]
        )
        window = window.reshape(own * (high - low) * frames, TAPS * TAPS * chans)
        part = jnp.dot(window, weight, preferred_element_type=f32)
        total[:, low:high] = total[:, low:high] + part.reshape(own, high - low, frames, chans)


def shift_kernel(count, rows, video, ids_far, *refs):
    conv_weight, far, (grid, total, bias, *near) = refs[0], refs[1:5], refs[5:12]
    vid, ids, sems, ids_sem = refs[12:]
    ids_copy = pltpu.make_async_copy(ids_far, ids, ids_sem)
    ids_copy.start()
    others = [pltpu.make_async_copy(src, dst, sems.at[i]) for i, (src, dst) in enumerate(zip(far, near))]
    for copy in others:
        copy.start()
    sources, step, chans = video.shape
    span = step // (count * rows)
    own = span - 2
    frames = sources * count
    half = own - own // 2
    fill(vid, 0, video[...].reshape(sources * step, chans).astype(f32))
    for w in range(span):
        for r in range(rows):
            now = frames_of(vid, w, r, count, rows, sources, step)
            grid[w, r] = shifted([activated(x) for x in now])
            if 1 <= w <= own:
                total[w - 1, r] = jnp.concatenate(now, 0)

    convolve(total.at[:half], grid, conv_weight, 0)
    ids_copy.wait()
    fill_bias(bias, ids, frames, count)
    for copy in others:
        copy.wait()


def main_kernel(
    count, rows, group, edge, grid, given, bias, conv_weight, w_query, w_key, w_value, w_output, *refs
):
    out, res, rest = refs
    own, _, frames, chans = given.shape
    sources = frames // count
    lines = count * rows
    heads = chans // HD
    back = own * lines
    area = bias.shape[0]
    several = area // (rows * frames)

    lower = lax.axis_index("height")
    b = (TAPS - 1) * (1 - lower)
    border = []
    for w in range(own + 2):
        x = edge[w].astype(f32)
        border.append(shifted([x[t * sources : (t + 1) * sources] for t in range(count)]))
    part = jnp.zeros((own * frames, chans), f32)
    for e in range(TAPS):
        window = jnp.concatenate(border[e : e + own], axis=0)
        weight = jnp.concatenate([conv_weight[a, b, e] for a in range(TAPS)], axis=0)
        part = part + jnp.dot(window, weight, preferred_element_type=f32)
    part = part.reshape(own, frames, chans)

    head_of = divided(lax.broadcasted_iota(jnp.int32, (area, chans), 1), HD)[0]
    single = [jnp.where(head_of == h, 1.0, 0.0).astype(bf16) for h in range(heads)]
    scaled = [mask * jnp.asarray(HD ** (-0.5), bf16) for mask in single]

    half = own - own // 2
    rest[...] = given[half:]
    for start, end, sums in ((0, half, given.at[:half]), (half, own, rest)):
        if start:
            convolve(rest, grid, conv_weight, half)
        lines_of = []
        for r in range(rows):
            row = sums[:, r] + jnp.where(r == (rows - 1) * (1 - lower), part[start:end], 0.0)
            lines_of.append(row[:, None])
        hidden = jnp.concatenate(lines_of, axis=1).reshape(-1, chans).astype(bf16).astype(f32)
        normed = rms(hidden).astype(bf16)
        query, keys, values = (
            jnp.dot(normed, weight[...], preferred_element_type=f32).astype(bf16)
            for weight in (w_query, w_key, w_value)
        )
        gone = []
        for at in range(0, (end - start) * rows * frames, area):
            group_of = slice(at, at + area)
            queries = jnp.concatenate([query[group_of] * mask for mask in scaled], axis=0)
            scores = lax.dot_general(
                queries, keys[group_of], (((1,), (1,)), ((), ())), preferred_element_type=f32
            )
            weights, under = [], jnp.zeros((area, chans), f32)
            for h in range(heads):
                score = scores[h * area : (h + 1) * area] + bias[...]
                expo = jnp.exp(score - jnp.max(score, axis=-1, keepdims=True))
                under = jnp.where(head_of == h, jnp.sum(expo, axis=-1, keepdims=True), under)
                weights.append(expo.astype(bf16))
            heads_values = jnp.concatenate([values[group_of] * mask for mask in single], axis=0)
            attended = jnp.dot(jnp.concatenate(weights, axis=1), heads_values, preferred_element_type=f32)
            gone.append((attended / under).astype(bf16))
        attended = jnp.concatenate(gone, axis=0)
        encoded = hidden + jnp.dot(attended, w_output[...], preferred_element_type=f32)
        for w in range(end - start):
            for r in range(rows):
                for t in range(count):
                    first = ((w * rows + r) * count + t + 1) * sources - group
                    place = (t * rows + r) * own + start + w
                    put(res, place, group, back, encoded[first : first + group])
    done = jnp.concatenate([res[i] for i in range(res.shape[0])], axis=1)
    out[...] = done.astype(bf16).reshape(out.shape)


def unpack_kernel(packed, out, local, sems):
    count, rows, cols, chans = out.shape
    lines = count * rows
    regions = packed.shape[0]
    own = cols // regions
    wide = packed[...].astype(f32).reshape(regions, lines, own, chans)
    copies = []
    for at in range(lines):
        place = (at // rows, at % rows)
        local[place] = wide[:, at].reshape(cols, chans).astype(bf16)
        copy = pltpu.make_async_copy(local.at[place], out.at[place], sems.at[at])
        copy.start()
        copies.append(copy)
    for copy in copies:
        copy.wait()


def exchanged(blocks):
    return lax.all_to_all(blocks, "tm", split_axis=0, concat_axis=0, tiled=True)


def per_device(outer, video, block_ids, conv_weight, w_query, w_key, w_value, w_output):
    count, rows, cols, chans = video.shape
    group = lax.axis_size("tm")
    own = cols // group
    span = own + 2
    lines = count * rows
    near = pl.BlockSpec(memory_space=pltpu.VMEM)
    far = pl.BlockSpec(memory_space=pltpu.HBM)
    params = pltpu.CompilerParams(vmem_limit_bytes=VMEM)
    in_far = functools.partial(pltpu.with_memory_space_constraint, memory_space=pltpu.HBM)
    weights = [in_far(x) for x in (w_query, w_key, w_value, w_output)]
    conv_weight = lax.ppermute(conv_weight, "height", [(0, 1), (1, 0)])

    blocks = pl.pallas_call(
        functools.partial(pack_kernel, group),
        out_shape=jax.ShapeDtypeStruct((group, span * lines, chans), bf16),
        in_specs=[far],
        out_specs=near,
        scratch_shapes=[
            pltpu.VMEM(video.shape, bf16),
            scratch(lines * (cols + 2 * EDGE), chans),
            pltpu.SemaphoreType.DMA((lines,)),
        ],
        compiler_params=params,
    )(in_far(video))
    piece = exchanged(blocks)
    ids = block_ids
    if outer > 1:
        before = lax.ppermute(piece, "outer", [(i, i + 1) for i in range(outer - 1)])
        piece = jnp.concatenate([before, piece], axis=0)
        ids = jnp.concatenate([jnp.full((group * count,), -2, jnp.int32), ids])
        ids = lax.dynamic_slice(ids, (lax.axis_index("outer") * group * count,), (2 * group * count,))
    sources = piece.shape[0]
    frames = sources * count
    stored = scratch(sources * span * lines, chans)
    edge = pl.pallas_call(
        functools.partial(edge_kernel, count, rows),
        out_shape=jax.ShapeDtypeStruct((span, frames, chans), bf16),
        in_specs=[near],
        out_specs=near,
        scratch_shapes=[stored],
        compiler_params=params,
    )(piece)
    edge = lax.ppermute(edge, "height", [(0, 1), (1, 0)])
    fitting = [n for n in range(2, own // 2 + 1) if own // 2 % n == 0 and own % n == 0 and n * rows * frames <= LANES]
    several = max([1] + fitting)
    area = several * rows * frames
    grid, total, bias, *weights = pl.pallas_call(
        functools.partial(shift_kernel, count, rows),
        out_shape=[
            jax.ShapeDtypeStruct((span, rows, frames, TAPS * chans), bf16),
            jax.ShapeDtypeStruct((own, rows, frames, chans), f32),
            jax.ShapeDtypeStruct((area, area), f32),
        ]
        + [jax.ShapeDtypeStruct(x.shape, bf16) for x in weights],
        in_specs=[near, far, near] + [far] * 4,
        out_specs=[near] * 7,
        scratch_shapes=[
            stored,
            pltpu.SMEM((frames,), jnp.int32),
            pltpu.SemaphoreType.DMA((4,)),
            pltpu.SemaphoreType.DMA(()),
        ],
        compiler_params=params,
    )(piece, in_far(ids), conv_weight, *weights)
    blocks = pl.pallas_call(
        functools.partial(main_kernel, count, rows, group),
        out_shape=jax.ShapeDtypeStruct((group, own * lines, chans), bf16),
        in_specs=[near] * 9,
        out_specs=near,
        scratch_shapes=[
            scratch(group * own * lines, chans),
            pltpu.VMEM((own // 2, rows, frames, chans), f32),
        ],
        compiler_params=params,
    )(edge, grid, total, bias, conv_weight, *weights)
    return pl.pallas_call(
        unpack_kernel,
        out_shape=jax.ShapeDtypeStruct(video.shape, bf16),
        in_specs=[near],
        out_specs=far,
        scratch_shapes=[
            pltpu.VMEM(video.shape, bf16),
            pltpu.SemaphoreType.DMA((lines,)),
        ],
        compiler_params=params,
    )(exchanged(blocks))


def solution(mesh):
    parts, along, halves = (mesh.shape[a] for a in ("groups", "tm", "height"))

    def run(video, *rest):
        count = video.shape[0] // (parts * along)
        group = min(g for g in range(1, along + 1) if along % g == 0 and (g * count >= REACH or g == along))
        outer = along // group
        split = Mesh(
            np.asarray(mesh.devices).reshape(parts, outer, group, halves),
            ("groups", "outer", "tm", "height"),
        )
        spec = P(("groups", "outer", "tm"), "height", None, None)
        placed = (spec, P("groups"), P(), P(), P(), P(), P())
        return jax.shard_map(
            functools.partial(per_device, outer),
            mesh=split,
            in_specs=placed,
            out_specs=spec,
            check_vma=False,
        )(video, *rest)

    return run
```

```python
import functools

import jax
import jax.numpy as jnp
import numpy as np
from jax import lax
from jax.experimental import pallas as pl
from jax.experimental.pallas import tpu as pltpu
from jax.sharding import Mesh, PartitionSpec as P

HD = 64
BLOCK = 4
TAPS = 3
REACH = 2 * BLOCK - 1 + TAPS - 1
LANES = 128
EDGE = 8
VMEM = 28 * 2**20

bf16, f32 = jnp.bfloat16, jnp.float32


def get(ref, start, size, stride):
    return jnp.concatenate([ref[i, pl.ds(start, size, stride=stride), :] for i in range(ref.shape[0])], axis=1)


def put(ref, start, size, stride, value):
    for i in range(ref.shape[0]):
        ref[i, pl.ds(start, size, stride=stride), :] = value[:, i * LANES : (i + 1) * LANES]


def fill(ref, start, value):
    for i in range(ref.shape[0]):
        ref[i, pl.ds(start, value.shape[0]), :] = value[:, i * LANES : (i + 1) * LANES]


def scratch(rows, chans):
    return pltpu.VMEM((chans // LANES, rows, LANES), f32)


def rms(wide):
    return wide * lax.rsqrt(jnp.mean(wide * wide, axis=-1, keepdims=True) + 1e-06)


def divided(at, by):
    if by & (by - 1) == 0:
        bits = by.bit_length() - 1
        return at >> bits, at & (by - 1)
    return lax.div(at, jnp.int32(by)), lax.rem(at, jnp.int32(by))


def fill_bias(bias, ids, frames, count):
    area = bias.shape[0]
    sources = frames // count

    def place_of(at):
        pixel, place = divided(at, frames)
        inner, source = divided(place, sources)
        frame = source * count + inner
        block = jnp.zeros(at.shape, jnp.int32)
        for s in range(frames):
            block = jnp.where(frame == s, ids[s], block)
        return pixel, frame, block

    row_p, row_t, row_b = place_of(lax.broadcasted_iota(jnp.int32, (area, area), 0))
    col_p, col_t, col_b = place_of(lax.broadcasted_iota(jnp.int32, (1, area), 1))
    permit = (row_p == col_p) & (col_t <= row_t) & (col_b >= row_b - 1)
    bias[...] = jnp.where(permit, 0.0, -1e30)


def pack_kernel(group, ids_far, video, *refs):
    out, bias, ids, local, wide, sems, ids_sem = refs
    ids_copy = pltpu.make_async_copy(ids_far, ids, ids_sem)
    ids_copy.start()
    count, rows, cols, chans = video.shape
    lines = count * rows
    stride = cols + 2 * EDGE
    own = cols // group
    span = own + 2
    copies = []
    for at in range(lines):
        place = (at // rows, at % rows)
        copy = pltpu.make_async_copy(video.at[place], local.at[place], sems.at[at])
        copy.start()
        copies.append(copy)
    nothing = jnp.zeros((EDGE, chans), f32)
    for at in range(lines):
        fill(wide, at * stride, nothing)
        fill(wide, at * stride + EDGE + cols, nothing)
    ids_copy.wait()
    fill_bias(bias, ids, ids.shape[0], count)
    for at, copy in enumerate(copies):
        copy.wait()
        fill(wide, at * stride + EDGE, local[at // rows, at % rows].astype(f32))
    together = 16 // lines
    for k in range(group):
        start = k * own + EDGE - 1
        for w in range(0, span, together):
            tile = jnp.concatenate([get(wide, start + w + i, lines, stride) for i in range(together)], axis=0)
            out[k, pl.ds(w * lines, 16), :] = tile.astype(bf16)


def frames_of(ref, w, r, count, rows, sources, step):
    return [get(ref, w * count * rows + t * rows + r, sources, step) for t in range(count)]


def shifted(now):
    count = len(now)
    sources, chans = now[0].shape
    first = lax.broadcasted_iota(jnp.int32, (sources, chans), 0) == 0
    past = [jnp.where(first, 0.0, pltpu.roll(x, 1, 0)) for x in now]
    ordered = past + now
    taps = []
    for a in range(TAPS):
        start = count - (TAPS - 1 - a)
        taps.append(jnp.concatenate(ordered[start : start + count], 0).astype(bf16))
    return jnp.concatenate(taps, axis=1)


def activated(wide):
    part = 0.5 * rms(wide)
    return part + part * jnp.tanh(part)


def depth(parts):
    return parts[0] if len(parts) == 1 else jnp.concatenate(parts, axis=-1)


def edge_kernel(count, rows, video, edge, vid):
    sources, step, chans = video.shape
    span = step // (count * rows)
    fill(vid, 0, video[...].reshape(sources * step, chans).astype(f32))
    row = (rows - 1) * (1 - lax.axis_index("height"))
    for w in range(span):
        edge[w] = shifted([activated(x) for x in frames_of(vid, w, row, count, rows, sources, step)])


def shift_kernel(count, rows, video, *refs):
    conv_weight, far, (total, *near), (vid, grid, sems) = refs[0], refs[1:5], refs[5:10], refs[10:]
    others = [pltpu.make_async_copy(src, dst, sems.at[i]) for i, (src, dst) in enumerate(zip(far, near))]
    for copy in others:
        copy.start()
    sources, step, chans = video.shape
    span = step // (count * rows)
    own = span - 2
    frames = sources * count
    half = own // 2 if own % 2 == 0 else own
    fill(vid, 0, video[...].reshape(sources * step, chans).astype(f32))
    for w in range(span):
        for r in range(rows):
            now = frames_of(vid, w, r, count, rows, sources, step)
            grid[w, r] = shifted([activated(x) for x in now])
            if 1 <= w <= own:
                total[w - 1, r] = jnp.concatenate(now, 0)

    for b in range(TAPS):
        low, high = max(0, 1 - b), min(rows, rows + 1 - b)
        weight = jnp.concatenate([conv_weight[a, b, e] for e in range(TAPS) for a in range(TAPS)], axis=0)
        for w in range(0, own, half):
            window = depth([grid[w + e : w + e + half, low + b - 1 : high + b - 1] for e in range(TAPS)])
            window = window.reshape(half * (high - low) * frames, TAPS * TAPS * chans)
            part = jnp.dot(window, weight, preferred_element_type=f32)
            some = total.at[w : w + half, low:high]
            some[...] = some[...] + part.reshape(half, high - low, frames, chans)
    for copy in others:
        copy.wait()


def main_kernel(
    count, rows, group, edge, given, bias, conv_weight, w_query, w_key, w_value, w_output, *refs
):
    out, res = refs
    own, _, frames, chans = given.shape
    sources = frames // count
    lines = count * rows
    heads = chans // HD
    back = own * lines
    area = bias.shape[0]
    several = area // (rows * frames)

    lower = lax.axis_index("height")
    b = (TAPS - 1) * (1 - lower)
    part = jnp.zeros((own * frames, chans), f32)
    for e in range(TAPS):
        window = edge[e : e + own].reshape(own * frames, TAPS * chans)
        weight = jnp.concatenate([conv_weight[a, b, e] for a in range(TAPS)], axis=0)
        part = part + jnp.dot(window, weight, preferred_element_type=f32)
    part = part.reshape(own, frames, chans)

    head_of = divided(lax.broadcasted_iota(jnp.int32, (area, chans), 1), HD)[0]
    single = [jnp.where(head_of == h, 1.0, 0.0).astype(bf16) for h in range(heads)]
    heads_lanes = jnp.concatenate(single, axis=0)
    scaled = [mask * jnp.asarray(HD ** (-0.5), bf16) for mask in single]

    lines_of = []
    for r in range(rows):
        row = given[:, r] + jnp.where(r == (rows - 1) * (1 - lower), part, 0.0)
        lines_of.append(row[:, None])
    hidden = jnp.concatenate(lines_of, axis=1).reshape(own * rows * frames, chans).astype(bf16).astype(f32)
    normed = rms(hidden).astype(bf16)
    query, keys, values = (
        jnp.dot(normed, weight[...], preferred_element_type=f32).astype(bf16) for weight in (w_query, w_key, w_value)
    )
    half = own // 2 if own % (2 * several) == 0 else own
    for start in range(0, own, half):
        gone = []
        for at in range(start * rows * frames, (start + half) * rows * frames, area):
            group_of = slice(at, at + area)
            queries = jnp.concatenate([query[group_of] * mask for mask in scaled], axis=0)
            scores = lax.dot_general(
                queries, keys[group_of], (((1,), (1,)), ((), ())), preferred_element_type=f32
            )
            weights = []
            for h in range(heads):
                score = scores[h * area : (h + 1) * area] + bias[...]
                weights.append(jnp.exp(score - jnp.max(score, axis=-1, keepdims=True)).astype(bf16))
            weights = jnp.concatenate(weights, axis=1)
            heads_values = jnp.concatenate([values[group_of] * mask for mask in single], axis=0)
            attended = jnp.dot(weights, heads_values, preferred_element_type=f32)
            under = jnp.dot(weights, heads_lanes, preferred_element_type=f32)
            gone.append((attended / under).astype(bf16))
        attended = jnp.concatenate(gone, axis=0)
        encoded = hidden[start * rows * frames : (start + half) * rows * frames] + jnp.dot(
            attended, w_output[...], preferred_element_type=f32
        )
        for w in range(half):
            for r in range(rows):
                for t in range(count):
                    first = ((w * rows + r) * count + t + 1) * sources - group
                    place = (t * rows + r) * own + start + w
                    put(res, place, group, back, encoded[first : first + group])
    done = jnp.concatenate([res[i] for i in range(res.shape[0])], axis=1)
    out[...] = done.astype(bf16).reshape(out.shape)


def unpack_kernel(packed, out, local, sems):
    count, rows, cols, chans = out.shape
    lines = count * rows
    regions = packed.shape[0]
    own = cols // regions
    wide = packed[...].astype(f32).reshape(regions, lines, own, chans)
    copies = []
    for at in range(lines):
        place = (at // rows, at % rows)
        local[place] = wide[:, at].reshape(cols, chans).astype(bf16)
        copy = pltpu.make_async_copy(local.at[place], out.at[place], sems.at[at])
        copy.start()
        copies.append(copy)
    for copy in copies:
        copy.wait()


def exchanged(blocks):
    return lax.all_to_all(blocks, "tm", split_axis=0, concat_axis=0, tiled=True)


def per_device(outer, video, block_ids, conv_weight, w_query, w_key, w_value, w_output):
    count, rows, cols, chans = video.shape
    group = lax.axis_size("tm")
    own = cols // group
    span = own + 2
    lines = count * rows
    near = pl.BlockSpec(memory_space=pltpu.VMEM)
    far = pl.BlockSpec(memory_space=pltpu.HBM)
    params = pltpu.CompilerParams(vmem_limit_bytes=VMEM)
    in_far = functools.partial(pltpu.with_memory_space_constraint, memory_space=pltpu.HBM)
    weights = [in_far(x) for x in (w_query, w_key, w_value, w_output)]
    conv_weight = lax.ppermute(conv_weight, "height", [(0, 1), (1, 0)])

    ids = block_ids
    sources = group * (2 if outer > 1 else 1)
    frames = sources * count
    if outer > 1:
        ids = jnp.concatenate([jnp.full((group * count,), -2, jnp.int32), ids])
        ids = lax.dynamic_slice(ids, (lax.axis_index("outer") * group * count,), (frames,))
    fitting = [n for n in range(2, own + 1) if own % n == 0 and n * rows * frames <= LANES]
    area = max([1] + fitting) * rows * frames
    blocks, bias = pl.pallas_call(
        functools.partial(pack_kernel, group),
        out_shape=[
            jax.ShapeDtypeStruct((group, span * lines, chans), bf16),
            jax.ShapeDtypeStruct((area, area), f32),
        ],
        in_specs=[far, far],
        out_specs=[near, near],
        scratch_shapes=[
            pltpu.SMEM((frames,), jnp.int32),
            pltpu.VMEM(video.shape, bf16),
            scratch(lines * (cols + 2 * EDGE), chans),
            pltpu.SemaphoreType.DMA((lines,)),
            pltpu.SemaphoreType.DMA(()),
        ],
        compiler_params=params,
    )(in_far(ids), in_far(video))
    piece = exchanged(blocks)
    if outer > 1:
        before = lax.ppermute(piece, "outer", [(i, i + 1) for i in range(outer - 1)])
        piece = jnp.concatenate([before, piece], axis=0)
    stored = scratch(sources * span * lines, chans)
    edge = pl.pallas_call(
        functools.partial(edge_kernel, count, rows),
        out_shape=jax.ShapeDtypeStruct((span, frames, TAPS * chans), bf16),
        in_specs=[near],
        out_specs=near,
        scratch_shapes=[stored],
        compiler_params=params,
    )(piece)
    edge = lax.ppermute(edge, "height", [(0, 1), (1, 0)])
    total, *weights = pl.pallas_call(
        functools.partial(shift_kernel, count, rows),
        out_shape=[jax.ShapeDtypeStruct((own, rows, frames, chans), f32)]
        + [jax.ShapeDtypeStruct(x.shape, bf16) for x in weights],
        in_specs=[near, near] + [far] * 4,
        out_specs=[near] * 5,
        scratch_shapes=[
            stored,
            pltpu.VMEM((span, rows, frames, TAPS * chans), bf16),
            pltpu.SemaphoreType.DMA((4,)),
        ],
        compiler_params=params,
    )(piece, conv_weight, *weights)
    blocks = pl.pallas_call(
        functools.partial(main_kernel, count, rows, group),
        out_shape=jax.ShapeDtypeStruct((group, own * lines, chans), bf16),
        in_specs=[near] * 8,
        out_specs=near,
        scratch_shapes=[scratch(group * own * lines, chans)],
        compiler_params=params,
    )(edge, total, bias, conv_weight, *weights)
    return pl.pallas_call(
        unpack_kernel,
        out_shape=jax.ShapeDtypeStruct(video.shape, bf16),
        in_specs=[near],
        out_specs=far,
        scratch_shapes=[
            pltpu.VMEM(video.shape, bf16),
            pltpu.SemaphoreType.DMA((lines,)),
        ],
        compiler_params=params,
    )(exchanged(blocks))


def solution(mesh):
    parts, along, halves = (mesh.shape[a] for a in ("groups", "tm", "height"))

    def run(video, *rest):
        count = video.shape[0] // (parts * along)
        group = min(g for g in range(1, along + 1) if along % g == 0 and (g * count >= REACH or g == along))
        outer = along // group
        split = Mesh(
            np.asarray(mesh.devices).reshape(parts, outer, group, halves),
            ("groups", "outer", "tm", "height"),
        )
        spec = P(("groups", "outer", "tm"), "height", None, None)
        placed = (spec, P("groups"), P(), P(), P(), P(), P())
        return jax.shard_map(
            functools.partial(per_device, outer),
            mesh=split,
            in_specs=placed,
            out_specs=spec,
            check_vma=False,
        )(video, *rest)

    return run
```

```python
import functools

import jax
import jax.numpy as jnp
import numpy as np
from jax import lax
from jax.experimental import pallas as pl
from jax.experimental.pallas import tpu as pltpu
from jax.sharding import Mesh, PartitionSpec as P

HD = 64
BLOCK = 4
TAPS = 3
REACH = 2 * BLOCK - 1 + TAPS - 1
LANES = 128
EDGE = 8
VMEM = 28 * 2**20

bf16, f32 = jnp.bfloat16, jnp.float32


def get(ref, start, size, stride):
    return jnp.concatenate([ref[i, pl.ds(start, size, stride=stride), :] for i in range(ref.shape[0])], axis=1)


def put(ref, start, size, stride, value):
    for i in range(ref.shape[0]):
        ref[i, pl.ds(start, size, stride=stride), :] = value[:, i * LANES : (i + 1) * LANES]


def fill(ref, start, value):
    for i in range(ref.shape[0]):
        ref[i, pl.ds(start, value.shape[0]), :] = value[:, i * LANES : (i + 1) * LANES]


def scratch(rows, chans):
    return pltpu.VMEM((chans // LANES, rows, LANES), f32)


def rms(wide):
    return wide * lax.rsqrt(jnp.mean(wide * wide, axis=-1, keepdims=True) + 1e-06)


def divided(at, by):
    if by & (by - 1) == 0:
        bits = by.bit_length() - 1
        return at >> bits, at & (by - 1)
    return lax.div(at, jnp.int32(by)), lax.rem(at, jnp.int32(by))


def pack_kernel(group, video, *refs):
    out, local, wide, sems = refs
    count, rows, cols, chans = video.shape
    lines = count * rows
    stride = cols + 2 * EDGE
    own = cols // group
    span = own + 2
    copies = []
    for at in range(lines):
        place = (at // rows, at % rows)
        copy = pltpu.make_async_copy(video.at[place], local.at[place], sems.at[at])
        copy.start()
        copies.append(copy)
    nothing = jnp.zeros((EDGE, chans), f32)
    for at in range(lines):
        fill(wide, at * stride, nothing)
        fill(wide, at * stride + EDGE + cols, nothing)
    for at, copy in enumerate(copies):
        copy.wait()
        fill(wide, at * stride + EDGE, local[at // rows, at % rows].astype(f32))
    together = 16 // lines
    for k in range(group):
        start = k * own + EDGE - 1
        for w in range(0, span, together):
            tile = jnp.concatenate([get(wide, start + w + i, lines, stride) for i in range(together)], axis=0)
            out[k, pl.ds(w * lines, 16), :] = tile.astype(bf16)


def frames_of(ref, w, r, count, rows, sources, step):
    return [get(ref, w * count * rows + t * rows + r, sources, step) for t in range(count)]


def shifted(now):
    count = len(now)
    sources, chans = now[0].shape
    first = lax.broadcasted_iota(jnp.int32, (sources, chans), 0) == 0
    past = [jnp.where(first, 0.0, pltpu.roll(x, 1, 0)) for x in now]
    ordered = past + now
    taps = []
    for a in range(TAPS):
        start = count - (TAPS - 1 - a)
        taps.append(jnp.concatenate(ordered[start : start + count], 0).astype(bf16))
    return jnp.concatenate(taps, axis=1)


def activated(wide):
    part = 0.5 * rms(wide)
    return part + part * jnp.tanh(part)


def depth(parts):
    return parts[0] if len(parts) == 1 else jnp.concatenate(parts, axis=-1)


def edge_kernel(count, rows, video, edge, vid):
    sources, step, chans = video.shape
    span = step // (count * rows)
    fill(vid, 0, video[...].reshape(sources * step, chans).astype(f32))
    row = (rows - 1) * (1 - lax.axis_index("height"))
    for w in range(span):
        edge[w] = shifted([activated(x) for x in frames_of(vid, w, row, count, rows, sources, step)])


def fill_bias(bias, ids, frames, count):
    area = bias.shape[0]
    sources = frames // count

    def place_of(at):
        pixel, place = divided(at, frames)
        inner, source = divided(place, sources)
        frame = source * count + inner
        block = jnp.zeros(at.shape, jnp.int32)
        for s in range(frames):
            block = jnp.where(frame == s, ids[s], block)
        return pixel, frame, block

    row_p, row_t, row_b = place_of(lax.broadcasted_iota(jnp.int32, (area, area), 0))
    col_p, col_t, col_b = place_of(lax.broadcasted_iota(jnp.int32, (1, area), 1))
    permit = (row_p == col_p) & (col_t <= row_t) & (col_b >= row_b - 1)
    bias[...] = jnp.where(permit, 0.0, -1e30)


def shift_kernel(count, rows, video, ids_far, *refs):
    conv_weight, far, (total, bias, *near) = refs[0], refs[1:5], refs[5:11]
    vid, grid, ids, sems, ids_sem = refs[11:]
    ids_copy = pltpu.make_async_copy(ids_far, ids, ids_sem)
    ids_copy.start()
    others = [pltpu.make_async_copy(src, dst, sems.at[i]) for i, (src, dst) in enumerate(zip(far, near))]
    for copy in others:
        copy.start()
    sources, step, chans = video.shape
    span = step // (count * rows)
    own = span - 2
    frames = sources * count
    half = own // 2 if own % 2 == 0 else own
    fill(vid, 0, video[...].reshape(sources * step, chans).astype(f32))
    for w in range(span):
        for r in range(rows):
            now = frames_of(vid, w, r, count, rows, sources, step)
            grid[w, r] = shifted([activated(x) for x in now])
            if 1 <= w <= own:
                total[w - 1, r] = jnp.concatenate(now, 0)

    for b in range(TAPS):
        low, high = max(0, 1 - b), min(rows, rows + 1 - b)
        weight = jnp.concatenate([conv_weight[a, b, e] for e in range(TAPS) for a in range(TAPS)], axis=0)
        for w in range(0, own, half):
            window = depth([grid[w + e : w + e + half, low + b - 1 : high + b - 1] for e in range(TAPS)])
            window = window.reshape(half * (high - low) * frames, TAPS * TAPS * chans)
            part = jnp.dot(window, weight, preferred_element_type=f32)
            some = total.at[w : w + half, low:high]
            some[...] = some[...] + part.reshape(half, high - low, frames, chans)
    ids_copy.wait()
    fill_bias(bias, ids, frames, count)
    for copy in others:
        copy.wait()


def main_kernel(
    count, rows, group, edge, given, bias, conv_weight, w_query, w_key, w_value, w_output, *refs
):
    out, res = refs
    own, _, frames, chans = given.shape
    sources = frames // count
    lines = count * rows
    heads = chans // HD
    back = own * lines
    area = bias.shape[0]
    several = area // (rows * frames)

    lower = lax.axis_index("height")
    b = (TAPS - 1) * (1 - lower)
    part = jnp.zeros((own * frames, chans), f32)
    for e in range(TAPS):
        window = edge[e : e + own].reshape(own * frames, TAPS * chans)
        weight = jnp.concatenate([conv_weight[a, b, e] for a in range(TAPS)], axis=0)
        part = part + jnp.dot(window, weight, preferred_element_type=f32)
    part = part.reshape(own, frames, chans)

    head_of = divided(lax.broadcasted_iota(jnp.int32, (area, chans), 1), HD)[0]
    single = [jnp.where(head_of == h, 1.0, 0.0).astype(bf16) for h in range(heads)]
    scaled = [mask * jnp.asarray(HD ** (-0.5), bf16) for mask in single]

    lines_of = []
    for r in range(rows):
        row = given[:, r] + jnp.where(r == (rows - 1) * (1 - lower), part, 0.0)
        lines_of.append(row[:, None])
    hidden = jnp.concatenate(lines_of, axis=1).reshape(own * rows * frames, chans).astype(bf16).astype(f32)
    normed = rms(hidden).astype(bf16)
    query, keys, values = (
        jnp.dot(normed, weight[...], preferred_element_type=f32).astype(bf16) for weight in (w_query, w_key, w_value)
    )
    half = own // 2 if own % (2 * several) == 0 else own
    for start in range(0, own, half):
        gone = []
        for at in range(start * rows * frames, (start + half) * rows * frames, area):
            group_of = slice(at, at + area)
            queries = jnp.concatenate([query[group_of] * mask for mask in scaled], axis=0)
            scores = lax.dot_general(
                queries, keys[group_of], (((1,), (1,)), ((), ())), preferred_element_type=f32
            )
            weights, under = [], jnp.zeros((area, chans), f32)
            for h in range(heads):
                score = scores[h * area : (h + 1) * area] + bias[...]
                expo = jnp.exp(score - jnp.max(score, axis=-1, keepdims=True))
                under = jnp.where(head_of == h, jnp.sum(expo, axis=-1, keepdims=True), under)
                weights.append(expo.astype(bf16))
            heads_values = jnp.concatenate([values[group_of] * mask for mask in single], axis=0)
            attended = jnp.dot(jnp.concatenate(weights, axis=1), heads_values, preferred_element_type=f32)
            gone.append((attended / under).astype(bf16))
        attended = jnp.concatenate(gone, axis=0)
        encoded = hidden[start * rows * frames : (start + half) * rows * frames] + jnp.dot(
            attended, w_output[...], preferred_element_type=f32
        )
        for w in range(half):
            for r in range(rows):
                for t in range(count):
                    first = ((w * rows + r) * count + t + 1) * sources - group
                    place = (t * rows + r) * own + start + w
                    put(res, place, group, back, encoded[first : first + group])
    done = jnp.concatenate([res[i] for i in range(res.shape[0])], axis=1)
    out[...] = done.astype(bf16).reshape(out.shape)


def unpack_kernel(packed, out, local, sems):
    count, rows, cols, chans = out.shape
    lines = count * rows
    regions = packed.shape[0]
    own = cols // regions
    wide = packed[...].astype(f32).reshape(regions, lines, own, chans)
    copies = []
    for at in range(lines):
        place = (at // rows, at % rows)
        local[place] = wide[:, at].reshape(cols, chans).astype(bf16)
        copy = pltpu.make_async_copy(local.at[place], out.at[place], sems.at[at])
        copy.start()
        copies.append(copy)
    for copy in copies:
        copy.wait()


def exchanged(blocks):
    return lax.all_to_all(blocks, "tm", split_axis=0, concat_axis=0, tiled=True)


def per_device(outer, video, block_ids, conv_weight, w_query, w_key, w_value, w_output):
    count, rows, cols, chans = video.shape
    group = lax.axis_size("tm")
    own = cols // group
    span = own + 2
    lines = count * rows
    near = pl.BlockSpec(memory_space=pltpu.VMEM)
    far = pl.BlockSpec(memory_space=pltpu.HBM)
    params = pltpu.CompilerParams(vmem_limit_bytes=VMEM)
    in_far = functools.partial(pltpu.with_memory_space_constraint, memory_space=pltpu.HBM)
    weights = [in_far(x) for x in (w_query, w_key, w_value, w_output)]

    blocks = pl.pallas_call(
        functools.partial(pack_kernel, group),
        out_shape=jax.ShapeDtypeStruct((group, span * lines, chans), bf16),
        in_specs=[far],
        out_specs=near,
        scratch_shapes=[
            pltpu.VMEM(video.shape, bf16),
            scratch(lines * (cols + 2 * EDGE), chans),
            pltpu.SemaphoreType.DMA((lines,)),
        ],
        compiler_params=params,
        cost_estimate=pl.CostEstimate(flops=2000000000, transcendentals=0, bytes_accessed=1000000),
    )(in_far(video))
    piece = exchanged(blocks)
    ids = block_ids
    if outer > 1:
        before = lax.ppermute(piece, "outer", [(i, i + 1) for i in range(outer - 1)])
        piece = jnp.concatenate([before, piece], axis=0)
        ids = jnp.concatenate([jnp.full((group * count,), -2, jnp.int32), ids])
        ids = lax.dynamic_slice(ids, (lax.axis_index("outer") * group * count,), (2 * group * count,))
    sources = piece.shape[0]
    frames = sources * count
    stored = scratch(sources * span * lines, chans)
    edge = pl.pallas_call(
        functools.partial(edge_kernel, count, rows),
        out_shape=jax.ShapeDtypeStruct((span, frames, TAPS * chans), bf16),
        in_specs=[near],
        out_specs=near,
        scratch_shapes=[stored],
        compiler_params=params,
    )(piece)
    edge = lax.ppermute(edge, "height", [(0, 1), (1, 0)])
    several = max(n for n in range(1, own + 1) if own % n == 0 and (n == 1 or n * rows * frames <= LANES))
    area = several * rows * frames
    total, bias, *weights = pl.pallas_call(
        functools.partial(shift_kernel, count, rows),
        out_shape=[
            jax.ShapeDtypeStruct((own, rows, frames, chans), f32),
            jax.ShapeDtypeStruct((area, area), f32),
        ]
        + [jax.ShapeDtypeStruct(x.shape, bf16) for x in weights],
        in_specs=[near, far, near] + [far] * 4,
        out_specs=[near] * 6,
        scratch_shapes=[
            stored,
            pltpu.VMEM((span, rows, frames, TAPS * chans), bf16),
            pltpu.SMEM((frames,), jnp.int32),
            pltpu.SemaphoreType.DMA((4,)),
            pltpu.SemaphoreType.DMA(()),
        ],
        compiler_params=params,
    )(piece, in_far(ids), conv_weight, *weights)
    blocks = pl.pallas_call(
        functools.partial(main_kernel, count, rows, group),
        out_shape=jax.ShapeDtypeStruct((group, own * lines, chans), bf16),
        in_specs=[near] * 8,
        out_specs=near,
        scratch_shapes=[scratch(group * own * lines, chans)],
        compiler_params=params,
    )(edge, total, bias, conv_weight, *weights)
    return pl.pallas_call(
        unpack_kernel,
        out_shape=jax.ShapeDtypeStruct(video.shape, bf16),
        in_specs=[near],
        out_specs=far,
        scratch_shapes=[
            pltpu.VMEM(video.shape, bf16),
            pltpu.SemaphoreType.DMA((lines,)),
        ],
        compiler_params=params,
    )(exchanged(blocks))


def solution(mesh):
    parts, along, halves = (mesh.shape[a] for a in ("groups", "tm", "height"))

    def run(video, *rest):
        count = video.shape[0] // (parts * along)
        group = min(g for g in range(1, along + 1) if along % g == 0 and (g * count >= REACH or g == along))
        outer = along // group
        split = Mesh(
            np.asarray(mesh.devices).reshape(parts, outer, group, halves),
            ("groups", "outer", "tm", "height"),
        )
        spec = P(("groups", "outer", "tm"), "height", None, None)
        placed = (spec, P("groups"), P(), P(), P(), P(), P())
        return jax.shard_map(
            functools.partial(per_device, outer),
            mesh=split,
            in_specs=placed,
            out_specs=spec,
            check_vma=False,
        )(video, *rest)

    return run
```

```python
import functools

import jax
import jax.numpy as jnp
import numpy as np
from jax import lax
from jax.experimental import pallas as pl
from jax.experimental.pallas import tpu as pltpu
from jax.sharding import Mesh, PartitionSpec as P

HD = 64
BLOCK = 4
TAPS = 3
REACH = 2 * BLOCK - 1 + TAPS - 1
LANES = 128
EDGE = 8
VMEM = 28 * 2**20

bf16, f32 = jnp.bfloat16, jnp.float32


def get(ref, start, size, stride):
    return jnp.concatenate([ref[i, pl.ds(start, size, stride=stride), :] for i in range(ref.shape[0])], axis=1)


def put(ref, start, size, stride, value):
    for i in range(ref.shape[0]):
        ref[i, pl.ds(start, size, stride=stride), :] = value[:, i * LANES : (i + 1) * LANES]


def fill(ref, start, value):
    for i in range(ref.shape[0]):
        ref[i, pl.ds(start, value.shape[0]), :] = value[:, i * LANES : (i + 1) * LANES]


def scratch(rows, chans):
    return pltpu.VMEM((chans // LANES, rows, LANES), f32)


def rms(wide):
    return wide * lax.rsqrt(jnp.mean(wide * wide, axis=-1, keepdims=True) + 1e-06)


def divided(at, by):
    if by & (by - 1) == 0:
        bits = by.bit_length() - 1
        return at >> bits, at & (by - 1)
    return lax.div(at, jnp.int32(by)), lax.rem(at, jnp.int32(by))


def pack_kernel(group, ids_far, video, out, ids, near_ids, local, wide, sems, ids_sem):
    ids_copy = pltpu.make_async_copy(ids_far, near_ids, ids_sem)
    ids_copy.start()
    count, rows, cols, chans = video.shape
    lines = count * rows
    stride = cols + 2 * EDGE
    own = cols // group
    span = own + 2
    copies = []
    for at in range(lines):
        place = (at // rows, at % rows)
        copy = pltpu.make_async_copy(video.at[place], local.at[place], sems.at[at])
        copy.start()
        copies.append(copy)
    nothing = jnp.zeros((EDGE, chans), f32)
    for at in range(lines):
        fill(wide, at * stride, nothing)
        fill(wide, at * stride + EDGE + cols, nothing)
    ids_copy.wait()
    for s in range(ids.shape[0]):
        ids[s : s + 1, :] = jnp.full((1, LANES), near_ids[s], jnp.int32)
    for at, copy in enumerate(copies):
        copy.wait()
        fill(wide, at * stride + EDGE, local[at // rows, at % rows].astype(f32))
    together = 16 // lines
    for k in range(group):
        start = k * own + EDGE - 1
        for w in range(0, span, together):
            tile = jnp.concatenate([get(wide, start + w + i, lines, stride) for i in range(together)], axis=0)
            out[k, pl.ds(w * lines, 16), :] = tile.astype(bf16)


def frames_of(ref, w, r, count, rows, sources, step):
    return [get(ref, w * count * rows + t * rows + r, sources, step) for t in range(count)]


def shifted(now):
    count = len(now)
    sources, chans = now[0].shape
    first = lax.broadcasted_iota(jnp.int32, (sources, chans), 0) == 0
    past = [jnp.where(first, 0.0, pltpu.roll(x, 1, 0)) for x in now]
    ordered = past + now
    taps = []
    for a in range(TAPS):
        start = count - (TAPS - 1 - a)
        taps.append(jnp.concatenate(ordered[start : start + count], 0).astype(bf16))
    return jnp.concatenate(taps, axis=1)


def activated(wide):
    part = 0.5 * rms(wide)
    return part + part * jnp.tanh(part)


def depth(parts):
    return parts[0] if len(parts) == 1 else jnp.concatenate(parts, axis=-1)


def edge_kernel(count, rows, video, edge, vid):
    sources, step, chans = video.shape
    span = step // (count * rows)
    fill(vid, 0, video[...].reshape(sources * step, chans).astype(f32))
    row = (rows - 1) * (1 - lax.axis_index("height"))
    for w in range(span):
        edge[w] = shifted([activated(x) for x in frames_of(vid, w, row, count, rows, sources, step)])


def fill_bias(bias, ids, frames, count):
    area = bias.shape[0]
    sources = frames // count

    def place_of(at):
        pixel, place = divided(at, frames)
        inner, source = divided(place, sources)
        frame = source * count + inner
        block = jnp.zeros(at.shape, jnp.int32)
        for s in range(frames):
            block = jnp.where(frame == s, ids[s : s + 1, :area], block)
        return pixel, frame, block

    row_p, row_t, row_b = place_of(lax.broadcasted_iota(jnp.int32, (area, area), 0))
    col_p, col_t, col_b = place_of(lax.broadcasted_iota(jnp.int32, (1, area), 1))
    permit = (row_p == col_p) & (col_t <= row_t) & (col_b >= row_b - 1)
    bias[...] = jnp.where(permit, 0.0, -1e30)


def shift_kernel(count, rows, video, ids, conv_weight, total, bias, vid, grid):
    sources, step, chans = video.shape
    span = step // (count * rows)
    own = span - 2
    frames = sources * count
    half = own // 2 if own % 2 == 0 else own
    fill(vid, 0, video[...].reshape(sources * step, chans).astype(f32))
    for w in range(span):
        for r in range(rows):
            now = frames_of(vid, w, r, count, rows, sources, step)
            grid[w, r] = shifted([activated(x) for x in now])
            if 1 <= w <= own:
                total[w - 1, r] = jnp.concatenate(now, 0)

    for b in range(TAPS):
        low, high = max(0, 1 - b), min(rows, rows + 1 - b)
        weight = jnp.concatenate([conv_weight[a, b, e] for e in range(TAPS) for a in range(TAPS)], axis=0)
        for w in range(0, own, half):
            window = depth([grid[w + e : w + e + half, low + b - 1 : high + b - 1] for e in range(TAPS)])
            window = window.reshape(half * (high - low) * frames, TAPS * TAPS * chans)
            part = jnp.dot(window, weight, preferred_element_type=f32)
            some = total.at[w : w + half, low:high]
            some[...] = some[...] + part.reshape(half, high - low, frames, chans)
    fill_bias(bias, ids, frames, count)


def main_kernel(
    count, rows, group, edge, given, bias, conv_weight, w_query, w_key, w_value, w_output, *refs
):
    out, res = refs
    own, _, frames, chans = given.shape
    sources = frames // count
    lines = count * rows
    heads = chans // HD
    back = own * lines
    area = bias.shape[0]
    several = area // (rows * frames)

    lower = lax.axis_index("height")
    b = (TAPS - 1) * (1 - lower)
    part = jnp.zeros((own * frames, chans), f32)
    for e in range(TAPS):
        window = edge[e : e + own].reshape(own * frames, TAPS * chans)
        weight = jnp.concatenate([conv_weight[a, b, e] for a in range(TAPS)], axis=0)
        part = part + jnp.dot(window, weight, preferred_element_type=f32)
    part = part.reshape(own, frames, chans)

    head_of = divided(lax.broadcasted_iota(jnp.int32, (area, chans), 1), HD)[0]
    single = [jnp.where(head_of == h, 1.0, 0.0).astype(bf16) for h in range(heads)]
    scaled = [mask * jnp.asarray(HD ** (-0.5), bf16) for mask in single]

    lines_of = []
    for r in range(rows):
        row = given[:, r] + jnp.where(r == (rows - 1) * (1 - lower), part, 0.0)
        lines_of.append(row[:, None])
    hidden = jnp.concatenate(lines_of, axis=1).reshape(own * rows * frames, chans).astype(bf16).astype(f32)
    normed = rms(hidden).astype(bf16)
    query, keys, values = (
        jnp.dot(normed, weight[...], preferred_element_type=f32).astype(bf16) for weight in (w_query, w_key, w_value)
    )
    half = own // 2 if own % (2 * several) == 0 else own
    for start in range(0, own, half):
        gone = []
        for at in range(start * rows * frames, (start + half) * rows * frames, area):
            group_of = slice(at, at + area)
            queries = jnp.concatenate([query[group_of] * mask for mask in scaled], axis=0)
            scores = lax.dot_general(
                queries, keys[group_of], (((1,), (1,)), ((), ())), preferred_element_type=f32
            )
            weights, under = [], jnp.zeros((area, chans), f32)
            for h in range(heads):
                score = scores[h * area : (h + 1) * area] + bias[...]
                expo = jnp.exp(score - jnp.max(score, axis=-1, keepdims=True))
                under = jnp.where(head_of == h, jnp.sum(expo, axis=-1, keepdims=True), under)
                weights.append(expo.astype(bf16))
            heads_values = jnp.concatenate([values[group_of] * mask for mask in single], axis=0)
            attended = jnp.dot(jnp.concatenate(weights, axis=1), heads_values, preferred_element_type=f32)
            gone.append((attended / under).astype(bf16))
        attended = jnp.concatenate(gone, axis=0)
        encoded = hidden[start * rows * frames : (start + half) * rows * frames] + jnp.dot(
            attended, w_output[...], preferred_element_type=f32
        )
        for w in range(half):
            for r in range(rows):
                for t in range(count):
                    first = ((w * rows + r) * count + t + 1) * sources - group
                    place = (t * rows + r) * own + start + w
                    put(res, place, group, back, encoded[first : first + group])
    done = jnp.concatenate([res[i] for i in range(res.shape[0])], axis=1)
    out[...] = done.astype(bf16).reshape(out.shape)


def unpack_kernel(packed, out, local, sems):
    count, rows, cols, chans = out.shape
    lines = count * rows
    regions = packed.shape[0]
    own = cols // regions
    wide = packed[...].astype(f32).reshape(regions, lines, own, chans)
    copies = []
    for at in range(lines):
        place = (at // rows, at % rows)
        local[place] = wide[:, at].reshape(cols, chans).astype(bf16)
        copy = pltpu.make_async_copy(local.at[place], out.at[place], sems.at[at])
        copy.start()
        copies.append(copy)
    for copy in copies:
        copy.wait()


def exchanged(blocks):
    return lax.all_to_all(blocks, "tm", split_axis=0, concat_axis=0, tiled=True)


def per_device(outer, video, block_ids, conv_weight, w_query, w_key, w_value, w_output):
    count, rows, cols, chans = video.shape
    group = lax.axis_size("tm")
    own = cols // group
    span = own + 2
    lines = count * rows
    near = pl.BlockSpec(memory_space=pltpu.VMEM)
    far = pl.BlockSpec(memory_space=pltpu.HBM)
    params = pltpu.CompilerParams(vmem_limit_bytes=VMEM)
    in_far = functools.partial(pltpu.with_memory_space_constraint, memory_space=pltpu.HBM)

    sources = group * (2 if outer > 1 else 1)
    frames = sources * count
    ids = block_ids
    if outer > 1:
        ids = jnp.concatenate([jnp.full((group * count,), -2, jnp.int32), ids])
        ids = lax.dynamic_slice(ids, (lax.axis_index("outer") * group * count,), (frames,))
    blocks, ids = pl.pallas_call(
        functools.partial(pack_kernel, group),
        out_shape=[
            jax.ShapeDtypeStruct((group, span * lines, chans), bf16),
            jax.ShapeDtypeStruct((frames, LANES), jnp.int32),
        ],
        in_specs=[far, far],
        out_specs=[near, near],
        scratch_shapes=[
            pltpu.SMEM((frames,), jnp.int32),
            pltpu.VMEM(video.shape, bf16),
            scratch(lines * (cols + 2 * EDGE), chans),
            pltpu.SemaphoreType.DMA((lines,)),
            pltpu.SemaphoreType.DMA(()),
        ],
        compiler_params=params,
        cost_estimate=pl.CostEstimate(flops=2000000000, transcendentals=0, bytes_accessed=1000000),
    )(in_far(ids), in_far(video))
    piece = exchanged(blocks)
    if outer > 1:
        before = lax.ppermute(piece, "outer", [(i, i + 1) for i in range(outer - 1)])
        piece = jnp.concatenate([before, piece], axis=0)
    stored = scratch(sources * span * lines, chans)
    edge = pl.pallas_call(
        functools.partial(edge_kernel, count, rows),
        out_shape=jax.ShapeDtypeStruct((span, frames, TAPS * chans), bf16),
        in_specs=[near],
        out_specs=near,
        scratch_shapes=[stored],
        compiler_params=params,
    )(piece)
    edge = lax.ppermute(edge, "height", [(0, 1), (1, 0)])
    fitting = [n for n in range(2, own + 1) if own % n == 0 and n * rows * frames <= LANES]
    area = max([1] + fitting) * rows * frames
    total, bias = pl.pallas_call(
        functools.partial(shift_kernel, count, rows),
        out_shape=[
            jax.ShapeDtypeStruct((own, rows, frames, chans), f32),
            jax.ShapeDtypeStruct((area, area), f32),
        ],
        in_specs=[near] * 3,
        out_specs=[near] * 2,
        scratch_shapes=[stored, pltpu.VMEM((span, rows, frames, TAPS * chans), bf16)],
        compiler_params=params,
    )(piece, ids, conv_weight)
    blocks = pl.pallas_call(
        functools.partial(main_kernel, count, rows, group),
        out_shape=jax.ShapeDtypeStruct((group, own * lines, chans), bf16),
        in_specs=[near] * 8,
        out_specs=near,
        scratch_shapes=[scratch(group * own * lines, chans)],
        compiler_params=params,
    )(edge, total, bias, conv_weight, w_query, w_key, w_value, w_output)
    return pl.pallas_call(
        unpack_kernel,
        out_shape=jax.ShapeDtypeStruct(video.shape, bf16),
        in_specs=[near],
        out_specs=far,
        scratch_shapes=[
            pltpu.VMEM(video.shape, bf16),
            pltpu.SemaphoreType.DMA((lines,)),
        ],
        compiler_params=params,
    )(exchanged(blocks))


def solution(mesh):
    parts, along, halves = (mesh.shape[a] for a in ("groups", "tm", "height"))

    def run(video, *rest):
        count = video.shape[0] // (parts * along)
        group = min(g for g in range(1, along + 1) if along % g == 0 and (g * count >= REACH or g == along))
        outer = along // group
        split = Mesh(
            np.asarray(mesh.devices).reshape(parts, outer, group, halves),
            ("groups", "outer", "tm", "height"),
        )
        spec = P(("groups", "outer", "tm"), "height", None, None)
        placed = (spec, P("groups"), P(), P(), P(), P(), P())
        return jax.shard_map(
            functools.partial(per_device, outer),
            mesh=split,
            in_specs=placed,
            out_specs=spec,
            check_vma=False,
        )(video, *rest)

    return run
```

```python
import functools

import jax
import jax.numpy as jnp
import numpy as np
from jax import lax
from jax.experimental import pallas as pl
from jax.experimental.pallas import tpu as pltpu
from jax.sharding import Mesh, PartitionSpec as P

HD = 64
BLOCK = 4
TAPS = 3
REACH = 2 * BLOCK - 1 + TAPS - 1
LANES = 128
EDGE = 8
VMEM = 28 * 2**20

bf16, f32 = jnp.bfloat16, jnp.float32


def get(ref, start, size, stride):
    return jnp.concatenate([ref[i, pl.ds(start, size, stride=stride), :] for i in range(ref.shape[0])], axis=1)


def put(ref, start, size, stride, value):
    for i in range(ref.shape[0]):
        ref[i, pl.ds(start, size, stride=stride), :] = value[:, i * LANES : (i + 1) * LANES]


def fill(ref, start, value):
    for i in range(ref.shape[0]):
        ref[i, pl.ds(start, value.shape[0]), :] = value[:, i * LANES : (i + 1) * LANES]


def scratch(rows, chans):
    return pltpu.VMEM((chans // LANES, rows, LANES), f32)


def rms(wide):
    return wide * lax.rsqrt(jnp.mean(wide * wide, axis=-1, keepdims=True) + 1e-06)


def divided(at, by):
    if by & (by - 1) == 0:
        bits = by.bit_length() - 1
        return at >> bits, at & (by - 1)
    return lax.div(at, jnp.int32(by)), lax.rem(at, jnp.int32(by))


def pack_kernel(group, video, *refs):
    out, local, wide, sems = refs
    count, rows, cols, chans = video.shape
    lines = count * rows
    stride = cols + 2 * EDGE
    own = cols // group
    span = own + 2
    copies = []
    for at in range(lines):
        place = (at // rows, at % rows)
        copy = pltpu.make_async_copy(video.at[place], local.at[place], sems.at[at])
        copy.start()
        copies.append(copy)
    nothing = jnp.zeros((EDGE, chans), f32)
    for at in range(lines):
        fill(wide, at * stride, nothing)
        fill(wide, at * stride + EDGE + cols, nothing)
    for at, copy in enumerate(copies):
        copy.wait()
        fill(wide, at * stride + EDGE, local[at // rows, at % rows].astype(f32))
    together = 16 // lines
    for k in range(group):
        start = k * own + EDGE - 1
        for w in range(0, span, together):
            tile = jnp.concatenate([get(wide, start + w + i, lines, stride) for i in range(together)], axis=0)
            out[k, pl.ds(w * lines, 16), :] = tile.astype(bf16)


def frames_of(ref, w, r, count, rows, sources, step):
    return [get(ref, w * count * rows + t * rows + r, sources, step) for t in range(count)]


def shifted(now):
    count = len(now)
    sources, chans = now[0].shape
    first = lax.broadcasted_iota(jnp.int32, (sources, chans), 0) == 0
    past = [jnp.where(first, 0.0, pltpu.roll(x, 1, 0)) for x in now]
    ordered = past + now
    taps = []
    for a in range(TAPS):
        start = count - (TAPS - 1 - a)
        taps.append(jnp.concatenate(ordered[start : start + count], 0).astype(bf16))
    return jnp.concatenate(taps, axis=1)


def activated(wide):
    part = 0.5 * rms(wide)
    return part + part * jnp.tanh(part)


def depth(parts):
    return parts[0] if len(parts) == 1 else jnp.concatenate(parts, axis=-1)


def edge_kernel(count, rows, video, edge, vid):
    sources, step, chans = video.shape
    span = step // (count * rows)
    fill(vid, 0, video[...].reshape(sources * step, chans).astype(f32))
    row = (rows - 1) * (1 - lax.axis_index("height"))
    for w in range(span):
        edge[w] = shifted([activated(x) for x in frames_of(vid, w, row, count, rows, sources, step)])


def fill_bias(bias, ids, frames, count):
    area = bias.shape[0]
    sources = frames // count

    def place_of(at):
        pixel, place = divided(at, frames)
        inner, source = divided(place, sources)
        frame = source * count + inner
        block = jnp.zeros(at.shape, jnp.int32)
        for s in range(frames):
            block = jnp.where(frame == s, ids[s], block)
        return pixel, frame, block

    row_p, row_t, row_b = place_of(lax.broadcasted_iota(jnp.int32, (area, area), 0))
    col_p, col_t, col_b = place_of(lax.broadcasted_iota(jnp.int32, (1, area), 1))
    permit = (row_p == col_p) & (col_t <= row_t) & (col_b >= row_b - 1)
    bias[...] = jnp.where(permit, 0.0, -1e30)


def shift_kernel(count, rows, video, ids_far, *refs):
    conv_weight, far, (total, bias, *near) = refs[0], refs[1:5], refs[5:11]
    vid, grid, ids, sems, ids_sem = refs[11:]
    ids_copy = pltpu.make_async_copy(ids_far, ids, ids_sem)
    ids_copy.start()
    others = [pltpu.make_async_copy(src, dst, sems.at[i]) for i, (src, dst) in enumerate(zip(far, near))]
    for copy in others:
        copy.start()
    sources, step, chans = video.shape
    span = step // (count * rows)
    own = span - 2
    frames = sources * count
    half = own // 2 if own % 2 == 0 else own
    fill(vid, 0, video[...].reshape(sources * step, chans).astype(f32))
    for w in range(span):
        for r in range(rows):
            now = frames_of(vid, w, r, count, rows, sources, step)
            grid[w, r] = shifted([activated(x) for x in now])
            if 1 <= w <= own:
                total[w - 1, r] = jnp.concatenate(now, 0)

    for b in range(TAPS):
        low, high = max(0, 1 - b), min(rows, rows + 1 - b)
        weight = jnp.concatenate([conv_weight[a, b, e] for e in range(TAPS) for a in range(TAPS)], axis=0)
        for w in range(0, own, half):
            window = depth([grid[w + e : w + e + half, low + b - 1 : high + b - 1] for e in range(TAPS)])
            window = window.reshape(half * (high - low) * frames, TAPS * TAPS * chans)
            part = jnp.dot(window, weight, preferred_element_type=f32)
            some = total.at[w : w + half, low:high]
            some[...] = some[...] + part.reshape(half, high - low, frames, chans)
    ids_copy.wait()
    fill_bias(bias, ids, frames, count)
    for copy in others:
        copy.wait()


def main_kernel(
    count, rows, group, edge, given, bias, conv_weight, w_query, w_key, w_value, w_output, *refs
):
    out, res = refs
    own, _, frames, chans = given.shape
    sources = frames // count
    lines = count * rows
    heads = chans // HD
    back = own * lines
    area = bias.shape[0]
    several = area // (rows * frames)

    lower = lax.axis_index("height")
    b = (TAPS - 1) * (1 - lower)
    part = jnp.zeros((own * frames, chans), f32)
    for e in range(TAPS):
        window = edge[e : e + own].reshape(own * frames, TAPS * chans)
        weight = jnp.concatenate([conv_weight[a, b, e] for a in range(TAPS)], axis=0)
        part = part + jnp.dot(window, weight, preferred_element_type=f32)
    part = part.reshape(own, frames, chans)

    head_of = divided(lax.broadcasted_iota(jnp.int32, (area, chans), 1), HD)[0]
    single = [jnp.where(head_of == h, 1.0, 0.0).astype(bf16) for h in range(heads)]
    scaled = [mask * jnp.asarray(HD ** (-0.5), bf16) for mask in single]

    half = own // 2 if own % (2 * several) == 0 else own
    for start in range(0, own, half):
        lines_of = []
        for r in range(rows):
            row = given[start : start + half, r]
            row = row + jnp.where(r == (rows - 1) * (1 - lower), part[start : start + half], 0.0)
            lines_of.append(row[:, None])
        hidden = jnp.concatenate(lines_of, axis=1).reshape(half * rows * frames, chans).astype(bf16).astype(f32)
        normed = rms(hidden).astype(bf16)
        query, keys, values = (
            jnp.dot(normed, weight[...], preferred_element_type=f32).astype(bf16)
            for weight in (w_query, w_key, w_value)
        )
        gone = []
        for at in range(0, half * rows * frames, area):
            group_of = slice(at, at + area)
            queries = jnp.concatenate([query[group_of] * mask for mask in scaled], axis=0)
            scores = lax.dot_general(
                queries, keys[group_of], (((1,), (1,)), ((), ())), preferred_element_type=f32
            )
            weights, under = [], jnp.zeros((area, chans), f32)
            for h in range(heads):
                score = scores[h * area : (h + 1) * area] + bias[...]
                expo = jnp.exp(score - jnp.max(score, axis=-1, keepdims=True))
                under = jnp.where(head_of == h, jnp.sum(expo, axis=-1, keepdims=True), under)
                weights.append(expo.astype(bf16))
            heads_values = jnp.concatenate([values[group_of] * mask for mask in single], axis=0)
            attended = jnp.dot(jnp.concatenate(weights, axis=1), heads_values, preferred_element_type=f32)
            gone.append((attended / under).astype(bf16))
        attended = jnp.concatenate(gone, axis=0)
        encoded = hidden + jnp.dot(attended, w_output[...], preferred_element_type=f32)
        for w in range(half):
            for r in range(rows):
                for t in range(count):
                    first = ((w * rows + r) * count + t + 1) * sources - group
                    place = (t * rows + r) * own + start + w
                    put(res, place, group, back, encoded[first : first + group])
    done = jnp.concatenate([res[i] for i in range(res.shape[0])], axis=1)
    out[...] = done.astype(bf16).reshape(out.shape)


def exchanged(blocks):
    return lax.all_to_all(blocks, "tm", split_axis=0, concat_axis=0, tiled=True)


def per_device(outer, video, block_ids, conv_weight, w_query, w_key, w_value, w_output):
    count, rows, cols, chans = video.shape
    group = lax.axis_size("tm")
    own = cols // group
    span = own + 2
    lines = count * rows
    near = pl.BlockSpec(memory_space=pltpu.VMEM)
    far = pl.BlockSpec(memory_space=pltpu.HBM)
    params = pltpu.CompilerParams(vmem_limit_bytes=VMEM)
    in_far = functools.partial(pltpu.with_memory_space_constraint, memory_space=pltpu.HBM)
    weights = [in_far(x) for x in (w_query, w_key, w_value, w_output)]

    blocks = pl.pallas_call(
        functools.partial(pack_kernel, group),
        out_shape=jax.ShapeDtypeStruct((group, span * lines, chans), bf16),
        in_specs=[far],
        out_specs=near,
        scratch_shapes=[
            pltpu.VMEM(video.shape, bf16),
            scratch(lines * (cols + 2 * EDGE), chans),
            pltpu.SemaphoreType.DMA((lines,)),
        ],
        compiler_params=params,
        cost_estimate=pl.CostEstimate(flops=2000000000, transcendentals=0, bytes_accessed=1000000),
    )(in_far(video))
    piece = exchanged(blocks)
    ids = block_ids
    if outer > 1:
        before = lax.ppermute(piece, "outer", [(i, i + 1) for i in range(outer - 1)])
        piece = jnp.concatenate([before, piece], axis=0)
        ids = jnp.concatenate([jnp.full((group * count,), -2, jnp.int32), ids])
        ids = lax.dynamic_slice(ids, (lax.axis_index("outer") * group * count,), (2 * group * count,))
    sources = piece.shape[0]
    frames = sources * count
    stored = scratch(sources * span * lines, chans)
    edge = pl.pallas_call(
        functools.partial(edge_kernel, count, rows),
        out_shape=jax.ShapeDtypeStruct((span, frames, TAPS * chans), bf16),
        in_specs=[near],
        out_specs=near,
        scratch_shapes=[stored],
        compiler_params=params,
    )(piece)
    edge = lax.ppermute(edge, "height", [(0, 1), (1, 0)])
    several = max(n for n in range(1, own + 1) if own % n == 0 and (n == 1 or n * rows * frames <= LANES))
    area = several * rows * frames
    total, bias, *weights = pl.pallas_call(
        functools.partial(shift_kernel, count, rows),
        out_shape=[
            jax.ShapeDtypeStruct((own, rows, frames, chans), f32),
            jax.ShapeDtypeStruct((area, area), f32),
        ]
        + [jax.ShapeDtypeStruct(x.shape, bf16) for x in weights],
        in_specs=[near, far, near] + [far] * 4,
        out_specs=[near] * 6,
        scratch_shapes=[
            stored,
            pltpu.VMEM((span, rows, frames, TAPS * chans), bf16),
            pltpu.SMEM((frames,), jnp.int32),
            pltpu.SemaphoreType.DMA((4,)),
            pltpu.SemaphoreType.DMA(()),
        ],
        compiler_params=params,
    )(piece, in_far(ids), conv_weight, *weights)
    blocks = pl.pallas_call(
        functools.partial(main_kernel, count, rows, group),
        out_shape=jax.ShapeDtypeStruct((group, own * lines, chans), bf16),
        in_specs=[near] * 8,
        out_specs=near,
        scratch_shapes=[scratch(group * own * lines, chans)],
        compiler_params=params,
    )(edge, total, bias, conv_weight, *weights)
    returned = exchanged(blocks).reshape(group, lines, own, chans)
    return jnp.swapaxes(returned, 0, 1).reshape(video.shape)


def solution(mesh):
    parts, along, halves = (mesh.shape[a] for a in ("groups", "tm", "height"))

    def run(video, *rest):
        count = video.shape[0] // (parts * along)
        group = min(g for g in range(1, along + 1) if along % g == 0 and (g * count >= REACH or g == along))
        outer = along // group
        split = Mesh(
            np.asarray(mesh.devices).reshape(parts, outer, group, halves),
            ("groups", "outer", "tm", "height"),
        )
        spec = P(("groups", "outer", "tm"), "height", None, None)
        placed = (spec, P("groups"), P(), P(), P(), P(), P())
        return jax.shard_map(
            functools.partial(per_device, outer),
            mesh=split,
            in_specs=placed,
            out_specs=spec,
            check_vma=False,
        )(video, *rest)

    return run
```

```python
import functools

import jax
import jax.numpy as jnp
import numpy as np
from jax import lax
from jax.experimental import pallas as pl
from jax.experimental.pallas import tpu as pltpu
from jax.sharding import Mesh, PartitionSpec as P

HD = 64
BLOCK = 4
TAPS = 3
REACH = 2 * BLOCK - 1 + TAPS - 1
LANES = 128
EDGE = 8
VMEM = 28 * 2**20

bf16, f32 = jnp.bfloat16, jnp.float32


def get(ref, start, size, stride):
    return jnp.concatenate([ref[i, pl.ds(start, size, stride=stride), :] for i in range(ref.shape[0])], axis=1)


def put(ref, start, size, stride, value):
    for i in range(ref.shape[0]):
        ref[i, pl.ds(start, size, stride=stride), :] = value[:, i * LANES : (i + 1) * LANES]


def fill(ref, start, value):
    for i in range(ref.shape[0]):
        ref[i, pl.ds(start, value.shape[0]), :] = value[:, i * LANES : (i + 1) * LANES]


def scratch(rows, chans):
    return pltpu.VMEM((chans // LANES, rows, LANES), f32)


def rms(wide):
    return wide * lax.rsqrt(jnp.mean(wide * wide, axis=-1, keepdims=True) + 1e-06)


def divided(at, by):
    if by & (by - 1) == 0:
        bits = by.bit_length() - 1
        return at >> bits, at & (by - 1)
    return lax.div(at, jnp.int32(by)), lax.rem(at, jnp.int32(by))


def pack_kernel(group, video, *refs):
    out, local, wide, sems = refs
    count, rows, cols, chans = video.shape
    lines = count * rows
    stride = cols + 2 * EDGE
    own = cols // group
    span = own + 2
    copies = []
    for at in range(lines):
        place = (at // rows, at % rows)
        copy = pltpu.make_async_copy(video.at[place], local.at[place], sems.at[at])
        copy.start()
        copies.append(copy)
    nothing = jnp.zeros((EDGE, chans), f32)
    for at in range(lines):
        fill(wide, at * stride, nothing)
        fill(wide, at * stride + EDGE + cols, nothing)
    for at, copy in enumerate(copies):
        copy.wait()
        fill(wide, at * stride + EDGE, local[at // rows, at % rows].astype(f32))
    together = 16 // lines
    for k in range(group):
        start = k * own + EDGE - 1
        for w in range(0, span, together):
            tile = jnp.concatenate([get(wide, start + w + i, lines, stride) for i in range(together)], axis=0)
            out[k, pl.ds(w * lines, 16), :] = tile.astype(bf16)


def frames_of(ref, w, r, count, rows, sources, step):
    return [get(ref, w * count * rows + t * rows + r, sources, step) for t in range(count)]


def shifted(now):
    count = len(now)
    sources, chans = now[0].shape
    first = lax.broadcasted_iota(jnp.int32, (sources, chans), 0) == 0
    past = [jnp.where(first, 0.0, pltpu.roll(x, 1, 0)) for x in now]
    ordered = past + now
    taps = []
    for a in range(TAPS):
        start = count - (TAPS - 1 - a)
        taps.append(jnp.concatenate(ordered[start : start + count], 0).astype(bf16))
    return jnp.concatenate(taps, axis=1)


def activated(wide):
    part = 0.5 * rms(wide)
    return part + part * jnp.tanh(part)


def depth(parts):
    return parts[0] if len(parts) == 1 else jnp.concatenate(parts, axis=-1)


def edge_kernel(count, rows, video, edge, vid):
    sources, step, chans = video.shape
    span = step // (count * rows)
    fill(vid, 0, video[...].reshape(sources * step, chans).astype(f32))
    row = (rows - 1) * (1 - lax.axis_index("height"))
    for w in range(span):
        edge[w] = shifted([activated(x) for x in frames_of(vid, w, row, count, rows, sources, step)])


def fill_bias(bias, ids, frames, count):
    area = bias.shape[0]
    sources = frames // count

    def place_of(at):
        pixel, place = divided(at, frames)
        inner, source = divided(place, sources)
        frame = source * count + inner
        block = jnp.zeros(at.shape, jnp.int32)
        for s in range(frames):
            block = jnp.where(frame == s, ids[s], block)
        return pixel, frame, block

    row_p, row_t, row_b = place_of(lax.broadcasted_iota(jnp.int32, (area, area), 0))
    col_p, col_t, col_b = place_of(lax.broadcasted_iota(jnp.int32, (1, area), 1))
    permit = (row_p == col_p) & (col_t <= row_t) & (col_b >= row_b - 1)
    bias[...] = jnp.where(permit, 0.0, -1e30)


def shift_kernel(count, rows, video, ids_far, *refs):
    conv_weight, far, (total, bias, *near) = refs[0], refs[1:5], refs[5:11]
    vid, grid, ids, sems, ids_sem = refs[11:]
    ids_copy = pltpu.make_async_copy(ids_far, ids, ids_sem)
    ids_copy.start()
    others = [pltpu.make_async_copy(src, dst, sems.at[i]) for i, (src, dst) in enumerate(zip(far, near))]
    for copy in others:
        copy.start()
    sources, step, chans = video.shape
    span = step // (count * rows)
    own = span - 2
    frames = sources * count
    half = own // 2 if own % 2 == 0 else own
    fill(vid, 0, video[...].reshape(sources * step, chans).astype(f32))
    for w in range(span):
        for r in range(rows):
            now = frames_of(vid, w, r, count, rows, sources, step)
            grid[w, r] = shifted([activated(x) for x in now])
            if 1 <= w <= own:
                total[w - 1, r] = jnp.concatenate(now, 0)

    for b in range(TAPS):
        low, high = max(0, 1 - b), min(rows, rows + 1 - b)
        weight = jnp.concatenate([conv_weight[a, b, e] for e in range(TAPS) for a in range(TAPS)], axis=0)
        for w in range(0, own, half):
            window = depth([grid[w + e : w + e + half, low + b - 1 : high + b - 1] for e in range(TAPS)])
            window = window.reshape(half * (high - low) * frames, TAPS * TAPS * chans)
            part = jnp.dot(window, weight, preferred_element_type=f32)
            some = total.at[w : w + half, low:high]
            some[...] = some[...] + part.reshape(half, high - low, frames, chans)
    ids_copy.wait()
    fill_bias(bias, ids, frames, count)
    for copy in others:
        copy.wait()


def main_kernel(
    count, rows, group, edge, given, bias, conv_weight, w_query, w_key, w_value, w_output, *refs
):
    out, res = refs
    own, _, frames, chans = given.shape
    sources = frames // count
    lines = count * rows
    back = own * lines
    area = bias.shape[0]

    lower = lax.axis_index("height")
    b = (TAPS - 1) * (1 - lower)
    part = jnp.zeros((own * frames, chans), f32)
    for e in range(TAPS):
        window = edge[e : e + own].reshape(own * frames, TAPS * chans)
        weight = jnp.concatenate([conv_weight[a, b, e] for a in range(TAPS)], axis=0)
        part = part + jnp.dot(window, weight, preferred_element_type=f32)
    part = part.reshape(own, frames, chans)

    head_of = divided(lax.broadcasted_iota(jnp.int32, (area, LANES), 1), HD)[0]
    single = [jnp.where(head_of == h, 1.0, 0.0).astype(bf16) for h in range(LANES // HD)]
    scaled = [mask * jnp.asarray(HD ** (-0.5), bf16) for mask in single]

    lines_of = []
    for r in range(rows):
        row = given[:, r] + jnp.where(r == (rows - 1) * (1 - lower), part, 0.0)
        lines_of.append(row[:, None])
    hidden = jnp.concatenate(lines_of, axis=1).reshape(own * rows * frames, chans).astype(bf16).astype(f32)
    normed = rms(hidden).astype(bf16)
    query, keys, values = (
        jnp.dot(normed, weight[...], preferred_element_type=f32).astype(bf16) for weight in (w_query, w_key, w_value)
    )
    gone = []
    for at in range(0, own * rows * frames, area):
        attended = []
        for lane in range(0, chans, LANES):
            block = (slice(at, at + area), slice(lane, lane + LANES))
            queries = jnp.concatenate([query[block] * mask for mask in scaled], axis=0)
            scores = lax.dot_general(queries, keys[block], (((1,), (1,)), ((), ())), preferred_element_type=f32)
            weights, under = [], jnp.zeros((area, LANES), f32)
            for h in range(len(single)):
                score = scores[h * area : (h + 1) * area] + bias[...]
                expo = jnp.exp(score - jnp.max(score, axis=-1, keepdims=True))
                under = jnp.where(head_of == h, jnp.sum(expo, axis=-1, keepdims=True), under)
                weights.append(expo.astype(bf16))
            heads_values = jnp.concatenate([values[block] * mask for mask in single], axis=0)
            mixed = jnp.dot(jnp.concatenate(weights, axis=1), heads_values, preferred_element_type=f32)
            attended.append((mixed / under).astype(bf16))
        gone.append(jnp.concatenate(attended, axis=1))
    encoded = hidden + jnp.dot(jnp.concatenate(gone, axis=0), w_output[...], preferred_element_type=f32)
    for w in range(own):
        for r in range(rows):
            for t in range(count):
                first = ((w * rows + r) * count + t + 1) * sources - group
                put(res, (t * rows + r) * own + w, group, back, encoded[first : first + group])
    done = jnp.concatenate([res[i] for i in range(res.shape[0])], axis=1)
    out[...] = done.astype(bf16).reshape(out.shape)


def exchanged(blocks):
    return lax.all_to_all(blocks, "tm", split_axis=0, concat_axis=0, tiled=True)


def per_device(outer, video, block_ids, conv_weight, w_query, w_key, w_value, w_output):
    count, rows, cols, chans = video.shape
    group = lax.axis_size("tm")
    own = cols // group
    span = own + 2
    lines = count * rows
    near = pl.BlockSpec(memory_space=pltpu.VMEM)
    far = pl.BlockSpec(memory_space=pltpu.HBM)
    params = pltpu.CompilerParams(vmem_limit_bytes=VMEM)
    in_far = functools.partial(pltpu.with_memory_space_constraint, memory_space=pltpu.HBM)
    weights = [in_far(x) for x in (w_query, w_key, w_value, w_output)]

    blocks = pl.pallas_call(
        functools.partial(pack_kernel, group),
        out_shape=jax.ShapeDtypeStruct((group, span * lines, chans), bf16),
        in_specs=[far],
        out_specs=near,
        scratch_shapes=[
            pltpu.VMEM(video.shape, bf16),
            scratch(lines * (cols + 2 * EDGE), chans),
            pltpu.SemaphoreType.DMA((lines,)),
        ],
        compiler_params=params,
        cost_estimate=pl.CostEstimate(flops=2000000000, transcendentals=0, bytes_accessed=1000000),
    )(in_far(video))
    piece = exchanged(blocks)
    ids = block_ids
    if outer > 1:
        before = lax.ppermute(piece, "outer", [(i, i + 1) for i in range(outer - 1)])
        piece = jnp.concatenate([before, piece], axis=0)
        ids = jnp.concatenate([jnp.full((group * count,), -2, jnp.int32), ids])
        ids = lax.dynamic_slice(ids, (lax.axis_index("outer") * group * count,), (2 * group * count,))
    sources = piece.shape[0]
    frames = sources * count
    stored = scratch(sources * span * lines, chans)
    edge = pl.pallas_call(
        functools.partial(edge_kernel, count, rows),
        out_shape=jax.ShapeDtypeStruct((span, frames, TAPS * chans), bf16),
        in_specs=[near],
        out_specs=near,
        scratch_shapes=[stored],
        compiler_params=params,
    )(piece)
    edge = lax.ppermute(edge, "height", [(0, 1), (1, 0)])
    several = max(n for n in range(1, own + 1) if own % n == 0 and (n == 1 or n * rows * frames <= LANES))
    area = several * rows * frames
    total, bias, *weights = pl.pallas_call(
        functools.partial(shift_kernel, count, rows),
        out_shape=[
            jax.ShapeDtypeStruct((own, rows, frames, chans), f32),
            jax.ShapeDtypeStruct((area, area), f32),
        ]
        + [jax.ShapeDtypeStruct(x.shape, bf16) for x in weights],
        in_specs=[near, far, near] + [far] * 4,
        out_specs=[near] * 6,
        scratch_shapes=[
            stored,
            pltpu.VMEM((span, rows, frames, TAPS * chans), bf16),
            pltpu.SMEM((frames,), jnp.int32),
            pltpu.SemaphoreType.DMA((4,)),
            pltpu.SemaphoreType.DMA(()),
        ],
        compiler_params=params,
    )(piece, in_far(ids), conv_weight, *weights)
    blocks = pl.pallas_call(
        functools.partial(main_kernel, count, rows, group),
        out_shape=jax.ShapeDtypeStruct((group, own * lines, chans), bf16),
        in_specs=[near] * 8,
        out_specs=near,
        scratch_shapes=[scratch(group * own * lines, chans)],
        compiler_params=params,
    )(edge, total, bias, conv_weight, *weights)
    returned = exchanged(blocks).reshape(group, lines, own, chans)
    return jnp.swapaxes(returned, 0, 1).reshape(video.shape)


def solution(mesh):
    parts, along, halves = (mesh.shape[a] for a in ("groups", "tm", "height"))

    def run(video, *rest):
        count = video.shape[0] // (parts * along)
        group = min(g for g in range(1, along + 1) if along % g == 0 and (g * count >= REACH or g == along))
        outer = along // group
        split = Mesh(
            np.asarray(mesh.devices).reshape(parts, outer, group, halves),
            ("groups", "outer", "tm", "height"),
        )
        spec = P(("groups", "outer", "tm"), "height", None, None)
        placed = (spec, P("groups"), P(), P(), P(), P(), P())
        return jax.shard_map(
            functools.partial(per_device, outer),
            mesh=split,
            in_specs=placed,
            out_specs=spec,
            check_vma=False,
        )(video, *rest)

    return run
```

```python
import functools

import jax
import jax.numpy as jnp
import numpy as np
from jax import lax
from jax.experimental import pallas as pl
from jax.experimental.pallas import tpu as pltpu
from jax.sharding import Mesh, PartitionSpec as P

HD = 64
BLOCK = 4
TAPS = 3
REACH = 2 * BLOCK - 1 + TAPS - 1
LANES = 128
EDGE = 8
VMEM = 28 * 2**20

bf16, f32 = jnp.bfloat16, jnp.float32


def get(ref, start, size, stride):
    return jnp.concatenate([ref[i, pl.ds(start, size, stride=stride), :] for i in range(ref.shape[0])], axis=1)


def put(ref, start, size, stride, value):
    for i in range(ref.shape[0]):
        ref[i, pl.ds(start, size, stride=stride), :] = value[:, i * LANES : (i + 1) * LANES]


def fill(ref, start, value):
    for i in range(ref.shape[0]):
        ref[i, pl.ds(start, value.shape[0]), :] = value[:, i * LANES : (i + 1) * LANES]


def scratch(rows, chans):
    return pltpu.VMEM((chans // LANES, rows, LANES), f32)


def rms(wide):
    return wide * lax.rsqrt(jnp.mean(wide * wide, axis=-1, keepdims=True) + 1e-06)


def divided(at, by):
    if by & (by - 1) == 0:
        bits = by.bit_length() - 1
        return at >> bits, at & (by - 1)
    return lax.div(at, jnp.int32(by)), lax.rem(at, jnp.int32(by))


def pack_kernel(group, video, *refs):
    out, local, wide, sems = refs
    count, rows, cols, chans = video.shape
    lines = count * rows
    stride = cols + 2 * EDGE
    own = cols // group
    span = own + 2
    copies = []
    for at in range(lines):
        place = (at // rows, at % rows)
        copy = pltpu.make_async_copy(video.at[place], local.at[place], sems.at[at])
        copy.start()
        copies.append(copy)
    nothing = jnp.zeros((EDGE, chans), f32)
    for at in range(lines):
        fill(wide, at * stride, nothing)
        fill(wide, at * stride + EDGE + cols, nothing)
    for at, copy in enumerate(copies):
        copy.wait()
        fill(wide, at * stride + EDGE, local[at // rows, at % rows].astype(f32))
    together = 16 // lines
    for k in range(group):
        start = k * own + EDGE - 1
        for w in range(0, span, together):
            tile = jnp.concatenate([get(wide, start + w + i, lines, stride) for i in range(together)], axis=0)
            out[k, pl.ds(w * lines, 16), :] = tile.astype(bf16)


def frames_of(ref, w, r, count, rows, sources, step):
    return [get(ref, w * count * rows + t * rows + r, sources, step) for t in range(count)]


def shifted(now):
    count = len(now)
    sources, chans = now[0].shape
    first = lax.broadcasted_iota(jnp.int32, (sources, chans), 0) == 0
    past = [jnp.where(first, 0.0, pltpu.roll(x, 1, 0)) for x in now]
    ordered = past + now
    taps = []
    for a in range(TAPS):
        start = count - (TAPS - 1 - a)
        taps.append(jnp.concatenate(ordered[start : start + count], 0).astype(bf16))
    return jnp.concatenate(taps, axis=1)


def activated(wide):
    part = 0.5 * rms(wide)
    return part + part * jnp.tanh(part)


def depth(parts):
    return parts[0] if len(parts) == 1 else jnp.concatenate(parts, axis=-1)


def edge_kernel(count, rows, video, edge, vid):
    sources, step, chans = video.shape
    span = step // (count * rows)
    fill(vid, 0, video[...].reshape(sources * step, chans).astype(f32))
    row = (rows - 1) * (1 - lax.axis_index("height"))
    for w in range(span):
        edge[w] = shifted([activated(x) for x in frames_of(vid, w, row, count, rows, sources, step)])


def fill_bias(bias, ids, frames, count):
    area = bias.shape[0]
    sources = frames // count

    def place_of(at):
        pixel, place = divided(at, frames)
        inner, source = divided(place, sources)
        frame = source * count + inner
        block = jnp.zeros(at.shape, jnp.int32)
        for s in range(frames):
            block = jnp.where(frame == s, ids[s], block)
        return pixel, frame, block

    row_p, row_t, row_b = place_of(lax.broadcasted_iota(jnp.int32, (area, area), 0))
    col_p, col_t, col_b = place_of(lax.broadcasted_iota(jnp.int32, (1, area), 1))
    permit = (row_p == col_p) & (col_t <= row_t) & (col_b >= row_b - 1)
    bias[...] = jnp.where(permit, 0.0, -1e30)


def shift_kernel(count, rows, video, ids_far, *refs):
    conv_weight, far, (total, bias, *near) = refs[0], refs[1:5], refs[5:11]
    vid, grid, ids, sems, ids_sem = refs[11:]
    ids_copy = pltpu.make_async_copy(ids_far, ids, ids_sem)
    ids_copy.start()
    others = [pltpu.make_async_copy(src, dst, sems.at[i]) for i, (src, dst) in enumerate(zip(far, near))]
    for copy in others:
        copy.start()
    sources, step, chans = video.shape
    span = step // (count * rows)
    own = span - 2
    frames = sources * count
    half = own // 2 if own % 2 == 0 else own
    fill(vid, 0, video[...].reshape(sources * step, chans).astype(f32))
    for w in range(span):
        for r in range(rows):
            now = frames_of(vid, w, r, count, rows, sources, step)
            grid[w, r] = shifted([activated(x) for x in now])
            if 1 <= w <= own:
                total[w - 1, r] = jnp.concatenate(now, 0)

    for w in range(0, own, half):
        for b in (1, 0, 2):
            low, high = max(0, 1 - b), min(rows, rows + 1 - b)
            weight = jnp.concatenate([conv_weight[a, b, e] for e in range(TAPS) for a in range(TAPS)], axis=0)
            window = depth([grid[w + e : w + e + half, low + b - 1 : high + b - 1] for e in range(TAPS)])
            window = window.reshape(half * (high - low) * frames, TAPS * TAPS * chans)
            part = jnp.dot(window, weight, preferred_element_type=f32)
            some = total.at[w : w + half, low:high]
            some[...] = some[...] + part.reshape(half, high - low, frames, chans)
    ids_copy.wait()
    fill_bias(bias, ids, frames, count)
    for copy in others:
        copy.wait()


def main_kernel(
    count, rows, group, edge, given, bias, conv_weight, w_query, w_key, w_value, w_output, *refs
):
    out, res = refs
    own, _, frames, chans = given.shape
    sources = frames // count
    lines = count * rows
    back = own * lines
    area = bias.shape[0]

    lower = lax.axis_index("height")
    b = (TAPS - 1) * (1 - lower)
    window = depth([edge[e : e + own] for e in range(TAPS)]).reshape(own * frames, TAPS * TAPS * chans)
    weight = jnp.concatenate([conv_weight[a, b, e] for e in range(TAPS) for a in range(TAPS)], axis=0)
    part = jnp.dot(window, weight, preferred_element_type=f32)
    part = part.reshape(own, frames, chans)

    head_of = divided(lax.broadcasted_iota(jnp.int32, (area, LANES), 1), HD)[0]
    single = [jnp.where(head_of == h, 1.0, 0.0).astype(bf16) for h in range(LANES // HD)]
    scaled = [mask * jnp.asarray(HD ** (-0.5), bf16) for mask in single]

    lines_of = []
    for r in range(rows):
        row = given[:, r]
        if r in (0, rows - 1):
            row = row + jnp.where(r == (rows - 1) * (1 - lower), part, 0.0)
        lines_of.append(row[:, None])
    hidden = jnp.concatenate(lines_of, axis=1).reshape(own * rows * frames, chans).astype(bf16).astype(f32)
    normed = rms(hidden).astype(bf16)
    query, keys, values = (
        jnp.dot(normed, weight[...], preferred_element_type=f32).astype(bf16) for weight in (w_query, w_key, w_value)
    )
    gone = []
    for at in range(0, own * rows * frames, area):
        attended = []
        for lane in range(0, chans, LANES):
            block = (slice(at, at + area), slice(lane, lane + LANES))
            queries = jnp.concatenate([query[block] * mask for mask in scaled], axis=0)
            scores = lax.dot_general(queries, keys[block], (((1,), (1,)), ((), ())), preferred_element_type=f32)
            weights, under = [], jnp.zeros((area, LANES), f32)
            for h in range(len(single)):
                score = scores[h * area : (h + 1) * area] + bias[...]
                expo = jnp.exp(score - jnp.max(score, axis=-1, keepdims=True))
                under = jnp.where(head_of == h, jnp.sum(expo, axis=-1, keepdims=True), under)
                weights.append(expo.astype(bf16))
            heads_values = jnp.concatenate([values[block] * mask for mask in single], axis=0)
            mixed = jnp.dot(jnp.concatenate(weights, axis=1), heads_values, preferred_element_type=f32)
            attended.append((mixed / under).astype(bf16))
        gone.append(jnp.concatenate(attended, axis=1))
    encoded = hidden + jnp.dot(jnp.concatenate(gone, axis=0), w_output[...], preferred_element_type=f32)
    for w in range(own):
        for r in range(rows):
            for t in range(count):
                first = ((w * rows + r) * count + t + 1) * sources - group
                put(res, (t * rows + r) * own + w, group, back, encoded[first : first + group])
    done = jnp.concatenate([res[i] for i in range(res.shape[0])], axis=1)
    out[...] = done.astype(bf16).reshape(out.shape)


def exchanged(blocks):
    return lax.all_to_all(blocks, "tm", split_axis=0, concat_axis=0, tiled=True)


def per_device(outer, video, block_ids, conv_weight, w_query, w_key, w_value, w_output):
    count, rows, cols, chans = video.shape
    group = lax.axis_size("tm")
    own = cols // group
    span = own + 2
    lines = count * rows
    near = pl.BlockSpec(memory_space=pltpu.VMEM)
    far = pl.BlockSpec(memory_space=pltpu.HBM)
    params = pltpu.CompilerParams(vmem_limit_bytes=VMEM)
    in_far = functools.partial(pltpu.with_memory_space_constraint, memory_space=pltpu.HBM)
    weights = [in_far(x) for x in (w_query, w_key, w_value, w_output)]

    blocks = pl.pallas_call(
        functools.partial(pack_kernel, group),
        out_shape=jax.ShapeDtypeStruct((group, span * lines, chans), bf16),
        in_specs=[far],
        out_specs=near,
        scratch_shapes=[
            pltpu.VMEM(video.shape, bf16),
            scratch(lines * (cols + 2 * EDGE), chans),
            pltpu.SemaphoreType.DMA((lines,)),
        ],
        compiler_params=params,
        cost_estimate=pl.CostEstimate(flops=2000000000, transcendentals=0, bytes_accessed=1000000),
    )(in_far(video))
    piece = exchanged(blocks)
    ids = block_ids
    if outer > 1:
        before = lax.ppermute(piece, "outer", [(i, i + 1) for i in range(outer - 1)])
        piece = jnp.concatenate([before, piece], axis=0)
        ids = jnp.concatenate([jnp.full((group * count,), -2, jnp.int32), ids])
        ids = lax.dynamic_slice(ids, (lax.axis_index("outer") * group * count,), (2 * group * count,))
    sources = piece.shape[0]
    frames = sources * count
    stored = scratch(sources * span * lines, chans)
    edge = pl.pallas_call(
        functools.partial(edge_kernel, count, rows),
        out_shape=jax.ShapeDtypeStruct((span, frames, TAPS * chans), bf16),
        in_specs=[near],
        out_specs=near,
        scratch_shapes=[stored],
        compiler_params=params,
    )(piece)
    edge = lax.ppermute(edge, "height", [(0, 1), (1, 0)])
    several = max(n for n in range(1, own + 1) if own % n == 0 and (n == 1 or n * rows * frames <= LANES))
    area = several * rows * frames
    total, bias, *weights = pl.pallas_call(
        functools.partial(shift_kernel, count, rows),
        out_shape=[
            jax.ShapeDtypeStruct((own, rows, frames, chans), f32),
            jax.ShapeDtypeStruct((area, area), f32),
        ]
        + [jax.ShapeDtypeStruct(x.shape, bf16) for x in weights],
        in_specs=[near, far, near] + [far] * 4,
        out_specs=[near] * 6,
        scratch_shapes=[
            stored,
            pltpu.VMEM((span, rows, frames, TAPS * chans), bf16),
            pltpu.SMEM((frames,), jnp.int32),
            pltpu.SemaphoreType.DMA((4,)),
            pltpu.SemaphoreType.DMA(()),
        ],
        compiler_params=params,
    )(piece, in_far(ids), conv_weight, *weights)
    blocks = pl.pallas_call(
        functools.partial(main_kernel, count, rows, group),
        out_shape=jax.ShapeDtypeStruct((group, own * lines, chans), bf16),
        in_specs=[near] * 8,
        out_specs=near,
        scratch_shapes=[scratch(group * own * lines, chans)],
        compiler_params=params,
    )(edge, total, bias, conv_weight, *weights)
    returned = exchanged(blocks).reshape(group, lines, own, chans)
    return jnp.swapaxes(returned, 0, 1).reshape(video.shape)


def solution(mesh):
    parts, along, halves = (mesh.shape[a] for a in ("groups", "tm", "height"))

    def run(video, *rest):
        count = video.shape[0] // (parts * along)
        group = min(g for g in range(1, along + 1) if along % g == 0 and (g * count >= REACH or g == along))
        outer = along // group
        split = Mesh(
            np.asarray(mesh.devices).reshape(parts, outer, group, halves),
            ("groups", "outer", "tm", "height"),
        )
        spec = P(("groups", "outer", "tm"), "height", None, None)
        placed = (spec, P("groups"), P(), P(), P(), P(), P())
        return jax.shard_map(
            functools.partial(per_device, outer),
            mesh=split,
            in_specs=placed,
            out_specs=spec,
            check_vma=False,
        )(video, *rest)

    return run
```

```python
import functools

import jax
import jax.numpy as jnp
import numpy as np
from jax import lax
from jax.experimental import pallas as pl
from jax.experimental.pallas import tpu as pltpu
from jax.sharding import Mesh, PartitionSpec as P

HD = 64
BLOCK = 4
TAPS = 3
REACH = 2 * BLOCK - 1 + TAPS - 1
LANES = 128
EDGE = 8
VMEM = 28 * 2**20

bf16, f32 = jnp.bfloat16, jnp.float32


def get(ref, start, size, stride):
    return jnp.concatenate([ref[i, pl.ds(start, size, stride=stride), :] for i in range(ref.shape[0])], axis=1)


def put(ref, start, size, stride, value):
    for i in range(ref.shape[0]):
        ref[i, pl.ds(start, size, stride=stride), :] = value[:, i * LANES : (i + 1) * LANES]


def fill(ref, start, value):
    for i in range(ref.shape[0]):
        ref[i, pl.ds(start, value.shape[0]), :] = value[:, i * LANES : (i + 1) * LANES]


def scratch(rows, chans):
    return pltpu.VMEM((chans // LANES, rows, LANES), f32)


def rms(wide):
    return wide * lax.rsqrt(jnp.mean(wide * wide, axis=-1, keepdims=True) + 1e-06)


def divided(at, by):
    if by & (by - 1) == 0:
        bits = by.bit_length() - 1
        return at >> bits, at & (by - 1)
    return lax.div(at, jnp.int32(by)), lax.rem(at, jnp.int32(by))


def pack_kernel(group, video, *refs):
    out, local, wide, sems = refs
    count, rows, cols, chans = video.shape
    lines = count * rows
    stride = cols + 2 * EDGE
    own = cols // group
    span = own + 2
    copies = [pltpu.make_async_copy(video.at[t], local.at[t], sems.at[t]) for t in range(count)]
    for copy in copies:
        copy.start()
    nothing = jnp.zeros((EDGE, chans), f32)
    for at in range(lines):
        fill(wide, at * stride, nothing)
        fill(wide, at * stride + EDGE + cols, nothing)
    for copy in copies:
        copy.wait()
    for at in range(lines):
        fill(wide, at * stride + EDGE, local[at // rows, at % rows].astype(f32))
    together = 16 // lines
    for k in range(group):
        start = k * own + EDGE - 1
        for w in range(0, span, together):
            tile = jnp.concatenate([get(wide, start + w + i, lines, stride) for i in range(together)], axis=0)
            out[k, pl.ds(w * lines, 16), :] = tile.astype(bf16)


def frames_of(ref, w, r, count, rows, sources, step):
    return [get(ref, w * count * rows + t * rows + r, sources, step) for t in range(count)]


def shifted(now):
    count = len(now)
    sources, chans = now[0].shape
    first = lax.broadcasted_iota(jnp.int32, (sources, chans), 0) == 0
    past = [jnp.where(first, 0.0, pltpu.roll(x, 1, 0)) for x in now]
    ordered = past + now
    taps = []
    for a in range(TAPS):
        start = count - (TAPS - 1 - a)
        taps.append(jnp.concatenate(ordered[start : start + count], 0).astype(bf16))
    return jnp.concatenate(taps, axis=1)


def activated(wide):
    part = 0.5 * rms(wide)
    return part + part * jnp.tanh(part)


def depth(parts):
    return parts[0] if len(parts) == 1 else jnp.concatenate(parts, axis=-1)


def edge_kernel(count, rows, video, edge, vid):
    sources, step, chans = video.shape
    span = step // (count * rows)
    fill(vid, 0, video[...].reshape(sources * step, chans).astype(f32))
    row = (rows - 1) * (1 - lax.axis_index("height"))
    for w in range(span):
        edge[w] = shifted([activated(x) for x in frames_of(vid, w, row, count, rows, sources, step)])


def fill_bias(bias, ids, frames, count):
    area = bias.shape[0]
    sources = frames // count

    def place_of(at):
        pixel, place = divided(at, frames)
        inner, source = divided(place, sources)
        frame = source * count + inner
        block = jnp.zeros(at.shape, jnp.int32)
        for s in range(frames):
            block = jnp.where(frame == s, ids[s], block)
        return pixel, frame, block

    row_p, row_t, row_b = place_of(lax.broadcasted_iota(jnp.int32, (area, area), 0))
    col_p, col_t, col_b = place_of(lax.broadcasted_iota(jnp.int32, (1, area), 1))
    permit = (row_p == col_p) & (col_t <= row_t) & (col_b >= row_b - 1)
    bias[...] = jnp.where(permit, 0.0, -1e30)


def shift_kernel(count, rows, video, ids_far, *refs):
    conv_weight, far, (total, bias, *near) = refs[0], refs[1:5], refs[5:11]
    vid, grid, ids, sems, ids_sem = refs[11:]
    ids_copy = pltpu.make_async_copy(ids_far, ids, ids_sem)
    ids_copy.start()
    others = [pltpu.make_async_copy(src, dst, sems.at[i]) for i, (src, dst) in enumerate(zip(far, near))]
    for copy in others:
        copy.start()
    sources, step, chans = video.shape
    span = step // (count * rows)
    own = span - 2
    frames = sources * count
    half = own // 2 if own % 2 == 0 else own
    fill(vid, 0, video[...].reshape(sources * step, chans).astype(f32))
    for w in range(span):
        for r in range(rows):
            now = frames_of(vid, w, r, count, rows, sources, step)
            grid[w, r] = shifted([activated(x) for x in now])
            if 1 <= w <= own:
                total[w - 1, r] = jnp.concatenate(now, 0)

    for b in range(TAPS):
        low, high = max(0, 1 - b), min(rows, rows + 1 - b)
        weight = jnp.concatenate([conv_weight[a, b, e] for e in range(TAPS) for a in range(TAPS)], axis=0)
        for w in range(0, own, half):
            window = depth([grid[w + e : w + e + half, low + b - 1 : high + b - 1] for e in range(TAPS)])
            window = window.reshape(half * (high - low) * frames, TAPS * TAPS * chans)
            part = jnp.dot(window, weight, preferred_element_type=f32)
            some = total.at[w : w + half, low:high]
            some[...] = some[...] + part.reshape(half, high - low, frames, chans)
    ids_copy.wait()
    fill_bias(bias, ids, frames, count)
    for copy in others:
        copy.wait()


def main_kernel(
    count, rows, group, edge, given, bias, conv_weight, w_query, w_key, w_value, w_output, *refs
):
    out, res = refs
    own, _, frames, chans = given.shape
    sources = frames // count
    lines = count * rows
    back = own * lines
    area = bias.shape[0]

    lower = lax.axis_index("height")
    b = (TAPS - 1) * (1 - lower)
    part = jnp.zeros((own * frames, chans), f32)
    for e in range(TAPS):
        window = edge[e : e + own].reshape(own * frames, TAPS * chans)
        weight = jnp.concatenate([conv_weight[a, b, e] for a in range(TAPS)], axis=0)
        part = part + jnp.dot(window, weight, preferred_element_type=f32)
    part = part.reshape(own, frames, chans)

    head_of = divided(lax.broadcasted_iota(jnp.int32, (area, LANES), 1), HD)[0]
    single = [jnp.where(head_of == h, 1.0, 0.0).astype(bf16) for h in range(LANES // HD)]
    scaled = [mask * jnp.asarray(HD ** (-0.5), bf16) for mask in single]

    lines_of = []
    for r in range(rows):
        row = given[:, r] + jnp.where(r == (rows - 1) * (1 - lower), part, 0.0)
        lines_of.append(row[:, None])
    hidden = jnp.concatenate(lines_of, axis=1).reshape(own * rows * frames, chans).astype(bf16).astype(f32)
    normed = rms(hidden).astype(bf16)
    query, keys, values = (
        jnp.dot(normed, weight[...], preferred_element_type=f32).astype(bf16) for weight in (w_query, w_key, w_value)
    )
    gone = []
    for at in range(0, own * rows * frames, area):
        attended = []
        for lane in range(0, chans, LANES):
            block = (slice(at, at + area), slice(lane, lane + LANES))
            queries = jnp.concatenate([query[block] * mask for mask in scaled], axis=0)
            scores = lax.dot_general(queries, keys[block], (((1,), (1,)), ((), ())), preferred_element_type=f32)
            weights, under = [], jnp.zeros((area, LANES), f32)
            for h in range(len(single)):
                score = scores[h * area : (h + 1) * area] + bias[...]
                expo = jnp.exp(score - jnp.max(score, axis=-1, keepdims=True))
                under = jnp.where(head_of == h, jnp.sum(expo, axis=-1, keepdims=True), under)
                weights.append(expo.astype(bf16))
            heads_values = jnp.concatenate([values[block] * mask for mask in single], axis=0)
            mixed = jnp.dot(jnp.concatenate(weights, axis=1), heads_values, preferred_element_type=f32)
            attended.append((mixed / under).astype(bf16))
        gone.append(jnp.concatenate(attended, axis=1))
    encoded = hidden + jnp.dot(jnp.concatenate(gone, axis=0), w_output[...], preferred_element_type=f32)
    for w in range(own):
        for r in range(rows):
            for t in range(count):
                first = ((w * rows + r) * count + t + 1) * sources - group
                put(res, (t * rows + r) * own + w, group, back, encoded[first : first + group])
    done = jnp.concatenate([res[i] for i in range(res.shape[0])], axis=1)
    out[...] = done.astype(bf16).reshape(out.shape)


def exchanged(blocks):
    return lax.all_to_all(blocks, "tm", split_axis=0, concat_axis=0, tiled=True)


def per_device(outer, video, block_ids, conv_weight, w_query, w_key, w_value, w_output):
    count, rows, cols, chans = video.shape
    group = lax.axis_size("tm")
    own = cols // group
    span = own + 2
    lines = count * rows
    near = pl.BlockSpec(memory_space=pltpu.VMEM)
    far = pl.BlockSpec(memory_space=pltpu.HBM)
    params = pltpu.CompilerParams(vmem_limit_bytes=VMEM)
    in_far = functools.partial(pltpu.with_memory_space_constraint, memory_space=pltpu.HBM)
    weights = [in_far(x) for x in (w_query, w_key, w_value, w_output)]

    blocks = pl.pallas_call(
        functools.partial(pack_kernel, group),
        out_shape=jax.ShapeDtypeStruct((group, span * lines, chans), bf16),
        in_specs=[far],
        out_specs=near,
        scratch_shapes=[
            pltpu.VMEM(video.shape, bf16),
            scratch(lines * (cols + 2 * EDGE), chans),
            pltpu.SemaphoreType.DMA((count,)),
        ],
        compiler_params=params,
        cost_estimate=pl.CostEstimate(flops=2000000000, transcendentals=0, bytes_accessed=1000000),
    )(in_far(video))
    piece = exchanged(blocks)
    ids = block_ids
    if outer > 1:
        before = lax.ppermute(piece, "outer", [(i, i + 1) for i in range(outer - 1)])
        piece = jnp.concatenate([before, piece], axis=0)
        ids = jnp.concatenate([jnp.full((group * count,), -2, jnp.int32), ids])
        ids = lax.dynamic_slice(ids, (lax.axis_index("outer") * group * count,), (2 * group * count,))
    sources = piece.shape[0]
    frames = sources * count
    stored = scratch(sources * span * lines, chans)
    edge = pl.pallas_call(
        functools.partial(edge_kernel, count, rows),
        out_shape=jax.ShapeDtypeStruct((span, frames, TAPS * chans), bf16),
        in_specs=[near],
        out_specs=near,
        scratch_shapes=[stored],
        compiler_params=params,
    )(piece)
    edge = lax.ppermute(edge, "height", [(0, 1), (1, 0)])
    several = max(n for n in range(1, own + 1) if own % n == 0 and (n == 1 or n * rows * frames <= LANES))
    area = several * rows * frames
    total, bias, *weights = pl.pallas_call(
        functools.partial(shift_kernel, count, rows),
        out_shape=[
            jax.ShapeDtypeStruct((own, rows, frames, chans), f32),
            jax.ShapeDtypeStruct((area, area), f32),
        ]
        + [jax.ShapeDtypeStruct(x.shape, bf16) for x in weights],
        in_specs=[near, far, near] + [far] * 4,
        out_specs=[near] * 6,
        scratch_shapes=[
            stored,
            pltpu.VMEM((span, rows, frames, TAPS * chans), bf16),
            pltpu.SMEM((frames,), jnp.int32),
            pltpu.SemaphoreType.DMA((4,)),
            pltpu.SemaphoreType.DMA(()),
        ],
        compiler_params=params,
    )(piece, in_far(ids), conv_weight, *weights)
    blocks = pl.pallas_call(
        functools.partial(main_kernel, count, rows, group),
        out_shape=jax.ShapeDtypeStruct((group, own * lines, chans), bf16),
        in_specs=[near] * 8,
        out_specs=near,
        scratch_shapes=[scratch(group * own * lines, chans)],
        compiler_params=params,
    )(edge, total, bias, conv_weight, *weights)
    returned = exchanged(blocks).reshape(group, lines, own, chans)
    return jnp.swapaxes(returned, 0, 1).reshape(video.shape)


def solution(mesh):
    parts, along, halves = (mesh.shape[a] for a in ("groups", "tm", "height"))

    def run(video, *rest):
        count = video.shape[0] // (parts * along)
        group = min(g for g in range(1, along + 1) if along % g == 0 and (g * count >= REACH or g == along))
        outer = along // group
        split = Mesh(
            np.asarray(mesh.devices).reshape(parts, outer, group, halves),
            ("groups", "outer", "tm", "height"),
        )
        spec = P(("groups", "outer", "tm"), "height", None, None)
        placed = (spec, P("groups"), P(), P(), P(), P(), P())
        return jax.shard_map(
            functools.partial(per_device, outer),
            mesh=split,
            in_specs=placed,
            out_specs=spec,
            check_vma=False,
        )(video, *rest)

    return run
```

```python
import functools

import jax
import jax.numpy as jnp
import numpy as np
from jax import lax
from jax.experimental import pallas as pl
from jax.experimental.pallas import tpu as pltpu
from jax.sharding import Mesh, PartitionSpec as P

HD = 64
BLOCK = 4
TAPS = 3
REACH = 2 * BLOCK - 1 + TAPS - 1
LANES = 128
EDGE = 8
VMEM = 28 * 2**20

bf16, f32 = jnp.bfloat16, jnp.float32


def get(ref, start, size, stride):
    return jnp.concatenate([ref[i, pl.ds(start, size, stride=stride), :] for i in range(ref.shape[0])], axis=1)


def put(ref, start, size, stride, value):
    for i in range(ref.shape[0]):
        ref[i, pl.ds(start, size, stride=stride), :] = value[:, i * LANES : (i + 1) * LANES]


def fill(ref, start, value):
    for i in range(ref.shape[0]):
        ref[i, pl.ds(start, value.shape[0]), :] = value[:, i * LANES : (i + 1) * LANES]


def scratch(rows, chans):
    return pltpu.VMEM((chans // LANES, rows, LANES), f32)


def rms(wide):
    return wide * lax.rsqrt(jnp.mean(wide * wide, axis=-1, keepdims=True) + 1e-06)


def divided(at, by):
    if by & (by - 1) == 0:
        bits = by.bit_length() - 1
        return at >> bits, at & (by - 1)
    return lax.div(at, jnp.int32(by)), lax.rem(at, jnp.int32(by))


def pack_kernel(group, video, *refs):
    out, local, wide, sems = refs
    count, rows, cols, chans = video.shape
    lines = count * rows
    stride = cols + 2 * EDGE
    own = cols // group
    span = own + 2
    copies = []
    for at in range(lines):
        place = (at // rows, at % rows)
        copy = pltpu.make_async_copy(video.at[place], local.at[place], sems.at[at])
        copy.start()
        copies.append(copy)
    nothing = jnp.zeros((EDGE, chans), f32)
    for at in range(lines):
        fill(wide, at * stride, nothing)
        fill(wide, at * stride + EDGE + cols, nothing)
    for at, copy in enumerate(copies):
        copy.wait()
        fill(wide, at * stride + EDGE, local[at // rows, at % rows].astype(f32))
    together = 16 // lines
    for k in range(group):
        start = k * own + EDGE - 1
        for w in range(0, span, together):
            tile = jnp.concatenate([get(wide, start + w + i, lines, stride) for i in range(together)], axis=0)
            out[k, pl.ds(w * lines, 16), :] = tile.astype(bf16)


def frames_of(ref, w, r, count, rows, sources, step):
    return [get(ref, w * count * rows + t * rows + r, sources, step) for t in range(count)]


def shifted(now):
    count = len(now)
    sources, chans = now[0].shape
    first = lax.broadcasted_iota(jnp.int32, (sources, chans), 0) == 0
    past = [jnp.where(first, 0.0, pltpu.roll(x, 1, 0)) for x in now]
    ordered = past + now
    taps = []
    for a in range(TAPS):
        start = count - (TAPS - 1 - a)
        taps.append(jnp.concatenate(ordered[start : start + count], 0).astype(bf16))
    return jnp.concatenate(taps, axis=1)


def activated(wide):
    part = 0.5 * rms(wide)
    return part + part * jnp.tanh(part)


def depth(parts):
    return parts[0] if len(parts) == 1 else jnp.concatenate(parts, axis=-1)


def edge_kernel(count, rows, video, edge, vid):
    sources, step, chans = video.shape
    span = step // (count * rows)
    fill(vid, 0, video[...].reshape(sources * step, chans).astype(f32))
    row = (rows - 1) * (1 - lax.axis_index("height"))
    for w in range(span):
        edge[w] = shifted([activated(x) for x in frames_of(vid, w, row, count, rows, sources, step)])


def fill_bias(bias, ids, frames, count):
    area = bias.shape[0]
    sources = frames // count

    def place_of(at):
        pixel, place = divided(at, frames)
        inner, source = divided(place, sources)
        frame = source * count + inner
        block = jnp.zeros(at.shape, jnp.int32)
        for s in range(frames):
            block = jnp.where(frame == s, ids[s], block)
        return pixel, frame, block

    row_p, row_t, row_b = place_of(lax.broadcasted_iota(jnp.int32, (area, area), 0))
    col_p, col_t, col_b = place_of(lax.broadcasted_iota(jnp.int32, (1, area), 1))
    permit = (row_p == col_p) & (col_t <= row_t) & (col_b >= row_b - 1)
    bias[...] = jnp.where(permit, 0.0, -1e30)


def shift_kernel(count, rows, video, ids_far, *refs):
    conv_weight, far, (total, bias, *near) = refs[0], refs[1:5], refs[5:11]
    vid, grid, ids, sems, ids_sem = refs[11:]
    ids_copy = pltpu.make_async_copy(ids_far, ids, ids_sem)
    ids_copy.start()
    others = [pltpu.make_async_copy(src, dst, sems.at[i]) for i, (src, dst) in enumerate(zip(far, near))]
    for copy in others:
        copy.start()
    sources, step, chans = video.shape
    span = step // (count * rows)
    own = span - 2
    frames = sources * count
    half = own // 2 if own % 2 == 0 else own
    fill(vid, 0, video[...].reshape(sources * step, chans).astype(f32))
    for w in range(span):
        for r in range(rows):
            now = frames_of(vid, w, r, count, rows, sources, step)
            grid[w, r] = shifted([activated(x) for x in now])
            if 1 <= w <= own:
                total[w - 1, r] = jnp.concatenate(now, 0)

    for b in range(TAPS):
        low, high = max(0, 1 - b), min(rows, rows + 1 - b)
        weight = jnp.concatenate([conv_weight[a, b, e] for e in range(TAPS) for a in range(TAPS)], axis=0)
        for w in range(0, own, half):
            window = depth([grid[w + e : w + e + half, low + b - 1 : high + b - 1] for e in range(TAPS)])
            window = window.reshape(half * (high - low) * frames, TAPS * TAPS * chans)
            part = jnp.dot(window, weight, preferred_element_type=f32)
            some = total.at[w : w + half, low:high]
            some[...] = some[...] + part.reshape(half, high - low, frames, chans)
    ids_copy.wait()
    fill_bias(bias, ids, frames, count)
    for copy in others:
        copy.wait()


def main_kernel(
    count, rows, group, edge, given, bias, conv_weight, w_query, w_key, w_value, w_output, *refs
):
    out, res = refs
    own, _, frames, chans = given.shape
    sources = frames // count
    lines = count * rows
    back = own * lines
    area = bias.shape[0]

    lower = lax.axis_index("height")
    b = (TAPS - 1) * (1 - lower)
    part = jnp.zeros((own * frames, chans), f32)
    for e in range(TAPS):
        window = edge[e : e + own].reshape(own * frames, TAPS * chans)
        weight = jnp.concatenate([conv_weight[a, b, e] for a in range(TAPS)], axis=0)
        part = part + jnp.dot(window, weight, preferred_element_type=f32)
    part = part.reshape(own, frames, chans)

    head_of = divided(lax.broadcasted_iota(jnp.int32, (area, LANES), 1), HD)[0]
    single = [jnp.where(head_of == h, 1.0, 0.0).astype(bf16) for h in range(LANES // HD)]
    scaled = [mask * jnp.asarray(HD ** (-0.5), bf16) for mask in single]

    lines_of = []
    for r in range(rows):
        row = given[:, r] + jnp.where(r == (rows - 1) * (1 - lower), part, 0.0)
        lines_of.append(row[:, None])
    hidden = jnp.concatenate(lines_of, axis=1).reshape(own * rows * frames, chans).astype(bf16).astype(f32)
    normed = rms(hidden).astype(bf16)
    query, keys, values = (
        jnp.dot(normed, weight[...], preferred_element_type=f32).astype(bf16) for weight in (w_query, w_key, w_value)
    )
    gone = []
    for at in range(0, own * rows * frames, area):
        attended = []
        for lane in range(0, chans, LANES):
            block = (slice(at, at + area), slice(lane, lane + LANES))
            queries = jnp.concatenate([query[block] * mask for mask in scaled], axis=0)
            scores = lax.dot_general(queries, keys[block], (((1,), (1,)), ((), ())), preferred_element_type=f32)
            weights = []
            for h in range(len(single)):
                score = scores[h * area : (h + 1) * area] + bias[...]
                weights.append(jnp.exp(score - jnp.max(score, axis=-1, keepdims=True)).astype(bf16))
            heads_values = jnp.concatenate(
                [jnp.concatenate([values[block] * mask, mask], axis=1) for mask in single], axis=0
            )
            mixed = jnp.dot(jnp.concatenate(weights, axis=1), heads_values, preferred_element_type=f32)
            attended.append((mixed[:, :LANES] / mixed[:, LANES:]).astype(bf16))
        gone.append(jnp.concatenate(attended, axis=1))
    encoded = hidden + jnp.dot(jnp.concatenate(gone, axis=0), w_output[...], preferred_element_type=f32)
    for w in range(own):
        for r in range(rows):
            for t in range(count):
                first = ((w * rows + r) * count + t + 1) * sources - group
                put(res, (t * rows + r) * own + w, group, back, encoded[first : first + group])
    done = jnp.concatenate([res[i] for i in range(res.shape[0])], axis=1)
    out[...] = done.astype(bf16).reshape(out.shape)


def exchanged(blocks):
    return lax.all_to_all(blocks, "tm", split_axis=0, concat_axis=0, tiled=True)


def per_device(outer, video, block_ids, conv_weight, w_query, w_key, w_value, w_output):
    count, rows, cols, chans = video.shape
    group = lax.axis_size("tm")
    own = cols // group
    span = own + 2
    lines = count * rows
    near = pl.BlockSpec(memory_space=pltpu.VMEM)
    far = pl.BlockSpec(memory_space=pltpu.HBM)
    params = pltpu.CompilerParams(vmem_limit_bytes=VMEM)
    in_far = functools.partial(pltpu.with_memory_space_constraint, memory_space=pltpu.HBM)
    weights = [in_far(x) for x in (w_query, w_key, w_value, w_output)]

    blocks = pl.pallas_call(
        functools.partial(pack_kernel, group),
        out_shape=jax.ShapeDtypeStruct((group, span * lines, chans), bf16),
        in_specs=[far],
        out_specs=near,
        scratch_shapes=[
            pltpu.VMEM(video.shape, bf16),
            scratch(lines * (cols + 2 * EDGE), chans),
            pltpu.SemaphoreType.DMA((lines,)),
        ],
        compiler_params=params,
        cost_estimate=pl.CostEstimate(flops=2000000000, transcendentals=0, bytes_accessed=1000000),
    )(in_far(video))
    piece = exchanged(blocks)
    ids = block_ids
    if outer > 1:
        before = lax.ppermute(piece, "outer", [(i, i + 1) for i in range(outer - 1)])
        piece = jnp.concatenate([before, piece], axis=0)
        ids = jnp.concatenate([jnp.full((group * count,), -2, jnp.int32), ids])
        ids = lax.dynamic_slice(ids, (lax.axis_index("outer") * group * count,), (2 * group * count,))
    sources = piece.shape[0]
    frames = sources * count
    stored = scratch(sources * span * lines, chans)
    edge = pl.pallas_call(
        functools.partial(edge_kernel, count, rows),
        out_shape=jax.ShapeDtypeStruct((span, frames, TAPS * chans), bf16),
        in_specs=[near],
        out_specs=near,
        scratch_shapes=[stored],
        compiler_params=params,
    )(piece)
    edge = lax.ppermute(edge, "height", [(0, 1), (1, 0)])
    several = max(n for n in range(1, own + 1) if own % n == 0 and (n == 1 or n * rows * frames <= LANES))
    area = several * rows * frames
    total, bias, *weights = pl.pallas_call(
        functools.partial(shift_kernel, count, rows),
        out_shape=[
            jax.ShapeDtypeStruct((own, rows, frames, chans), f32),
            jax.ShapeDtypeStruct((area, area), f32),
        ]
        + [jax.ShapeDtypeStruct(x.shape, bf16) for x in weights],
        in_specs=[near, far, near] + [far] * 4,
        out_specs=[near] * 6,
        scratch_shapes=[
            stored,
            pltpu.VMEM((span, rows, frames, TAPS * chans), bf16),
            pltpu.SMEM((frames,), jnp.int32),
            pltpu.SemaphoreType.DMA((4,)),
            pltpu.SemaphoreType.DMA(()),
        ],
        compiler_params=params,
    )(piece, in_far(ids), conv_weight, *weights)
    blocks = pl.pallas_call(
        functools.partial(main_kernel, count, rows, group),
        out_shape=jax.ShapeDtypeStruct((group, own * lines, chans), bf16),
        in_specs=[near] * 8,
        out_specs=near,
        scratch_shapes=[scratch(group * own * lines, chans)],
        compiler_params=params,
    )(edge, total, bias, conv_weight, *weights)
    returned = exchanged(blocks).reshape(group, lines, own, chans)
    return jnp.swapaxes(returned, 0, 1).reshape(video.shape)


def solution(mesh):
    parts, along, halves = (mesh.shape[a] for a in ("groups", "tm", "height"))

    def run(video, *rest):
        count = video.shape[0] // (parts * along)
        group = min(g for g in range(1, along + 1) if along % g == 0 and (g * count >= REACH or g == along))
        outer = along // group
        split = Mesh(
            np.asarray(mesh.devices).reshape(parts, outer, group, halves),
            ("groups", "outer", "tm", "height"),
        )
        spec = P(("groups", "outer", "tm"), "height", None, None)
        placed = (spec, P("groups"), P(), P(), P(), P(), P())
        return jax.shard_map(
            functools.partial(per_device, outer),
            mesh=split,
            in_specs=placed,
            out_specs=spec,
            check_vma=False,
        )(video, *rest)

    return run
```

```python
import functools

import jax
import jax.numpy as jnp
import numpy as np
from jax import lax
from jax.experimental import pallas as pl
from jax.experimental.pallas import tpu as pltpu
from jax.sharding import Mesh, PartitionSpec as P

HD = 64
BLOCK = 4
TAPS = 3
REACH = 2 * BLOCK - 1 + TAPS - 1
LANES = 128
EDGE = 8
VMEM = 28 * 2**20

bf16, f32 = jnp.bfloat16, jnp.float32


def get(ref, start, size, stride):
    return jnp.concatenate([ref[i, pl.ds(start, size, stride=stride), :] for i in range(ref.shape[0])], axis=1)


def put(ref, start, size, stride, value):
    for i in range(ref.shape[0]):
        ref[i, pl.ds(start, size, stride=stride), :] = value[:, i * LANES : (i + 1) * LANES]


def fill(ref, start, value):
    for i in range(ref.shape[0]):
        ref[i, pl.ds(start, value.shape[0]), :] = value[:, i * LANES : (i + 1) * LANES]


def scratch(rows, chans):
    return pltpu.VMEM((chans // LANES, rows, LANES), f32)


def rms(wide):
    return wide * lax.rsqrt(jnp.mean(wide * wide, axis=-1, keepdims=True) + 1e-06)


def divided(at, by):
    if by & (by - 1) == 0:
        bits = by.bit_length() - 1
        return at >> bits, at & (by - 1)
    return lax.div(at, jnp.int32(by)), lax.rem(at, jnp.int32(by))


def pack_kernel(group, ids_far, video, out, ids, near_ids, local, wide, sems, ids_sem):
    ids_copy = pltpu.make_async_copy(ids_far, near_ids, ids_sem)
    ids_copy.start()
    count, rows, cols, chans = video.shape
    lines = count * rows
    stride = cols + 2 * EDGE
    own = cols // group
    span = own + 2
    copies = []
    for at in range(lines):
        place = (at // rows, at % rows)
        copy = pltpu.make_async_copy(video.at[place], local.at[place], sems.at[at])
        copy.start()
        copies.append(copy)
    nothing = jnp.zeros((EDGE, chans), f32)
    for at in range(lines):
        fill(wide, at * stride, nothing)
        fill(wide, at * stride + EDGE + cols, nothing)
    ids_copy.wait()
    for s in range(ids.shape[0]):
        ids[s : s + 1, :] = jnp.full((1, LANES), near_ids[s], jnp.int32)
    for at, copy in enumerate(copies):
        copy.wait()
        fill(wide, at * stride + EDGE, local[at // rows, at % rows].astype(f32))
    together = 16 // lines
    for k in range(group):
        start = k * own + EDGE - 1
        for w in range(0, span, together):
            tile = jnp.concatenate([get(wide, start + w + i, lines, stride) for i in range(together)], axis=0)
            out[k, pl.ds(w * lines, 16), :] = tile.astype(bf16)


def frames_of(ref, w, r, count, rows, sources, step):
    return [get(ref, w * count * rows + t * rows + r, sources, step) for t in range(count)]


def shifted(now):
    count = len(now)
    sources, chans = now[0].shape
    first = lax.broadcasted_iota(jnp.int32, (sources, chans), 0) == 0
    past = [jnp.where(first, 0.0, pltpu.roll(x, 1, 0)) for x in now]
    ordered = past + now
    taps = []
    for a in range(TAPS):
        start = count - (TAPS - 1 - a)
        taps.append(jnp.concatenate(ordered[start : start + count], 0).astype(bf16))
    return jnp.concatenate(taps, axis=1)


def activated(wide):
    part = 0.5 * rms(wide)
    return part + part * jnp.tanh(part)


def depth(parts):
    return parts[0] if len(parts) == 1 else jnp.concatenate(parts, axis=-1)


def edge_kernel(count, rows, video, edge, vid):
    sources, step, chans = video.shape
    span = step // (count * rows)
    fill(vid, 0, video[...].reshape(sources * step, chans).astype(f32))
    row = (rows - 1) * (1 - lax.axis_index("height"))
    for w in range(span):
        edge[w] = shifted([activated(x) for x in frames_of(vid, w, row, count, rows, sources, step)])


def fill_bias(bias, ids, frames, count):
    area = bias.shape[0]
    sources = frames // count

    def place_of(at):
        pixel, place = divided(at, frames)
        inner, source = divided(place, sources)
        frame = source * count + inner
        block = jnp.zeros(at.shape, jnp.int32)
        for s in range(frames):
            block = jnp.where(frame == s, ids[s : s + 1, :area], block)
        return pixel, frame, block

    row_p, row_t, row_b = place_of(lax.broadcasted_iota(jnp.int32, (area, area), 0))
    col_p, col_t, col_b = place_of(lax.broadcasted_iota(jnp.int32, (1, area), 1))
    permit = (row_p == col_p) & (col_t <= row_t) & (col_b >= row_b - 1)
    bias[...] = jnp.where(permit, 0.0, -1e30)


def shift_kernel(count, rows, vid, ids, conv_weight, *refs):
    far, (total, bias, *near), (grid, sems) = refs[:4], refs[4:10], refs[10:]
    others = [pltpu.make_async_copy(src, dst, sems.at[i]) for i, (src, dst) in enumerate(zip(far, near))]
    for copy in others:
        copy.start()
    own, _, frames, chans = total.shape
    span = own + 2
    sources = frames // count
    step = span * count * rows
    half = own // 2 if own % 2 == 0 else own
    for w in range(span):
        for r in range(rows):
            now = frames_of(vid, w, r, count, rows, sources, step)
            grid[w, r] = shifted([activated(x) for x in now])
            if 1 <= w <= own:
                total[w - 1, r] = jnp.concatenate(now, 0)

    for b in range(TAPS):
        low, high = max(0, 1 - b), min(rows, rows + 1 - b)
        weight = jnp.concatenate([conv_weight[a, b, e] for e in range(TAPS) for a in range(TAPS)], axis=0)
        for w in range(0, own, half):
            window = depth([grid[w + e : w + e + half, low + b - 1 : high + b - 1] for e in range(TAPS)])
            window = window.reshape(half * (high - low) * frames, TAPS * TAPS * chans)
            part = jnp.dot(window, weight, preferred_element_type=f32)
            some = total.at[w : w + half, low:high]
            some[...] = some[...] + part.reshape(half, high - low, frames, chans)
    fill_bias(bias, ids, frames, count)
    for copy in others:
        copy.wait()


def main_kernel(
    count, rows, group, edge, given, bias, conv_weight, w_query, w_key, w_value, w_output, *refs
):
    out, res = refs
    own, _, frames, chans = given.shape
    sources = frames // count
    lines = count * rows
    back = own * lines
    area = bias.shape[0]

    lower = lax.axis_index("height")
    b = (TAPS - 1) * (1 - lower)
    part = jnp.zeros((own * frames, chans), f32)
    for e in range(TAPS):
        window = edge[e : e + own].reshape(own * frames, TAPS * chans)
        weight = jnp.concatenate([conv_weight[a, b, e] for a in range(TAPS)], axis=0)
        part = part + jnp.dot(window, weight, preferred_element_type=f32)
    part = part.reshape(own, frames, chans)

    head_of = divided(lax.broadcasted_iota(jnp.int32, (area, LANES), 1), HD)[0]
    single = [jnp.where(head_of == h, 1.0, 0.0).astype(bf16) for h in range(LANES // HD)]
    scaled = [mask * jnp.asarray(HD ** (-0.5), bf16) for mask in single]

    lines_of = []
    for r in range(rows):
        row = given[:, r] + jnp.where(r == (rows - 1) * (1 - lower), part, 0.0)
        lines_of.append(row[:, None])
    hidden = jnp.concatenate(lines_of, axis=1).reshape(own * rows * frames, chans).astype(bf16).astype(f32)
    normed = rms(hidden).astype(bf16)
    query, keys, values = (
        jnp.dot(normed, weight[...], preferred_element_type=f32).astype(bf16) for weight in (w_query, w_key, w_value)
    )
    gone = []
    for at in range(0, own * rows * frames, area):
        attended = []
        for lane in range(0, chans, LANES):
            block = (slice(at, at + area), slice(lane, lane + LANES))
            queries = jnp.concatenate([query[block] * mask for mask in scaled], axis=0)
            scores = lax.dot_general(queries, keys[block], (((1,), (1,)), ((), ())), preferred_element_type=f32)
            weights = []
            for h in range(len(single)):
                score = scores[h * area : (h + 1) * area] + bias[...]
                weights.append(jnp.exp(score - jnp.max(score, axis=-1, keepdims=True)).astype(bf16))
            heads_values = jnp.concatenate(
                [jnp.concatenate([values[block] * mask, mask], axis=1) for mask in single], axis=0
            )
            mixed = jnp.dot(jnp.concatenate(weights, axis=1), heads_values, preferred_element_type=f32)
            attended.append((mixed[:, :LANES] / mixed[:, LANES:]).astype(bf16))
        gone.append(jnp.concatenate(attended, axis=1))
    encoded = hidden + jnp.dot(jnp.concatenate(gone, axis=0), w_output[...], preferred_element_type=f32)
    for w in range(own):
        for r in range(rows):
            for t in range(count):
                first = ((w * rows + r) * count + t + 1) * sources - group
                put(res, (t * rows + r) * own + w, group, back, encoded[first : first + group])
    done = jnp.concatenate([res[i] for i in range(res.shape[0])], axis=1)
    out[...] = done.astype(bf16).reshape(out.shape)


def exchanged(blocks):
    return lax.all_to_all(blocks, "tm", split_axis=0, concat_axis=0, tiled=True)


def per_device(outer, video, block_ids, conv_weight, w_query, w_key, w_value, w_output):
    count, rows, cols, chans = video.shape
    group = lax.axis_size("tm")
    own = cols // group
    span = own + 2
    lines = count * rows
    near = pl.BlockSpec(memory_space=pltpu.VMEM)
    far = pl.BlockSpec(memory_space=pltpu.HBM)
    params = pltpu.CompilerParams(vmem_limit_bytes=VMEM)
    in_far = functools.partial(pltpu.with_memory_space_constraint, memory_space=pltpu.HBM)
    weights = [in_far(x) for x in (w_query, w_key, w_value, w_output)]

    sources = group * (2 if outer > 1 else 1)
    frames = sources * count
    ids = block_ids
    if outer > 1:
        ids = jnp.concatenate([jnp.full((group * count,), -2, jnp.int32), ids])
        ids = lax.dynamic_slice(ids, (lax.axis_index("outer") * group * count,), (frames,))
    blocks, ids = pl.pallas_call(
        functools.partial(pack_kernel, group),
        out_shape=[
            jax.ShapeDtypeStruct((group, span * lines, chans), bf16),
            jax.ShapeDtypeStruct((frames, LANES), jnp.int32),
        ],
        in_specs=[far, far],
        out_specs=[near, near],
        scratch_shapes=[
            pltpu.SMEM((frames,), jnp.int32),
            pltpu.VMEM(video.shape, bf16),
            scratch(lines * (cols + 2 * EDGE), chans),
            pltpu.SemaphoreType.DMA((lines,)),
            pltpu.SemaphoreType.DMA(()),
        ],
        compiler_params=params,
        cost_estimate=pl.CostEstimate(flops=2000000000, transcendentals=0, bytes_accessed=1000000),
    )(in_far(ids), in_far(video))
    piece = exchanged(blocks)
    if outer > 1:
        before = lax.ppermute(piece, "outer", [(i, i + 1) for i in range(outer - 1)])
        piece = jnp.concatenate([before, piece], axis=0)
    edge, wide = pl.pallas_call(
        functools.partial(edge_kernel, count, rows),
        out_shape=[
            jax.ShapeDtypeStruct((span, frames, TAPS * chans), bf16),
            jax.ShapeDtypeStruct((chans // LANES, sources * span * lines, LANES), f32),
        ],
        in_specs=[near],
        out_specs=[near, near],
        compiler_params=params,
    )(piece)
    edge = lax.ppermute(edge, "height", [(0, 1), (1, 0)])
    several = max(n for n in range(1, own + 1) if own % n == 0 and (n == 1 or n * rows * frames <= LANES))
    area = several * rows * frames
    total, bias, *weights = pl.pallas_call(
        functools.partial(shift_kernel, count, rows),
        out_shape=[
            jax.ShapeDtypeStruct((own, rows, frames, chans), f32),
            jax.ShapeDtypeStruct((area, area), f32),
        ]
        + [jax.ShapeDtypeStruct(x.shape, bf16) for x in weights],
        in_specs=[near] * 3 + [far] * 4,
        out_specs=[near] * 6,
        scratch_shapes=[
            pltpu.VMEM((span, rows, frames, TAPS * chans), bf16),
            pltpu.SemaphoreType.DMA((4,)),
        ],
        compiler_params=params,
    )(wide, ids, conv_weight, *weights)
    blocks = pl.pallas_call(
        functools.partial(main_kernel, count, rows, group),
        out_shape=jax.ShapeDtypeStruct((group, own * lines, chans), bf16),
        in_specs=[near] * 8,
        out_specs=near,
        scratch_shapes=[scratch(group * own * lines, chans)],
        compiler_params=params,
    )(edge, total, bias, conv_weight, *weights)
    returned = exchanged(blocks).reshape(group, lines, own, chans)
    return jnp.swapaxes(returned, 0, 1).reshape(video.shape)


def solution(mesh):
    parts, along, halves = (mesh.shape[a] for a in ("groups", "tm", "height"))

    def run(video, *rest):
        count = video.shape[0] // (parts * along)
        group = min(g for g in range(1, along + 1) if along % g == 0 and (g * count >= REACH or g == along))
        outer = along // group
        split = Mesh(
            np.asarray(mesh.devices).reshape(parts, outer, group, halves),
            ("groups", "outer", "tm", "height"),
        )
        spec = P(("groups", "outer", "tm"), "height", None, None)
        placed = (spec, P("groups"), P(), P(), P(), P(), P())
        return jax.shard_map(
            functools.partial(per_device, outer),
            mesh=split,
            in_specs=placed,
            out_specs=spec,
            check_vma=False,
        )(video, *rest)

    return run
```

```python
import functools

import jax
import jax.numpy as jnp
import numpy as np
from jax import lax
from jax.experimental import pallas as pl
from jax.experimental.pallas import tpu as pltpu
from jax.sharding import Mesh, PartitionSpec as P

HD = 64
BLOCK = 4
TAPS = 3
REACH = 2 * BLOCK - 1 + TAPS - 1
LANES = 128
EDGE = 8
VMEM = 28 * 2**20

bf16, f32 = jnp.bfloat16, jnp.float32


def get(ref, start, size, stride):
    return jnp.concatenate([ref[i, pl.ds(start, size, stride=stride), :] for i in range(ref.shape[0])], axis=1)


def put(ref, start, size, stride, value):
    for i in range(ref.shape[0]):
        ref[i, pl.ds(start, size, stride=stride), :] = value[:, i * LANES : (i + 1) * LANES]


def fill(ref, start, value):
    for i in range(ref.shape[0]):
        ref[i, pl.ds(start, value.shape[0]), :] = value[:, i * LANES : (i + 1) * LANES]


def scratch(rows, chans):
    return pltpu.VMEM((chans // LANES, rows, LANES), f32)


def rms(wide):
    return wide * lax.rsqrt(jnp.mean(wide * wide, axis=-1, keepdims=True) + 1e-06)


def divided(at, by):
    if by & (by - 1) == 0:
        bits = by.bit_length() - 1
        return at >> bits, at & (by - 1)
    return lax.div(at, jnp.int32(by)), lax.rem(at, jnp.int32(by))


def pack_kernel(group, video, *refs):
    out, local, wide, sems = refs
    count, rows, cols, chans = video.shape
    lines = count * rows
    stride = cols + 2 * EDGE
    own = cols // group
    span = own + 2
    copies = []
    for at in range(lines):
        place = (at // rows, at % rows)
        copy = pltpu.make_async_copy(video.at[place], local.at[place], sems.at[at])
        copy.start()
        copies.append(copy)
    nothing = jnp.zeros((EDGE, chans), f32)
    for at in range(lines):
        fill(wide, at * stride, nothing)
        fill(wide, at * stride + EDGE + cols, nothing)
    for at, copy in enumerate(copies):
        copy.wait()
        fill(wide, at * stride + EDGE, local[at // rows, at % rows].astype(f32))
    together = 16 // lines
    for k in range(group):
        start = k * own + EDGE - 1
        for w in range(0, span, together):
            tile = jnp.concatenate([get(wide, start + w + i, lines, stride) for i in range(together)], axis=0)
            out[k, pl.ds(w * lines, 16), :] = tile.astype(bf16)


def frames_of(ref, w, r, count, rows, sources, step):
    return [get(ref, w * count * rows + t * rows + r, sources, step) for t in range(count)]


def shifted(now):
    count = len(now)
    sources, chans = now[0].shape
    first = lax.broadcasted_iota(jnp.int32, (sources, chans), 0) == 0
    past = [jnp.where(first, 0.0, pltpu.roll(x, 1, 0)) for x in now]
    ordered = past + now
    taps = []
    for a in range(TAPS):
        start = count - (TAPS - 1 - a)
        taps.append(jnp.concatenate(ordered[start : start + count], 0).astype(bf16))
    return jnp.concatenate(taps, axis=1)


def activated(wide):
    part = 0.5 * rms(wide)
    return part + part * jnp.tanh(part)


def depth(parts):
    return parts[0] if len(parts) == 1 else jnp.concatenate(parts, axis=-1)


def edge_kernel(count, rows, video, edge, vid):
    sources, step, chans = video.shape
    span = step // (count * rows)
    fill(vid, 0, video[...].reshape(sources * step, chans).astype(f32))
    row = (rows - 1) * (1 - lax.axis_index("height"))
    for w in range(span):
        edge[w] = shifted([activated(x) for x in frames_of(vid, w, row, count, rows, sources, step)])


def fill_bias(bias, ids, frames, count):
    area = bias.shape[0]
    sources = frames // count

    def place_of(at):
        pixel, place = divided(at, frames)
        inner, source = divided(place, sources)
        frame = source * count + inner
        block = jnp.zeros(at.shape, jnp.int32)
        for s in range(frames):
            block = jnp.where(frame == s, ids[s], block)
        return pixel, frame, block

    row_p, row_t, row_b = place_of(lax.broadcasted_iota(jnp.int32, (area, area), 0))
    col_p, col_t, col_b = place_of(lax.broadcasted_iota(jnp.int32, (1, area), 1))
    permit = (row_p == col_p) & (col_t <= row_t) & (col_b >= row_b - 1)
    bias[...] = jnp.where(permit, 0.0, -1e30)


def shift_kernel(count, rows, video, ids_far, *refs):
    conv_weight, far, (total, bias, *near) = refs[0], refs[1:5], refs[5:11]
    vid, grid, ids, sems, ids_sem = refs[11:]
    ids_copy = pltpu.make_async_copy(ids_far, ids, ids_sem)
    ids_copy.start()
    others = [pltpu.make_async_copy(src, dst, sems.at[i]) for i, (src, dst) in enumerate(zip(far, near))]
    for copy in others:
        copy.start()
    sources, step, chans = video.shape
    span = step // (count * rows)
    own = span - 2
    frames = sources * count
    half = own // 2 if own % 2 == 0 else own
    fill(vid, 0, video[...].reshape(sources * step, chans).astype(f32))
    for w in range(span):
        for r in range(rows):
            now = frames_of(vid, w, r, count, rows, sources, step)
            grid[w, r] = shifted([activated(x) for x in now])
            if 1 <= w <= own:
                total[w - 1, r] = jnp.concatenate(now, 0)

    for b in range(TAPS):
        low, high = max(0, 1 - b), min(rows, rows + 1 - b)
        weight = jnp.concatenate([conv_weight[a, b, e] for e in range(TAPS) for a in range(TAPS)], axis=0)
        for w in range(0, own, half):
            window = depth([grid[w + e : w + e + half, low + b - 1 : high + b - 1] for e in range(TAPS)])
            window = window.reshape(half * (high - low) * frames, TAPS * TAPS * chans)
            part = jnp.dot(window, weight, preferred_element_type=f32)
            some = total.at[w : w + half, low:high]
            some[...] = some[...] + part.reshape(half, high - low, frames, chans)
    ids_copy.wait()
    fill_bias(bias, ids, frames, count)
    for copy in others:
        copy.wait()


def main_kernel(
    count, rows, group, edge, given, bias, conv_weight, w_query, w_key, w_value, w_output, *refs
):
    out, res = refs
    own, _, frames, chans = given.shape
    sources = frames // count
    lines = count * rows
    back = own * lines
    area = bias.shape[0]

    lower = lax.axis_index("height")
    b = (TAPS - 1) * (1 - lower)
    part = jnp.zeros((own * frames, chans), f32)
    for e in range(TAPS):
        window = edge[e : e + own].reshape(own * frames, TAPS * chans)
        weight = jnp.concatenate([conv_weight[a, b, e] for a in range(TAPS)], axis=0)
        part = part + jnp.dot(window, weight, preferred_element_type=f32)
    part = part.reshape(own, frames, chans)

    head_of = divided(lax.broadcasted_iota(jnp.int32, (area, LANES), 1), HD)[0]
    single = [jnp.where(head_of == h, 1.0, 0.0).astype(bf16) for h in range(LANES // HD)]
    scaled = [mask * jnp.asarray(HD ** (-0.5), bf16) for mask in single]

    lines_of = []
    for r in range(rows):
        row = given[:, r] + jnp.where(r == (rows - 1) * (1 - lower), part, 0.0)
        lines_of.append(row[:, None])
    hidden = jnp.concatenate(lines_of, axis=1).reshape(own * rows * frames, chans).astype(bf16).astype(f32)
    normed = rms(hidden).astype(bf16)
    weight = jnp.concatenate([w_query[...], w_key[...], w_value[...]], axis=1)
    projected = jnp.dot(normed, weight, preferred_element_type=f32).astype(bf16)
    query, keys, values = (projected[:, i * chans : (i + 1) * chans] for i in range(3))
    gone = []
    for at in range(0, own * rows * frames, area):
        attended = []
        for lane in range(0, chans, LANES):
            block = (slice(at, at + area), slice(lane, lane + LANES))
            queries = jnp.concatenate([query[block] * mask for mask in scaled], axis=0)
            scores = lax.dot_general(queries, keys[block], (((1,), (1,)), ((), ())), preferred_element_type=f32)
            weights = []
            for h in range(len(single)):
                score = scores[h * area : (h + 1) * area] + bias[...]
                weights.append(jnp.exp(score - jnp.max(score, axis=-1, keepdims=True)).astype(bf16))
            heads_values = jnp.concatenate(
                [jnp.concatenate([values[block] * mask, mask], axis=1) for mask in single], axis=0
            )
            mixed = jnp.dot(jnp.concatenate(weights, axis=1), heads_values, preferred_element_type=f32)
            attended.append((mixed[:, :LANES] / mixed[:, LANES:]).astype(bf16))
        gone.append(jnp.concatenate(attended, axis=1))
    encoded = hidden + jnp.dot(jnp.concatenate(gone, axis=0), w_output[...], preferred_element_type=f32)
    for w in range(own):
        for r in range(rows):
            for t in range(count):
                first = ((w * rows + r) * count + t + 1) * sources - group
                put(res, (t * rows + r) * own + w, group, back, encoded[first : first + group])
    done = jnp.concatenate([res[i] for i in range(res.shape[0])], axis=1)
    out[...] = done.astype(bf16).reshape(out.shape)


def exchanged(blocks):
    return lax.all_to_all(blocks, "tm", split_axis=0, concat_axis=0, tiled=True)


def per_device(outer, video, block_ids, conv_weight, w_query, w_key, w_value, w_output):
    count, rows, cols, chans = video.shape
    group = lax.axis_size("tm")
    own = cols // group
    span = own + 2
    lines = count * rows
    near = pl.BlockSpec(memory_space=pltpu.VMEM)
    far = pl.BlockSpec(memory_space=pltpu.HBM)
    params = pltpu.CompilerParams(vmem_limit_bytes=VMEM)
    in_far = functools.partial(pltpu.with_memory_space_constraint, memory_space=pltpu.HBM)
    weights = [in_far(x) for x in (w_query, w_key, w_value, w_output)]

    blocks = pl.pallas_call(
        functools.partial(pack_kernel, group),
        out_shape=jax.ShapeDtypeStruct((group, span * lines, chans), bf16),
        in_specs=[far],
        out_specs=near,
        scratch_shapes=[
            pltpu.VMEM(video.shape, bf16),
            scratch(lines * (cols + 2 * EDGE), chans),
            pltpu.SemaphoreType.DMA((lines,)),
        ],
        compiler_params=params,
        cost_estimate=pl.CostEstimate(flops=2000000000, transcendentals=0, bytes_accessed=1000000),
    )(in_far(video))
    piece = exchanged(blocks)
    ids = block_ids
    if outer > 1:
        before = lax.ppermute(piece, "outer", [(i, i + 1) for i in range(outer - 1)])
        piece = jnp.concatenate([before, piece], axis=0)
        ids = jnp.concatenate([jnp.full((group * count,), -2, jnp.int32), ids])
        ids = lax.dynamic_slice(ids, (lax.axis_index("outer") * group * count,), (2 * group * count,))
    sources = piece.shape[0]
    frames = sources * count
    stored = scratch(sources * span * lines, chans)
    edge = pl.pallas_call(
        functools.partial(edge_kernel, count, rows),
        out_shape=jax.ShapeDtypeStruct((span, frames, TAPS * chans), bf16),
        in_specs=[near],
        out_specs=near,
        scratch_shapes=[stored],
        compiler_params=params,
    )(piece)
    edge = lax.ppermute(edge, "height", [(0, 1), (1, 0)])
    several = max(n for n in range(1, own + 1) if own % n == 0 and (n == 1 or n * rows * frames <= LANES))
    area = several * rows * frames
    total, bias, *weights = pl.pallas_call(
        functools.partial(shift_kernel, count, rows),
        out_shape=[
            jax.ShapeDtypeStruct((own, rows, frames, chans), f32),
            jax.ShapeDtypeStruct((area, area), f32),
        ]
        + [jax.ShapeDtypeStruct(x.shape, bf16) for x in weights],
        in_specs=[near, far, near] + [far] * 4,
        out_specs=[near] * 6,
        scratch_shapes=[
            stored,
            pltpu.VMEM((span, rows, frames, TAPS * chans), bf16),
            pltpu.SMEM((frames,), jnp.int32),
            pltpu.SemaphoreType.DMA((4,)),
            pltpu.SemaphoreType.DMA(()),
        ],
        compiler_params=params,
    )(piece, in_far(ids), conv_weight, *weights)
    blocks = pl.pallas_call(
        functools.partial(main_kernel, count, rows, group),
        out_shape=jax.ShapeDtypeStruct((group, own * lines, chans), bf16),
        in_specs=[near] * 8,
        out_specs=near,
        scratch_shapes=[scratch(group * own * lines, chans)],
        compiler_params=params,
    )(edge, total, bias, conv_weight, *weights)
    returned = exchanged(blocks).reshape(group, lines, own, chans)
    return jnp.swapaxes(returned, 0, 1).reshape(video.shape)


def solution(mesh):
    parts, along, halves = (mesh.shape[a] for a in ("groups", "tm", "height"))

    def run(video, *rest):
        count = video.shape[0] // (parts * along)
        group = min(g for g in range(1, along + 1) if along % g == 0 and (g * count >= REACH or g == along))
        outer = along // group
        split = Mesh(
            np.asarray(mesh.devices).reshape(parts, outer, group, halves),
            ("groups", "outer", "tm", "height"),
        )
        spec = P(("groups", "outer", "tm"), "height", None, None)
        placed = (spec, P("groups"), P(), P(), P(), P(), P())
        return jax.shard_map(
            functools.partial(per_device, outer),
            mesh=split,
            in_specs=placed,
            out_specs=spec,
            check_vma=False,
        )(video, *rest)

    return run
```

```python
import functools

import jax
import jax.numpy as jnp
import numpy as np
from jax import lax
from jax.experimental import pallas as pl
from jax.experimental.pallas import tpu as pltpu
from jax.sharding import Mesh, PartitionSpec as P

HD = 64
BLOCK = 4
TAPS = 3
REACH = 2 * BLOCK - 1 + TAPS - 1
LANES = 128
EDGE = 8
VMEM = 28 * 2**20

bf16, f32 = jnp.bfloat16, jnp.float32


def get(ref, start, size, stride):
    return jnp.concatenate([ref[i, pl.ds(start, size, stride=stride), :] for i in range(ref.shape[0])], axis=1)


def put(ref, start, size, stride, value):
    for i in range(ref.shape[0]):
        ref[i, pl.ds(start, size, stride=stride), :] = value[:, i * LANES : (i + 1) * LANES]


def fill(ref, start, value):
    for i in range(ref.shape[0]):
        ref[i, pl.ds(start, value.shape[0]), :] = value[:, i * LANES : (i + 1) * LANES]


def scratch(rows, chans):
    return pltpu.VMEM((chans // LANES, rows, LANES), f32)


def rms(wide):
    return wide * lax.rsqrt(jnp.mean(wide * wide, axis=-1, keepdims=True) + 1e-06)


def divided(at, by):
    if by & (by - 1) == 0:
        bits = by.bit_length() - 1
        return at >> bits, at & (by - 1)
    return lax.div(at, jnp.int32(by)), lax.rem(at, jnp.int32(by))


def pack_kernel(group, video, *refs):
    out, local, wide, sems = refs
    count, rows, cols, chans = video.shape
    lines = count * rows
    stride = cols + 2 * EDGE
    own = cols // group
    span = own + 2
    copies = []
    for at in range(lines):
        place = (at // rows, at % rows)
        copy = pltpu.make_async_copy(video.at[place], local.at[place], sems.at[at])
        copy.start()
        copies.append(copy)
    nothing = jnp.zeros((EDGE, chans), f32)
    for at in range(lines):
        fill(wide, at * stride, nothing)
        fill(wide, at * stride + EDGE + cols, nothing)
    for at, copy in enumerate(copies):
        copy.wait()
        fill(wide, at * stride + EDGE, local[at // rows, at % rows].astype(f32))
    together = 16 // lines
    for k in range(group):
        start = k * own + EDGE - 1
        for w in range(0, span, together):
            tile = jnp.concatenate([get(wide, start + w + i, lines, stride) for i in range(together)], axis=0)
            out[k, pl.ds(w * lines, 16), :] = tile.astype(bf16)


def frames_of(ref, w, r, count, rows, sources, step):
    return [get(ref, w * count * rows + t * rows + r, sources, step) for t in range(count)]


def shifted(now):
    count = len(now)
    sources, chans = now[0].shape
    first = lax.broadcasted_iota(jnp.int32, (sources, chans), 0) == 0
    past = [jnp.where(first, 0.0, pltpu.roll(x, 1, 0)) for x in now]
    ordered = past + now
    taps = []
    for a in range(TAPS):
        start = count - (TAPS - 1 - a)
        taps.append(jnp.concatenate(ordered[start : start + count], 0).astype(bf16))
    return jnp.concatenate(taps, axis=1)


def activated(wide):
    part = 0.5 * rms(wide)
    return part + part * jnp.tanh(part)


def depth(parts):
    return parts[0] if len(parts) == 1 else jnp.concatenate(parts, axis=-1)


def edge_kernel(count, rows, video, edge, vid):
    sources, step, chans = video.shape
    span = step // (count * rows)
    fill(vid, 0, video[...].reshape(sources * step, chans).astype(f32))
    lower = lax.axis_index("height") == 1
    for w in range(span):
        first, last = (frames_of(vid, w, r, count, rows, sources, step) for r in (0, rows - 1))
        edge[w] = shifted([activated(jnp.where(lower, x, y)) for x, y in zip(first, last)])


def fill_bias(bias, ids, frames, count):
    area = bias.shape[0]
    sources = frames // count

    def place_of(at):
        pixel, place = divided(at, frames)
        inner, source = divided(place, sources)
        frame = source * count + inner
        block = jnp.zeros(at.shape, jnp.int32)
        for s in range(frames):
            block = jnp.where(frame == s, ids[s], block)
        return pixel, frame, block

    row_p, row_t, row_b = place_of(lax.broadcasted_iota(jnp.int32, (area, area), 0))
    col_p, col_t, col_b = place_of(lax.broadcasted_iota(jnp.int32, (1, area), 1))
    permit = (row_p == col_p) & (col_t <= row_t) & (col_b >= row_b - 1)
    bias[...] = jnp.where(permit, 0.0, -1e30)


def shift_kernel(count, rows, video, ids_far, *refs):
    conv_weight, far, (total, bias, *near) = refs[0], refs[1:5], refs[5:11]
    vid, grid, ids, sems, ids_sem = refs[11:]
    ids_copy = pltpu.make_async_copy(ids_far, ids, ids_sem)
    ids_copy.start()
    others = [pltpu.make_async_copy(src, dst, sems.at[i]) for i, (src, dst) in enumerate(zip(far, near))]
    for copy in others:
        copy.start()
    sources, step, chans = video.shape
    span = step // (count * rows)
    own = span - 2
    frames = sources * count
    half = own // 2 if own % 2 == 0 else own
    fill(vid, 0, video[...].reshape(sources * step, chans).astype(f32))
    for w in range(span):
        for r in range(rows):
            now = frames_of(vid, w, r, count, rows, sources, step)
            grid[w, r] = shifted([activated(x) for x in now])
            if 1 <= w <= own:
                total[w - 1, r] = jnp.concatenate(now, 0)

    for b in range(TAPS):
        low, high = max(0, 1 - b), min(rows, rows + 1 - b)
        weight = jnp.concatenate([conv_weight[a, b, e] for e in range(TAPS) for a in range(TAPS)], axis=0)
        for w in range(0, own, half):
            window = depth([grid[w + e : w + e + half, low + b - 1 : high + b - 1] for e in range(TAPS)])
            window = window.reshape(half * (high - low) * frames, TAPS * TAPS * chans)
            part = jnp.dot(window, weight, preferred_element_type=f32)
            some = total.at[w : w + half, low:high]
            some[...] = some[...] + part.reshape(half, high - low, frames, chans)
    ids_copy.wait()
    fill_bias(bias, ids, frames, count)
    for copy in others:
        copy.wait()


def main_kernel(
    count, rows, group, edge, given, bias, conv_weight, w_query, w_key, w_value, w_output, *refs
):
    out, res = refs
    own, _, frames, chans = given.shape
    sources = frames // count
    lines = count * rows
    back = own * lines
    area = bias.shape[0]

    lower = lax.axis_index("height")
    b = (TAPS - 1) * (1 - lower)
    part = jnp.zeros((own * frames, chans), f32)
    for e in range(TAPS):
        window = edge[e : e + own].reshape(own * frames, TAPS * chans)
        weight = jnp.concatenate([conv_weight[a, b, e] for a in range(TAPS)], axis=0)
        part = part + jnp.dot(window, weight, preferred_element_type=f32)
    part = part.reshape(own, frames, chans)

    head_of = divided(lax.broadcasted_iota(jnp.int32, (area, LANES), 1), HD)[0]
    single = [jnp.where(head_of == h, 1.0, 0.0).astype(bf16) for h in range(LANES // HD)]
    scaled = [mask * jnp.asarray(HD ** (-0.5), bf16) for mask in single]

    lines_of = []
    for r in range(rows):
        row = given[:, r] + jnp.where(r == (rows - 1) * (1 - lower), part, 0.0)
        lines_of.append(row[:, None])
    hidden = jnp.concatenate(lines_of, axis=1).reshape(own * rows * frames, chans).astype(bf16).astype(f32)
    normed = rms(hidden).astype(bf16)
    weight = jnp.concatenate([w_query[...], w_key[...], w_value[...]], axis=1)
    projected = jnp.dot(normed, weight, preferred_element_type=f32).astype(bf16)
    query, keys, values = (projected[:, i * chans : (i + 1) * chans] for i in range(3))
    gone = []
    for at in range(0, own * rows * frames, area):
        attended = []
        for lane in range(0, chans, LANES):
            block = (slice(at, at + area), slice(lane, lane + LANES))
            queries = jnp.concatenate([query[block] * mask for mask in scaled], axis=0)
            scores = lax.dot_general(queries, keys[block], (((1,), (1,)), ((), ())), preferred_element_type=f32)
            weights = []
            for h in range(len(single)):
                score = scores[h * area : (h + 1) * area] + bias[...]
                weights.append(jnp.exp(score - jnp.max(score, axis=-1, keepdims=True)).astype(bf16))
            heads_values = jnp.concatenate(
                [jnp.concatenate([values[block] * mask, mask], axis=1) for mask in single], axis=0
            )
            mixed = jnp.dot(jnp.concatenate(weights, axis=1), heads_values, preferred_element_type=f32)
            attended.append((mixed[:, :LANES] / mixed[:, LANES:]).astype(bf16))
        gone.append(jnp.concatenate(attended, axis=1))
    encoded = hidden + jnp.dot(jnp.concatenate(gone, axis=0), w_output[...], preferred_element_type=f32)
    for w in range(own):
        for r in range(rows):
            for t in range(count):
                first = ((w * rows + r) * count + t + 1) * sources - group
                put(res, (t * rows + r) * own + w, group, back, encoded[first : first + group])
    done = jnp.concatenate([res[i] for i in range(res.shape[0])], axis=1)
    out[...] = done.astype(bf16).reshape(out.shape)


def exchanged(blocks):
    return lax.all_to_all(blocks, "tm", split_axis=0, concat_axis=0, tiled=True)


def per_device(outer, video, block_ids, conv_weight, w_query, w_key, w_value, w_output):
    count, rows, cols, chans = video.shape
    group = lax.axis_size("tm")
    own = cols // group
    span = own + 2
    lines = count * rows
    near = pl.BlockSpec(memory_space=pltpu.VMEM)
    far = pl.BlockSpec(memory_space=pltpu.HBM)
    params = pltpu.CompilerParams(vmem_limit_bytes=VMEM)
    in_far = functools.partial(pltpu.with_memory_space_constraint, memory_space=pltpu.HBM)
    weights = [in_far(x) for x in (w_query, w_key, w_value, w_output)]

    blocks = pl.pallas_call(
        functools.partial(pack_kernel, group),
        out_shape=jax.ShapeDtypeStruct((group, span * lines, chans), bf16),
        in_specs=[far],
        out_specs=near,
        scratch_shapes=[
            pltpu.VMEM(video.shape, bf16),
            scratch(lines * (cols + 2 * EDGE), chans),
            pltpu.SemaphoreType.DMA((lines,)),
        ],
        compiler_params=params,
        cost_estimate=pl.CostEstimate(flops=2000000000, transcendentals=0, bytes_accessed=1000000),
    )(in_far(video))
    piece = exchanged(blocks)
    ids = block_ids
    if outer > 1:
        before = lax.ppermute(piece, "outer", [(i, i + 1) for i in range(outer - 1)])
        piece = jnp.concatenate([before, piece], axis=0)
        ids = jnp.concatenate([jnp.full((group * count,), -2, jnp.int32), ids])
        ids = lax.dynamic_slice(ids, (lax.axis_index("outer") * group * count,), (2 * group * count,))
    sources = piece.shape[0]
    frames = sources * count
    stored = scratch(sources * span * lines, chans)
    edge = pl.pallas_call(
        functools.partial(edge_kernel, count, rows),
        out_shape=jax.ShapeDtypeStruct((span, frames, TAPS * chans), bf16),
        in_specs=[near],
        out_specs=near,
        scratch_shapes=[stored],
        compiler_params=params,
    )(piece)
    edge = lax.ppermute(edge, "height", [(0, 1), (1, 0)])
    several = max(n for n in range(1, own + 1) if own % n == 0 and (n == 1 or n * rows * frames <= LANES))
    area = several * rows * frames
    total, bias, *weights = pl.pallas_call(
        functools.partial(shift_kernel, count, rows),
        out_shape=[
            jax.ShapeDtypeStruct((own, rows, frames, chans), f32),
            jax.ShapeDtypeStruct((area, area), f32),
        ]
        + [jax.ShapeDtypeStruct(x.shape, bf16) for x in weights],
        in_specs=[near, far, near] + [far] * 4,
        out_specs=[near] * 6,
        scratch_shapes=[
            stored,
            pltpu.VMEM((span, rows, frames, TAPS * chans), bf16),
            pltpu.SMEM((frames,), jnp.int32),
            pltpu.SemaphoreType.DMA((4,)),
            pltpu.SemaphoreType.DMA(()),
        ],
        compiler_params=params,
    )(piece, in_far(ids), conv_weight, *weights)
    blocks = pl.pallas_call(
        functools.partial(main_kernel, count, rows, group),
        out_shape=jax.ShapeDtypeStruct((group, own * lines, chans), bf16),
        in_specs=[near] * 8,
        out_specs=near,
        scratch_shapes=[scratch(group * own * lines, chans)],
        compiler_params=params,
    )(edge, total, bias, conv_weight, *weights)
    returned = exchanged(blocks).reshape(group, lines, own, chans)
    return jnp.swapaxes(returned, 0, 1).reshape(video.shape)


def solution(mesh):
    parts, along, halves = (mesh.shape[a] for a in ("groups", "tm", "height"))

    def run(video, *rest):
        count = video.shape[0] // (parts * along)
        group = min(g for g in range(1, along + 1) if along % g == 0 and (g * count >= REACH or g == along))
        outer = along // group
        split = Mesh(
            np.asarray(mesh.devices).reshape(parts, outer, group, halves),
            ("groups", "outer", "tm", "height"),
        )
        spec = P(("groups", "outer", "tm"), "height", None, None)
        placed = (spec, P("groups"), P(), P(), P(), P(), P())
        return jax.shard_map(
            functools.partial(per_device, outer),
            mesh=split,
            in_specs=placed,
            out_specs=spec,
            check_vma=False,
        )(video, *rest)

    return run
```

```python
import functools

import jax
import jax.numpy as jnp
import numpy as np
from jax import lax
from jax.experimental import pallas as pl
from jax.experimental.pallas import tpu as pltpu
from jax.sharding import Mesh, PartitionSpec as P

HD = 64
BLOCK = 4
TAPS = 3
REACH = 2 * BLOCK - 1 + TAPS - 1
LANES = 128
EDGE = 8
VMEM = 28 * 2**20

bf16, f32 = jnp.bfloat16, jnp.float32


def get(ref, start, size, stride):
    return jnp.concatenate([ref[i, pl.ds(start, size, stride=stride), :] for i in range(ref.shape[0])], axis=1)


def put(ref, start, size, stride, value):
    for i in range(ref.shape[0]):
        ref[i, pl.ds(start, size, stride=stride), :] = value[:, i * LANES : (i + 1) * LANES]


def fill(ref, start, value):
    for i in range(ref.shape[0]):
        ref[i, pl.ds(start, value.shape[0]), :] = value[:, i * LANES : (i + 1) * LANES]


def scratch(rows, chans):
    return pltpu.VMEM((chans // LANES, rows, LANES), f32)


def rms(wide):
    return wide * lax.rsqrt(jnp.mean(wide * wide, axis=-1, keepdims=True) + 1e-06)


def divided(at, by):
    if by & (by - 1) == 0:
        bits = by.bit_length() - 1
        return at >> bits, at & (by - 1)
    return lax.div(at, jnp.int32(by)), lax.rem(at, jnp.int32(by))


def pack_kernel(group, video, *refs):
    out, local, wide, sems = refs
    count, rows, cols, chans = video.shape
    lines = count * rows
    stride = cols + 2 * EDGE
    own = cols // group
    span = own + 2
    copies = []
    for at in range(lines):
        place = (at // rows, at % rows)
        copy = pltpu.make_async_copy(video.at[place], local.at[place], sems.at[at])
        copy.start()
        copies.append(copy)
    nothing = jnp.zeros((EDGE, chans), f32)
    for at in range(lines):
        fill(wide, at * stride, nothing)
        fill(wide, at * stride + EDGE + cols, nothing)
    for at, copy in enumerate(copies):
        copy.wait()
        fill(wide, at * stride + EDGE, local[at // rows, at % rows].astype(f32))
    together = 16 // lines
    for k in range(group):
        start = k * own + EDGE - 1
        for w in range(0, span, together):
            tile = jnp.concatenate([get(wide, start + w + i, lines, stride) for i in range(together)], axis=0)
            out[k, pl.ds(w * lines, 16), :] = tile.astype(bf16)


def frames_of(ref, w, r, count, rows, sources, step):
    return [get(ref, w * count * rows + t * rows + r, sources, step) for t in range(count)]


def shifted(now):
    count = len(now)
    sources, chans = now[0].shape
    first = lax.broadcasted_iota(jnp.int32, (sources, chans), 0) == 0
    past = [jnp.where(first, 0.0, pltpu.roll(x, 1, 0)) for x in now]
    ordered = past + now
    taps = []
    for a in range(TAPS):
        start = count - (TAPS - 1 - a)
        taps.append(jnp.concatenate(ordered[start : start + count], 0).astype(bf16))
    return jnp.concatenate(taps, axis=1)


def activated(wide):
    part = 0.5 * rms(wide)
    return part + part * jnp.tanh(part)


def depth(parts):
    return parts[0] if len(parts) == 1 else jnp.concatenate(parts, axis=-1)


def edge_kernel(count, rows, video, edge, vid):
    sources, step, chans = video.shape
    span = step // (count * rows)
    fill(vid, 0, video[...].reshape(sources * step, chans).astype(f32))
    lower = lax.axis_index("height") == 1
    for w in range(span):
        first, last = (frames_of(vid, w, r, count, rows, sources, step) for r in (0, rows - 1))
        edge[w] = shifted([activated(jnp.where(lower, x, y)) for x, y in zip(first, last)])


def fill_bias(bias, ids, frames, count):
    area = bias.shape[0]
    sources = frames // count

    def place_of(at):
        pixel, place = divided(at, frames)
        inner, source = divided(place, sources)
        frame = source * count + inner
        block = jnp.zeros(at.shape, jnp.int32)
        for s in range(frames):
            block = jnp.where(frame == s, ids[s], block)
        return pixel, frame, block

    row_p, row_t, row_b = place_of(lax.broadcasted_iota(jnp.int32, (area, area), 0))
    col_p, col_t, col_b = place_of(lax.broadcasted_iota(jnp.int32, (1, area), 1))
    permit = (row_p == col_p) & (col_t <= row_t) & (col_b >= row_b - 1)
    bias[...] = jnp.where(permit, 0.0, -1e30)


def shift_kernel(count, rows, video, ids_far, *refs):
    conv_weight, far, (total, bias, *near) = refs[0], refs[1:5], refs[5:11]
    vid, grid, ids, sems, ids_sem = refs[11:]
    ids_copy = pltpu.make_async_copy(ids_far, ids, ids_sem)
    ids_copy.start()
    others = [pltpu.make_async_copy(src, dst, sems.at[i]) for i, (src, dst) in enumerate(zip(far, near))]
    for copy in others:
        copy.start()
    sources, step, chans = video.shape
    span = step // (count * rows)
    own = span - 2
    frames = sources * count
    half = own // 2 if own % 2 == 0 else own
    fill(vid, 0, video[...].reshape(sources * step, chans).astype(f32))
    for w in range(span):
        for r in range(rows):
            now = frames_of(vid, w, r, count, rows, sources, step)
            grid[w, r] = shifted([activated(x) for x in now])

    for b in (1, 0, 2):
        low, high = max(0, 1 - b), min(rows, rows + 1 - b)
        weight = jnp.concatenate([conv_weight[a, b, e] for e in range(TAPS) for a in range(TAPS)], axis=0)
        for w in range(0, own, half):
            window = depth([grid[w + e : w + e + half, low + b - 1 : high + b - 1] for e in range(TAPS)])
            window = window.reshape(half * (high - low) * frames, TAPS * TAPS * chans)
            part = jnp.dot(window, weight, preferred_element_type=f32)
            some = total.at[w : w + half, low:high]
            part = part.reshape(half, high - low, frames, chans)
            if b == 1:
                for i in range(half):
                    for r in range(rows):
                        now = frames_of(vid, w + i + 1, r, count, rows, sources, step)
                        total[w + i, r] = jnp.concatenate(now, 0) + part[i, r]
            else:
                some[...] = some[...] + part
    ids_copy.wait()
    fill_bias(bias, ids, frames, count)
    for copy in others:
        copy.wait()


def main_kernel(
    count, rows, group, edge, given, bias, conv_weight, w_query, w_key, w_value, w_output, *refs
):
    out, res = refs
    own, _, frames, chans = given.shape
    sources = frames // count
    lines = count * rows
    back = own * lines
    area = bias.shape[0]

    lower = lax.axis_index("height")
    b = (TAPS - 1) * (1 - lower)
    part = jnp.zeros((own * frames, chans), f32)
    for e in range(TAPS):
        window = edge[e : e + own].reshape(own * frames, TAPS * chans)
        weight = jnp.concatenate([conv_weight[a, b, e] for a in range(TAPS)], axis=0)
        part = part + jnp.dot(window, weight, preferred_element_type=f32)
    part = part.reshape(own, frames, chans)

    head_of = divided(lax.broadcasted_iota(jnp.int32, (area, LANES), 1), HD)[0]
    single = [jnp.where(head_of == h, 1.0, 0.0).astype(bf16) for h in range(LANES // HD)]
    scaled = [mask * jnp.asarray(HD ** (-0.5), bf16) for mask in single]

    lines_of = []
    for r in range(rows):
        row = given[:, r] + jnp.where(r == (rows - 1) * (1 - lower), part, 0.0)
        lines_of.append(row[:, None])
    hidden = jnp.concatenate(lines_of, axis=1).reshape(own * rows * frames, chans).astype(bf16).astype(f32)
    normed = rms(hidden).astype(bf16)
    weight = jnp.concatenate([w_query[...], w_key[...], w_value[...]], axis=1)
    projected = jnp.dot(normed, weight, preferred_element_type=f32).astype(bf16)
    query, keys, values = (projected[:, i * chans : (i + 1) * chans] for i in range(3))
    gone = []
    for at in range(0, own * rows * frames, area):
        attended = []
        for lane in range(0, chans, LANES):
            block = (slice(at, at + area), slice(lane, lane + LANES))
            queries = jnp.concatenate([query[block] * mask for mask in scaled], axis=0)
            scores = lax.dot_general(queries, keys[block], (((1,), (1,)), ((), ())), preferred_element_type=f32)
            weights = []
            for h in range(len(single)):
                score = scores[h * area : (h + 1) * area] + bias[...]
                weights.append(jnp.exp(score - jnp.max(score, axis=-1, keepdims=True)).astype(bf16))
            heads_values = jnp.concatenate(
                [jnp.concatenate([values[block] * mask, mask], axis=1) for mask in single], axis=0
            )
            mixed = jnp.dot(jnp.concatenate(weights, axis=1), heads_values, preferred_element_type=f32)
            attended.append((mixed[:, :LANES] / mixed[:, LANES:]).astype(bf16))
        gone.append(jnp.concatenate(attended, axis=1))
    encoded = hidden + jnp.dot(jnp.concatenate(gone, axis=0), w_output[...], preferred_element_type=f32)
    for w in range(own):
        for r in range(rows):
            for t in range(count):
                first = ((w * rows + r) * count + t + 1) * sources - group
                put(res, (t * rows + r) * own + w, group, back, encoded[first : first + group])
    done = jnp.concatenate([res[i] for i in range(res.shape[0])], axis=1)
    out[...] = done.astype(bf16).reshape(out.shape)


def exchanged(blocks):
    return lax.all_to_all(blocks, "tm", split_axis=0, concat_axis=0, tiled=True)


def per_device(outer, video, block_ids, conv_weight, w_query, w_key, w_value, w_output):
    count, rows, cols, chans = video.shape
    group = lax.axis_size("tm")
    own = cols // group
    span = own + 2
    lines = count * rows
    near = pl.BlockSpec(memory_space=pltpu.VMEM)
    far = pl.BlockSpec(memory_space=pltpu.HBM)
    params = pltpu.CompilerParams(vmem_limit_bytes=VMEM)
    in_far = functools.partial(pltpu.with_memory_space_constraint, memory_space=pltpu.HBM)
    weights = [in_far(x) for x in (w_query, w_key, w_value, w_output)]

    blocks = pl.pallas_call(
        functools.partial(pack_kernel, group),
        out_shape=jax.ShapeDtypeStruct((group, span * lines, chans), bf16),
        in_specs=[far],
        out_specs=near,
        scratch_shapes=[
            pltpu.VMEM(video.shape, bf16),
            scratch(lines * (cols + 2 * EDGE), chans),
            pltpu.SemaphoreType.DMA((lines,)),
        ],
        compiler_params=params,
        cost_estimate=pl.CostEstimate(flops=2000000000, transcendentals=0, bytes_accessed=1000000),
    )(in_far(video))
    piece = exchanged(blocks)
    ids = block_ids
    if outer > 1:
        before = lax.ppermute(piece, "outer", [(i, i + 1) for i in range(outer - 1)])
        piece = jnp.concatenate([before, piece], axis=0)
        ids = jnp.concatenate([jnp.full((group * count,), -2, jnp.int32), ids])
        ids = lax.dynamic_slice(ids, (lax.axis_index("outer") * group * count,), (2 * group * count,))
    sources = piece.shape[0]
    frames = sources * count
    stored = scratch(sources * span * lines, chans)
    edge = pl.pallas_call(
        functools.partial(edge_kernel, count, rows),
        out_shape=jax.ShapeDtypeStruct((span, frames, TAPS * chans), bf16),
        in_specs=[near],
        out_specs=near,
        scratch_shapes=[stored],
        compiler_params=params,
    )(piece)
    edge = lax.ppermute(edge, "height", [(0, 1), (1, 0)])
    several = max(n for n in range(1, own + 1) if own % n == 0 and (n == 1 or n * rows * frames <= LANES))
    area = several * rows * frames
    total, bias, *weights = pl.pallas_call(
        functools.partial(shift_kernel, count, rows),
        out_shape=[
            jax.ShapeDtypeStruct((own, rows, frames, chans), f32),
            jax.ShapeDtypeStruct((area, area), f32),
        ]
        + [jax.ShapeDtypeStruct(x.shape, bf16) for x in weights],
        in_specs=[near, far, near] + [far] * 4,
        out_specs=[near] * 6,
        scratch_shapes=[
            stored,
            pltpu.VMEM((span, rows, frames, TAPS * chans), bf16),
            pltpu.SMEM((frames,), jnp.int32),
            pltpu.SemaphoreType.DMA((4,)),
            pltpu.SemaphoreType.DMA(()),
        ],
        compiler_params=params,
    )(piece, in_far(ids), conv_weight, *weights)
    blocks = pl.pallas_call(
        functools.partial(main_kernel, count, rows, group),
        out_shape=jax.ShapeDtypeStruct((group, own * lines, chans), bf16),
        in_specs=[near] * 8,
        out_specs=near,
        scratch_shapes=[scratch(group * own * lines, chans)],
        compiler_params=params,
    )(edge, total, bias, conv_weight, *weights)
    returned = exchanged(blocks).reshape(group, lines, own, chans)
    return jnp.swapaxes(returned, 0, 1).reshape(video.shape)


def solution(mesh):
    parts, along, halves = (mesh.shape[a] for a in ("groups", "tm", "height"))

    def run(video, *rest):
        count = video.shape[0] // (parts * along)
        group = min(g for g in range(1, along + 1) if along % g == 0 and (g * count >= REACH or g == along))
        outer = along // group
        split = Mesh(
            np.asarray(mesh.devices).reshape(parts, outer, group, halves),
            ("groups", "outer", "tm", "height"),
        )
        spec = P(("groups", "outer", "tm"), "height", None, None)
        placed = (spec, P("groups"), P(), P(), P(), P(), P())
        return jax.shard_map(
            functools.partial(per_device, outer),
            mesh=split,
            in_specs=placed,
            out_specs=spec,
            check_vma=False,
        )(video, *rest)

    return run
```

```python
import functools

import jax
import jax.numpy as jnp
import numpy as np
from jax import lax
from jax.experimental import pallas as pl
from jax.experimental.pallas import tpu as pltpu
from jax.sharding import Mesh, PartitionSpec as P

HD = 64
BLOCK = 4
TAPS = 3
REACH = 2 * BLOCK - 1 + TAPS - 1
LANES = 128
EDGE = 8
VMEM = 28 * 2**20

bf16, f32 = jnp.bfloat16, jnp.float32


def get(ref, start, size, stride):
    return jnp.concatenate([ref[i, pl.ds(start, size, stride=stride), :] for i in range(ref.shape[0])], axis=1)


def put(ref, start, size, stride, value):
    for i in range(ref.shape[0]):
        ref[i, pl.ds(start, size, stride=stride), :] = value[:, i * LANES : (i + 1) * LANES]


def fill(ref, start, value):
    for i in range(ref.shape[0]):
        ref[i, pl.ds(start, value.shape[0]), :] = value[:, i * LANES : (i + 1) * LANES]


def scratch(rows, chans):
    return pltpu.VMEM((chans // LANES, rows, LANES), f32)


def rms(wide):
    return wide * lax.rsqrt(jnp.mean(wide * wide, axis=-1, keepdims=True) + 1e-06)


def divided(at, by):
    if by & (by - 1) == 0:
        bits = by.bit_length() - 1
        return at >> bits, at & (by - 1)
    return lax.div(at, jnp.int32(by)), lax.rem(at, jnp.int32(by))


def pack_kernel(group, video, *refs):
    out, local, wide, sems = refs
    count, rows, cols, chans = video.shape
    lines = count * rows
    stride = cols + 2 * EDGE
    own = cols // group
    span = own + 2
    copies = []
    for at in range(2 * lines):
        place = (at // 2 // rows, at // 2 % rows, pl.ds(at % 2 * (cols // 2), cols // 2))
        copy = pltpu.make_async_copy(video.at[place], local.at[place], sems.at[at])
        copy.start()
        copies.append(copy)
    nothing = jnp.zeros((EDGE, chans), f32)
    for at in range(lines):
        fill(wide, at * stride, nothing)
        fill(wide, at * stride + EDGE + cols, nothing)
    for at in range(lines):
        copies[2 * at].wait()
        copies[2 * at + 1].wait()
        fill(wide, at * stride + EDGE, local[at // rows, at % rows].astype(f32))
    together = 16 // lines
    for k in range(group):
        start = k * own + EDGE - 1
        for w in range(0, span, together):
            tile = jnp.concatenate([get(wide, start + w + i, lines, stride) for i in range(together)], axis=0)
            out[k, pl.ds(w * lines, 16), :] = tile.astype(bf16)


def frames_of(ref, w, r, count, rows, sources, step):
    return [get(ref, w * count * rows + t * rows + r, sources, step) for t in range(count)]


def shifted(now):
    count = len(now)
    sources, chans = now[0].shape
    first = lax.broadcasted_iota(jnp.int32, (sources, chans), 0) == 0
    past = [jnp.where(first, 0.0, pltpu.roll(x, 1, 0)) for x in now]
    ordered = past + now
    taps = []
    for a in range(TAPS):
        start = count - (TAPS - 1 - a)
        taps.append(jnp.concatenate(ordered[start : start + count], 0).astype(bf16))
    return jnp.concatenate(taps, axis=1)


def activated(wide):
    part = 0.5 * rms(wide)
    return part + part * jnp.tanh(part)


def depth(parts):
    return parts[0] if len(parts) == 1 else jnp.concatenate(parts, axis=-1)


def edge_kernel(count, rows, video, edge, vid):
    sources, step, chans = video.shape
    span = step // (count * rows)
    fill(vid, 0, video[...].reshape(sources * step, chans).astype(f32))
    lower = lax.axis_index("height") == 1
    for w in range(span):
        first, last = (frames_of(vid, w, r, count, rows, sources, step) for r in (0, rows - 1))
        edge[w] = shifted([activated(jnp.where(lower, x, y)) for x, y in zip(first, last)])


def fill_bias(bias, ids, frames, count):
    area = bias.shape[0]
    sources = frames // count

    def place_of(at):
        pixel, place = divided(at, frames)
        inner, source = divided(place, sources)
        frame = source * count + inner
        block = jnp.zeros(at.shape, jnp.int32)
        for s in range(frames):
            block = jnp.where(frame == s, ids[s], block)
        return pixel, frame, block

    row_p, row_t, row_b = place_of(lax.broadcasted_iota(jnp.int32, (area, area), 0))
    col_p, col_t, col_b = place_of(lax.broadcasted_iota(jnp.int32, (1, area), 1))
    permit = (row_p == col_p) & (col_t <= row_t) & (col_b >= row_b - 1)
    bias[...] = jnp.where(permit, 0.0, -1e30)


def shift_kernel(count, rows, video, ids_far, *refs):
    conv_weight, far, (total, bias, *near) = refs[0], refs[1:5], refs[5:11]
    vid, grid, ids, sems, ids_sem = refs[11:]
    ids_copy = pltpu.make_async_copy(ids_far, ids, ids_sem)
    ids_copy.start()
    others = [pltpu.make_async_copy(src, dst, sems.at[i]) for i, (src, dst) in enumerate(zip(far, near))]
    for copy in others:
        copy.start()
    sources, step, chans = video.shape
    span = step // (count * rows)
    own = span - 2
    frames = sources * count
    half = own // 2 if own % 2 == 0 else own
    fill(vid, 0, video[...].reshape(sources * step, chans).astype(f32))
    for w in range(span):
        for r in range(rows):
            now = frames_of(vid, w, r, count, rows, sources, step)
            grid[w, r] = shifted([activated(x) for x in now])
            if 1 <= w <= own:
                total[w - 1, r] = jnp.concatenate(now, 0)

    for b in range(TAPS):
        low, high = max(0, 1 - b), min(rows, rows + 1 - b)
        weight = jnp.concatenate([conv_weight[a, b, e] for e in range(TAPS) for a in range(TAPS)], axis=0)
        for w in range(0, own, half):
            window = depth([grid[w + e : w + e + half, low + b - 1 : high + b - 1] for e in range(TAPS)])
            window = window.reshape(half * (high - low) * frames, TAPS * TAPS * chans)
            part = jnp.dot(window, weight, preferred_element_type=f32)
            some = total.at[w : w + half, low:high]
            some[...] = some[...] + part.reshape(half, high - low, frames, chans)
    ids_copy.wait()
    fill_bias(bias, ids, frames, count)
    for copy in others:
        copy.wait()


def main_kernel(
    count, rows, group, edge, given, bias, conv_weight, w_query, w_key, w_value, w_output, *refs
):
    out, res = refs
    own, _, frames, chans = given.shape
    sources = frames // count
    lines = count * rows
    back = own * lines
    area = bias.shape[0]

    lower = lax.axis_index("height")
    b = (TAPS - 1) * (1 - lower)
    part = jnp.zeros((own * frames, chans), f32)
    for e in range(TAPS):
        window = edge[e : e + own].reshape(own * frames, TAPS * chans)
        weight = jnp.concatenate([conv_weight[a, b, e] for a in range(TAPS)], axis=0)
        part = part + jnp.dot(window, weight, preferred_element_type=f32)
    part = part.reshape(own, frames, chans)

    head_of = divided(lax.broadcasted_iota(jnp.int32, (area, LANES), 1), HD)[0]
    single = [jnp.where(head_of == h, 1.0, 0.0).astype(bf16) for h in range(LANES // HD)]
    scaled = [mask * jnp.asarray(HD ** (-0.5), bf16) for mask in single]

    lines_of = []
    for r in range(rows):
        row = given[:, r] + jnp.where(r == (rows - 1) * (1 - lower), part, 0.0)
        lines_of.append(row[:, None])
    hidden = jnp.concatenate(lines_of, axis=1).reshape(own * rows * frames, chans).astype(bf16).astype(f32)
    normed = rms(hidden).astype(bf16)
    weight = jnp.concatenate([w_query[...], w_key[...], w_value[...]], axis=1)
    projected = jnp.dot(normed, weight, preferred_element_type=f32).astype(bf16)
    query, keys, values = (projected[:, i * chans : (i + 1) * chans] for i in range(3))
    gone = []
    for at in range(0, own * rows * frames, area):
        attended = []
        for lane in range(0, chans, LANES):
            block = (slice(at, at + area), slice(lane, lane + LANES))
            queries = jnp.concatenate([query[block] * mask for mask in scaled], axis=0)
            scores = lax.dot_general(queries, keys[block], (((1,), (1,)), ((), ())), preferred_element_type=f32)
            weights = []
            for h in range(len(single)):
                score = scores[h * area : (h + 1) * area] + bias[...]
                weights.append(jnp.exp(score - jnp.max(score, axis=-1, keepdims=True)).astype(bf16))
            heads_values = jnp.concatenate(
                [jnp.concatenate([values[block] * mask, mask], axis=1) for mask in single], axis=0
            )
            mixed = jnp.dot(jnp.concatenate(weights, axis=1), heads_values, preferred_element_type=f32)
            attended.append((mixed[:, :LANES] / mixed[:, LANES:]).astype(bf16))
        gone.append(jnp.concatenate(attended, axis=1))
    encoded = hidden + jnp.dot(jnp.concatenate(gone, axis=0), w_output[...], preferred_element_type=f32)
    for w in range(own):
        for r in range(rows):
            for t in range(count):
                first = ((w * rows + r) * count + t + 1) * sources - group
                put(res, (t * rows + r) * own + w, group, back, encoded[first : first + group])
    done = jnp.concatenate([res[i] for i in range(res.shape[0])], axis=1)
    out[...] = done.astype(bf16).reshape(out.shape)


def exchanged(blocks):
    return lax.all_to_all(blocks, "tm", split_axis=0, concat_axis=0, tiled=True)


def per_device(outer, video, block_ids, conv_weight, w_query, w_key, w_value, w_output):
    count, rows, cols, chans = video.shape
    group = lax.axis_size("tm")
    own = cols // group
    span = own + 2
    lines = count * rows
    near = pl.BlockSpec(memory_space=pltpu.VMEM)
    far = pl.BlockSpec(memory_space=pltpu.HBM)
    params = pltpu.CompilerParams(vmem_limit_bytes=VMEM)
    in_far = functools.partial(pltpu.with_memory_space_constraint, memory_space=pltpu.HBM)
    weights = [in_far(x) for x in (w_query, w_key, w_value, w_output)]

    blocks = pl.pallas_call(
        functools.partial(pack_kernel, group),
        out_shape=jax.ShapeDtypeStruct((group, span * lines, chans), bf16),
        in_specs=[far],
        out_specs=near,
        scratch_shapes=[
            pltpu.VMEM(video.shape, bf16),
            scratch(lines * (cols + 2 * EDGE), chans),
            pltpu.SemaphoreType.DMA((2 * lines,)),
        ],
        compiler_params=params,
        cost_estimate=pl.CostEstimate(flops=2000000000, transcendentals=0, bytes_accessed=1000000),
    )(in_far(video))
    piece = exchanged(blocks)
    ids = block_ids
    if outer > 1:
        before = lax.ppermute(piece, "outer", [(i, i + 1) for i in range(outer - 1)])
        piece = jnp.concatenate([before, piece], axis=0)
        ids = jnp.concatenate([jnp.full((group * count,), -2, jnp.int32), ids])
        ids = lax.dynamic_slice(ids, (lax.axis_index("outer") * group * count,), (2 * group * count,))
    sources = piece.shape[0]
    frames = sources * count
    stored = scratch(sources * span * lines, chans)
    edge = pl.pallas_call(
        functools.partial(edge_kernel, count, rows),
        out_shape=jax.ShapeDtypeStruct((span, frames, TAPS * chans), bf16),
        in_specs=[near],
        out_specs=near,
        scratch_shapes=[stored],
        compiler_params=params,
    )(piece)
    edge = lax.ppermute(edge, "height", [(0, 1), (1, 0)])
    several = max(n for n in range(1, own + 1) if own % n == 0 and (n == 1 or n * rows * frames <= LANES))
    area = several * rows * frames
    total, bias, *weights = pl.pallas_call(
        functools.partial(shift_kernel, count, rows),
        out_shape=[
            jax.ShapeDtypeStruct((own, rows, frames, chans), f32),
            jax.ShapeDtypeStruct((area, area), f32),
        ]
        + [jax.ShapeDtypeStruct(x.shape, bf16) for x in weights],
        in_specs=[near, far, near] + [far] * 4,
        out_specs=[near] * 6,
        scratch_shapes=[
            stored,
            pltpu.VMEM((span, rows, frames, TAPS * chans), bf16),
            pltpu.SMEM((frames,), jnp.int32),
            pltpu.SemaphoreType.DMA((4,)),
            pltpu.SemaphoreType.DMA(()),
        ],
        compiler_params=params,
    )(piece, in_far(ids), conv_weight, *weights)
    blocks = pl.pallas_call(
        functools.partial(main_kernel, count, rows, group),
        out_shape=jax.ShapeDtypeStruct((group, own * lines, chans), bf16),
        in_specs=[near] * 8,
        out_specs=near,
        scratch_shapes=[scratch(group * own * lines, chans)],
        compiler_params=params,
    )(edge, total, bias, conv_weight, *weights)
    returned = exchanged(blocks).reshape(group, lines, own, chans)
    return jnp.swapaxes(returned, 0, 1).reshape(video.shape)


def solution(mesh):
    parts, along, halves = (mesh.shape[a] for a in ("groups", "tm", "height"))

    def run(video, *rest):
        count = video.shape[0] // (parts * along)
        group = min(g for g in range(1, along + 1) if along % g == 0 and (g * count >= REACH or g == along))
        outer = along // group
        split = Mesh(
            np.asarray(mesh.devices).reshape(parts, outer, group, halves),
            ("groups", "outer", "tm", "height"),
        )
        spec = P(("groups", "outer", "tm"), "height", None, None)
        placed = (spec, P("groups"), P(), P(), P(), P(), P())
        return jax.shard_map(
            functools.partial(per_device, outer),
            mesh=split,
            in_specs=placed,
            out_specs=spec,
            check_vma=False,
        )(video, *rest)

    return run
```

```python
import functools

import jax
import jax.numpy as jnp
import numpy as np
from jax import lax
from jax.experimental import pallas as pl
from jax.experimental.pallas import tpu as pltpu
from jax.sharding import Mesh, PartitionSpec as P

HD = 64
BLOCK = 4
TAPS = 3
REACH = 2 * BLOCK - 1 + TAPS - 1
LANES = 128
EDGE = 8
VMEM = 28 * 2**20

bf16, f32 = jnp.bfloat16, jnp.float32


def get(ref, start, size, stride):
    return jnp.concatenate([ref[i, pl.ds(start, size, stride=stride), :] for i in range(ref.shape[0])], axis=1)


def put(ref, start, size, stride, value):
    for i in range(ref.shape[0]):
        ref[i, pl.ds(start, size, stride=stride), :] = value[:, i * LANES : (i + 1) * LANES]


def fill(ref, start, value):
    for i in range(ref.shape[0]):
        ref[i, pl.ds(start, value.shape[0]), :] = value[:, i * LANES : (i + 1) * LANES]


def scratch(rows, chans):
    return pltpu.VMEM((chans // LANES, rows, LANES), f32)


def rms(wide):
    return wide * lax.rsqrt(jnp.mean(wide * wide, axis=-1, keepdims=True) + 1e-06)


def divided(at, by):
    if by & (by - 1) == 0:
        bits = by.bit_length() - 1
        return at >> bits, at & (by - 1)
    return lax.div(at, jnp.int32(by)), lax.rem(at, jnp.int32(by))


def pack_kernel(group, video, *refs):
    out, local, wide, sems = refs
    count, rows, cols, chans = video.shape
    lines = count * rows
    stride = cols + 2 * EDGE
    own = cols // group
    span = own + 2
    copies = []
    for at in range(lines):
        place = (at // rows, at % rows)
        copy = pltpu.make_async_copy(video.at[place], local.at[place], sems.at[at])
        copy.start()
        copies.append(copy)
    nothing = jnp.zeros((EDGE, chans), f32)
    for at in range(lines):
        fill(wide, at * stride, nothing)
        fill(wide, at * stride + EDGE + cols, nothing)
    for at, copy in enumerate(copies):
        copy.wait()
        fill(wide, at * stride + EDGE, local[at // rows, at % rows].astype(f32))
    together = 16 // lines
    for k in range(group):
        start = k * own + EDGE - 1
        for w in range(0, span, together):
            tile = jnp.concatenate([get(wide, start + w + i, lines, stride) for i in range(together)], axis=0)
            out[k, pl.ds(w * lines, 16), :] = tile.astype(bf16)


def frames_of(ref, w, r, count, rows, sources, step):
    return [get(ref, w * count * rows + t * rows + r, sources, step) for t in range(count)]


def shifted(now):
    count = len(now)
    sources, chans = now[0].shape
    first = lax.broadcasted_iota(jnp.int32, (sources, chans), 0) == 0
    past = [jnp.where(first, 0.0, pltpu.roll(x, 1, 0)) for x in now]
    ordered = past + now
    taps = []
    for a in range(TAPS):
        start = count - (TAPS - 1 - a)
        taps.append(jnp.concatenate(ordered[start : start + count], 0).astype(bf16))
    return jnp.concatenate(taps, axis=1)


def activated(wide):
    part = 0.5 * rms(wide)
    return part + part * jnp.tanh(part)


def depth(parts):
    return parts[0] if len(parts) == 1 else jnp.concatenate(parts, axis=-1)


def edge_kernel(count, rows, video, edge, vid):
    sources, step, chans = video.shape
    span = step // (count * rows)
    fill(vid, 0, video[...].reshape(sources * step, chans).astype(f32))
    lower = lax.axis_index("height") == 1
    for w in range(span):
        first, last = (frames_of(vid, w, r, count, rows, sources, step) for r in (0, rows - 1))
        edge[w] = shifted([activated(jnp.where(lower, x, y)) for x, y in zip(first, last)])


def fill_bias(bias, ids, frames, count):
    area = bias.shape[0]
    sources = frames // count

    def place_of(at):
        pixel, place = divided(at, frames)
        inner, source = divided(place, sources)
        frame = source * count + inner
        block = jnp.zeros(at.shape, jnp.int32)
        for s in range(frames):
            block = jnp.where(frame == s, ids[s], block)
        return pixel, frame, block

    row_p, row_t, row_b = place_of(lax.broadcasted_iota(jnp.int32, (area, area), 0))
    col_p, col_t, col_b = place_of(lax.broadcasted_iota(jnp.int32, (1, area), 1))
    permit = (row_p == col_p) & (col_t <= row_t) & (col_b >= row_b - 1)
    bias[...] = jnp.where(permit, 0.0, -1e30)


def shift_kernel(count, rows, video, ids_far, *refs):
    conv_weight, far, (total, bias, *near) = refs[0], refs[1:5], refs[5:11]
    vid, grid, ids, sems, ids_sem = refs[11:]
    ids_copy = pltpu.make_async_copy(ids_far, ids, ids_sem)
    ids_copy.start()
    others = [pltpu.make_async_copy(src, dst, sems.at[i]) for i, (src, dst) in enumerate(zip(far, near))]
    for copy in others:
        copy.start()
    sources, step, chans = video.shape
    span = step // (count * rows)
    own = span - 2
    frames = sources * count
    half = own // 2 if own % 2 == 0 else own
    fill(vid, 0, video[...].reshape(sources * step, chans).astype(f32))
    for w in range(span):
        for r in range(rows):
            now = frames_of(vid, w, r, count, rows, sources, step)
            grid[w, r] = shifted([activated(x) for x in now])
            if 1 <= w <= own:
                total[w - 1, r] = jnp.concatenate(now, 0)

    for b in range(TAPS):
        low, high = max(0, 1 - b), min(rows, rows + 1 - b)
        weight = jnp.concatenate([conv_weight[a, b, e] for e in range(TAPS) for a in range(TAPS)], axis=0)
        for w in range(0, own, half):
            window = depth([grid[w + e : w + e + half, low + b - 1 : high + b - 1] for e in range(TAPS)])
            window = window.reshape(half * (high - low) * frames, TAPS * TAPS * chans)
            part = jnp.dot(window, weight, preferred_element_type=f32)
            some = total.at[w : w + half, low:high]
            some[...] = some[...] + part.reshape(half, high - low, frames, chans)
    ids_copy.wait()
    fill_bias(bias, ids, frames, count)
    for copy in others:
        copy.wait()


def main_kernel(
    count, rows, group, edge, given, bias, conv_weight, w_query, w_key, w_value, w_output, *refs
):
    out, res = refs
    own, _, frames, chans = given.shape
    sources = frames // count
    lines = count * rows
    back = own * lines
    area = bias.shape[0]

    lower = lax.axis_index("height")
    b = (TAPS - 1) * (1 - lower)
    part = jnp.zeros((own * frames, chans), f32)
    for e in range(TAPS):
        window = edge[e : e + own].reshape(own * frames, TAPS * chans)
        weight = jnp.concatenate([conv_weight[a, b, e] for a in range(TAPS)], axis=0)
        part = part + jnp.dot(window, weight, preferred_element_type=f32)
    part = part.reshape(own, frames, chans)

    head_of = divided(lax.broadcasted_iota(jnp.int32, (area, LANES), 1), HD)[0]
    single = [jnp.where(head_of == h, 1.0, 0.0).astype(bf16) for h in range(LANES // HD)]
    scaled = [mask * jnp.asarray(HD ** (-0.5), bf16) for mask in single]

    lines_of = []
    for r in range(rows):
        row = given[:, r]
        if r in (0, rows - 1):
            row = row + jnp.where(r == (rows - 1) * (1 - lower), part, 0.0)
        lines_of.append(row[:, None])
    hidden = jnp.concatenate(lines_of, axis=1).reshape(own * rows * frames, chans).astype(bf16).astype(f32)
    normed = rms(hidden).astype(bf16)
    weight = jnp.concatenate([w_query[...], w_key[...], w_value[...]], axis=1)
    projected = jnp.dot(normed, weight, preferred_element_type=f32).astype(bf16)
    query, keys, values = (projected[:, i * chans : (i + 1) * chans] for i in range(3))
    gone = []
    for at in range(0, own * rows * frames, area):
        attended = []
        for lane in range(0, chans, LANES):
            block = (slice(at, at + area), slice(lane, lane + LANES))
            queries = jnp.concatenate([query[block] * mask for mask in scaled], axis=0)
            scores = lax.dot_general(queries, keys[block], (((1,), (1,)), ((), ())), preferred_element_type=f32)
            weights = []
            for h in range(len(single)):
                score = scores[h * area : (h + 1) * area] + bias[...]
                weights.append(jnp.exp(score - jnp.max(score, axis=-1, keepdims=True)).astype(bf16))
            heads_values = jnp.concatenate(
                [jnp.concatenate([values[block] * mask, mask], axis=1) for mask in single], axis=0
            )
            mixed = jnp.dot(jnp.concatenate(weights, axis=1), heads_values, preferred_element_type=f32)
            attended.append((mixed[:, :LANES] / mixed[:, LANES:]).astype(bf16))
        gone.append(jnp.concatenate(attended, axis=1))
    encoded = hidden + jnp.dot(jnp.concatenate(gone, axis=0), w_output[...], preferred_element_type=f32)
    for w in range(own):
        for r in range(rows):
            for t in range(count):
                first = ((w * rows + r) * count + t + 1) * sources - group
                put(res, (t * rows + r) * own + w, group, back, encoded[first : first + group])
    done = jnp.concatenate([res[i] for i in range(res.shape[0])], axis=1)
    out[...] = done.astype(bf16).reshape(out.shape)


def exchanged(blocks):
    return lax.all_to_all(blocks, "tm", split_axis=0, concat_axis=0, tiled=True)


def per_device(outer, video, block_ids, conv_weight, w_query, w_key, w_value, w_output):
    count, rows, cols, chans = video.shape
    group = lax.axis_size("tm")
    own = cols // group
    span = own + 2
    lines = count * rows
    near = pl.BlockSpec(memory_space=pltpu.VMEM)
    far = pl.BlockSpec(memory_space=pltpu.HBM)
    params = pltpu.CompilerParams(vmem_limit_bytes=VMEM)
    in_far = functools.partial(pltpu.with_memory_space_constraint, memory_space=pltpu.HBM)
    weights = [in_far(x) for x in (w_query, w_key, w_value, w_output)]

    blocks = pl.pallas_call(
        functools.partial(pack_kernel, group),
        out_shape=jax.ShapeDtypeStruct((group, span * lines, chans), bf16),
        in_specs=[far],
        out_specs=near,
        scratch_shapes=[
            pltpu.VMEM(video.shape, bf16),
            scratch(lines * (cols + 2 * EDGE), chans),
            pltpu.SemaphoreType.DMA((lines,)),
        ],
        compiler_params=params,
        cost_estimate=pl.CostEstimate(flops=2000000000, transcendentals=0, bytes_accessed=1000000),
    )(in_far(video))
    piece = exchanged(blocks)
    ids = block_ids
    if outer > 1:
        before = lax.ppermute(piece, "outer", [(i, i + 1) for i in range(outer - 1)])
        piece = jnp.concatenate([before, piece], axis=0)
        ids = jnp.concatenate([jnp.full((group * count,), -2, jnp.int32), ids])
        ids = lax.dynamic_slice(ids, (lax.axis_index("outer") * group * count,), (2 * group * count,))
    sources = piece.shape[0]
    frames = sources * count
    stored = scratch(sources * span * lines, chans)
    edge = pl.pallas_call(
        functools.partial(edge_kernel, count, rows),
        out_shape=jax.ShapeDtypeStruct((span, frames, TAPS * chans), bf16),
        in_specs=[near],
        out_specs=near,
        scratch_shapes=[stored],
        compiler_params=params,
    )(piece)
    edge = lax.ppermute(edge, "height", [(0, 1), (1, 0)])
    several = max(n for n in range(1, own + 1) if own % n == 0 and (n == 1 or n * rows * frames <= LANES))
    area = several * rows * frames
    total, bias, *weights = pl.pallas_call(
        functools.partial(shift_kernel, count, rows),
        out_shape=[
            jax.ShapeDtypeStruct((own, rows, frames, chans), f32),
            jax.ShapeDtypeStruct((area, area), f32),
        ]
        + [jax.ShapeDtypeStruct(x.shape, bf16) for x in weights],
        in_specs=[near, far, near] + [far] * 4,
        out_specs=[near] * 6,
        scratch_shapes=[
            stored,
            pltpu.VMEM((span, rows, frames, TAPS * chans), bf16),
            pltpu.SMEM((frames,), jnp.int32),
            pltpu.SemaphoreType.DMA((4,)),
            pltpu.SemaphoreType.DMA(()),
        ],
        compiler_params=params,
    )(piece, in_far(ids), conv_weight, *weights)
    blocks = pl.pallas_call(
        functools.partial(main_kernel, count, rows, group),
        out_shape=jax.ShapeDtypeStruct((group, own * lines, chans), bf16),
        in_specs=[near] * 8,
        out_specs=near,
        scratch_shapes=[scratch(group * own * lines, chans)],
        compiler_params=params,
    )(edge, total, bias, conv_weight, *weights)
    returned = exchanged(blocks).reshape(group, lines, own, chans)
    return jnp.swapaxes(returned, 0, 1).reshape(video.shape)


def solution(mesh):
    parts, along, halves = (mesh.shape[a] for a in ("groups", "tm", "height"))

    def run(video, *rest):
        count = video.shape[0] // (parts * along)
        group = min(g for g in range(1, along + 1) if along % g == 0 and (g * count >= REACH or g == along))
        outer = along // group
        split = Mesh(
            np.asarray(mesh.devices).reshape(parts, outer, group, halves),
            ("groups", "outer", "tm", "height"),
        )
        spec = P(("groups", "outer", "tm"), "height", None, None)
        placed = (spec, P("groups"), P(), P(), P(), P(), P())
        return jax.shard_map(
            functools.partial(per_device, outer),
            mesh=split,
            in_specs=placed,
            out_specs=spec,
            check_vma=False,
        )(video, *rest)

    return run
```
